128 devices in a mesh: section: 2 (over core), dp: 4 (over z), ctx: 16 (over y, x).
Axes of the slice: x: 4, y: 4, z: 4, core: 2. Of those that a mesh axis runs over, the one named last changes fastest.
Arguments:
- boundary: bfloat16 [2, 2, 8192, 1536], P('section', None, ('dp', 'ctx')), may hold values from -6 to 6
- lengths: int32 [4, 2, 2], replicated, may hold values from 0 to 2048, as said below
- norm_gain: bfloat16 [2, 1536], P('section', 'dp'), may hold values from 0.5 to 1.5
- w_z: bfloat16 [2, 1536, 3072], P('section', 'dp'), may hold values from -0.15625 to 0.15625
- w_xbc: bfloat16 [2, 1536, 3328], P('section', 'dp'), may hold values from -0.15625 to 0.15625
- w_dt: bfloat16 [2, 1536, 48], P('section', 'dp'), may hold values from -0.15625 to 0.15625
- conv_weight: bfloat16 [2, 4, 3328], P('section', None, 'dp'), may hold values from -3 to 3
- conv_bias: bfloat16 [2, 3328], P('section', 'dp'), may hold values from -3 to 3
- dt_bias: float32 [2, 48], P('section')
- a_log: float32 [2, 48], P('section'), may hold values from -1 to 1
- d_skip: float32 [2, 48], P('section'), may hold values from 0.5 to 1.5
- gate_gain: bfloat16 [2, 3072], P('section', 'dp'), may hold values from 0.5 to 1.5
- w_out: bfloat16 [2, 3072, 1536], P('section', 'dp'), may hold values from -0.109375 to 0.109375
Outputs:
- boundary_out: float32 [2, 2, 8192, 1536], P('section', None, ('dp', 'ctx'))
- grad_norm_gain: float32 [2, 1536], P('section', ('dp', 'ctx'))
- grad_w_z: float32 [2, 1536, 3072], P('section', ('dp', 'ctx'))
- grad_w_xbc: float32 [2, 1536, 3328], P('section', ('dp', 'ctx'))
- grad_w_dt: float32 [2, 1536, 48], P('section', ('dp', 'ctx'))
- grad_conv_weight: float32 [2, 4, 3328], P('section', None, ('dp', 'ctx'))
- grad_conv_bias: float32 [2, 3328], P('section', ('dp', 'ctx'))
- grad_dt_bias: float32 [2, 48], P('section')
- grad_a_log: float32 [2, 48], P('section')
- grad_d_skip: float32 [2, 48], P('section')
- grad_gate_gain: float32 [2, 3072], P('section', ('dp', 'ctx'))
- grad_w_out: float32 [2, 3072, 1536], P('section', ('dp', 'ctx'))
The draws below stay inside these ranges and needn't reach their ends.
Inputs may be any that keep to these rules, and one draw needn't show every extreme that they name: `lengths`: of each group and micro-batch, sequence one padded to a multiple of 256 plus sequence two fit in 2048 positions; in one micro-batch of each group, drawn from the seed, sequence one has all 2048 positions and sequence two is empty; otherwise both are at least 1 long.
All inputs are finite; a program needn't handle non-finite values.
Results may differ from the reference program's by a relative error of at most 0.013.
Values may be sent and summed in bfloat16 or wider, within the bound.
No kernel may reach another device: no remote copies, remote signals or barrier semaphores. Data moves between devices by JAX's collectives and lax.ppermute only.
A program may use at most 320 MiB of HBM per device.

```python
import jax
import jax.numpy as jnp
from jax import lax

D = 1536
HEADS = 48
HEADDIM = 64
STATE = 128
KERNEL = 4
SPAN = 256
MICRO = 2
INNER = 3072
CONV_CH = 3328
CAP = 2048
TOKENS = 8192
N_SECTION = 2
N_DP = 4


def draw_lengths(key, part):
    key = jax.random.fold_in(key, 11)
    key_long, key_first, key_second = jax.random.split(key, 3)
    long_micro = jax.random.randint(key_long, (N_DP,), 0, MICRO)
    first_len = jax.random.randint(key_first, (N_DP, MICRO), 1, CAP - SPAN + 1)
    padded = (first_len + SPAN - 1) // SPAN * SPAN
    room_left = CAP - padded
    second_len = jax.random.randint(key_second, (N_DP, MICRO), 1, room_left + 1)
    is_long = jnp.arange(MICRO)[None, :] == long_micro[:, None]
    first_len = jnp.where(is_long, CAP, first_len)
    second_len = jnp.where(is_long, 0, second_len)
    return jnp.stack([first_len, second_len], -1).astype(jnp.int32)


def step_bias(key, low_step, high_step):
    spread = jax.random.uniform(key, (N_SECTION, HEADS), jnp.float32, 0.0, 1.0)
    step = jnp.exp(jnp.log(low_step) + spread * (jnp.log(high_step) - jnp.log(low_step)))
    return jnp.log(jnp.expm1(step))


def draw_dt_bias(key, part):
    key = jax.random.fold_in(key, 7)
    return step_bias(key, 0.2 / CAP, 0.1)


def block_scale(rng, extent, cuts, low, top_value):
    def one(dim, blocks):
        draws = jax.random.uniform(jax.random.fold_in(jax.random.fold_in(rng, 6), dim), (blocks,), jnp.float32, low / len(cuts), top_value / len(cuts))
        return jnp.repeat(jnp.exp(draws), extent[dim] // blocks).reshape((-1,) + (1,) * (len(extent) - dim - 1))

    loudness = one(*cuts[0])
    for cut in cuts[1:]:
        loudness = loudness * one(*cut)
    return loudness


def gaussian(own_key, extent, scale, bound, cuts=(), kind=jnp.bfloat16):
    loudness = block_scale(own_key, extent, cuts, -0.22, 0.18) if cuts else 1.0
    array = jax.random.normal(own_key, extent, jnp.float32) * scale * loudness
    return jnp.minimum(jnp.maximum(array, -bound), bound).astype(kind)


def setup_inputs(seed: int = 0) -> dict:
    seeds = jax.random.split(jax.random.key(seed), 14)
    boundary = gaussian(seeds[0], (2, MICRO, TOKENS, D), 1.0, 6.0, ((0, 2), (2, 64)))
    lengths = draw_lengths(jax.random.fold_in(seeds[13], 71), 0)
    norm_gain = jnp.clip(1.0 + 0.1 * jax.random.normal(seeds[2], (N_SECTION, D), jnp.float32), 0.5, 1.5).astype(jnp.bfloat16)
    w_z = gaussian(seeds[3], (N_SECTION, D, INNER), D ** -0.5, 0.15625, ((0, 2), (1, 4)))
    w_xbc = gaussian(seeds[4], (N_SECTION, D, CONV_CH), D ** -0.5, 0.15625, ((0, 2), (1, 4)))
    w_dt = gaussian(seeds[5], (N_SECTION, D, HEADS), D ** -0.5, 0.15625, ((0, 2), (1, 4)))
    conv_weight = gaussian(seeds[6], (N_SECTION, KERNEL, CONV_CH), KERNEL ** -0.5, 3.0, ((0, 2), (2, 4)))
    conv_bias = gaussian(seeds[7], (N_SECTION, CONV_CH), 0.5, 3.0, ((0, 2), (1, 4)))
    dt_bias = draw_dt_bias(jax.random.fold_in(seeds[13], 71), 0)
    a_log = jnp.clip(jax.random.uniform(seeds[9], (N_SECTION, HEADS), jnp.float32, -1.0, 1.0) * block_scale(seeds[9], (N_SECTION, HEADS), ((0, 2),), -0.4, 0.0), -1.0, 1.0)
    d_skip = jnp.clip(1.0 + 0.1 * jax.random.normal(seeds[10], (N_SECTION, HEADS), jnp.float32), 0.5, 1.5)
    gate_gain = jnp.clip(1.0 + 0.1 * jax.random.normal(seeds[11], (N_SECTION, INNER), jnp.float32), 0.5, 1.5).astype(jnp.bfloat16)
    w_out = gaussian(seeds[12], (N_SECTION, INNER, D), INNER ** -0.5, 0.109375, ((0, 2), (1, 4)))
    return {"boundary": boundary, "lengths": lengths, "norm_gain": norm_gain, "w_z": w_z, "w_xbc": w_xbc, "w_dt": w_dt, "conv_weight": conv_weight, "conv_bias": conv_bias, "dt_bias": dt_bias, "a_log": a_log, "d_skip": d_skip, "gate_gain": gate_gain, "w_out": w_out}


@jax.custom_vjp
def low(v):
    return lax.optimization_barrier(v.astype(jnp.bfloat16)).astype(jnp.float32)

@jax.custom_vjp
def low_back(v):
    return v

def low_keep(v):
    return (low(v), None)

def low_pass(kept, grad):
    return (grad,)

def back_keep(v):
    return (v, None)

def back_low(kept, grad):
    return (low(grad),)
low.defvjp(low_keep, low_pass)
low_back.defvjp(back_keep, back_low)
EPSILON = 1e-05
PRECISE = lax.Precision.HIGHEST

def rms_scale(values, gain_vec):
    return values * lax.rsqrt(lax.optimization_barrier(jnp.mean(values * values, axis=-1, keepdims=True)) + EPSILON) * gain_vec

def token_info(length_pair, row_count, offset):
    position = offset + jnp.arange(row_count, dtype=jnp.int32)
    first_len = length_pair[0]
    second_len = length_pair[1]
    padded = (first_len + SPAN - 1) // SPAN * SPAN
    in_second = position >= padded
    within = jnp.where(in_second, position - padded, position)
    usable = jnp.where(in_second, within < second_len, within < first_len)
    return (within, usable.astype(jnp.float32), (within == 0).astype(jnp.int32))

def mixer_inputs(extended, rate_in, conv_w, conv_b, dt_b, a_rate, within, usable):
    row_count = rate_in.shape[0]
    reach_back = conv_w.shape[0] - 1
    conv_sum = conv_b[None, :]
    for tap_index in range(reach_back + 1):
        allowed = (within >= reach_back - tap_index).astype(extended.dtype)
        conv_sum = conv_sum + conv_w[tap_index][None, :] * extended[tap_index:tap_index + row_count] * allowed[:, None]
    activated = jax.nn.silu(conv_sum)
    inner_width = HEADS * HEADDIM
    head_in = activated[:, :inner_width].reshape(row_count, HEADS, HEADDIM)
    b_proj = activated[:, inner_width:inner_width + STATE]
    c_proj = activated[:, inner_width + STATE:]
    dt_step = usable[:, None] * jax.nn.softplus(rate_in + dt_b[None, :])
    log_decay = dt_step * (-jnp.exp(a_rate))[None, :]
    return (head_in, b_proj, c_proj, dt_step, log_decay)

def ssd_output(head_in, b_proj, c_proj, dt_step, log_decay, starts, state_in):
    row_count = head_in.shape[0]
    cum_decay = jnp.cumsum(log_decay, axis=0)
    segment = jnp.cumsum(starts)
    row_index = jnp.arange(row_count, dtype=jnp.int32)
    visible = (row_index[:, None] >= row_index[None, :]) & (segment[:, None] == segment[None, :])
    gaps = cum_decay[:, None, :] - cum_decay[None, :, :]
    decay_mat = jnp.exp(jnp.where(visible[:, :, None], gaps, -1e+30))
    scores = jnp.dot(c_proj, b_proj.T, precision=PRECISE)
    weights = decay_mat * scores[:, :, None] * dt_step[None, :, :]
    inside = jnp.einsum('ijh,jhp->ihp', weights, head_in, precision=PRECISE)
    entering = jnp.exp(cum_decay) * (segment == 0).astype(cum_decay.dtype)[:, None]
    carried = jnp.einsum('hpn,in->ihp', state_in, c_proj, precision=PRECISE)
    return inside + entering[:, :, None] * carried

def ssd_state(head_in, b_proj, dt_step, log_decay, starts):
    cum_decay = jnp.cumsum(log_decay, axis=0)
    segment = jnp.cumsum(starts)
    final_seg = segment[-1]
    tail_decay = jnp.exp(cum_decay[-1][None, :] - cum_decay) * (segment == final_seg).astype(cum_decay.dtype)[:, None]
    fresh_part = jnp.einsum('jh,jhp,jn->hpn', tail_decay * dt_step, head_in, b_proj, precision=PRECISE)
    damping = jnp.exp(cum_decay[-1]) * (final_seg == 0).astype(cum_decay.dtype)
    return (damping, fresh_part)

def gate_norm(y_heads, head_in, skip_vec, gate_in, gain_vec):
    row_count = y_heads.shape[0]
    joined = (y_heads + skip_vec[None, :, None] * head_in).reshape(row_count, HEADS * HEADDIM)
    return rms_scale(joined * jax.nn.silu(gate_in), gain_vec)

def run_layer(hidden, layer_params, info):
    norm_g, weight_z, weight_xbc, weight_dt, conv_w, conv_b, dt_b, a_rate, skip_vec, gain_two, weight_out = layer_params
    within, usable, starts = info
    normed = low(rms_scale(hidden, norm_g))
    gate_in = low_back(jnp.dot(normed, weight_z, precision=PRECISE))
    mixed_in = low(low_back(jnp.dot(normed, weight_xbc, precision=PRECISE)))
    rate_in = low_back(jnp.dot(normed, weight_dt, precision=PRECISE))
    reach_back = KERNEL - 1
    extended = jnp.concatenate([jnp.zeros((reach_back, mixed_in.shape[1]), mixed_in.dtype), mixed_in], 0)
    head_in, b_proj, c_proj, dt_step, log_decay = mixer_inputs(extended, rate_in, conv_w, conv_b, dt_b, a_rate, within, usable)
    blocks = hidden.shape[0] // SPAN

    def to_blocks(values):
        return values.reshape((blocks, SPAN) + values.shape[1:])

    def advance(carry_state, pieces):
        part_x, part_b, part_c, part_dt, part_log, part_start = pieces
        y_part = ssd_output(part_x, part_b, part_c, part_dt, part_log, part_start, carry_state)
        damping, fresh_part = ssd_state(part_x, part_b, part_dt, part_log, part_start)
        return (damping[:, None, None] * carry_state + fresh_part, y_part)
    zero_state = jnp.zeros((HEADS, HEADDIM, STATE), hidden.dtype)
    _, y_blocks = lax.scan(jax.checkpoint(advance), zero_state, (to_blocks(head_in), to_blocks(b_proj), to_blocks(c_proj), to_blocks(dt_step), to_blocks(log_decay), to_blocks(starts)))
    y_heads = y_blocks.reshape(head_in.shape)
    normed_two = low(gate_norm(y_heads, head_in, skip_vec, gate_in, gain_two))
    branch = low_back(jnp.dot(normed_two, weight_out, precision=PRECISE))
    return hidden + usable[:, None] * branch

def reference(boundary, lengths, norm_gain, w_z, w_xbc, w_dt, conv_weight, conv_bias, dt_bias, a_log, d_skip, gate_gain, w_out):
    params = tuple((p.astype(jnp.float32) for p in (norm_gain, w_z, w_xbc, w_dt, conv_weight, conv_bias, dt_bias, a_log, d_skip, gate_gain, w_out)))
    inputs = boundary[0].astype(jnp.float32).reshape(MICRO * N_DP, CAP, D)
    cotangent = boundary[1].astype(jnp.float32).reshape(MICRO * N_DP, CAP, D)
    pairs = jnp.transpose(lengths, (1, 0, 2)).reshape(MICRO * N_DP, 2)

    def whole_net(values, weight_set):

        def one_stream(item):
            stream, length_pair = item
            info = token_info(length_pair, CAP, 0)
            hidden = stream
            for layer_index in range(N_SECTION):
                hidden = run_layer(hidden, tuple((w[layer_index] for w in weight_set)), info)
                if layer_index + 1 < N_SECTION:
                    hidden = low(low_back(hidden))
            return hidden
        return lax.map(jax.checkpoint(one_stream), (values, pairs))
    outputs, pull_back = jax.vjp(whole_net, inputs, params)
    d_inputs, d_params = pull_back(cotangent)
    top = jnp.stack([d_inputs.reshape(MICRO, TOKENS, D), outputs.reshape(MICRO, TOKENS, D)])
    return (top, d_params[0], d_params[1], d_params[2], d_params[3], d_params[4], d_params[5], d_params[6], d_params[7], d_params[8], d_params[9], d_params[10])
```

```python
import functools

import jax
import jax.numpy as jnp
from jax import lax
from jax.experimental import pallas as pl
from jax.experimental.pallas import tpu as pltpu
from jax.sharding import PartitionSpec as P

HEADS = 48
HEADDIM = 64
STATE = 128
KERNEL = 4
SPAN = 256
MICRO = 2
WIDTH = 1536
INNER = 3072
CONV_CH = 3328
LANES = 128
GROUPS = 8
OWN = HEADS // GROUPS
BLOCK = OWN * HEADDIM
ROWS = 256
HALF = 128
PACKED = CONV_CH + LANES
EPSILON = 1e-05
PRECISE = lax.Precision.HIGHEST
F32 = jnp.float32
BF16 = jnp.bfloat16
VMEM_LIMIT = 56 * 1024 * 1024


def params(**more):
    return pltpu.CompilerParams(vmem_limit_bytes=VMEM_LIMIT, **more)


def whole(shape):
    return pl.BlockSpec(shape, lambda *_: (0,) * len(shape))


def columns(rows, width):
    return pl.BlockSpec((rows, width), lambda g: (0, g))


def grouped(rows):
    return pl.BlockSpec((1, rows, BLOCK), lambda g: (g, 0, 0))


SMEM = pl.BlockSpec(memory_space=pltpu.SMEM)
ANYWHERE = pl.BlockSpec(memory_space=pl.ANY)


def shape(dims, kind=F32):
    return jax.ShapeDtypeStruct(dims, kind)


def dot(a, b):
    return jnp.dot(a, b, preferred_element_type=F32)


def dot_nt(a, b):
    return lax.dot_general(a, b, (((1,), (1,)), ((), ())), preferred_element_type=F32)


def exact_dot(a, b):
    return jnp.dot(a, b, precision=PRECISE, preferred_element_type=F32)


def lane_of(dims):
    return lax.broadcasted_iota(jnp.int32, dims, len(dims) - 1)


def row_of(dims):
    return lax.broadcasted_iota(jnp.int32, dims, len(dims) - 2)


def sigmoid(v):
    return 1.0 / (1.0 + jnp.exp(-v))


def softplus(v):
    return jnp.maximum(v, 0.0) + jnp.log1p(jnp.exp(-jnp.abs(v)))


def rolled(values, g):
    return pltpu.roll(values, lax.rem(LANES - 8 * g, LANES), axis=1)


def pair_lanes(values, p):
    low = lane_of((values.shape[0], LANES)) < HEADDIM
    return jnp.where(low, values[:, 2 * p : 2 * p + 1], values[:, 2 * p + 1 : 2 * p + 2])


def spread(values):
    return jnp.concatenate([pair_lanes(values, p) for p in range(OWN // 2)], axis=1)


def head_sum_matrix(g):
    head = row_of((BLOCK, LANES)) // HEADDIM
    return (lane_of((BLOCK, LANES)) == head + 8 * g).astype(BF16)


def lower_triangle(strict=False):
    i, j = row_of((HALF, HALF)), lane_of((HALF, HALF))
    return ((i > j) if strict else (i >= j)).astype(F32)


def usable_rows(info):
    return (row_of((ROWS, 1)) < info[0]).astype(F32)


def half(values, q):
    return values[q * HALF : (q + 1) * HALF]


def copies_of(plan, refs, buffer, sems, info, part, sizes, by_rows):
    out = []
    for n, (which, index, row, count, place) in enumerate(plan(info)):
        source = refs[which] if index is None else refs[which].at[index]
        if by_rows:
            src = source.at[pl.ds(row, count)]
            dst = buffer.at[pl.ds(place, count)]
        else:
            cols = pl.ds(pl.multiple_of(part * sizes, LANES), sizes)
            src = source.at[pl.ds(row, count), cols]
            dst = buffer.at[pl.ds(place, count), cols]
        out.append(pltpu.make_async_copy(src, dst, sems.at[n, part]))
    return out


def whole_plan(rows):
    def plan(info):
        return [(0, None, 0, rows, 0)]

    return plan


def in_proj_body(plan, refs, info, h_ref, gain_ref, *rest):
    w_refs, (normed_ref, mixed_ref, rate_ref, buffer, sems) = rest[:refs], rest[refs:]
    parts = PACKED // 384

    def start(part, _):
        for c in copies_of(plan, w_refs, buffer, sems, info, part, 384, False):
            c.start()
        return 0

    lax.fori_loop(0, parts, start, 0)
    h = h_ref[...].astype(F32)
    scale = lax.rsqrt(jnp.mean(h * h, axis=1, keepdims=True) + EPSILON)
    normed_ref[...] = (h * scale * gain_ref[...]).astype(BF16)

    def one(part, _):
        for c in copies_of(plan, w_refs, buffer, sems, info, part, 384, False):
            c.wait()
        cols = pl.ds(pl.multiple_of(part * 384, LANES), 384)
        value = dot(normed_ref[...], buffer[:, cols])

        @pl.when(part < parts - 1)
        def _():
            mixed_ref[:, cols] = value.astype(BF16)

        @pl.when(part == parts - 1)
        def _():
            mixed_ref[:, CONV_CH - 256 :] = value[:, :256].astype(BF16)
            rate_ref[...] = value[:, 256:]

        return 0

    lax.fori_loop(0, parts, one, 0)


def in_proj(info, h, gain, weights, plan, count):
    return pl.pallas_call(
        functools.partial(in_proj_body, plan, len(weights)),
        out_shape=(shape((ROWS, WIDTH), BF16), shape((ROWS, CONV_CH), BF16), shape((ROWS, LANES))),
        in_specs=[SMEM, whole((ROWS, WIDTH)), whole((1, WIDTH))] + [ANYWHERE] * len(weights),
        out_specs=(whole((ROWS, WIDTH)), whole((ROWS, CONV_CH)), whole((ROWS, LANES))),
        scratch_shapes=[
            pltpu.VMEM((WIDTH, PACKED), BF16),
            pltpu.SemaphoreType.DMA((count, PACKED // 384)),
        ],
        compiler_params=params(),
        cost_estimate=pl.CostEstimate(
            flops=2 * ROWS * WIDTH * PACKED, bytes_accessed=14_000_000, transcendentals=0
        ),
        name="in_proj",
    )(info, h, gain, *weights)


def gate_proj_body(plan, refs, info, normed_ref, *rest):
    w_refs, (gate_ref, buffer, sems) = rest[:refs], rest[refs:]
    parts = INNER // 512

    def start(part, _):
        for c in copies_of(plan, w_refs, buffer, sems, info, part, 512, False):
            c.start()
        return 0

    lax.fori_loop(0, parts, start, 0)

    def one(part, _):
        for c in copies_of(plan, w_refs, buffer, sems, info, part, 512, False):
            c.wait()
        cols = pl.ds(pl.multiple_of(part * 512, LANES), 512)
        gate_ref[:, cols] = dot(normed_ref[...], buffer[:, cols])
        return 0

    lax.fori_loop(0, parts, one, 0)


def gate_proj(info, normed, weights, plan, count):
    return pl.pallas_call(
        functools.partial(gate_proj_body, plan, len(weights)),
        out_shape=shape((ROWS, INNER)),
        in_specs=[SMEM, whole((ROWS, WIDTH))] + [ANYWHERE] * len(weights),
        out_specs=whole((ROWS, INNER)),
        scratch_shapes=[
            pltpu.VMEM((WIDTH, INNER), BF16),
            pltpu.SemaphoreType.DMA((count, INNER // 512)),
        ],
        compiler_params=params(),
        cost_estimate=pl.CostEstimate(
            flops=2 * ROWS * WIDTH * INNER, bytes_accessed=14_000_000, transcendentals=0
        ),
        name="gate_proj",
    )(info, normed, *weights)


def conv_sum_of(values, halo, cpar, keep, ext):
    width = values.shape[1]
    ext[0:16, :width] = halo.astype(F32) * keep
    ext[16 : 16 + ROWS, :width] = values.astype(F32)
    total = cpar[4:5, :]
    for k in range(KERNEL):
        total = total + cpar[k : k + 1, :] * ext[13 + k : 13 + k + ROWS, :width]
    return total


def state_body(
    info, mixed, halo, cpar, bc, halo_bc, cpar_bc, rate, hpar,
    xa_ref, bca_ref, cum_ref, dt_ref, s0_ref, msg_ref, ext, bt, tail,
):
    g = pl.program_id(0)
    keep = info[1].astype(F32)

    @pl.when(g == 0)
    def _():
        total = conv_sum_of(bc[...], halo_bc[...], cpar_bc[...], keep, ext)
        active = total * sigmoid(total)
        bca_ref[...] = active
        bt[...] = active[:, :STATE].T.astype(BF16)
        dt = usable_rows(info) * softplus(rate[...] + hpar[0:1, :])
        log_decay = dt * -jnp.exp(hpar[1:2, :])
        dt_ref[...] = dt
        tri = lower_triangle()
        for q in range(2):
            rows = pl.ds(q * HALF, HALF)
            cum = exact_dot(tri, half(log_decay, q))
            cum_ref[rows, :] = cum
            tail[rows, :] = jnp.exp(cum[HALF - 1 :, :] - cum) * half(dt, q)

    total = conv_sum_of(mixed[...], halo[...], cpar[...], keep, ext)
    xa = total * sigmoid(total)
    xa_ref[...] = xa
    weighted = (xa * spread(rolled(tail[...], g))).astype(BF16)
    ends = rolled(cum_ref[...], g)
    end0, end1 = ends[HALF - 1 : HALF], ends[ROWS - 1 : ROWS]
    s0 = dot(bt[:, :HALF], half(weighted, 0))
    s1 = dot(bt[:, HALF:], half(weighted, 1))
    s0_ref[0] = s0
    msg_ref[0, :STATE, :] = (spread(jnp.exp(end1)) * s0 + s1).astype(BF16)
    damp = spread(jnp.exp(end0 + end1))
    high = damp.astype(BF16)
    low = (damp - high.astype(F32)).astype(BF16)
    row = row_of((16, BLOCK))
    msg_ref[0, STATE:, :] = jnp.where(row == 0, high.astype(F32), low.astype(F32)).astype(BF16)


def state_call(info, mixed, halo, cpar, rate, hpar):
    bc_at = INNER // 256
    return pl.pallas_call(
        state_body,
        grid=(GROUPS,),
        out_shape=(
            shape((ROWS, INNER)),
            shape((ROWS, 256)),
            shape((ROWS, LANES)),
            shape((ROWS, LANES)),
            shape((GROUPS, STATE, BLOCK)),
            shape((GROUPS, STATE + 16, BLOCK), BF16),
        ),
        in_specs=[
            SMEM,
            columns(ROWS, BLOCK),
            columns(16, BLOCK),
            columns(8, BLOCK),
            pl.BlockSpec((ROWS, 256), lambda g: (0, bc_at)),
            pl.BlockSpec((16, 256), lambda g: (0, bc_at)),
            pl.BlockSpec((8, 256), lambda g: (0, bc_at)),
            whole((ROWS, LANES)),
            whole((8, LANES)),
        ],
        out_specs=(
            columns(ROWS, BLOCK),
            whole((ROWS, 256)),
            whole((ROWS, LANES)),
            whole((ROWS, LANES)),
            grouped(STATE),
            grouped(STATE + 16),
        ),
        scratch_shapes=[
            pltpu.VMEM((ROWS + 32, BLOCK), F32),
            pltpu.VMEM((STATE, ROWS), BF16),
            pltpu.VMEM((ROWS, LANES), F32),
        ],
        compiler_params=params(),
        cost_estimate=pl.CostEstimate(
            flops=2 * ROWS * STATE * INNER, bytes_accessed=9_000_000, transcendentals=800_000
        ),
        name="conv_state",
    )(info, mixed, halo, cpar, mixed, halo, cpar, rate, hpar)


def inside_body(xa, bca, cum, dt, hpar, y_ref, cum_t, scores):
    g = pl.program_id(0)

    @pl.when(g == 0)
    def _():
        tri = lower_triangle()
        for q in range(2):
            b, c = half(bca[:, :STATE], q).astype(BF16), half(bca[:, STATE:], q).astype(BF16)
            scores[q] = dot_nt(c, b) * tri
            cum_t[:, q * HALF : (q + 1) * HALF] = half(cum[...], q).T

    cols = rolled(cum[...], g)
    rows = cum_t[pl.ds(pl.multiple_of(8 * g, 8), 8), :]
    steps = rolled(dt[...], g)
    skips = rolled(hpar[...], g)[2:3, :]
    low = lane_of((HALF, LANES)) < HEADDIM
    for q in range(2):
        for p in range(OWN // 2):
            lanes = slice(p * LANES, (p + 1) * LANES)
            x = xa[q * HALF : (q + 1) * HALF, lanes]
            xdt = x * pair_lanes(half(steps, q), p)
            both = jnp.concatenate([jnp.where(low, xdt, 0.0), jnp.where(low, 0.0, xdt)], axis=0)
            mats = []
            for i in (2 * p, 2 * p + 1):
                gap = half(cols, q)[:, i : i + 1] - rows[i : i + 1, q * HALF : (q + 1) * HALF]
                mats.append((jnp.exp(jnp.minimum(gap, 0.0)) * scores[q]).astype(BF16))
            y = dot(jnp.concatenate(mats, axis=1), both.astype(BF16))
            y_ref[q * HALF : (q + 1) * HALF, lanes] = y + x * pair_lanes(skips, p)


def inside_call(xa, bca, cum, dt, hpar):
    return pl.pallas_call(
        inside_body,
        grid=(GROUPS,),
        out_shape=shape((ROWS, INNER)),
        in_specs=[
            columns(ROWS, BLOCK),
            whole((ROWS, 256)),
            whole((ROWS, LANES)),
            whole((ROWS, LANES)),
            whole((8, LANES)),
        ],
        out_specs=columns(ROWS, BLOCK),
        scratch_shapes=[pltpu.VMEM((LANES, ROWS), F32), pltpu.VMEM((2, HALF, HALF), F32)],
        compiler_params=params(),
        cost_estimate=pl.CostEstimate(
            flops=4 * HEADS * HALF * HALF * LANES, bytes_accessed=6_500_000, transcendentals=1_600_000
        ),
        name="inside",
    )(xa, bca, cum, dt, hpar)


def scan_body(backward, info, msg, out_ref):
    carry = jnp.zeros((STATE, BLOCK), F32)
    for k in reversed(range(GROUPS)) if backward else range(GROUPS):
        keep = info[2 + k].astype(F32)
        if not backward:
            carry = carry * keep
        out_ref[k] = carry.astype(BF16)
        damp = msg[k, STATE : STATE + 1, :].astype(F32) + msg[k, STATE + 1 : STATE + 2, :].astype(F32)
        carry = damp * carry + msg[k, :STATE, :].astype(F32)
        if backward:
            carry = carry * keep


def scan_call(info, msg, backward):
    return pl.pallas_call(
        functools.partial(scan_body, backward),
        out_shape=shape((GROUPS, STATE, BLOCK), BF16),
        in_specs=[SMEM, whole((GROUPS, STATE + 16, BLOCK))],
        out_specs=whole((GROUPS, STATE, BLOCK)),
        compiler_params=params(),
        name="chunk_scan",
    )(info, msg)


def out_proj_body(
    plan, refs, info, y_in, bca, cum, hin, s0, gate, gain, h_ref, *rest,
):
    w_refs, (y_ref, n_ref, res_ref, buffer, sems, sums) = rest[:refs], rest[refs:]
    parts = WIDTH // 384

    def start(part, _):
        for c in copies_of(plan, w_refs, buffer, sems, info, part, 384, False):
            c.start()
        return 0

    lax.fori_loop(0, parts, start, 0)
    c_all = bca[:, STATE:].astype(BF16)
    grow = jnp.exp(cum[...])
    sums[...] = jnp.zeros((ROWS, LANES), F32)

    def group(g, _):
        lanes = pl.ds(pl.multiple_of(g * BLOCK, LANES), BLOCK)
        factor = rolled(grow, g)
        first = hin[g]
        second = spread(factor[HALF - 1 : HALF]) * first.astype(F32) + s0[g]
        carried = jnp.concatenate(
            [dot(half(c_all, 0), first), dot(half(c_all, 1), second.astype(BF16))], axis=0
        )
        y = y_in[:, lanes] + spread(factor) * carried
        y_ref[:, lanes] = y
        z = gate[:, lanes]
        gated = y * z * sigmoid(z)
        square = gated * gated
        sums[...] += sum(square[:, i * LANES : (i + 1) * LANES] for i in range(BLOCK // LANES))
        return 0

    lax.fori_loop(0, GROUPS, group, 0)
    scale = lax.rsqrt(jnp.sum(sums[...], axis=1, keepdims=True) / INNER + EPSILON)

    def norm(g, _):
        lanes = pl.ds(pl.multiple_of(g * BLOCK, LANES), BLOCK)
        z = gate[:, lanes]
        gated = y_ref[:, lanes] * z * sigmoid(z)
        n_ref[:, lanes] = (gated * scale * gain[:, lanes]).astype(BF16)
        return 0

    lax.fori_loop(0, GROUPS, norm, 0)
    usable = usable_rows(info)

    def one(part, _):
        for c in copies_of(plan, w_refs, buffer, sems, info, part, 384, False):
            c.wait()
        cols = pl.ds(pl.multiple_of(part * 384, LANES), 384)
        branch = dot(n_ref[...], buffer[:, cols])
        res_ref[:, cols] = h_ref[:, cols].astype(F32) + usable * branch
        return 0

    lax.fori_loop(0, parts, one, 0)


def out_proj(info, y_in, bca, cum, hin, s0, gate, gain, h, weights, plan, count):
    return pl.pallas_call(
        functools.partial(out_proj_body, plan, len(weights)),
        out_shape=(shape((ROWS, INNER)), shape((ROWS, INNER), BF16), shape((ROWS, WIDTH))),
        in_specs=[
            SMEM,
            whole((ROWS, INNER)),
            whole((ROWS, 256)),
            whole((ROWS, LANES)),
            whole((GROUPS, STATE, BLOCK)),
            whole((GROUPS, STATE, BLOCK)),
            whole((ROWS, INNER)),
            whole((1, INNER)),
            whole((ROWS, WIDTH)),
        ]
        + [ANYWHERE] * len(weights),
        out_specs=(whole((ROWS, INNER)), whole((ROWS, INNER)), whole((ROWS, WIDTH))),
        scratch_shapes=[
            pltpu.VMEM((INNER, WIDTH), BF16),
            pltpu.SemaphoreType.DMA((count, WIDTH // 384)),
            pltpu.VMEM((ROWS, LANES), F32),
        ],
        compiler_params=params(),
        cost_estimate=pl.CostEstimate(
            flops=2 * ROWS * WIDTH * INNER, bytes_accessed=26_000_000, transcendentals=1_600_000
        ),
        name="out_proj",
    )(info, y_in, bca, cum, hin, s0, gate, gain, h, *weights)


def gate_back_body(plan, refs, info, cot, y, gate, gain, *rest):
    w_refs, (bg_ref, dy_ref, dz_ref, dgain_ref, buffer, sems, dn, sums) = rest[:refs], rest[refs:]
    blocks = 4
    size = INNER // blocks

    for b in range(blocks):
        for c in copies_of(plan(b), w_refs, buffer, sems, info, b, None, True):
            c.start()
    bg_ref[...] = (usable_rows(info) * cot[...].astype(F32)).astype(BF16)
    sums[...] = jnp.zeros((2, ROWS, LANES), F32)
    for b in range(blocks):
        for c in copies_of(plan(b), w_refs, buffer, sems, info, b, None, True):
            c.wait()
        dn[:, b * size : (b + 1) * size] = dot_nt(bg_ref[...], buffer[b * size : (b + 1) * size, :])

        def first(i, _, b=b):
            lanes = pl.ds(pl.multiple_of(b * size + i * LANES, LANES), LANES)
            z = gate[:, lanes]
            gated = y[:, lanes] * z * sigmoid(z)
            sums[0] += gated * gated
            sums[1] += gated * dn[:, lanes] * gain[:, lanes]
            return 0

        lax.fori_loop(0, size // LANES, first, 0)
    scale = lax.rsqrt(jnp.sum(sums[0], axis=1, keepdims=True) / INNER + EPSILON)
    inner = jnp.sum(sums[1], axis=1, keepdims=True) * scale * scale * scale / INNER

    def second(i, _):
        lanes = pl.ds(pl.multiple_of(i * LANES, LANES), LANES)
        z = gate[:, lanes]
        sig = sigmoid(z)
        silu = z * sig
        y_here = y[:, lanes]
        gated = y_here * silu
        d_norm = dn[:, lanes]
        d_gated = scale * d_norm * gain[:, lanes] - gated * inner
        total = jnp.sum(d_norm * gated * scale, axis=0, keepdims=True)
        dgain_ref[:, lanes] = jnp.broadcast_to(total, (8, LANES))
        dy_ref[:, lanes] = (d_gated * silu).astype(BF16)
        dz_ref[:, lanes] = (d_gated * y_here * sig * (1.0 + z * (1.0 - sig))).astype(BF16)
        return 0

    lax.fori_loop(0, INNER // LANES, second, 0)


def gate_back(info, cot, y, gate, gain, weights, plan, count):
    return pl.pallas_call(
        functools.partial(gate_back_body, plan, len(weights)),
        out_shape=(
            shape((ROWS, WIDTH), BF16),
            shape((ROWS, INNER), BF16),
            shape((ROWS, INNER), BF16),
            shape((8, INNER)),
        ),
        in_specs=[
            SMEM,
            whole((ROWS, WIDTH)),
            whole((ROWS, INNER)),
            whole((ROWS, INNER)),
            whole((1, INNER)),
        ]
        + [ANYWHERE] * len(weights),
        out_specs=(
            whole((ROWS, WIDTH)),
            whole((ROWS, INNER)),
            whole((ROWS, INNER)),
            whole((8, INNER)),
        ),
        scratch_shapes=[
            pltpu.VMEM((INNER, WIDTH), BF16),
            pltpu.SemaphoreType.DMA((count, 4)),
            pltpu.VMEM((ROWS, INNER), F32),
            pltpu.VMEM((2, ROWS, LANES), F32),
        ],
        compiler_params=params(),
        cost_estimate=pl.CostEstimate(
            flops=2 * ROWS * WIDTH * INNER, bytes_accessed=20_000_000, transcendentals=1_600_000
        ),
        name="gate_back",
    )(info, cot, y, gate, gain, *weights)


def own_grad_body(dy, bca, cum, msg_in, own1_ref, msg_ref, ct, grow):
    g = pl.program_id(0)

    @pl.when(g == 0)
    def _():
        ct[...] = bca[:, STATE:].T.astype(BF16)
        grow[...] = jnp.exp(cum[...])

    factor = rolled(grow[...], g)
    weighted = (dy[...].astype(F32) * spread(factor)).astype(BF16)
    own0 = dot(ct[:, :HALF], half(weighted, 0))
    own1 = dot(ct[:, HALF:], half(weighted, 1))
    own1_ref[0] = own1
    msg_ref[0, :STATE, :] = (spread(factor[HALF - 1 : HALF]) * own1 + own0).astype(BF16)
    msg_ref[0, STATE:, :] = msg_in[0]


def own_grad(dy, bca, cum, msg):
    return pl.pallas_call(
        own_grad_body,
        grid=(GROUPS,),
        out_shape=(
            shape((GROUPS, STATE, BLOCK)),
            shape((GROUPS, STATE + 16, BLOCK), BF16),
        ),
        in_specs=[
            columns(ROWS, BLOCK),
            whole((ROWS, 256)),
            whole((ROWS, LANES)),
            pl.BlockSpec((1, 16, BLOCK), lambda g: (g, STATE // 16, 0)),
        ],
        out_specs=(grouped(STATE), grouped(STATE + 16)),
        scratch_shapes=[pltpu.VMEM((STATE, ROWS), BF16), pltpu.VMEM((ROWS, LANES), F32)],
        compiler_params=params(),
        cost_estimate=pl.CostEstimate(
            flops=2 * ROWS * STATE * INNER, bytes_accessed=5_000_000, transcendentals=0
        ),
        name="own_grad",
    )(dy, bca, cum, msg)


def inside_back_body(
    dy, xa, bca, cum, dt, hpar,
    dx_ref, dskip_ref, gsum_ref, u_ref, dbc_ref, cum_t, scores, dscores,
):
    g = pl.program_id(0)

    @pl.when(g == 0)
    def _():
        tri = lower_triangle()
        for q in range(2):
            b, c = half(bca[:, :STATE], q).astype(BF16), half(bca[:, STATE:], q).astype(BF16)
            scores[q] = dot_nt(b, c) * tri.T
            cum_t[:, q * HALF : (q + 1) * HALF] = half(cum[...], q).T
        dscores[...] = jnp.zeros((2, HALF, HALF), F32)
        u_ref[...] = jnp.zeros((ROWS, LANES), F32)

    cols = rolled(cum[...], g)
    rows = cum_t[pl.ds(pl.multiple_of(8 * g, 8), 8), :]
    steps = rolled(dt[...], g)
    skips = rolled(hpar[...], g)[2:3, :]
    low = lane_of((HALF, LANES)) < HEADDIM
    lane = lane_of((HALF, LANES))
    gsum_ref[...] = jnp.zeros((8, ROWS), F32)
    for q in range(2):
        here = slice(q * HALF, (q + 1) * HALF)
        u_here = u_ref[here, :]
        for p in range(OWN // 2):
            lanes = slice(p * LANES, (p + 1) * LANES)
            dy_pair = dy[here, lanes]
            x = xa[here, lanes]
            zero = jnp.zeros_like(dy_pair)
            both = jnp.concatenate(
                [jnp.where(low, dy_pair, zero), jnp.where(low, zero, dy_pair)], axis=0
            )
            dw = dot_nt(x.astype(BF16), both)
            mats = []
            for n, i in enumerate((2 * p, 2 * p + 1)):
                gap = rows[i : i + 1, here] - half(cols, q)[:, i : i + 1]
                decay = jnp.exp(jnp.minimum(gap, 0.0))
                step = half(steps, q)[:, i : i + 1]
                weight = decay * scores[q]
                mats.append(weight.astype(BF16))
                dw_here = dw[:, n * HALF : (n + 1) * HALF]
                dscores[q] += decay * dw_here * step
                direct = weight * dw_here
                total = jnp.sum(direct, axis=1, keepdims=True)
                u_here = jnp.where(lane == 8 * g + i, total, u_here)
                gsum_ref[i : i + 1, here] = jnp.sum(direct * step, axis=0, keepdims=True)
            dx = dot(jnp.concatenate(mats, axis=1), both)
            dy_wide = dy_pair.astype(F32)
            dx_ref[here, lanes] = dx * pair_lanes(half(steps, q), p) + dy_wide * pair_lanes(skips, p)
            skip_sum = jnp.sum(dy_wide * x, axis=0, keepdims=True)
            if q == 0:
                dskip_ref[:, lanes] = jnp.broadcast_to(skip_sum, (8, LANES))
            else:
                dskip_ref[:, lanes] += skip_sum
        u_ref[here, :] = u_here

    @pl.when(g == GROUPS - 1)
    def _():
        tri = lower_triangle()
        for q in range(2):
            b, c = half(bca[:, :STATE], q).astype(BF16), half(bca[:, STATE:], q).astype(BF16)
            ds_t = dscores[q] * tri.T
            dbc_ref[q * HALF : (q + 1) * HALF, :STATE] = dot(ds_t.astype(BF16), c)
            dbc_ref[q * HALF : (q + 1) * HALF, STATE:] = dot(ds_t.T.astype(BF16), b)


def inside_back(dy, xa, bca, cum, dt, hpar):
    return pl.pallas_call(
        inside_back_body,
        grid=(GROUPS,),
        out_shape=(
            shape((ROWS, INNER)),
            shape((8, INNER)),
            shape((8 * GROUPS, ROWS)),
            shape((ROWS, LANES)),
            shape((ROWS, 256)),
        ),
        in_specs=[
            columns(ROWS, BLOCK),
            columns(ROWS, BLOCK),
            whole((ROWS, 256)),
            whole((ROWS, LANES)),
            whole((ROWS, LANES)),
            whole((8, LANES)),
        ],
        out_specs=(
            columns(ROWS, BLOCK),
            columns(8, BLOCK),
            pl.BlockSpec((8, ROWS), lambda g: (g, 0)),
            whole((ROWS, LANES)),
            whole((ROWS, 256)),
        ),
        scratch_shapes=[
            pltpu.VMEM((LANES, ROWS), F32),
            pltpu.VMEM((2, HALF, HALF), F32),
            pltpu.VMEM((2, HALF, HALF), F32),
        ],
        compiler_params=params(),
        cost_estimate=pl.CostEstimate(
            flops=8 * HEADS * HALF * HALF * LANES, bytes_accessed=9_000_000, transcendentals=1_600_000
        ),
        name="inside_back",
    )(dy, xa, bca, cum, dt, hpar)


def conv_back(d_active, values, halo, cpar, keep, ext, ext_d):
    width = values.shape[1]
    total = conv_sum_of(values, halo, cpar, keep, ext)
    sig = sigmoid(total)
    d_sum = d_active * sig * (1.0 + total * (1.0 - sig))
    ext_d[0:16, :width] = jnp.zeros((16, width), F32)
    ext_d[16 : 16 + ROWS, :width] = d_sum
    ext_d[16 + ROWS :, :width] = jnp.zeros((16, width), F32)
    d_in = jnp.zeros((ROWS + 16, width), F32)
    for k in range(KERNEL):
        d_in = d_in + cpar[k : k + 1, :] * ext_d[3 - k : 3 - k + ROWS + 16, :width]
    row = row_of((8, width))
    d_par = jnp.where(row == 4, jnp.sum(d_sum, axis=0, keepdims=True), 0.0)
    for k in range(KERNEL):
        tap = jnp.sum(d_sum * ext[13 + k : 13 + k + ROWS, :width], axis=0, keepdims=True)
        d_par = jnp.where(row == k, tap, d_par)
    return d_in, d_par


def finish_body(
    info, xa, dxi, dy, mixed, halo, cpar, bc, halo_bc, cpar_bc, bca, cum, dt, rate, hpar, lam, hin, s0, own1, u, gsum, dbc,
    dmx_ref, dmbc_ref, tailx_ref, tailbc_ref, edgex_ref, edgebc_ref, dcx_ref, dcbc_ref, dhead_ref,
    ext, ext_d, grow, tail, v_sum, q_sum, end_sum, dbc_sum,
):
    g = pl.program_id(0)
    keep = info[1].astype(F32)

    @pl.when(g == 0)
    def _():
        grow[...] = jnp.exp(cum[...])
        for q in range(2):
            here = half(cum[...], q)
            tail[q * HALF : (q + 1) * HALF, :] = jnp.exp(here[HALF - 1 :, :] - here)
        v_sum[...] = jnp.zeros((ROWS, LANES), F32)
        q_sum[...] = jnp.zeros((ROWS, LANES), F32)
        end_sum[...] = jnp.zeros((16, LANES), F32)
        dbc_sum[...] = dbc[...]

    sums = head_sum_matrix(g)
    factor = rolled(grow[...], g)
    tails = rolled(tail[...], g)
    steps = rolled(dt[...], g)
    ends = [spread(factor[HALF - 1 : HALF]), spread(factor[ROWS - 1 : ROWS])]
    lam1 = lam[0].astype(F32)
    lams = [ends[1] * lam1 + own1[0], lam1]
    first = hin[0].astype(F32)
    states = [first, ends[0] * first + s0[0]]
    d_x = []
    for q in range(2):
        here = slice(q * HALF, (q + 1) * HALF)
        b, c = bca[here, :STATE].astype(BF16), bca[here, STATE:].astype(BF16)
        lam_q, state_q = lams[q].astype(BF16), states[q].astype(BF16)
        tail_wide = spread(half(tails, q))
        tail_step = tail_wide * spread(half(steps, q))
        x, dy_q = xa[here, :], dy[here, :].astype(F32)
        lb = dot(b, lam_q) * tail_wide
        d_x.append(dxi[here, :] + lb * spread(half(steps, q)))
        v_sum[here, :] += dot((x * lb).astype(BF16), sums)
        grow_wide = spread(half(factor, q))
        dy_grow = (dy_q * grow_wide).astype(BF16)
        carried = dot(c, state_q)
        q_sum[here, :] += dot((dy_q * grow_wide * carried).astype(BF16), sums)
        dbc_sum[here, :STATE] += dot_nt((x * tail_step).astype(BF16), lam_q)
        dbc_sum[here, STATE:] += dot_nt(dy_grow, state_q)
        last = jnp.sum(lams[q] * states[q], axis=0, keepdims=True) * ends[q]
        end_sum[8 * q : 8 * q + 8, :] += exact_dot(
            jnp.broadcast_to(last, (8, BLOCK)), sums.astype(F32)
        )
    d_in, d_par = conv_back(
        jnp.concatenate(d_x, axis=0), mixed[...], halo[...], cpar[...], keep, ext, ext_d
    )
    dmx_ref[...] = d_in[16:].astype(BF16)
    tailx_ref[...] = d_in[ROWS:]
    edgex_ref[...] = (d_in[:16] * keep).astype(BF16)
    dcx_ref[...] = d_par

    @pl.when(g == GROUPS - 1)
    def _():
        d_bc, d_par_bc = conv_back(
            dbc_sum[...], bc[...], halo_bc[...], cpar_bc[...], keep, ext, ext_d
        )
        dmbc_ref[:, :256] = d_bc[16:].astype(BF16)
        tailbc_ref[...] = d_bc[ROWS:]
        edgebc_ref[...] = (d_bc[:16] * keep).astype(BF16)
        dcbc_ref[...] = d_par_bc
        rates = -jnp.exp(hpar[1:2, :])
        logit = rate[...] + hpar[0:1, :]
        upper = lower_triangle().T
        before = lower_triangle(True)
        d_bias = jnp.zeros((1, LANES), F32)
        d_log = jnp.zeros((1, LANES), F32)
        usable = usable_rows(info)
        for q in range(2):
            here = slice(q * HALF, (q + 1) * HALF)
            step = dt[here, :]
            gs = gsum[...][:, here].T
            gs = jnp.concatenate([gs, jnp.zeros((HALF, LANES - 8 * GROUPS), F32)], axis=1)
            d_decay = exact_dot(upper, gs - step * u[here, :] + q_sum[here, :])
            d_decay = d_decay + exact_dot(before, step * v_sum[here, :])
            d_decay = d_decay + end_sum[8 * q : 8 * q + 1, :]
            d_step = u[here, :] + v_sum[here, :] + rates * d_decay
            d_rate = half(usable, q) * d_step * sigmoid(half(logit, q))
            d_bias += jnp.sum(d_rate, axis=0, keepdims=True)
            d_log += jnp.sum(d_decay * step * rates, axis=0, keepdims=True)
            dmbc_ref[here, 256:] = d_rate.astype(BF16)
        row = row_of((8, LANES))
        dhead_ref[...] = jnp.where(row == 0, d_bias, jnp.where(row == 1, d_log, 0.0))


def finish_call(
    info, xa, dxi, dy, mixed, halo, cpar, bca, cum, dt, rate, hpar, lam, hin, s0, own1, u, gsum, dbc
):
    bc_at = INNER // 256
    wide = whole((ROWS, LANES))
    return pl.pallas_call(
        finish_body,
        grid=(GROUPS,),
        out_shape=(
            shape((ROWS, INNER), BF16),
            shape((ROWS, 384), BF16),
            shape((16, INNER)),
            shape((16, 256)),
            shape((16, INNER), BF16),
            shape((16, 256), BF16),
            shape((8, INNER)),
            shape((8, 256)),
            shape((8, LANES)),
        ),
        in_specs=[
            SMEM,
            columns(ROWS, BLOCK),
            columns(ROWS, BLOCK),
            columns(ROWS, BLOCK),
            columns(ROWS, BLOCK),
            columns(16, BLOCK),
            columns(8, BLOCK),
            pl.BlockSpec((ROWS, 256), lambda g: (0, bc_at)),
            pl.BlockSpec((16, 256), lambda g: (0, bc_at)),
            pl.BlockSpec((8, 256), lambda g: (0, bc_at)),
            whole((ROWS, 256)),
            wide,
            wide,
            wide,
            whole((8, LANES)),
            grouped(STATE),
            grouped(STATE),
            grouped(STATE),
            grouped(STATE),
            wide,
            whole((8 * GROUPS, ROWS)),
            whole((ROWS, 256)),
        ],
        out_specs=(
            columns(ROWS, BLOCK),
            whole((ROWS, 384)),
            columns(16, BLOCK),
            whole((16, 256)),
            columns(16, BLOCK),
            whole((16, 256)),
            columns(8, BLOCK),
            whole((8, 256)),
            whole((8, LANES)),
        ),
        scratch_shapes=[
            pltpu.VMEM((ROWS + 32, BLOCK), F32),
            pltpu.VMEM((ROWS + 32, BLOCK), F32),
            pltpu.VMEM((ROWS, LANES), F32),
            pltpu.VMEM((ROWS, LANES), F32),
            pltpu.VMEM((ROWS, LANES), F32),
            pltpu.VMEM((ROWS, LANES), F32),
            pltpu.VMEM((16, LANES), F32),
            pltpu.VMEM((ROWS, 256), F32),
        ],
        compiler_params=params(),
        cost_estimate=pl.CostEstimate(
            flops=10 * ROWS * STATE * INNER, bytes_accessed=15_000_000, transcendentals=1_600_000
        ),
        name="finish_back",
    )(
        info, xa, dxi, dy, mixed, halo, cpar, mixed, halo, cpar, bca, cum, dt, rate, hpar,
        lam, hin, s0, own1, u, gsum, dbc,
    )


def gate_in_back_body(plan, refs, info, dz, *rest):
    w_refs, (out_ref, buffer, sems) = rest[:refs], rest[refs:]
    size = WIDTH // 4
    for b in range(4):
        for c in copies_of(plan(b), w_refs, buffer, sems, info, b, None, True):
            c.start()
    for b in range(4):
        for c in copies_of(plan(b), w_refs, buffer, sems, info, b, None, True):
            c.wait()
        out_ref[:, b * size : (b + 1) * size] = dot_nt(dz[...], buffer[b * size : (b + 1) * size, :])


def gate_in_back(info, dz, weights, plan, count):
    return pl.pallas_call(
        functools.partial(gate_in_back_body, plan, len(weights)),
        out_shape=shape((ROWS, WIDTH)),
        in_specs=[SMEM, whole((ROWS, INNER))] + [ANYWHERE] * len(weights),
        out_specs=whole((ROWS, WIDTH)),
        scratch_shapes=[
            pltpu.VMEM((WIDTH, INNER), BF16),
            pltpu.SemaphoreType.DMA((count, 4)),
        ],
        compiler_params=params(),
        cost_estimate=pl.CostEstimate(
            flops=2 * ROWS * WIDTH * INNER, bytes_accessed=13_000_000, transcendentals=0
        ),
        name="gate_in_back",
    )(info, dz, *weights)


def mixed_back_body(
    plan, refs, info, dmx, dmbc, tailx, tailbc, edge, part, h_ref, cot, gain, *rest
):
    w_refs, (dh_ref, dxc_ref, dgain_ref, buffer, sems) = rest[:refs], rest[refs:]
    size = WIDTH // 4
    for b in range(4):
        for c in copies_of(plan(b), w_refs, buffer, sems, info, b, None, True):
            c.start()
    dxc_ref[:, :INNER] = dmx[...]
    dxc_ref[:, INNER:] = dmbc[...]
    late = edge[...].astype(F32)
    dxc_ref[ROWS - 16 :, :INNER] = (tailx[...] + late[:, :INNER]).astype(BF16)
    dxc_ref[ROWS - 16 :, INNER:CONV_CH] = (tailbc[...] + late[:, INNER:]).astype(BF16)
    for b in range(4):
        cols = slice(b * size, (b + 1) * size)
        for c in copies_of(plan(b), w_refs, buffer, sems, info, b, None, True):
            c.wait()
        dh_ref[:, cols] = part[:, cols] + dot_nt(dxc_ref[...], buffer[cols, :])
    h = h_ref[...].astype(F32)
    scale = lax.rsqrt(jnp.mean(h * h, axis=1, keepdims=True) + EPSILON)
    d_norm = dh_ref[...]
    inner = jnp.mean(d_norm * gain[...] * h, axis=1, keepdims=True) * scale * scale * scale
    dgain_ref[...] = jnp.broadcast_to(
        jnp.sum(d_norm * h * scale, axis=0, keepdims=True), (8, WIDTH)
    )
    dh_ref[...] = cot[...].astype(F32) + scale * d_norm * gain[...] - h * inner


def mixed_back(info, dmx, dmbc, tailx, tailbc, edge, part, h, cot, gain, weights, plan, count):
    return pl.pallas_call(
        functools.partial(mixed_back_body, plan, len(weights)),
        out_shape=(shape((ROWS, WIDTH)), shape((ROWS, PACKED), BF16), shape((8, WIDTH))),
        in_specs=[
            SMEM,
            whole((ROWS, INNER)),
            whole((ROWS, 384)),
            whole((16, INNER)),
            whole((16, 256)),
            whole((16, CONV_CH)),
            whole((ROWS, WIDTH)),
            whole((ROWS, WIDTH)),
            whole((ROWS, WIDTH)),
            whole((1, WIDTH)),
        ]
        + [ANYWHERE] * len(weights),
        out_specs=(whole((ROWS, WIDTH)), whole((ROWS, PACKED)), whole((8, WIDTH))),
        scratch_shapes=[
            pltpu.VMEM((WIDTH, PACKED), BF16),
            pltpu.SemaphoreType.DMA((count, 4)),
        ],
        compiler_params=params(),
        cost_estimate=pl.CostEstimate(
            flops=2 * ROWS * WIDTH * PACKED, bytes_accessed=18_000_000, transcendentals=0
        ),
        name="mixed_back",
    )(info, dmx, dmbc, tailx, tailbc, edge, part, h, cot, gain, *weights)


def z_shift(r):
    return "dp", [(z, (z + r) % 4) for z in range(4)]


def y_shift(r):
    return "ctx", [(j, (j + 4 * r) % 16) for j in range(16)]


def x_shift(r):
    return "ctx", [(j, j - j % 4 + (j + r) % 4) for j in range(16)]


SHIFTS = {"z": z_shift, "y": y_shift, "x": x_shift}


def send(value, axis, r, section=None):
    name, pairs = SHIFTS[axis](r)
    if section is None:
        return lax.ppermute(value, name, pairs)
    base = section * lax.axis_size(name)
    return lax.ppermute(value, ("section", name), [(base + a, base + b) for a, b in pairs])


def swapped(value, section_from=None):
    pairs = [(0, 1), (1, 0)] if section_from is None else [(section_from, 1 - section_from)]
    return lax.ppermute(value, "section", pairs)


def reduced(first, order, place, section):
    axes = ["z", "y", "x"]
    axis = order[0]
    terms = [first((place[axis] + r) % 4) for r in range(4)]
    total = terms[0].astype(F32)
    for r in range(1, 4):
        total = total + send(terms[r].astype(BF16), axis, r, section).astype(F32)
    axes.remove(axis)
    for axis in order[1:]:
        at = axes.index(axis)
        parts = [
            lax.dynamic_index_in_dim(total, (place[axis] + r) % 4, at, False) for r in range(4)
        ]
        total = parts[0]
        for r in range(1, 4):
            total = total + send(parts[r].astype(BF16), axis, r, section).astype(F32)
        axes.remove(axis)
    return total


PARITY = [[j for j in range(16) if j % 2 == e] for e in range(2)]


def exchange(value):
    return lax.all_to_all(value, "ctx", 0, 0, axis_index_groups=PARITY)


def halo_shift(value, step):
    pairs = [(j, j + 2 * step) for j in range(16) if 0 <= j + 2 * step < 16]
    return lax.ppermute(value, "ctx", pairs)


def head_lanes(values):
    rows = values.shape[0]
    grid = jnp.pad(values.reshape(rows, GROUPS, OWN), ((0, 0), (0, 0), (0, 8 - OWN)))
    return jnp.pad(grid.reshape(rows, 8 * GROUPS), ((0, 0), (0, LANES - 8 * GROUPS)))


def lanes_heads(values):
    rows = values.shape[0]
    return values[:, : 8 * GROUPS].reshape(rows, GROUPS, 8)[:, :, :OWN].reshape(rows, HEADS)


def block_plan(rows):
    def plan(b):
        return lambda info: [(0, None, b * rows, rows, b * rows)]

    return plan


def on_device(
    boundary,
    lengths,
    norm_gain,
    w_z,
    w_xbc,
    w_dt,
    conv_weight,
    conv_bias,
    dt_bias,
    a_log,
    d_skip,
    gate_gain,
    w_out,
):
    section = lax.axis_index("section")
    group = lax.axis_index("dp")
    ctx = lax.axis_index("ctx")
    place = {"z": group, "y": ctx // 4, "x": ctx % 4}
    micro = ctx % 2
    chunk = ctx // 2

    own_rows = lax.dynamic_index_in_dim(boundary[0], micro, 0, False)
    other_rows = lax.dynamic_index_in_dim(boundary[0], 1 - micro, 0, False)
    pairs = [(j, j ^ 1) for j in range(16)]
    came = lax.ppermute(other_rows, "ctx", pairs)
    block = jnp.where(
        micro == 0, jnp.concatenate([own_rows, came]), jnp.concatenate([came, own_rows])
    )

    pair = lengths[group, micro]
    padded = (pair[0] + SPAN - 1) // SPAN * SPAN
    offset = chunk * ROWS
    begin = jnp.where(offset >= padded, padded, 0)
    length = jnp.where(offset >= padded, pair[1], pair[0])
    live = jnp.clip(length - (offset - begin), 0, ROWS)
    offsets = jnp.arange(GROUPS, dtype=jnp.int32) * ROWS
    keeps = ((offsets != 0) & (offsets != padded)).astype(jnp.int32)
    keep = ((offset != 0) & (offset != padded)).astype(jnp.int32)
    info = jnp.concatenate([jnp.stack([live, keep]).astype(jnp.int32), keeps])

    packed = jnp.concatenate([w_xbc[0], head_lanes(w_dt[0])], axis=1)
    small = jnp.zeros((8, 832), BF16)
    small = small.at[:4].set(conv_weight[0]).at[4].set(conv_bias[0])
    small = small.at[5, :384].set(norm_gain[0]).at[6, :768].set(gate_gain[0])
    smalls = lax.all_gather(small, "dp").astype(F32)
    cpar = jnp.transpose(smalls, (1, 0, 2)).reshape(8, CONV_CH)
    gain_one = smalls[:, 5, :384].reshape(1, WIDTH)
    gain_two = smalls[:, 6, :768].reshape(1, INNER)
    hpar = jnp.pad(
        jnp.concatenate([head_lanes(dt_bias), head_lanes(a_log), head_lanes(d_skip)]),
        ((0, 5), (0, 0)),
    )
    full_x = lax.all_gather(packed, "dp", axis=0, tiled=True)
    full_z = lax.all_gather(w_z[0], "dp", axis=0, tiled=True)
    full_o = lax.all_gather(w_out[0], "dp", axis=0, tiled=True)

    def forward(h):
        normed, mixed, rate = in_proj(info, h, gain_one, [full_x], whole_plan(WIDTH), 1)
        halo = halo_shift(mixed[ROWS - 16 :], 1)
        gate = gate_proj(info, normed, [full_z], whole_plan(WIDTH), 1)
        xa, bca, cum, dt, s0, msg = state_call(info, mixed, halo, cpar, rate, hpar)
        came = exchange(msg)
        y_in = inside_call(xa, bca, cum, dt, hpar)
        hin = exchange(scan_call(info, came, False))
        y, normed_two, result = out_proj(
            info, y_in, bca, cum, hin, s0, gate, gain_two, h, [full_o], whole_plan(INNER), 1
        )
        saved = (h, normed, mixed, halo, rate, gate, xa, bca, cum, dt, s0, msg, hin, y, normed_two)
        return result, saved

    def backward(cot, saved, own):
        h, normed, mixed, halo, rate, gate, xa, bca, cum, dt, s0, msg, hin, y, normed_two = saved
        bg, dy, dz, d_gain_two = gate_back(
            info, cot, y, gate, gain_two, [full_o], block_plan(INNER // 4), 1
        )
        own1, msg_back = own_grad(dy, bca, cum, msg)
        came = exchange(msg_back)
        normed_two_t = normed_two.T.reshape(4, 4, 4, 48, ROWS)
        normed_t = normed.T.reshape(4, 4, 4, 24, ROWS)

        def product(source, axis, other):
            at = "zyx".index(axis)

            def term(n):
                rows = lax.dynamic_index_in_dim(source, n, at, False)
                lead = rows.shape[:3]
                value = jnp.dot(rows.reshape(-1, ROWS), other, preferred_element_type=F32)
                return value.reshape(lead + (other.shape[1],))

            return term

        sum_out = reduced(product(normed_two_t, "x", bg), "xzy", place, own)
        sum_z = reduced(product(normed_t, "z", dz), "zyx", place, own)
        dxi, d_skips, gsum, u, dbc = inside_back(dy, xa, bca, cum, dt, hpar)
        lam = exchange(scan_call(info, came, True))
        part = gate_in_back(info, dz, [full_z], block_plan(WIDTH // 4), 1)
        dmx, dmbc, tailx, tailbc, edgex, edgebc, d_parx, d_parbc, d_heads = finish_call(
            info, xa, dxi, dy, mixed, halo, cpar, bca, cum, dt, rate, hpar, lam, hin, s0, own1, u, gsum, dbc
        )
        edge = halo_shift(jnp.concatenate([edgex, edgebc], axis=1), -1)
        dh, dxc, d_gain_one = mixed_back(
            info, dmx, dmbc, tailx, tailbc, edge, part, h, cot, gain_one, [full_x],
            block_plan(WIDTH // 4), 1,
        )
        third = PACKED // 3
        sum_x = jnp.concatenate(
            [
                reduced(product(normed_t, order[0], dxc[:, i * third : (i + 1) * third]), order, place, own)
                for i, order in enumerate(("zyx", "yxz", "xzy"))
            ],
            axis=1,
        )
        d_skip_row = jnp.sum(d_skips[0].reshape(HEADS, HEADDIM), axis=1)
        wide = jnp.zeros((16, CONV_CH), F32)
        wide = wide.at[:8, :INNER].set(d_parx).at[:8, INNER:].set(d_parbc)
        wide = wide.at[8, :WIDTH].set(d_gain_one[0]).at[9, :INNER].set(d_gain_two[0])
        wide = wide.at[10, :LANES].set(d_heads[0]).at[11, :LANES].set(d_heads[1])
        wide = wide.at[12, :HEADS].set(d_skip_row)
        return dh, (sum_z, sum_x, sum_out, wide)

    out_low, saved_low = forward(block)
    out_high, saved_high = forward(swapped(out_low.astype(BF16), 0))
    dh_high, sums_high = backward(block, saved_high, 1)
    dh_low, sums_low = backward(swapped(dh_high.astype(BF16), 1), saved_low, 0)

    sum_z, sum_x, sum_out, wide = jax.tree.map(
        lambda a, b: jnp.where(section == 0, a, b), sums_low, sums_high
    )
    wide = lax.psum(wide, ("dp", "ctx"))
    index = group * 16 + ctx
    d_conv = lax.dynamic_slice(wide, (0, index * 52), (8, 52))
    d_gain_one = lax.dynamic_slice(wide, (8, index * 24), (1, 24))
    d_gain_two = lax.dynamic_slice(wide, (9, index * 48), (1, 48))
    d_bias, d_log = lanes_heads(wide[10:11, :LANES]), lanes_heads(wide[11:12, :LANES])

    rows = jnp.where(section == 0, dh_low, out_high)
    mine = jnp.where(micro == 0, rows[:HALF], rows[HALF:])
    other = lax.ppermute(jnp.where(micro == 0, rows[HALF:], rows[:HALF]), "ctx", pairs)
    top = jnp.where(micro == 0, jnp.stack([mine, other]), jnp.stack([other, mine]))
    return (
        top[None],
        d_gain_one,
        sum_z[None],
        sum_x[None, :, :CONV_CH],
        lanes_heads(sum_x[:, CONV_CH:])[None],
        d_conv[None, :4],
        d_conv[4:5],
        d_bias,
        d_log,
        wide[12:13, :HEADS],
        d_gain_two,
        sum_out[None],
    )


def solution(mesh):
    in_specs = (
        P("section", None, ("dp", "ctx"), None),
        P(),
        P("section", "dp"),
        P("section", "dp", None),
        P("section", "dp", None),
        P("section", "dp", None),
        P("section", None, "dp"),
        P("section", "dp"),
        P("section", None),
        P("section", None),
        P("section", None),
        P("section", "dp"),
        P("section", "dp", None),
    )
    out_specs = (
        P("section", None, ("dp", "ctx"), None),
        P("section", ("dp", "ctx")),
        P("section", ("dp", "ctx"), None),
        P("section", ("dp", "ctx"), None),
        P("section", ("dp", "ctx"), None),
        P("section", None, ("dp", "ctx")),
        P("section", ("dp", "ctx")),
        P("section", None),
        P("section", None),
        P("section", None),
        P("section", ("dp", "ctx")),
        P("section", ("dp", "ctx"), None),
    )
    return jax.shard_map(
        on_device, mesh=mesh, in_specs=in_specs, out_specs=out_specs, check_vma=False
    )
```

```python
import functools

import jax
import jax.numpy as jnp
from jax import lax
from jax.experimental import pallas as pl
from jax.experimental.pallas import tpu as pltpu
from jax.sharding import PartitionSpec as P

HEADS = 48
HEADDIM = 64
STATE = 128
KERNEL = 4
SPAN = 256
MICRO = 2
WIDTH = 1536
INNER = 3072
CONV_CH = 3328
LANES = 128
CHUNKS = 8
GROUPS = 4
OWN = 6
BLOCK = OWN * HEADDIM
LOCAL = GROUPS * BLOCK
MIXED = LOCAL + 2 * STATE
PACKED = MIXED + LANES
ROWS = 256
HALF = 128
SHARD = 384
PIECE = 48
STATE_HALF = STATE // 2
MESSAGE = STATE_HALF + 16
EPSILON = 1e-05
PRECISE = lax.Precision.HIGHEST
F32 = jnp.float32
BF16 = jnp.bfloat16
VMEM_LIMIT = 56 * 1024 * 1024


def params(**more):
    return pltpu.CompilerParams(vmem_limit_bytes=VMEM_LIMIT, **more)


def whole(shape):
    return pl.BlockSpec(shape, lambda *_: (0,) * len(shape))


def columns(rows, width):
    return pl.BlockSpec((rows, width), lambda g: (0, g))


def grouped(rows):
    return pl.BlockSpec((1, rows, BLOCK), lambda g: (g, 0, 0))


MESSAGES = pl.BlockSpec((2, MESSAGE, BLOCK), lambda g: (g, 0, 0))
SMEM = pl.BlockSpec(memory_space=pltpu.SMEM)
ANYWHERE = pl.BlockSpec(memory_space=pl.ANY)


def shape(dims, kind=F32):
    return jax.ShapeDtypeStruct(dims, kind)


def dot(a, b):
    return jnp.dot(a, b, preferred_element_type=F32)


def dot_nt(a, b):
    return lax.dot_general(a, b, (((1,), (1,)), ((), ())), preferred_element_type=F32)


def exact_dot(a, b):
    return jnp.dot(a, b, precision=PRECISE, preferred_element_type=F32)


def lane_of(dims):
    return lax.broadcasted_iota(jnp.int32, dims, len(dims) - 1)


def row_of(dims):
    return lax.broadcasted_iota(jnp.int32, dims, len(dims) - 2)


def sigmoid(v):
    return 1.0 / (1.0 + jnp.exp(-v))


def softplus(v):
    return jnp.maximum(v, 0.0) + jnp.log1p(jnp.exp(-jnp.abs(v)))


def rolled(values, g):
    return pltpu.roll(values, lax.rem(LANES - 8 * g, LANES), axis=1)


def pair_lanes(values, p):
    low = lane_of((values.shape[0], LANES)) < HEADDIM
    return jnp.where(low, values[:, 2 * p : 2 * p + 1], values[:, 2 * p + 1 : 2 * p + 2])


def spread(values):
    return jnp.concatenate([pair_lanes(values, p) for p in range(OWN // 2)], axis=1)


def head_sum_matrix(g):
    head = row_of((BLOCK, LANES)) // HEADDIM
    return (lane_of((BLOCK, LANES)) == head + 8 * g).astype(BF16)


def lower_triangle(strict=False):
    i, j = row_of((HALF, HALF)), lane_of((HALF, HALF))
    return ((i > j) if strict else (i >= j)).astype(F32)


def usable_rows(info):
    return (row_of((ROWS, 1)) < info[0]).astype(F32)


def half(values, q):
    return values[q * HALF : (q + 1) * HALF]


class Weight:
    def __init__(self, arrays, layer, width, first=0):
        self.arrays = arrays
        self.layer = layer
        self.width = width
        self.columns = pl.ds(first, width)

    def block(self, info, b):
        return lax.rem(info[10] + b, 4) * SHARD

    def parts(self, refs, info, b):
        start = self.block(info, b)
        if len(refs) == 1:
            return [(refs[0].at[pl.ds(pl.multiple_of(start, SHARD), SHARD)], start, SHARD)]
        out = []
        for side in range(2):
            mine = info[12 - side]
            for step in range(4):
                source = refs[2 + 4 * side + step].at[pl.ds((b - 1) * PIECE, PIECE)]
                row = start + side * (SHARD // 2) + lax.rem(mine + step, 4) * PIECE
                out.append((source, row, PIECE))
        return out

    def copies(self, refs, info, b, buffer, sems):
        return [
            pltpu.make_async_copy(
                source.at[:, self.columns],
                buffer.at[pl.ds(pl.multiple_of(row, 16), count)],
                sems.at[b, n],
            )
            for n, (source, row, count) in enumerate(self.parts(refs, info, b))
        ]

    def own_copy(self, source, info, buffer, sems):
        rows = pl.ds(pl.multiple_of(self.block(info, 0), SHARD), SHARD)
        return pltpu.make_async_copy(source.at[:, self.columns], buffer.at[rows], sems.at[0, 0])

    def start(self, refs, info, buffer, sems):
        whole_array = len(refs) == 1
        if not whole_array:
            for n in range(2):

                @pl.when((info[13] == self.layer) == (n == 0))
                def _(n=n):
                    self.own_copy(refs[n], info, buffer, sems).start()

        for b in range(0 if whole_array else 1, 4):
            for c in self.copies(refs, info, b, buffer, sems):
                c.start()

    def wait(self, refs, info, b, buffer, sems):
        if b == 0 and len(refs) > 1:
            self.own_copy(refs[0], info, buffer, sems).wait()
        else:
            for c in self.copies(refs, info, b, buffer, sems):
                c.wait()
        return pl.ds(pl.multiple_of(self.block(info, b), SHARD), SHARD)

    def specs(self):
        return [ANYWHERE] * len(self.arrays)

    def scratch(self):
        return [pltpu.VMEM((4 * SHARD, self.width), BF16), pltpu.SemaphoreType.DMA((4, 8))]

    def product(self, refs, info, left, buffer, sems, total):
        for b in range(4):
            self.wait(refs, info, b, buffer, sems)
        step = 512 if self.width % 512 == 0 else 640
        for at in range(0, self.width, step):
            total[:, at : at + step] = dot(left[...], buffer[:, at : at + step])


def in_proj_body(weight, info, h_ref, gain_ref, *rest):
    refs = len(weight.arrays)
    w_refs, (normed_ref, mixed_ref, rate_ref, buffer, sems, total) = rest[:refs], rest[refs:]
    weight.start(w_refs, info, buffer, sems)
    h = h_ref[...].astype(F32)
    scale = lax.rsqrt(jnp.mean(h * h, axis=1, keepdims=True) + EPSILON)
    normed_ref[...] = (h * scale * gain_ref[...]).astype(BF16)
    weight.product(w_refs, info, normed_ref, buffer, sems, total)
    mixed_ref[...] = total[:, :MIXED].astype(BF16)
    rate_ref[...] = total[:, MIXED:]


def in_proj(info, h, gain, weight):
    return pl.pallas_call(
        functools.partial(in_proj_body, weight),
        out_shape=(shape((ROWS, WIDTH), BF16), shape((ROWS, MIXED), BF16), shape((ROWS, LANES))),
        in_specs=[SMEM, whole((ROWS, WIDTH)), whole((1, WIDTH))] + weight.specs(),
        out_specs=(whole((ROWS, WIDTH)), whole((ROWS, MIXED)), whole((ROWS, LANES))),
        scratch_shapes=weight.scratch() + [pltpu.VMEM((ROWS, PACKED), F32)],
        compiler_params=params(),
        cost_estimate=pl.CostEstimate(
            flops=2 * ROWS * WIDTH * PACKED, bytes_accessed=8_000_000, transcendentals=0
        ),
        name="in_proj",
    )(info, h, gain, *weight.arrays)


def gate_proj_body(weight, info, normed_ref, *rest):
    refs = len(weight.arrays)
    w_refs, (gate_ref, buffer, sems) = rest[:refs], rest[refs:]
    weight.start(w_refs, info, buffer, sems)
    weight.product(w_refs, info, normed_ref, buffer, sems, gate_ref)


def gate_proj(info, normed, weight):
    return pl.pallas_call(
        functools.partial(gate_proj_body, weight),
        out_shape=shape((ROWS, LOCAL)),
        in_specs=[SMEM, whole((ROWS, WIDTH))] + weight.specs(),
        out_specs=whole((ROWS, LOCAL)),
        scratch_shapes=weight.scratch(),
        compiler_params=params(),
        cost_estimate=pl.CostEstimate(
            flops=2 * ROWS * WIDTH * LOCAL, bytes_accessed=7_000_000, transcendentals=0
        ),
        name="gate_proj",
    )(info, normed, *weight.arrays)


def conv_sum_of(values, halo, cpar, keep, ext):
    width = values.shape[1]
    ext[0:16, :width] = halo.astype(F32) * keep
    ext[16 : 16 + ROWS, :width] = values.astype(F32)
    total = cpar[4:5, :]
    for k in range(KERNEL):
        total = total + cpar[k : k + 1, :] * ext[13 + k : 13 + k + ROWS, :width]
    return total


def state_body(
    info, mixed, halo, cpar, bc, halo_bc, cpar_bc, rate, hpar,
    xa_ref, bca_ref, cum_ref, dt_ref, s0_ref, msg_ref, ext, bt, tail,
):
    g = pl.program_id(0)
    keep = info[1].astype(F32)

    @pl.when(g == 0)
    def _():
        total = conv_sum_of(bc[...], halo_bc[...], cpar_bc[...], keep, ext)
        active = total * sigmoid(total)
        bca_ref[...] = active
        bt[...] = active[:, :STATE].T.astype(BF16)
        dt = usable_rows(info) * softplus(rate[...] + hpar[0:1, :])
        log_decay = dt * -jnp.exp(hpar[1:2, :])
        dt_ref[...] = dt
        tri = lower_triangle()
        for q in range(2):
            rows = pl.ds(q * HALF, HALF)
            cum = exact_dot(tri, half(log_decay, q))
            cum_ref[rows, :] = cum
            tail[rows, :] = jnp.exp(cum[HALF - 1 :, :] - cum) * half(dt, q)

    total = conv_sum_of(mixed[...], halo[...], cpar[...], keep, ext)
    xa = total * sigmoid(total)
    xa_ref[...] = xa
    weighted = (xa * spread(rolled(tail[...], g))).astype(BF16)
    ends = rolled(cum_ref[...], g)
    end0, end1 = ends[HALF - 1 : HALF], ends[ROWS - 1 : ROWS]
    s0 = dot(bt[:, :HALF], half(weighted, 0))
    s1 = dot(bt[:, HALF:], half(weighted, 1))
    s0_ref[0] = s0
    state = (spread(jnp.exp(end1)) * s0 + s1).astype(BF16)
    damp = spread(jnp.exp(end0 + end1))
    high = damp.astype(BF16)
    low = (damp - high.astype(F32)).astype(BF16)
    row = row_of((16, BLOCK))
    damps = jnp.where(row == 0, high.astype(F32), low.astype(F32)).astype(BF16)
    for r in range(2):
        msg_ref[r, :STATE_HALF, :] = state[r * STATE_HALF : (r + 1) * STATE_HALF]
        msg_ref[r, STATE_HALF:, :] = damps


def state_call(info, mixed, halo, cpar, rate, hpar):
    bc_at = LOCAL // 256
    return pl.pallas_call(
        state_body,
        grid=(GROUPS,),
        out_shape=(
            shape((ROWS, LOCAL)),
            shape((ROWS, 256)),
            shape((ROWS, LANES)),
            shape((ROWS, LANES)),
            shape((GROUPS, STATE, BLOCK)),
            shape((CHUNKS, MESSAGE, BLOCK), BF16),
        ),
        in_specs=[
            SMEM,
            columns(ROWS, BLOCK),
            columns(16, BLOCK),
            columns(8, BLOCK),
            pl.BlockSpec((ROWS, 256), lambda g: (0, bc_at)),
            pl.BlockSpec((16, 256), lambda g: (0, bc_at)),
            pl.BlockSpec((8, 256), lambda g: (0, bc_at)),
            whole((ROWS, LANES)),
            whole((8, LANES)),
        ],
        out_specs=(
            columns(ROWS, BLOCK),
            whole((ROWS, 256)),
            whole((ROWS, LANES)),
            whole((ROWS, LANES)),
            grouped(STATE),
            MESSAGES,
        ),
        scratch_shapes=[
            pltpu.VMEM((ROWS + 32, BLOCK), F32),
            pltpu.VMEM((STATE, ROWS), BF16),
            pltpu.VMEM((ROWS, LANES), F32),
        ],
        compiler_params=params(),
        cost_estimate=pl.CostEstimate(
            flops=2 * ROWS * STATE * LOCAL, bytes_accessed=4_500_000, transcendentals=400_000
        ),
        name="conv_state",
    )(info, mixed, halo, cpar, mixed, halo, cpar, rate, hpar)


def inside_body(xa, bca, cum, dt, hpar, y_ref, cum_t, scores):
    g = pl.program_id(0)

    @pl.when(g == 0)
    def _():
        tri = lower_triangle()
        for q in range(2):
            b, c = half(bca[:, :STATE], q).astype(BF16), half(bca[:, STATE:], q).astype(BF16)
            scores[q] = dot_nt(c, b) * tri
            cum_t[:, q * HALF : (q + 1) * HALF] = half(cum[...], q).T

    cols = rolled(cum[...], g)
    rows = cum_t[pl.ds(pl.multiple_of(8 * g, 8), 8), :]
    steps = rolled(dt[...], g)
    skips = rolled(hpar[...], g)[2:3, :]
    low = lane_of((HALF, LANES)) < HEADDIM
    for q in range(2):
        for p in range(OWN // 2):
            lanes = slice(p * LANES, (p + 1) * LANES)
            x = xa[q * HALF : (q + 1) * HALF, lanes]
            xdt = x * pair_lanes(half(steps, q), p)
            both = jnp.concatenate([jnp.where(low, xdt, 0.0), jnp.where(low, 0.0, xdt)], axis=0)
            mats = []
            for i in (2 * p, 2 * p + 1):
                gap = half(cols, q)[:, i : i + 1] - rows[i : i + 1, q * HALF : (q + 1) * HALF]
                mats.append((jnp.exp(jnp.minimum(gap, 0.0)) * scores[q]).astype(BF16))
            y = dot(jnp.concatenate(mats, axis=1), both.astype(BF16))
            y_ref[q * HALF : (q + 1) * HALF, lanes] = y + x * pair_lanes(skips, p)


def inside_call(xa, bca, cum, dt, hpar):
    return pl.pallas_call(
        inside_body,
        grid=(GROUPS,),
        out_shape=shape((ROWS, LOCAL)),
        in_specs=[
            columns(ROWS, BLOCK),
            whole((ROWS, 256)),
            whole((ROWS, LANES)),
            whole((ROWS, LANES)),
            whole((8, LANES)),
        ],
        out_specs=columns(ROWS, BLOCK),
        scratch_shapes=[pltpu.VMEM((LANES, ROWS), F32), pltpu.VMEM((2, HALF, HALF), F32)],
        compiler_params=params(),
        cost_estimate=pl.CostEstimate(
            flops=2 * HEADS * HALF * HALF * LANES, bytes_accessed=3_300_000, transcendentals=800_000
        ),
        name="inside",
    )(xa, bca, cum, dt, hpar)


def scan_body(backward, info, msg, token, out_ref):
    carry = jnp.zeros((STATE_HALF, BLOCK), F32)
    for k in reversed(range(CHUNKS)) if backward else range(CHUNKS):
        keep = info[2 + k].astype(F32)
        if not backward:
            carry = carry * keep
        out_ref[k] = carry.astype(BF16)
        damps = msg[k, STATE_HALF:, :].astype(F32)
        carry = (damps[0:1] + damps[1:2]) * carry + msg[k, :STATE_HALF, :].astype(F32)
        if backward:
            carry = carry * keep


def scan_call(info, msg, backward, token):
    return pl.pallas_call(
        functools.partial(scan_body, backward),
        out_shape=shape((CHUNKS, STATE_HALF, BLOCK), BF16),
        in_specs=[SMEM, whole((CHUNKS, MESSAGE, BLOCK)), ANYWHERE],
        out_specs=whole((CHUNKS, STATE_HALF, BLOCK)),
        compiler_params=params(),
        name="chunk_scan",
    )(info, msg, token)


def out_proj_body(weight, info, y_in, bca, cum, hin, s0, gate, gain, *rest):
    refs = len(weight.arrays)
    w_refs, (y_ref, part_ref, buffer, sems, sums, gained) = rest[:refs], rest[refs:]
    weight.start(w_refs, info, buffer, sems)
    c_all = bca[:, STATE:].astype(BF16)
    grow = jnp.exp(cum[...])
    sums[...] = jnp.zeros((ROWS, LANES), F32)

    def group(g, _):
        lanes = pl.ds(pl.multiple_of(g * BLOCK, LANES), BLOCK)
        factor = rolled(grow, g)
        first = hin[g]
        second = spread(factor[HALF - 1 : HALF]) * first.astype(F32) + s0[g]
        carried = jnp.concatenate(
            [dot(half(c_all, 0), first), dot(half(c_all, 1), second.astype(BF16))], axis=0
        )
        y = y_in[:, lanes] + spread(factor) * carried
        y_ref[:, lanes] = y
        z = gate[:, lanes]
        gated = y * z * sigmoid(z)
        square = gated * gated
        sums[...] += sum(square[:, i * LANES : (i + 1) * LANES] for i in range(BLOCK // LANES))
        gained[:, lanes] = (gated * gain[:, lanes]).astype(BF16)
        return 0

    lax.fori_loop(0, GROUPS, group, 0)
    part_ref[:, WIDTH:] = sums[...]
    weight.product(w_refs, info, gained, buffer, sems, part_ref)


def out_proj(info, y_in, bca, cum, hin, s0, gate, gain, weight):
    return pl.pallas_call(
        functools.partial(out_proj_body, weight),
        out_shape=(shape((ROWS, LOCAL)), shape((ROWS, WIDTH + LANES))),
        in_specs=[
            SMEM,
            whole((ROWS, LOCAL)),
            whole((ROWS, 256)),
            whole((ROWS, LANES)),
            whole((GROUPS, STATE, BLOCK)),
            whole((GROUPS, STATE, BLOCK)),
            whole((ROWS, LOCAL)),
            whole((1, LOCAL)),
        ]
        + weight.specs(),
        out_specs=(whole((ROWS, LOCAL)), whole((ROWS, WIDTH + LANES))),
        scratch_shapes=weight.scratch()
        + [pltpu.VMEM((ROWS, LANES), F32), pltpu.VMEM((ROWS, LOCAL), BF16)],
        compiler_params=params(),
        cost_estimate=pl.CostEstimate(
            flops=2 * ROWS * WIDTH * LOCAL, bytes_accessed=13_000_000, transcendentals=800_000
        ),
        name="out_proj",
    )(info, y_in, bca, cum, hin, s0, gate, gain, *weight.arrays)


def join_body(info, h_ref, own, came, res_ref, low_ref, branch_ref, scale_ref):
    squares = jnp.sum(own[:, WIDTH:] + came[:, WIDTH:], axis=1, keepdims=True)
    scale = lax.rsqrt(squares / INNER + EPSILON)
    branch = scale * (own[:, :WIDTH] + came[:, :WIDTH])
    branch_ref[...] = branch
    scale_ref[...] = jnp.broadcast_to(scale, (ROWS, LANES))
    result = h_ref[...].astype(F32) + usable_rows(info) * branch
    res_ref[...] = result
    low_ref[...] = result.astype(BF16)


def join(info, h, own, came):
    wide = whole((ROWS, WIDTH))
    parts = whole((ROWS, WIDTH + LANES))
    return pl.pallas_call(
        join_body,
        out_shape=(
            shape((ROWS, WIDTH)),
            shape((ROWS, WIDTH), BF16),
            shape((ROWS, WIDTH)),
            shape((ROWS, LANES)),
        ),
        in_specs=[SMEM, wide, parts, parts],
        out_specs=(wide, wide, wide, whole((ROWS, LANES))),
        compiler_params=params(),
        cost_estimate=pl.CostEstimate(flops=2_000_000, bytes_accessed=8_000_000, transcendentals=0),
        name="join",
    )(info, h, own, came)


def gate_back_body(weight, info, cot, y, gate, gain, branch, scale_ref, *rest):
    refs = len(weight.arrays)
    w_refs, rest = rest[:refs], rest[refs:]
    bg_ref, dy_ref, dz_ref, n_ref, dgain_ref, buffer, sems, dn = rest
    weight.start(w_refs, info, buffer, sems)
    bg = usable_rows(info) * cot[...].astype(F32)
    bg_ref[...] = bg.astype(BF16)
    scale = scale_ref[:, :1]
    inner = jnp.sum(bg_ref[...].astype(F32) * branch[...], axis=1, keepdims=True)
    inner = inner * scale * scale / INNER
    for b in range(4):
        rows = weight.wait(w_refs, info, b, buffer, sems)
        dn[...] = dot_nt(bg_ref[...], buffer[rows, :])

        def one(i, _, rows=rows):
            here = pl.ds(pl.multiple_of(i * LANES, LANES), LANES)
            lanes = pl.ds(pl.multiple_of(rows.start + i * LANES, LANES), LANES)
            z = gate[:, lanes]
            sig = sigmoid(z)
            silu = z * sig
            y_here = y[:, lanes]
            gated = y_here * silu
            d_norm = dn[:, here]
            gained = scale * gain[:, lanes]
            n_ref[:, lanes] = (gated * gained).astype(BF16)
            d_gated = d_norm * gained - gated * inner
            total = jnp.sum(d_norm * gated * scale, axis=0, keepdims=True)
            dgain_ref[:, lanes] = jnp.broadcast_to(total, (8, LANES))
            dy_ref[:, lanes] = (d_gated * silu).astype(BF16)
            dz_ref[:, lanes] = (d_gated * y_here * sig * (1.0 + z * (1.0 - sig))).astype(BF16)
            return 0

        lax.fori_loop(0, SHARD // LANES, one, 0)


def gate_back(info, cot, y, gate, gain, branch, scale, weight):
    wide, local = whole((ROWS, WIDTH)), whole((ROWS, LOCAL))
    return pl.pallas_call(
        functools.partial(gate_back_body, weight),
        out_shape=(
            shape((ROWS, WIDTH), BF16),
            shape((ROWS, LOCAL), BF16),
            shape((ROWS, LOCAL), BF16),
            shape((ROWS, LOCAL), BF16),
            shape((8, LOCAL)),
        ),
        in_specs=[SMEM, wide, local, local, whole((1, LOCAL)), wide, whole((ROWS, LANES))]
        + weight.specs(),
        out_specs=(wide, local, local, local, whole((8, LOCAL))),
        scratch_shapes=weight.scratch() + [pltpu.VMEM((ROWS, SHARD), F32)],
        compiler_params=params(),
        cost_estimate=pl.CostEstimate(
            flops=2 * ROWS * WIDTH * LOCAL, bytes_accessed=13_000_000, transcendentals=800_000
        ),
        name="gate_back",
    )(info, cot, y, gate, gain, branch, scale, *weight.arrays)


def own_grad_body(dy, bca, cum, msg_in, own1_ref, msg_ref, ct, grow):
    g = pl.program_id(0)

    @pl.when(g == 0)
    def _():
        ct[...] = bca[:, STATE:].T.astype(BF16)
        grow[...] = jnp.exp(cum[...])

    factor = rolled(grow[...], g)
    weighted = (dy[...].astype(F32) * spread(factor)).astype(BF16)
    own0 = dot(ct[:, :HALF], half(weighted, 0))
    own1 = dot(ct[:, HALF:], half(weighted, 1))
    own1_ref[0] = own1
    grad = (spread(factor[HALF - 1 : HALF]) * own1 + own0).astype(BF16)
    for r in range(2):
        msg_ref[r, :STATE_HALF, :] = grad[r * STATE_HALF : (r + 1) * STATE_HALF]
        msg_ref[r, STATE_HALF:, :] = msg_in[r, STATE_HALF:, :]


def own_grad(dy, bca, cum, msg):
    return pl.pallas_call(
        own_grad_body,
        grid=(GROUPS,),
        out_shape=(
            shape((GROUPS, STATE, BLOCK)),
            shape((CHUNKS, MESSAGE, BLOCK), BF16),
        ),
        in_specs=[columns(ROWS, BLOCK), whole((ROWS, 256)), whole((ROWS, LANES)), MESSAGES],
        out_specs=(grouped(STATE), MESSAGES),
        scratch_shapes=[pltpu.VMEM((STATE, ROWS), BF16), pltpu.VMEM((ROWS, LANES), F32)],
        compiler_params=params(),
        cost_estimate=pl.CostEstimate(
            flops=2 * ROWS * STATE * LOCAL, bytes_accessed=2_500_000, transcendentals=0
        ),
        name="own_grad",
    )(dy, bca, cum, msg)


def inside_back_body(
    dy, xa, bca, cum, dt, hpar,
    dx_ref, dskip_ref, gsum_ref, u_ref, dbc_ref, cum_t, scores, dscores,
):
    g = pl.program_id(0)

    @pl.when(g == 0)
    def _():
        tri = lower_triangle()
        for q in range(2):
            b, c = half(bca[:, :STATE], q).astype(BF16), half(bca[:, STATE:], q).astype(BF16)
            scores[q] = dot_nt(b, c) * tri.T
            cum_t[:, q * HALF : (q + 1) * HALF] = half(cum[...], q).T
        dscores[...] = jnp.zeros((2, HALF, HALF), F32)
        u_ref[...] = jnp.zeros((ROWS, LANES), F32)

    cols = rolled(cum[...], g)
    rows = cum_t[pl.ds(pl.multiple_of(8 * g, 8), 8), :]
    steps = rolled(dt[...], g)
    skips = rolled(hpar[...], g)[2:3, :]
    low = lane_of((HALF, LANES)) < HEADDIM
    lane = lane_of((HALF, LANES))
    gsum_ref[...] = jnp.zeros((8, ROWS), F32)
    for q in range(2):
        here = slice(q * HALF, (q + 1) * HALF)
        u_here = u_ref[here, :]
        for p in range(OWN // 2):
            lanes = slice(p * LANES, (p + 1) * LANES)
            dy_pair = dy[here, lanes]
            x = xa[here, lanes]
            zero = jnp.zeros_like(dy_pair)
            both = jnp.concatenate(
                [jnp.where(low, dy_pair, zero), jnp.where(low, zero, dy_pair)], axis=0
            )
            dw = dot_nt(x.astype(BF16), both)
            mats = []
            for n, i in enumerate((2 * p, 2 * p + 1)):
                gap = rows[i : i + 1, here] - half(cols, q)[:, i : i + 1]
                decay = jnp.exp(jnp.minimum(gap, 0.0))
                step = half(steps, q)[:, i : i + 1]
                weight = decay * scores[q]
                mats.append(weight.astype(BF16))
                dw_here = dw[:, n * HALF : (n + 1) * HALF]
                dscores[q] += decay * dw_here * step
                direct = weight * dw_here
                total = jnp.sum(direct, axis=1, keepdims=True)
                u_here = jnp.where(lane == 8 * g + i, total, u_here)
                gsum_ref[i : i + 1, here] = jnp.sum(direct * step, axis=0, keepdims=True)
            dx = dot(jnp.concatenate(mats, axis=1), both)
            dy_wide = dy_pair.astype(F32)
            dx_ref[here, lanes] = dx * pair_lanes(half(steps, q), p) + dy_wide * pair_lanes(skips, p)
            skip_sum = jnp.sum(dy_wide * x, axis=0, keepdims=True)
            if q == 0:
                dskip_ref[:, lanes] = jnp.broadcast_to(skip_sum, (8, LANES))
            else:
                dskip_ref[:, lanes] += skip_sum
        u_ref[here, :] = u_here

    @pl.when(g == GROUPS - 1)
    def _():
        tri = lower_triangle()
        for q in range(2):
            b, c = half(bca[:, :STATE], q).astype(BF16), half(bca[:, STATE:], q).astype(BF16)
            ds_t = dscores[q] * tri.T
            dbc_ref[q * HALF : (q + 1) * HALF, :STATE] = dot(ds_t.astype(BF16), c)
            dbc_ref[q * HALF : (q + 1) * HALF, STATE:] = dot(ds_t.T.astype(BF16), b)


def inside_back(dy, xa, bca, cum, dt, hpar):
    return pl.pallas_call(
        inside_back_body,
        grid=(GROUPS,),
        out_shape=(
            shape((ROWS, LOCAL)),
            shape((8, LOCAL)),
            shape((8 * GROUPS, ROWS)),
            shape((ROWS, LANES)),
            shape((ROWS, 256)),
        ),
        in_specs=[
            columns(ROWS, BLOCK),
            columns(ROWS, BLOCK),
            whole((ROWS, 256)),
            whole((ROWS, LANES)),
            whole((ROWS, LANES)),
            whole((8, LANES)),
        ],
        out_specs=(
            columns(ROWS, BLOCK),
            columns(8, BLOCK),
            pl.BlockSpec((8, ROWS), lambda g: (g, 0)),
            whole((ROWS, LANES)),
            whole((ROWS, 256)),
        ),
        scratch_shapes=[
            pltpu.VMEM((LANES, ROWS), F32),
            pltpu.VMEM((2, HALF, HALF), F32),
            pltpu.VMEM((2, HALF, HALF), F32),
        ],
        compiler_params=params(),
        cost_estimate=pl.CostEstimate(
            flops=4 * HEADS * HALF * HALF * LANES, bytes_accessed=4_500_000, transcendentals=800_000
        ),
        name="inside_back",
    )(dy, xa, bca, cum, dt, hpar)


def conv_back(d_active, values, halo, cpar, keep, ext, ext_d):
    width = values.shape[1]
    total = conv_sum_of(values, halo, cpar, keep, ext)
    sig = sigmoid(total)
    d_sum = d_active * sig * (1.0 + total * (1.0 - sig))
    ext_d[0:16, :width] = jnp.zeros((16, width), F32)
    ext_d[16 : 16 + ROWS, :width] = d_sum
    ext_d[16 + ROWS :, :width] = jnp.zeros((16, width), F32)
    d_in = jnp.zeros((ROWS + 16, width), F32)
    for k in range(KERNEL):
        d_in = d_in + cpar[k : k + 1, :] * ext_d[3 - k : 3 - k + ROWS + 16, :width]
    row = row_of((8, width))
    d_par = jnp.where(row == 4, jnp.sum(d_sum, axis=0, keepdims=True), 0.0)
    for k in range(KERNEL):
        tap = jnp.sum(d_sum * ext[13 + k : 13 + k + ROWS, :width], axis=0, keepdims=True)
        d_par = jnp.where(row == k, tap, d_par)
    return d_in, d_par


def finish_body(
    info, xa, dxi, dy, mixed, halo, cpar, bc, halo_bc, cpar_bc, bca, cum, dt, rate, hpar, lam, hin, s0, own1, u, gsum, dbc,
    dmx_ref, dmbc_ref, tailx_ref, tailbc_ref, edgex_ref, edgebc_ref, dcx_ref, dcbc_ref, dhead_ref,
    ext, ext_d, grow, tail, v_sum, q_sum, end_sum, dbc_sum,
):
    g = pl.program_id(0)
    keep = info[1].astype(F32)

    @pl.when(g == 0)
    def _():
        grow[...] = jnp.exp(cum[...])
        for q in range(2):
            here = half(cum[...], q)
            tail[q * HALF : (q + 1) * HALF, :] = jnp.exp(here[HALF - 1 :, :] - here)
        v_sum[...] = jnp.zeros((ROWS, LANES), F32)
        q_sum[...] = jnp.zeros((ROWS, LANES), F32)
        end_sum[...] = jnp.zeros((16, LANES), F32)
        dbc_sum[...] = dbc[...]

    sums = head_sum_matrix(g)
    factor = rolled(grow[...], g)
    tails = rolled(tail[...], g)
    steps = rolled(dt[...], g)
    ends = [spread(factor[HALF - 1 : HALF]), spread(factor[ROWS - 1 : ROWS])]
    lam1 = lam[0].astype(F32)
    lams = [ends[1] * lam1 + own1[0], lam1]
    first = hin[0].astype(F32)
    states = [first, ends[0] * first + s0[0]]
    d_x = []
    for q in range(2):
        here = slice(q * HALF, (q + 1) * HALF)
        b, c = bca[here, :STATE].astype(BF16), bca[here, STATE:].astype(BF16)
        lam_q, state_q = lams[q].astype(BF16), states[q].astype(BF16)
        tail_wide = spread(half(tails, q))
        tail_step = tail_wide * spread(half(steps, q))
        x, dy_q = xa[here, :], dy[here, :].astype(F32)
        lb = dot(b, lam_q) * tail_wide
        d_x.append(dxi[here, :] + lb * spread(half(steps, q)))
        v_sum[here, :] += dot((x * lb).astype(BF16), sums)
        grow_wide = spread(half(factor, q))
        dy_grow = (dy_q * grow_wide).astype(BF16)
        carried = dot(c, state_q)
        q_sum[here, :] += dot((dy_q * grow_wide * carried).astype(BF16), sums)
        dbc_sum[here, :STATE] += dot_nt((x * tail_step).astype(BF16), lam_q)
        dbc_sum[here, STATE:] += dot_nt(dy_grow, state_q)
        last = jnp.sum(lams[q] * states[q], axis=0, keepdims=True) * ends[q]
        end_sum[8 * q : 8 * q + 8, :] += exact_dot(
            jnp.broadcast_to(last, (8, BLOCK)), sums.astype(F32)
        )
    d_in, d_par = conv_back(
        jnp.concatenate(d_x, axis=0), mixed[...], halo[...], cpar[...], keep, ext, ext_d
    )
    dmx_ref[...] = d_in[16:].astype(BF16)
    tailx_ref[...] = d_in[ROWS:]
    edgex_ref[...] = (d_in[:16] * keep).astype(BF16)
    dcx_ref[...] = d_par

    @pl.when(g == GROUPS - 1)
    def _():
        d_bc, d_par_bc = conv_back(
            dbc_sum[...], bc[...], halo_bc[...], cpar_bc[...], keep, ext, ext_d
        )
        dmbc_ref[:, :256] = d_bc[16:].astype(BF16)
        tailbc_ref[...] = d_bc[ROWS:]
        edgebc_ref[...] = (d_bc[:16] * keep).astype(BF16)
        dcbc_ref[...] = d_par_bc
        rates = -jnp.exp(hpar[1:2, :])
        logit = rate[...] + hpar[0:1, :]
        upper = lower_triangle().T
        before = lower_triangle(True)
        d_bias = jnp.zeros((1, LANES), F32)
        d_log = jnp.zeros((1, LANES), F32)
        usable = usable_rows(info)
        for q in range(2):
            here = slice(q * HALF, (q + 1) * HALF)
            step = dt[here, :]
            gs = gsum[...][:, here].T
            gs = jnp.concatenate([gs, jnp.zeros((HALF, LANES - 8 * GROUPS), F32)], axis=1)
            d_decay = exact_dot(upper, gs - step * u[here, :] + q_sum[here, :])
            d_decay = d_decay + exact_dot(before, step * v_sum[here, :])
            d_decay = d_decay + end_sum[8 * q : 8 * q + 1, :]
            d_step = u[here, :] + v_sum[here, :] + rates * d_decay
            d_rate = half(usable, q) * d_step * sigmoid(half(logit, q))
            d_bias += jnp.sum(d_rate, axis=0, keepdims=True)
            d_log += jnp.sum(d_decay * step * rates, axis=0, keepdims=True)
            dmbc_ref[here, 256:] = d_rate.astype(BF16)
        row = row_of((8, LANES))
        dhead_ref[...] = jnp.where(row == 0, d_bias, jnp.where(row == 1, d_log, 0.0))


def finish_call(
    info, xa, dxi, dy, mixed, halo, cpar, bca, cum, dt, rate, hpar, lam, hin, s0, own1, u, gsum, dbc
):
    bc_at = LOCAL // 256
    wide = whole((ROWS, LANES))
    return pl.pallas_call(
        finish_body,
        grid=(GROUPS,),
        out_shape=(
            shape((ROWS, LOCAL), BF16),
            shape((ROWS, 384), BF16),
            shape((16, LOCAL)),
            shape((16, 256)),
            shape((16, LOCAL), BF16),
            shape((16, 256), BF16),
            shape((8, LOCAL)),
            shape((8, 256)),
            shape((8, LANES)),
        ),
        in_specs=[
            SMEM,
            columns(ROWS, BLOCK),
            columns(ROWS, BLOCK),
            columns(ROWS, BLOCK),
            columns(ROWS, BLOCK),
            columns(16, BLOCK),
            columns(8, BLOCK),
            pl.BlockSpec((ROWS, 256), lambda g: (0, bc_at)),
            pl.BlockSpec((16, 256), lambda g: (0, bc_at)),
            pl.BlockSpec((8, 256), lambda g: (0, bc_at)),
            whole((ROWS, 256)),
            wide,
            wide,
            wide,
            whole((8, LANES)),
            grouped(STATE),
            grouped(STATE),
            grouped(STATE),
            grouped(STATE),
            wide,
            whole((8 * GROUPS, ROWS)),
            whole((ROWS, 256)),
        ],
        out_specs=(
            columns(ROWS, BLOCK),
            whole((ROWS, 384)),
            columns(16, BLOCK),
            whole((16, 256)),
            columns(16, BLOCK),
            whole((16, 256)),
            columns(8, BLOCK),
            whole((8, 256)),
            whole((8, LANES)),
        ),
        scratch_shapes=[
            pltpu.VMEM((ROWS + 32, BLOCK), F32),
            pltpu.VMEM((ROWS + 32, BLOCK), F32),
            pltpu.VMEM((ROWS, LANES), F32),
            pltpu.VMEM((ROWS, LANES), F32),
            pltpu.VMEM((ROWS, LANES), F32),
            pltpu.VMEM((ROWS, LANES), F32),
            pltpu.VMEM((16, LANES), F32),
            pltpu.VMEM((ROWS, 256), F32),
        ],
        compiler_params=params(),
        cost_estimate=pl.CostEstimate(
            flops=10 * ROWS * STATE * LOCAL, bytes_accessed=7_500_000, transcendentals=800_000
        ),
        name="finish_back",
    )(
        info, xa, dxi, dy, mixed, halo, cpar, mixed, halo, cpar, bca, cum, dt, rate, hpar,
        lam, hin, s0, own1, u, gsum, dbc,
    )


def gate_in_back_body(weight, info, dz, *rest):
    refs = len(weight.arrays)
    w_refs, (out_ref, buffer, sems) = rest[:refs], rest[refs:]
    weight.start(w_refs, info, buffer, sems)
    for b in range(4):
        rows = weight.wait(w_refs, info, b, buffer, sems)
        out_ref[:, rows] = dot_nt(dz[...], buffer[rows, :])


def gate_in_back(info, dz, weight):
    return pl.pallas_call(
        functools.partial(gate_in_back_body, weight),
        out_shape=shape((ROWS, WIDTH)),
        in_specs=[SMEM, whole((ROWS, LOCAL))] + weight.specs(),
        out_specs=whole((ROWS, WIDTH)),
        scratch_shapes=weight.scratch(),
        compiler_params=params(),
        cost_estimate=pl.CostEstimate(
            flops=2 * ROWS * WIDTH * LOCAL, bytes_accessed=7_000_000, transcendentals=0
        ),
        name="gate_in_back",
    )(info, dz, *weight.arrays)


def patch_body(dmx, dmbc, tailx, tailbc, edge, token, dxc_ref):
    dxc_ref[:, :LOCAL] = dmx[...]
    dxc_ref[:, LOCAL:] = dmbc[...]
    late = edge[...].astype(F32)
    dxc_ref[ROWS - 16 :, :LOCAL] = (tailx[...] + late[:, :LOCAL]).astype(BF16)
    dxc_ref[ROWS - 16 :, LOCAL:MIXED] = (tailbc[...] + late[:, LOCAL:]).astype(BF16)


def patch(dmx, dmbc, tailx, tailbc, edge, token):
    arrays = (dmx, dmbc, tailx, tailbc, edge)
    return pl.pallas_call(
        patch_body,
        out_shape=shape((ROWS, PACKED), BF16),
        in_specs=[whole(v.shape) for v in arrays] + [ANYWHERE],
        out_specs=whole((ROWS, PACKED)),
        compiler_params=params(),
        cost_estimate=pl.CostEstimate(flops=100_000, bytes_accessed=2_000_000, transcendentals=0),
        name="patch",
    )(*arrays, token)


def mixed_back_body(weight, info, dxc, part, *rest):
    refs = len(weight.arrays)
    w_refs, (out_ref, buffer, sems) = rest[:refs], rest[refs:]
    weight.start(w_refs, info, buffer, sems)
    for b in range(4):
        rows = weight.wait(w_refs, info, b, buffer, sems)
        out_ref[:, rows] = part[:, rows] + dot_nt(dxc[...], buffer[rows, :])


def mixed_back(info, dxc, part, weight):
    return pl.pallas_call(
        functools.partial(mixed_back_body, weight),
        out_shape=shape((ROWS, WIDTH)),
        in_specs=[SMEM, whole((ROWS, PACKED)), whole((ROWS, WIDTH))] + weight.specs(),
        out_specs=whole((ROWS, WIDTH)),
        scratch_shapes=weight.scratch(),
        compiler_params=params(),
        cost_estimate=pl.CostEstimate(
            flops=2 * ROWS * WIDTH * PACKED, bytes_accessed=9_000_000, transcendentals=0
        ),
        name="mixed_back",
    )(info, dxc, part, *weight.arrays)


def norm_back_body(own, came, h_ref, cot, gain, dh_ref, low_ref, dgain_ref):
    h = h_ref[...].astype(F32)
    scale = lax.rsqrt(jnp.mean(h * h, axis=1, keepdims=True) + EPSILON)
    d_norm = own[...] + came[...]
    inner = jnp.mean(d_norm * gain[...] * h, axis=1, keepdims=True) * scale * scale * scale
    dgain_ref[...] = jnp.broadcast_to(
        jnp.sum(d_norm * h * scale, axis=0, keepdims=True), (8, WIDTH)
    )
    dh = cot[...].astype(F32) + scale * d_norm * gain[...] - h * inner
    dh_ref[...] = dh
    low_ref[...] = dh.astype(BF16)


def norm_back(own, came, h, cot, gain):
    return pl.pallas_call(
        norm_back_body,
        out_shape=(shape((ROWS, WIDTH)), shape((ROWS, WIDTH), BF16), shape((8, WIDTH))),
        compiler_params=params(),
        cost_estimate=pl.CostEstimate(flops=3_000_000, bytes_accessed=8_000_000, transcendentals=0),
        name="norm_back",
    )(own, came, h, cot, gain)


def z_shift(r):
    return "dp", [(z, (z + r) % 4) for z in range(4)]


def y_shift(r):
    return "ctx", [(j, (j + 4 * r) % 16) for j in range(16)]


def x_shift(r):
    return "ctx", [(j, j - j % 4 + (j + r) % 4) for j in range(16)]


SHIFTS = {"z": z_shift, "y": y_shift, "x": x_shift}


def send(value, axis, r):
    name, pairs = SHIFTS[axis](r % 4)
    return lax.ppermute(value, name, pairs)


def swapped(value):
    return lax.ppermute(value, "section", [(0, 1), (1, 0)])


def after(values, place):
    nothing = jnp.int32(0)
    for value in values:
        corner = lax.slice(value, (0,) * value.ndim, (1,) * value.ndim).reshape(())
        nothing = nothing + (corner != corner).astype(jnp.int32)
    return {axis: n + nothing for axis, n in place.items()}


def pieces(mine, came, layer, section, place):
    rows = SHARD // 2

    def piece(source, side, axis):
        return lax.dynamic_slice_in_dim(source, side * rows + place[axis] * PIECE, PIECE, 0)

    first = jnp.concatenate(
        [
            jnp.where(section == layer, piece(mine, side, axis), piece(came, side, axis))
            for side, axis in enumerate("xy")
        ]
    )
    got = [send(first, "z", -r) for r in range(1, 4)]
    out = [mine, came]
    for side, axis in enumerate("xy"):
        stack = jnp.concatenate([g[side * PIECE : (side + 1) * PIECE] for g in got])
        out += [stack] + [send(stack, axis, -r) for r in range(1, 4)]
    return out, got


def summed(terms):
    a, b, c, d = (t.astype(F32) for t in terms)
    return (a + c) + (b + d)


def arrived(terms, axis):
    return [terms[0]] + [send(terms[r], axis, r) for r in range(1, 4)]


def total_of(value):
    for axis in "xyz":
        low = value.astype(BF16)
        value = summed([low] + [send(low, axis, r) for r in range(1, 4)])
    return value


def fold_body(slot, counts, outer, inner, info, *rest):
    refs, outs, total = rest[: sum(counts)], rest[sum(counts) + 1 : -1], rest[-1]
    column = 0
    for count in counts:
        arrays, refs = refs[:count], refs[count:]
        cols = slice(column, column + arrays[0].shape[1])
        total[:, cols] = summed([a[...] for a in arrays]) if count == 4 else arrays[0][...].astype(F32)
        column = cols.stop
    for r in range(4):
        first = lax.rem(info[slot] + r, 4) * inner
        parts = [
            total[pl.ds(pl.multiple_of(n * 4 * inner + first, 8), inner), :] for n in range(outer)
        ]
        outs[r][...] = jnp.concatenate(parts, axis=0).astype(BF16)


def fold(info, axis, groups, outer, inner, token):
    slot = 10 + "zyx".index(axis)
    arrays = [a for group in groups for a in group]
    rows, width = arrays[0].shape[0], sum(group[0].shape[1] for group in groups)
    return pl.pallas_call(
        functools.partial(fold_body, slot, [len(group) for group in groups], outer, inner),
        out_shape=[shape((rows // 4, width), BF16)] * 4,
        in_specs=[SMEM] + [whole(a.shape) for a in arrays] + [ANYWHERE],
        out_specs=[whole((rows // 4, width))] * 4,
        scratch_shapes=[pltpu.VMEM((rows, width), F32)],
        compiler_params=params(),
        cost_estimate=pl.CostEstimate(flops=2_000_000, bytes_accessed=8_000_000, transcendentals=0),
        name="fold",
    )(info, *arrays, token)


PARITY = [[j for j in range(16) if j % 2 == e] for e in range(2)]
NEIGHBOURS = [(j, j ^ 1) for j in range(16)]


def exchange(value):
    return lax.all_to_all(value, "ctx", 0, 0, axis_index_groups=PARITY)


def halo_shift(value, step):
    pairs = [(j, j + 2 * step) for j in range(16) if 0 <= j + 2 * step < 16]
    return lax.ppermute(value, "ctx", pairs)


def halves(values, section):
    grid = values.reshape(values.shape[0], GROUPS, 2, -1)
    size = values.shape[1] // 2
    return [
        lax.dynamic_index_in_dim(grid, i, 2, False).reshape(-1, size)
        for i in (section, 1 - section)
    ]


def turns(low, high):
    rows = low.shape[0]
    parts = [v.reshape(rows, GROUPS, 1, -1) for v in (low, high)]
    return jnp.concatenate(parts, axis=2).reshape(rows, -1)


def pick_x_body(info, x_ref, dt_ref, *outs):
    head, lane = row_of((HEADS, LANES)), lane_of((HEADS, LANES))
    for out, side in zip(outs, (info[0], 1 - info[0]), strict=True):
        for d in range(GROUPS):
            cols = pl.ds(pl.multiple_of((2 * d + side) * BLOCK, LANES), BLOCK)
            out[:, d * BLOCK : (d + 1) * BLOCK] = x_ref[:, cols]
        out[:, LOCAL:MIXED] = x_ref[:, INNER:]
        here = (head // OWN == 2 * (lane // 8) + side) & (head % OWN == lane % 8)
        out[:, MIXED:] = dot(dt_ref[...], here.astype(BF16)).astype(BF16)


def pick_x(section, x, dt):
    return pl.pallas_call(
        pick_x_body,
        out_shape=[shape((SHARD, PACKED), BF16)] * 2,
        in_specs=[SMEM, whole((SHARD, CONV_CH)), whole((SHARD, HEADS))],
        out_specs=[whole((SHARD, PACKED))] * 2,
        compiler_params=params(),
        cost_estimate=pl.CostEstimate(flops=0, bytes_accessed=6_000_000, transcendentals=0),
        name="pick_x",
    )(section, x, dt)


def pick_zo_body(info, z_ref, o_ref, token, *outs):
    for out, side in zip(outs, (info[0], 1 - info[0]), strict=True):
        for d in range(GROUPS):
            cols = pl.ds(pl.multiple_of((2 * d + side) * BLOCK, LANES), BLOCK)
            out[:, d * BLOCK : (d + 1) * BLOCK] = z_ref[:, cols]
        rows = pl.ds(pl.multiple_of(side * SHARD, SHARD), SHARD)
        out[:, LOCAL:] = o_ref[rows, :]


def pick_zo(section, z, o, token):
    return pl.pallas_call(
        pick_zo_body,
        out_shape=[shape((SHARD, LOCAL + WIDTH), BF16)] * 2,
        in_specs=[SMEM, whole((SHARD, INNER)), whole((2 * SHARD, WIDTH)), ANYWHERE],
        out_specs=[whole((SHARD, LOCAL + WIDTH))] * 2,
        compiler_params=params(),
        cost_estimate=pl.CostEstimate(flops=0, bytes_accessed=9_000_000, transcendentals=0),
        name="pick_zo",
    )(section, z, o, token)


def head_lanes(values):
    rows = values.shape[0]
    grid = jnp.pad(values.reshape(rows, GROUPS, OWN), ((0, 0), (0, 0), (0, 8 - OWN)))
    return jnp.pad(grid.reshape(rows, 8 * GROUPS), ((0, 0), (0, LANES - 8 * GROUPS)))


def lanes_heads(values):
    rows = values.shape[0]
    return values[:, : 8 * GROUPS].reshape(rows, GROUPS, 8)[:, :, :OWN].reshape(rows, -1)


def on_device(
    boundary,
    lengths,
    norm_gain,
    w_z,
    w_xbc,
    w_dt,
    conv_weight,
    conv_bias,
    dt_bias,
    a_log,
    d_skip,
    gate_gain,
    w_out,
):
    section = lax.axis_index("section")
    group = lax.axis_index("dp")
    ctx = lax.axis_index("ctx")
    place = {"z": group, "y": ctx // 4, "x": ctx % 4}
    micro = ctx % 2
    chunk = ctx // 2

    def ordered(mine, came):
        return jnp.where(section == 0, mine, came), jnp.where(section == 0, came, mine)

    at = section.reshape(1).astype(jnp.int32)
    mine_x, other_x = pick_x(at, w_xbc[0], w_dt[0])
    came_x = swapped(other_x)
    mine_zo, other_zo = pick_zo(at, w_z[0], w_out[0], mine_x)
    came_zo = swapped(other_zo)
    low_x, got = pieces(mine_x, came_x, 0, section, place)
    low_zo, got = pieces(mine_zo, came_zo, 0, section, after(got, place))
    here = after(got, {"section": section})["section"]
    high_x = [lax.all_gather(jnp.where(here == 1, mine_x, came_x), "dp", tiled=True)]
    high_zo = [lax.all_gather(jnp.where(here == 1, mine_zo, came_zo), "dp", tiled=True)]
    weights_x = [Weight(v, n, PACKED) for n, v in enumerate((low_x, high_x))]
    weights_z = [Weight(v, n, LOCAL) for n, v in enumerate((low_zo, high_zo))]
    weights_o = [Weight(v, n, WIDTH, LOCAL) for n, v in enumerate((low_zo, high_zo))]

    small = jnp.zeros((16, 832), F32)
    small = small.at[:4].set(conv_weight[0].astype(F32)).at[4].set(conv_bias[0].astype(F32))
    small = small.at[5, :384].set(norm_gain[0].astype(F32))
    small = small.at[6, :768].set(gate_gain[0].astype(F32))
    small = small.at[8, :HEADS].set(dt_bias[0]).at[9, :HEADS].set(a_log[0])
    small = small.at[10, :HEADS].set(d_skip[0])
    smalls = jnp.stack([small] + [send(small, "z", -r) for r in range(1, 4)])
    smalls = lax.dynamic_slice_in_dim(jnp.concatenate([smalls, smalls]), (4 - group) % 4, 4)
    cpars, gains_one, gains_two, hpars = [], [], [], []
    for values in ordered(smalls, swapped(smalls)):
        full = jnp.transpose(values[:, :8], (1, 0, 2)).reshape(8, CONV_CH)
        local = halves(full[:, :INNER], section)[0]
        cpars.append(jnp.concatenate([local, full[:, INNER:]], axis=1))
        gains_one.append(values[:, 5, :384].reshape(1, WIDTH))
        gains_two.append(halves(values[:, 6, :768].reshape(1, INNER), section)[0])
        hpars.append(jnp.pad(head_lanes(halves(values[0, 8:11, :HEADS], section)[0]), ((0, 5), (0, 0))))

    own_rows = lax.dynamic_index_in_dim(boundary[0], micro, 0, False)
    other_rows = lax.dynamic_index_in_dim(boundary[0], 1 - micro, 0, False)
    came = lax.ppermute(other_rows, "ctx", NEIGHBOURS)
    block = jnp.where(
        micro == 0, jnp.concatenate([own_rows, came]), jnp.concatenate([came, own_rows])
    )
    hidden, cotangent = ordered(block, swapped(block))

    pair = lengths[group, micro]
    padded = (pair[0] + SPAN - 1) // SPAN * SPAN
    offset = chunk * ROWS
    begin = jnp.where(offset >= padded, padded, 0)
    length = jnp.where(offset >= padded, pair[1], pair[0])
    live = jnp.clip(length - (offset - begin), 0, ROWS)
    offsets = jnp.arange(CHUNKS, dtype=jnp.int32) * ROWS
    keeps = ((offsets != 0) & (offsets != padded)).astype(jnp.int32)
    keep = (offset != 0) & (offset != padded)
    at = [place["z"], place["y"], place["x"], section]
    info = jnp.concatenate(
        [jnp.stack([live, keep]).astype(jnp.int32), keeps, jnp.stack(at).astype(jnp.int32)]
    )

    def forward(h, layer):
        cpar, hpar = cpars[layer], hpars[layer]
        normed, mixed, rate = in_proj(info, h, gains_one[layer], weights_x[layer])
        halo = halo_shift(mixed[ROWS - 16 :], 1)
        gate = gate_proj(info, normed, weights_z[layer])
        xa, bca, cum, dt, s0, msg = state_call(info, mixed, halo, cpar, rate, hpar)
        came = exchange(msg)
        y_in = inside_call(xa, bca, cum, dt, hpar)
        hin = exchange(scan_call(info, came, False, gate)).reshape(GROUPS, STATE, BLOCK)
        y, part = out_proj(
            info, y_in, bca, cum, hin, s0, gate, gains_two[layer], weights_o[layer]
        )
        result, low, branch, scale = join(info, h, part, swapped(part))
        saved = (h, normed, mixed, halo, rate, gate, xa, bca, cum, dt, s0, msg, hin, y, branch, scale)
        return result, low, saved

    def backward(cot, saved, layer, higher=None):
        h, normed, mixed, halo, rate, gate, xa, bca, cum, dt, s0, msg, hin, y, branch, scale = saved
        cpar, hpar = cpars[layer], hpars[layer]
        bg, dy, dz, normed_two, d_gain_two = gate_back(
            info, cot, y, gate, gains_two[layer], branch, scale, weights_o[layer]
        )
        own1, msg_back = own_grad(dy, bca, cum, msg)
        came = exchange(msg_back)
        normed_two_t, normed_t = normed_two.T, normed.T

        def terms(source, axis, other, place):
            grid = source.reshape((4, 4, 96, ROWS) if axis == "y" else (4, 4, 4, 24, ROWS))
            out = []
            for r in range(4):
                rows = lax.dynamic_index_in_dim(
                    grid, (place[axis] + r) % 4, "zyx".index(axis), False
                )
                out.append(dot(rows.reshape(SHARD, ROWS), other).astype(BF16))
            return out

        def first_stage(source, other):
            return lax.psum_scatter(dot(source, other).astype(BF16), "dp", tiled=True)

        if layer == 1:
            sums = [first_stage(normed_two_t, bg), first_stage(normed_t, dz)]
        dxi, d_skips, gsum, u, dbc = inside_back(dy, xa, bca, cum, dt, hpar)
        part = gate_in_back(info, dz, weights_z[layer])
        lam = exchange(scan_call(info, came, True, part)).reshape(GROUPS, STATE, BLOCK)
        if layer == 0:
            here = after([lam], place)
            sent_z = arrived(terms(normed_t, "y", dz, here), "y")
            sent_o = arrived(terms(normed_two_t, "x", bg, here), "x")
        dmx, dmbc, tailx, tailbc, edgex, edgebc, d_parx, d_parbc, d_heads = finish_call(
            info, xa, dxi, dy, mixed, halo, cpar, bca, cum, dt, rate, hpar, lam, hin, s0, own1, u, gsum, dbc
        )
        edge = halo_shift(jnp.concatenate([edgex, edgebc], axis=1), -1)
        token = d_heads
        if layer == 0:
            higher = fold(info, "y", [[v] for v in higher], 1, 96, d_heads)
            token = higher[0]
        dxc = patch(dmx, dmbc, tailx, tailbc, edge, token)
        part = mixed_back(info, dxc, part, weights_x[layer])
        dh, dh_low, d_gain_one = norm_back(part, swapped(part), h, cot, gains_one[layer])

        if layer == 0:
            middle = PACKED // 2
            sent_l = arrived(terms(normed_t, "y", dxc[:, :middle], place), "y")
            sent_r = arrived(terms(normed_t, "x", dxc[:, middle:], place), "x")
            left = arrived(fold(info, "x", [sent_z, sent_l], 4, 24, dh_low), "x")
            right = arrived(fold(info, "y", [sent_o, sent_r], 4, 24, dh_low), "y")
            sums = higher, summed(arrived(fold(info, "z", [left, right], 1, 24, dh_low), "z"))
        else:
            sums.append(first_stage(normed_t, dxc))
        d_skip_row = jnp.sum(d_skips[0:1].reshape(1, 4 * OWN, HEADDIM), axis=2)
        rows = jnp.where(jnp.arange(8)[:, None] == 5, d_gain_two, d_parx)
        rows = jnp.concatenate([rows, d_parbc], axis=1)
        more = jnp.concatenate(
            [
                d_gain_one[:1],
                jnp.pad(d_heads[:2], ((0, 0), (0, WIDTH - LANES))),
                jnp.pad(head_lanes(d_skip_row), ((0, 4), (0, WIDTH - LANES))),
            ]
        )
        rows = jnp.concatenate([rows, jnp.pad(more, ((0, 0), (0, 2 * STATE)))])
        return dh, dh_low, sums, rows

    _, middle, saved_low = forward(hidden, 0)
    out_high, _, saved_high = forward(middle, 1)
    _, back, higher, rows_high = backward(cotangent, saved_high, 1)
    dh_low, back, (higher, low), rows_low = backward(back, saved_low, 0, higher)

    higher = fold(info, "x", [arrived(higher, "y")], 1, 24, back)
    high = summed(arrived(higher, "x"))
    high_o, high_z, high_x = jnp.split(high, (WIDTH, WIDTH + LOCAL), axis=1)
    at = (LOCAL, LOCAL + PACKED // 2, LOCAL + PACKED // 2 + WIDTH)
    low_z, low_l, low_o, low_r = jnp.split(low, at, axis=1)

    rows = total_of(jnp.concatenate([rows_low, rows_high]))
    own, given = ordered(rows[:16], rows[16:])
    rows_0, rows_1 = ordered(own, swapped(given))
    wide = jnp.concatenate(
        [turns(rows_0[:8, :LOCAL], rows_1[:8, :LOCAL]), rows_0[:8, LOCAL:] + rows_1[:8, LOCAL:]],
        axis=1,
    )
    head_rows = turns(lanes_heads(rows_0[9:12, :LANES]), lanes_heads(rows_1[9:12, :LANES]))
    index = group * 16 + ctx
    d_conv = lax.dynamic_slice(wide, (0, index * 52), (5, 52))
    d_gain_two = lax.dynamic_slice(wide, (5, index * 48), (1, 48))
    d_gain_one = lax.dynamic_slice(rows_0, (8, index * 24), (1, 24))

    own, given = ordered(
        jnp.concatenate([low_z, low_l, low_r], axis=1), jnp.concatenate([high_z, high_x], axis=1)
    )
    first, second = ordered(own, swapped(given))
    sum_z = turns(first[:, :LOCAL], second[:, :LOCAL])
    at_x, at_bc, at_dt = LOCAL, LOCAL + LOCAL, LOCAL + MIXED
    sum_x = turns(first[:, at_x:at_bc], second[:, at_x:at_bc])
    sum_bc = first[:, at_bc:at_dt] + second[:, at_bc:at_dt]
    sum_dt = turns(lanes_heads(first[:, at_dt:]), lanes_heads(second[:, at_dt:]))

    trips = []
    for flip in range(2):
        pairs = [
            (c * 16 + j, (flip ^ (j % 2)) * 16 + 8 * c + j // 2) for c in range(2) for j in range(16)
        ]
        value = jnp.where(micro == flip, low_o, high_o)
        trips.append(lax.ppermute(value, ("section", "ctx"), pairs))
    sum_o = jnp.concatenate(ordered(*trips))

    def returned(rows, layer):
        pairs = [(layer * 16 + a, layer * 16 + b) for a, b in NEIGHBOURS]
        other = lax.ppermute(
            jnp.where(micro == 0, rows[HALF:], rows[:HALF]), ("section", "ctx"), pairs
        )
        mine = jnp.where(micro == 0, rows[:HALF], rows[HALF:])
        return jnp.where(micro == 0, jnp.stack([mine, other]), jnp.stack([other, mine]))

    top = jnp.where(section == 0, returned(dh_low, 0), returned(out_high, 1))
    return (
        top[None],
        d_gain_one,
        sum_z[None],
        jnp.concatenate([sum_x, sum_bc], axis=1)[None],
        sum_dt[None],
        d_conv[None, :4],
        d_conv[4:5],
        head_rows[0:1],
        head_rows[1:2],
        head_rows[2:3],
        d_gain_two,
        sum_o[None],
    )


def solution(mesh):
    in_specs = (
        P("section", None, ("dp", "ctx"), None),
        P(),
        P("section", "dp"),
        P("section", "dp", None),
        P("section", "dp", None),
        P("section", "dp", None),
        P("section", None, "dp"),
        P("section", "dp"),
        P("section", None),
        P("section", None),
        P("section", None),
        P("section", "dp"),
        P("section", "dp", None),
    )
    out_specs = (
        P("section", None, ("dp", "ctx"), None),
        P("section", ("dp", "ctx")),
        P("section", ("dp", "ctx"), None),
        P("section", ("dp", "ctx"), None),
        P("section", ("dp", "ctx"), None),
        P("section", None, ("dp", "ctx")),
        P("section", ("dp", "ctx")),
        P("section", None),
        P("section", None),
        P("section", None),
        P("section", ("dp", "ctx")),
        P("section", ("dp", "ctx"), None),
    )
    return jax.shard_map(
        on_device, mesh=mesh, in_specs=in_specs, out_specs=out_specs, check_vma=False
    )
```

```python
import functools

import jax
import jax.numpy as jnp
from jax import lax
from jax.experimental import pallas as pl
from jax.experimental.pallas import tpu as pltpu
from jax.sharding import PartitionSpec as P

HEADS = 48
HEADDIM = 64
STATE = 128
KERNEL = 4
SPAN = 256
MICRO = 2
WIDTH = 1536
INNER = 3072
CONV_CH = 3328
LANES = 128
CHUNKS = 8
GROUPS = 4
OWN = 6
BLOCK = OWN * HEADDIM
LOCAL = GROUPS * BLOCK
MIXED = LOCAL + 2 * STATE
PACKED = MIXED + LANES
ROWS = 256
HALF = 128
SHARD = 384
TALL = SHARD + 16
PIECE = 48
STATE_HALF = STATE // 2
MESSAGE = STATE_HALF + 16
SMALL = 64
EPSILON = 1e-05
PRECISE = lax.Precision.HIGHEST
F32 = jnp.float32
BF16 = jnp.bfloat16
VMEM_LIMIT = 56 * 1024 * 1024


def params(**more):
    return pltpu.CompilerParams(vmem_limit_bytes=VMEM_LIMIT, **more)


def whole(shape):
    return pl.BlockSpec(shape, lambda *_: (0,) * len(shape))


def columns(rows, width):
    return pl.BlockSpec((rows, width), lambda g: (0, g))


def grouped(rows):
    return pl.BlockSpec((1, rows, BLOCK), lambda g: (g, 0, 0))


MESSAGES = pl.BlockSpec((2, MESSAGE, BLOCK), lambda g: (g, 0, 0))
SMEM = pl.BlockSpec(memory_space=pltpu.SMEM)
ANYWHERE = pl.BlockSpec(memory_space=pl.ANY)


def shape(dims, kind=F32):
    return jax.ShapeDtypeStruct(dims, kind)


def dot(a, b):
    return jnp.dot(a, b, preferred_element_type=F32)


def dot_nt(a, b):
    return lax.dot_general(a, b, (((1,), (1,)), ((), ())), preferred_element_type=F32)


def exact_dot(a, b):
    return jnp.dot(a, b, precision=PRECISE, preferred_element_type=F32)


def lane_of(dims):
    return lax.broadcasted_iota(jnp.int32, dims, len(dims) - 1)


def row_of(dims):
    return lax.broadcasted_iota(jnp.int32, dims, len(dims) - 2)


def sigmoid(v):
    return 1.0 / (1.0 + jnp.exp(-v))


def softplus(v):
    return jnp.maximum(v, 0.0) + jnp.log1p(jnp.exp(-jnp.abs(v)))


def rolled(values, g):
    return pltpu.roll(values, lax.rem(LANES - 8 * g, LANES), axis=1)


def pair_lanes(values, p):
    low = lane_of((values.shape[0], LANES)) < HEADDIM
    return jnp.where(low, values[:, 2 * p : 2 * p + 1], values[:, 2 * p + 1 : 2 * p + 2])


def spread(values):
    return jnp.concatenate([pair_lanes(values, p) for p in range(OWN // 2)], axis=1)


def head_sum_matrix(g):
    head = row_of((BLOCK, LANES)) // HEADDIM
    return (lane_of((BLOCK, LANES)) == head + 8 * g).astype(BF16)


def lower_triangle(strict=False):
    i, j = row_of((HALF, HALF)), lane_of((HALF, HALF))
    return ((i > j) if strict else (i >= j)).astype(F32)


def usable_rows(info):
    return (row_of((ROWS, 1)) < info[0]).astype(F32)


def half(values, q):
    return values[q * HALF : (q + 1) * HALF]


class Weight:
    def __init__(self, arrays, layer, width, first=0):
        self.arrays = arrays
        self.stride = arrays[0].shape[0] // 4
        self.layer = layer
        self.width = width
        self.columns = pl.ds(first, width)

    def block(self, info, b):
        return lax.rem(info[10] + b, 4) * SHARD

    def parts(self, refs, info, b):
        start = self.block(info, b)
        if len(refs) == 1:
            there = pl.multiple_of(start // SHARD * self.stride, 16)
            return [(refs[0].at[pl.ds(there, SHARD)], start, SHARD)]
        out = []
        for side in range(2):
            mine = info[12 - side]
            for step in range(4):
                source = refs[2 + 4 * side + step].at[pl.ds((b - 1) * PIECE, PIECE)]
                row = start + side * (SHARD // 2) + lax.rem(mine + step, 4) * PIECE
                out.append((source, row, PIECE))
        return out

    def copies(self, refs, info, b, buffer, sems):
        return [
            pltpu.make_async_copy(
                source.at[:, self.columns],
                buffer.at[pl.ds(pl.multiple_of(row, 16), count)],
                sems.at[b, n],
            )
            for n, (source, row, count) in enumerate(self.parts(refs, info, b))
        ]

    def own_copy(self, source, info, buffer, sems):
        rows = pl.ds(pl.multiple_of(self.block(info, 0), SHARD), SHARD)
        source = source.at[pl.ds(0, SHARD), self.columns]
        return pltpu.make_async_copy(source, buffer.at[rows], sems.at[0, 0])

    def start(self, refs, info, buffer, sems):
        whole_array = len(refs) == 1
        if not whole_array:
            for n in range(2):

                @pl.when((info[13] == self.layer) == (n == 0))
                def _(n=n):
                    self.own_copy(refs[n], info, buffer, sems).start()

        for b in range(0 if whole_array else 1, 4):
            for c in self.copies(refs, info, b, buffer, sems):
                c.start()

    def wait(self, refs, info, b, buffer, sems):
        if b == 0 and len(refs) > 1:
            self.own_copy(refs[0], info, buffer, sems).wait()
        else:
            for c in self.copies(refs, info, b, buffer, sems):
                c.wait()
        return pl.ds(pl.multiple_of(self.block(info, b), SHARD), SHARD)

    def specs(self):
        return [ANYWHERE] * len(self.arrays)

    def scratch(self):
        return [pltpu.VMEM((4 * SHARD, self.width), BF16), pltpu.SemaphoreType.DMA((4, 8))]

    def product(self, refs, info, left, buffer, sems, total):
        for b in range(4):
            self.wait(refs, info, b, buffer, sems)
        step = 512 if self.width % 512 == 0 else 640
        for at in range(0, self.width, step):
            total[:, at : at + step] = dot(left[...], buffer[:, at : at + step])


def in_proj_body(weight, tokens, info, h_ref, gain_ref, *rest):
    refs = len(weight.arrays)
    w_refs, rest = rest[:refs], rest[refs + tokens :]
    (normed_ref, mixed_ref, rate_ref, buffer, sems, total) = rest
    weight.start(w_refs, info, buffer, sems)
    h = h_ref[...].astype(F32)
    scale = lax.rsqrt(jnp.mean(h * h, axis=1, keepdims=True) + EPSILON)
    normed_ref[...] = (h * scale * gain_ref[...]).astype(BF16)
    weight.product(w_refs, info, normed_ref, buffer, sems, total)
    mixed_ref[...] = total[:, :MIXED].astype(BF16)
    rate_ref[...] = total[:, MIXED:]


def in_proj(info, h, gain, weight, tokens):
    return pl.pallas_call(
        functools.partial(in_proj_body, weight, len(tokens)),
        out_shape=(shape((ROWS, WIDTH), BF16), shape((ROWS, MIXED), BF16), shape((ROWS, LANES))),
        in_specs=[SMEM, whole((ROWS, WIDTH)), whole((1, WIDTH))]
        + weight.specs()
        + [ANYWHERE] * len(tokens),
        out_specs=(whole((ROWS, WIDTH)), whole((ROWS, MIXED)), whole((ROWS, LANES))),
        scratch_shapes=weight.scratch() + [pltpu.VMEM((ROWS, PACKED), F32)],
        compiler_params=params(),
        cost_estimate=pl.CostEstimate(
            flops=2 * ROWS * WIDTH * PACKED, bytes_accessed=8_000_000, transcendentals=0
        ),
        name="in_proj",
    )(info, h, gain, *weight.arrays, *tokens)


def gate_proj_body(weight, tokens, info, normed_ref, *rest):
    refs = len(weight.arrays)
    w_refs, (gate_ref, buffer, sems) = rest[:refs], rest[refs + tokens :]
    weight.start(w_refs, info, buffer, sems)
    weight.product(w_refs, info, normed_ref, buffer, sems, gate_ref)


def gate_proj(info, normed, weight, tokens):
    return pl.pallas_call(
        functools.partial(gate_proj_body, weight, len(tokens)),
        out_shape=shape((ROWS, LOCAL)),
        in_specs=[SMEM, whole((ROWS, WIDTH))] + weight.specs() + [ANYWHERE] * len(tokens),
        out_specs=whole((ROWS, LOCAL)),
        scratch_shapes=weight.scratch(),
        compiler_params=params(),
        cost_estimate=pl.CostEstimate(
            flops=2 * ROWS * WIDTH * LOCAL, bytes_accessed=7_000_000, transcendentals=0
        ),
        name="gate_proj",
    )(info, normed, *weight.arrays, *tokens)


def conv_sum_of(values, halo, cpar, keep, ext):
    width = values.shape[1]
    ext[0:16, :width] = halo.astype(F32) * keep
    ext[16 : 16 + ROWS, :width] = values.astype(F32)
    total = cpar[4:5, :]
    for k in range(KERNEL):
        total = total + cpar[k : k + 1, :] * ext[13 + k : 13 + k + ROWS, :width]
    return total


def state_body(
    info, mixed, halo, cpar, bc, halo_bc, cpar_bc, rate, hpar,
    xa_ref, bca_ref, cum_ref, dt_ref, s0_ref, msg_ref, ext, bt, tail,
):
    g = pl.program_id(0)
    keep = info[1].astype(F32)

    @pl.when(g == 0)
    def _():
        total = conv_sum_of(bc[...], halo_bc[...], cpar_bc[...], keep, ext)
        active = total * sigmoid(total)
        bca_ref[...] = active
        bt[...] = active[:, :STATE].T.astype(BF16)
        dt = usable_rows(info) * softplus(rate[...] + hpar[0:1, :])
        log_decay = dt * -jnp.exp(hpar[1:2, :])
        dt_ref[...] = dt
        tri = lower_triangle()
        for q in range(2):
            rows = pl.ds(q * HALF, HALF)
            cum = exact_dot(tri, half(log_decay, q))
            cum_ref[rows, :] = cum
            tail[rows, :] = jnp.exp(cum[HALF - 1 :, :] - cum) * half(dt, q)

    total = conv_sum_of(mixed[...], halo[...], cpar[...], keep, ext)
    xa = total * sigmoid(total)
    xa_ref[...] = xa
    weighted = (xa * spread(rolled(tail[...], g))).astype(BF16)
    ends = rolled(cum_ref[...], g)
    end0, end1 = ends[HALF - 1 : HALF], ends[ROWS - 1 : ROWS]
    s0 = dot(bt[:, :HALF], half(weighted, 0))
    s1 = dot(bt[:, HALF:], half(weighted, 1))
    s0_ref[0] = s0
    state = (spread(jnp.exp(end1)) * s0 + s1).astype(BF16)
    damp = spread(jnp.exp(end0 + end1))
    high = damp.astype(BF16)
    low = (damp - high.astype(F32)).astype(BF16)
    row = row_of((16, BLOCK))
    damps = jnp.where(row == 0, high.astype(F32), low.astype(F32)).astype(BF16)
    for r in range(2):
        msg_ref[r, :STATE_HALF, :] = state[r * STATE_HALF : (r + 1) * STATE_HALF]
        msg_ref[r, STATE_HALF:, :] = damps


def state_call(info, mixed, halo, cpar, rate, hpar):
    bc_at = LOCAL // 256
    return pl.pallas_call(
        state_body,
        grid=(GROUPS,),
        out_shape=(
            shape((ROWS, LOCAL)),
            shape((ROWS, 256)),
            shape((ROWS, LANES)),
            shape((ROWS, LANES)),
            shape((GROUPS, STATE, BLOCK)),
            shape((CHUNKS, MESSAGE, BLOCK), BF16),
        ),
        in_specs=[
            SMEM,
            columns(ROWS, BLOCK),
            columns(16, BLOCK),
            columns(8, BLOCK),
            pl.BlockSpec((ROWS, 256), lambda g: (0, bc_at)),
            pl.BlockSpec((16, 256), lambda g: (0, bc_at)),
            pl.BlockSpec((8, 256), lambda g: (0, bc_at)),
            whole((ROWS, LANES)),
            whole((8, LANES)),
        ],
        out_specs=(
            columns(ROWS, BLOCK),
            whole((ROWS, 256)),
            whole((ROWS, LANES)),
            whole((ROWS, LANES)),
            grouped(STATE),
            MESSAGES,
        ),
        scratch_shapes=[
            pltpu.VMEM((ROWS + 32, BLOCK), F32),
            pltpu.VMEM((STATE, ROWS), BF16),
            pltpu.VMEM((ROWS, LANES), F32),
        ],
        compiler_params=params(),
        cost_estimate=pl.CostEstimate(
            flops=2 * ROWS * STATE * LOCAL, bytes_accessed=4_500_000, transcendentals=400_000
        ),
        name="conv_state",
    )(info, mixed, halo, cpar, mixed, halo, cpar, rate, hpar)


def inside_body(xa, bca, cum, dt, hpar, y_ref, cum_t, scores):
    g = pl.program_id(0)

    @pl.when(g == 0)
    def _():
        tri = lower_triangle()
        for q in range(2):
            b, c = half(bca[:, :STATE], q).astype(BF16), half(bca[:, STATE:], q).astype(BF16)
            scores[q] = dot_nt(c, b) * tri
            cum_t[:, q * HALF : (q + 1) * HALF] = half(cum[...], q).T

    cols = rolled(cum[...], g)
    rows = cum_t[pl.ds(pl.multiple_of(8 * g, 8), 8), :]
    steps = rolled(dt[...], g)
    skips = rolled(hpar[...], g)[2:3, :]
    low = lane_of((HALF, LANES)) < HEADDIM
    for q in range(2):
        for p in range(OWN // 2):
            lanes = slice(p * LANES, (p + 1) * LANES)
            x = xa[q * HALF : (q + 1) * HALF, lanes]
            xdt = x * pair_lanes(half(steps, q), p)
            both = jnp.concatenate([jnp.where(low, xdt, 0.0), jnp.where(low, 0.0, xdt)], axis=0)
            mats = []
            for i in (2 * p, 2 * p + 1):
                gap = half(cols, q)[:, i : i + 1] - rows[i : i + 1, q * HALF : (q + 1) * HALF]
                mats.append((jnp.exp(jnp.minimum(gap, 0.0)) * scores[q]).astype(BF16))
            y = dot(jnp.concatenate(mats, axis=1), both.astype(BF16))
            y_ref[q * HALF : (q + 1) * HALF, lanes] = y + x * pair_lanes(skips, p)


def inside_call(xa, bca, cum, dt, hpar):
    return pl.pallas_call(
        inside_body,
        grid=(GROUPS,),
        out_shape=shape((ROWS, LOCAL)),
        in_specs=[
            columns(ROWS, BLOCK),
            whole((ROWS, 256)),
            whole((ROWS, LANES)),
            whole((ROWS, LANES)),
            whole((8, LANES)),
        ],
        out_specs=columns(ROWS, BLOCK),
        scratch_shapes=[pltpu.VMEM((LANES, ROWS), F32), pltpu.VMEM((2, HALF, HALF), F32)],
        compiler_params=params(),
        cost_estimate=pl.CostEstimate(
            flops=2 * HEADS * HALF * HALF * LANES, bytes_accessed=3_300_000, transcendentals=800_000
        ),
        name="inside",
    )(xa, bca, cum, dt, hpar)


def scan_body(backward, info, msg, *rest):
    out_ref = rest[-1]
    carry = jnp.zeros((STATE_HALF, BLOCK), F32)
    for k in reversed(range(CHUNKS)) if backward else range(CHUNKS):
        keep = info[2 + k].astype(F32)
        if not backward:
            carry = carry * keep
        out_ref[k] = carry.astype(BF16)
        damps = msg[k, STATE_HALF:, :].astype(F32)
        carry = (damps[0:1] + damps[1:2]) * carry + msg[k, :STATE_HALF, :].astype(F32)
        if backward:
            carry = carry * keep


def scan_call(info, msg, backward, *tokens):
    return pl.pallas_call(
        functools.partial(scan_body, backward),
        out_shape=shape((CHUNKS, STATE_HALF, BLOCK), BF16),
        in_specs=[SMEM, whole((CHUNKS, MESSAGE, BLOCK))] + [ANYWHERE] * len(tokens),
        out_specs=whole((CHUNKS, STATE_HALF, BLOCK)),
        compiler_params=params(),
        name="chunk_scan",
    )(info, msg, *tokens)


def out_proj_body(weight, info, y_in, bca, cum, hin, s0, gate, gain, *rest):
    refs = len(weight.arrays)
    w_refs, (y_ref, part_ref, buffer, sems, sums, gained) = rest[:refs], rest[refs:]
    weight.start(w_refs, info, buffer, sems)
    c_all = bca[:, STATE:].astype(BF16)
    grow = jnp.exp(cum[...])
    sums[...] = jnp.zeros((ROWS, LANES), F32)

    def group(g, _):
        lanes = pl.ds(pl.multiple_of(g * BLOCK, LANES), BLOCK)
        factor = rolled(grow, g)
        first = hin[g]
        second = spread(factor[HALF - 1 : HALF]) * first.astype(F32) + s0[g]
        carried = jnp.concatenate(
            [dot(half(c_all, 0), first), dot(half(c_all, 1), second.astype(BF16))], axis=0
        )
        y = y_in[:, lanes] + spread(factor) * carried
        y_ref[:, lanes] = y
        z = gate[:, lanes]
        gated = y * z * sigmoid(z)
        square = gated * gated
        sums[...] += sum(square[:, i * LANES : (i + 1) * LANES] for i in range(BLOCK // LANES))
        gained[:, lanes] = (gated * gain[:, lanes]).astype(BF16)
        return 0

    lax.fori_loop(0, GROUPS, group, 0)
    part_ref[:, WIDTH:] = sums[...]
    weight.product(w_refs, info, gained, buffer, sems, part_ref)


def out_proj(info, y_in, bca, cum, hin, s0, gate, gain, weight):
    return pl.pallas_call(
        functools.partial(out_proj_body, weight),
        out_shape=(shape((ROWS, LOCAL)), shape((ROWS, WIDTH + LANES))),
        in_specs=[
            SMEM,
            whole((ROWS, LOCAL)),
            whole((ROWS, 256)),
            whole((ROWS, LANES)),
            whole((GROUPS, STATE, BLOCK)),
            whole((GROUPS, STATE, BLOCK)),
            whole((ROWS, LOCAL)),
            whole((1, LOCAL)),
        ]
        + weight.specs(),
        out_specs=(whole((ROWS, LOCAL)), whole((ROWS, WIDTH + LANES))),
        scratch_shapes=weight.scratch()
        + [pltpu.VMEM((ROWS, LANES), F32), pltpu.VMEM((ROWS, LOCAL), BF16)],
        compiler_params=params(),
        cost_estimate=pl.CostEstimate(
            flops=2 * ROWS * WIDTH * LOCAL, bytes_accessed=13_000_000, transcendentals=800_000
        ),
        name="out_proj",
    )(info, y_in, bca, cum, hin, s0, gate, gain, *weight.arrays)


def join_body(info, h_ref, own, came, res_ref, branch_ref, scale_ref):
    squares = jnp.sum(own[:, WIDTH:] + came[:, WIDTH:], axis=1, keepdims=True)
    scale = lax.rsqrt(squares / INNER + EPSILON)
    branch = scale * (own[:, :WIDTH] + came[:, :WIDTH])
    branch_ref[...] = branch.astype(BF16)
    scale_ref[...] = jnp.broadcast_to(scale, (HALF // 2, LANES))
    first = pl.program_id(0) * (HALF // 2)
    usable = (row_of((HALF // 2, 1)) + first < info[0]).astype(F32)
    result = h_ref[...].astype(F32) + usable * branch
    res_ref[...] = result.astype(res_ref.dtype)


def join(info, h, own, came, kind):
    def rows(width):
        return pl.BlockSpec((HALF // 2, width), lambda i: (i, 0))

    return pl.pallas_call(
        join_body,
        grid=(4,),
        out_shape=(shape((ROWS, WIDTH), kind), shape((ROWS, WIDTH), BF16), shape((ROWS, LANES))),
        in_specs=[SMEM, rows(WIDTH), rows(WIDTH + LANES), rows(WIDTH + LANES)],
        out_specs=(rows(WIDTH), rows(WIDTH), rows(LANES)),
        compiler_params=params(),
        cost_estimate=pl.CostEstimate(flops=2_000_000, bytes_accessed=8_000_000, transcendentals=0),
        name="join",
    )(info, h, own, came)


def gate_back_body(weight, info, cot, y, gate, gain, branch, scale_ref, *rest):
    refs = len(weight.arrays)
    w_refs, rest = rest[:refs], rest[refs:]
    bg_ref, dy_ref, dz_ref, n_ref, dgain_ref, buffer, sems, dn = rest
    weight.start(w_refs, info, buffer, sems)
    bg = usable_rows(info) * cot[...].astype(F32)
    bg_ref[...] = bg.astype(BF16)
    scale = scale_ref[:, :1]
    inner = jnp.sum(bg_ref[...].astype(F32) * branch[...].astype(F32), axis=1, keepdims=True)
    inner = inner * scale * scale / INNER
    for b in range(4):
        rows = weight.wait(w_refs, info, b, buffer, sems)
        dn[...] = dot_nt(bg_ref[...], buffer[rows, :])

        def one(i, _, rows=rows):
            here = pl.ds(pl.multiple_of(i * LANES, LANES), LANES)
            lanes = pl.ds(pl.multiple_of(rows.start + i * LANES, LANES), LANES)
            z = gate[:, lanes]
            sig = sigmoid(z)
            silu = z * sig
            y_here = y[:, lanes]
            gated = y_here * silu
            d_norm = dn[:, here]
            gained = scale * gain[:, lanes]
            n_ref[:, lanes] = (gated * gained).astype(BF16)
            d_gated = d_norm * gained - gated * inner
            total = jnp.sum(d_norm * gated * scale, axis=0, keepdims=True)
            dgain_ref[:, lanes] = jnp.broadcast_to(total, (8, LANES))
            dy_ref[:, lanes] = (d_gated * silu).astype(BF16)
            dz_ref[:, lanes] = (d_gated * y_here * sig * (1.0 + z * (1.0 - sig))).astype(BF16)
            return 0

        lax.fori_loop(0, SHARD // LANES, one, 0)


def gate_back(info, cot, y, gate, gain, branch, scale, weight):
    wide, local = whole((ROWS, WIDTH)), whole((ROWS, LOCAL))
    return pl.pallas_call(
        functools.partial(gate_back_body, weight),
        out_shape=(
            shape((ROWS, WIDTH), BF16),
            shape((ROWS, LOCAL), BF16),
            shape((ROWS, LOCAL), BF16),
            shape((ROWS, LOCAL), BF16),
            shape((8, LOCAL)),
        ),
        in_specs=[SMEM, wide, local, local, whole((1, LOCAL)), wide, whole((ROWS, LANES))]
        + weight.specs(),
        out_specs=(wide, local, local, local, whole((8, LOCAL))),
        scratch_shapes=weight.scratch() + [pltpu.VMEM((ROWS, SHARD), F32)],
        compiler_params=params(),
        cost_estimate=pl.CostEstimate(
            flops=2 * ROWS * WIDTH * LOCAL, bytes_accessed=13_000_000, transcendentals=800_000
        ),
        name="gate_back",
    )(info, cot, y, gate, gain, branch, scale, *weight.arrays)


def own_grad_body(dy, bca, cum, msg_in, own1_ref, msg_ref, ct, grow):
    g = pl.program_id(0)

    @pl.when(g == 0)
    def _():
        ct[...] = bca[:, STATE:].T.astype(BF16)
        grow[...] = jnp.exp(cum[...])

    factor = rolled(grow[...], g)
    weighted = (dy[...].astype(F32) * spread(factor)).astype(BF16)
    own0 = dot(ct[:, :HALF], half(weighted, 0))
    own1 = dot(ct[:, HALF:], half(weighted, 1))
    own1_ref[0] = own1
    grad = (spread(factor[HALF - 1 : HALF]) * own1 + own0).astype(BF16)
    for r in range(2):
        msg_ref[r, :STATE_HALF, :] = grad[r * STATE_HALF : (r + 1) * STATE_HALF]
        msg_ref[r, STATE_HALF:, :] = msg_in[r, STATE_HALF:, :]


def own_grad(dy, bca, cum, msg):
    return pl.pallas_call(
        own_grad_body,
        grid=(GROUPS,),
        out_shape=(
            shape((GROUPS, STATE, BLOCK)),
            shape((CHUNKS, MESSAGE, BLOCK), BF16),
        ),
        in_specs=[columns(ROWS, BLOCK), whole((ROWS, 256)), whole((ROWS, LANES)), MESSAGES],
        out_specs=(grouped(STATE), MESSAGES),
        scratch_shapes=[pltpu.VMEM((STATE, ROWS), BF16), pltpu.VMEM((ROWS, LANES), F32)],
        compiler_params=params(),
        cost_estimate=pl.CostEstimate(
            flops=2 * ROWS * STATE * LOCAL, bytes_accessed=2_500_000, transcendentals=0
        ),
        name="own_grad",
    )(dy, bca, cum, msg)


def inside_back_body(
    dy, xa, bca, cum, dt, hpar,
    dx_ref, dskip_ref, gsum_ref, u_ref, dbc_ref, cum_t, scores, dscores,
):
    g = pl.program_id(0)

    @pl.when(g == 0)
    def _():
        tri = lower_triangle()
        for q in range(2):
            b, c = half(bca[:, :STATE], q).astype(BF16), half(bca[:, STATE:], q).astype(BF16)
            scores[q] = dot_nt(b, c) * tri.T
            cum_t[:, q * HALF : (q + 1) * HALF] = half(cum[...], q).T
        dscores[...] = jnp.zeros((2, HALF, HALF), F32)
        u_ref[...] = jnp.zeros((ROWS, LANES), F32)

    cols = rolled(cum[...], g)
    rows = cum_t[pl.ds(pl.multiple_of(8 * g, 8), 8), :]
    steps = rolled(dt[...], g)
    skips = rolled(hpar[...], g)[2:3, :]
    low = lane_of((HALF, LANES)) < HEADDIM
    lane = lane_of((HALF, LANES))
    gsum_ref[...] = jnp.zeros((8, ROWS), F32)
    for q in range(2):
        here = slice(q * HALF, (q + 1) * HALF)
        u_here = u_ref[here, :]
        for p in range(OWN // 2):
            lanes = slice(p * LANES, (p + 1) * LANES)
            dy_pair = dy[here, lanes]
            x = xa[here, lanes]
            zero = jnp.zeros_like(dy_pair)
            both = jnp.concatenate(
                [jnp.where(low, dy_pair, zero), jnp.where(low, zero, dy_pair)], axis=0
            )
            dw = dot_nt(x.astype(BF16), both)
            mats = []
            for n, i in enumerate((2 * p, 2 * p + 1)):
                gap = rows[i : i + 1, here] - half(cols, q)[:, i : i + 1]
                decay = jnp.exp(jnp.minimum(gap, 0.0))
                step = half(steps, q)[:, i : i + 1]
                weight = decay * scores[q]
                mats.append(weight.astype(BF16))
                dw_here = dw[:, n * HALF : (n + 1) * HALF]
                dscores[q] += decay * dw_here * step
                direct = weight * dw_here
                total = jnp.sum(direct, axis=1, keepdims=True)
                u_here = jnp.where(lane == 8 * g + i, total, u_here)
                gsum_ref[i : i + 1, here] = jnp.sum(direct * step, axis=0, keepdims=True)
            dx = dot(jnp.concatenate(mats, axis=1), both)
            dy_wide = dy_pair.astype(F32)
            dx_ref[here, lanes] = dx * pair_lanes(half(steps, q), p) + dy_wide * pair_lanes(skips, p)
            skip_sum = jnp.sum(dy_wide * x, axis=0, keepdims=True)
            if q == 0:
                dskip_ref[:, lanes] = jnp.broadcast_to(skip_sum, (8, LANES))
            else:
                dskip_ref[:, lanes] += skip_sum
        u_ref[here, :] = u_here

    @pl.when(g == GROUPS - 1)
    def _():
        tri = lower_triangle()
        for q in range(2):
            b, c = half(bca[:, :STATE], q).astype(BF16), half(bca[:, STATE:], q).astype(BF16)
            ds_t = dscores[q] * tri.T
            dbc_ref[q * HALF : (q + 1) * HALF, :STATE] = dot(ds_t.astype(BF16), c)
            dbc_ref[q * HALF : (q + 1) * HALF, STATE:] = dot(ds_t.T.astype(BF16), b)


def inside_back(dy, xa, bca, cum, dt, hpar):
    return pl.pallas_call(
        inside_back_body,
        grid=(GROUPS,),
        out_shape=(
            shape((ROWS, LOCAL)),
            shape((8, LOCAL)),
            shape((8 * GROUPS, ROWS)),
            shape((ROWS, LANES)),
            shape((ROWS, 256)),
        ),
        in_specs=[
            columns(ROWS, BLOCK),
            columns(ROWS, BLOCK),
            whole((ROWS, 256)),
            whole((ROWS, LANES)),
            whole((ROWS, LANES)),
            whole((8, LANES)),
        ],
        out_specs=(
            columns(ROWS, BLOCK),
            columns(8, BLOCK),
            pl.BlockSpec((8, ROWS), lambda g: (g, 0)),
            whole((ROWS, LANES)),
            whole((ROWS, 256)),
        ),
        scratch_shapes=[
            pltpu.VMEM((LANES, ROWS), F32),
            pltpu.VMEM((2, HALF, HALF), F32),
            pltpu.VMEM((2, HALF, HALF), F32),
        ],
        compiler_params=params(),
        cost_estimate=pl.CostEstimate(
            flops=4 * HEADS * HALF * HALF * LANES, bytes_accessed=4_500_000, transcendentals=800_000
        ),
        name="inside_back",
    )(dy, xa, bca, cum, dt, hpar)


def conv_back(d_active, values, halo, cpar, keep, ext, ext_d):
    width = values.shape[1]
    total = conv_sum_of(values, halo, cpar, keep, ext)
    sig = sigmoid(total)
    d_sum = d_active * sig * (1.0 + total * (1.0 - sig))
    ext_d[0:16, :width] = jnp.zeros((16, width), F32)
    ext_d[16 : 16 + ROWS, :width] = d_sum
    ext_d[16 + ROWS :, :width] = jnp.zeros((16, width), F32)
    d_in = jnp.zeros((ROWS + 16, width), F32)
    for k in range(KERNEL):
        d_in = d_in + cpar[k : k + 1, :] * ext_d[3 - k : 3 - k + ROWS + 16, :width]
    row = row_of((8, width))
    d_par = jnp.where(row == 4, jnp.sum(d_sum, axis=0, keepdims=True), 0.0)
    for k in range(KERNEL):
        tap = jnp.sum(d_sum * ext[13 + k : 13 + k + ROWS, :width], axis=0, keepdims=True)
        d_par = jnp.where(row == k, tap, d_par)
    return d_in, d_par


def finish_body(
    info, xa, dxi, dy, mixed, halo, cpar, bc, halo_bc, cpar_bc, bca, cum, dt, rate, hpar, lam, hin, s0, own1, u, gsum, dbc,
    dmx_ref, dmbc_ref, tailx_ref, tailbc_ref, edgex_ref, edgebc_ref, dcx_ref, dcbc_ref, dhead_ref,
    ext, ext_d, grow, tail, v_sum, q_sum, end_sum, dbc_sum,
):
    g = pl.program_id(0)
    keep = info[1].astype(F32)

    @pl.when(g == 0)
    def _():
        grow[...] = jnp.exp(cum[...])
        for q in range(2):
            here = half(cum[...], q)
            tail[q * HALF : (q + 1) * HALF, :] = jnp.exp(here[HALF - 1 :, :] - here)
        v_sum[...] = jnp.zeros((ROWS, LANES), F32)
        q_sum[...] = jnp.zeros((ROWS, LANES), F32)
        end_sum[...] = jnp.zeros((16, LANES), F32)
        dbc_sum[...] = dbc[...]

    sums = head_sum_matrix(g)
    factor = rolled(grow[...], g)
    tails = rolled(tail[...], g)
    steps = rolled(dt[...], g)
    ends = [spread(factor[HALF - 1 : HALF]), spread(factor[ROWS - 1 : ROWS])]
    lam1 = lam[0].astype(F32)
    lams = [ends[1] * lam1 + own1[0], lam1]
    first = hin[0].astype(F32)
    states = [first, ends[0] * first + s0[0]]
    d_x = []
    for q in range(2):
        here = slice(q * HALF, (q + 1) * HALF)
        b, c = bca[here, :STATE].astype(BF16), bca[here, STATE:].astype(BF16)
        lam_q, state_q = lams[q].astype(BF16), states[q].astype(BF16)
        tail_wide = spread(half(tails, q))
        tail_step = tail_wide * spread(half(steps, q))
        x, dy_q = xa[here, :], dy[here, :].astype(F32)
        lb = dot(b, lam_q) * tail_wide
        d_x.append(dxi[here, :] + lb * spread(half(steps, q)))
        v_sum[here, :] += dot((x * lb).astype(BF16), sums)
        grow_wide = spread(half(factor, q))
        dy_grow = (dy_q * grow_wide).astype(BF16)
        carried = dot(c, state_q)
        q_sum[here, :] += dot((dy_q * grow_wide * carried).astype(BF16), sums)
        dbc_sum[here, :STATE] += dot_nt((x * tail_step).astype(BF16), lam_q)
        dbc_sum[here, STATE:] += dot_nt(dy_grow, state_q)
        last = jnp.sum(lams[q] * states[q], axis=0, keepdims=True) * ends[q]
        end_sum[8 * q : 8 * q + 8, :] += exact_dot(
            jnp.broadcast_to(last, (8, BLOCK)), sums.astype(F32)
        )
    d_in, d_par = conv_back(
        jnp.concatenate(d_x, axis=0), mixed[...], halo[...], cpar[...], keep, ext, ext_d
    )
    dmx_ref[...] = d_in[16:].astype(BF16)
    tailx_ref[...] = d_in[ROWS:]
    edgex_ref[...] = (d_in[:16] * keep).astype(BF16)
    dcx_ref[...] = d_par

    @pl.when(g == GROUPS - 1)
    def _():
        d_bc, d_par_bc = conv_back(
            dbc_sum[...], bc[...], halo_bc[...], cpar_bc[...], keep, ext, ext_d
        )
        dmbc_ref[:, :256] = d_bc[16:].astype(BF16)
        tailbc_ref[...] = d_bc[ROWS:]
        edgebc_ref[...] = (d_bc[:16] * keep).astype(BF16)
        dcbc_ref[...] = d_par_bc
        rates = -jnp.exp(hpar[1:2, :])
        logit = rate[...] + hpar[0:1, :]
        upper = lower_triangle().T
        before = lower_triangle(True)
        d_bias = jnp.zeros((1, LANES), F32)
        d_log = jnp.zeros((1, LANES), F32)
        usable = usable_rows(info)
        for q in range(2):
            here = slice(q * HALF, (q + 1) * HALF)
            step = dt[here, :]
            gs = gsum[...][:, here].T
            gs = jnp.concatenate([gs, jnp.zeros((HALF, LANES - 8 * GROUPS), F32)], axis=1)
            d_decay = exact_dot(upper, gs - step * u[here, :] + q_sum[here, :])
            d_decay = d_decay + exact_dot(before, step * v_sum[here, :])
            d_decay = d_decay + end_sum[8 * q : 8 * q + 1, :]
            d_step = u[here, :] + v_sum[here, :] + rates * d_decay
            d_rate = half(usable, q) * d_step * sigmoid(half(logit, q))
            d_bias += jnp.sum(d_rate, axis=0, keepdims=True)
            d_log += jnp.sum(d_decay * step * rates, axis=0, keepdims=True)
            dmbc_ref[here, 256:] = d_rate.astype(BF16)
        row = row_of((8, LANES))
        dhead_ref[...] = jnp.where(row == 0, d_bias, jnp.where(row == 1, d_log, 0.0))


def finish_call(
    info, xa, dxi, dy, mixed, halo, cpar, bca, cum, dt, rate, hpar, lam, hin, s0, own1, u, gsum, dbc
):
    bc_at = LOCAL // 256
    wide = whole((ROWS, LANES))
    return pl.pallas_call(
        finish_body,
        grid=(GROUPS,),
        out_shape=(
            shape((ROWS, LOCAL), BF16),
            shape((ROWS, 384), BF16),
            shape((16, LOCAL)),
            shape((16, 256)),
            shape((16, LOCAL), BF16),
            shape((16, 256), BF16),
            shape((8, LOCAL)),
            shape((8, 256)),
            shape((8, LANES)),
        ),
        in_specs=[
            SMEM,
            columns(ROWS, BLOCK),
            columns(ROWS, BLOCK),
            columns(ROWS, BLOCK),
            columns(ROWS, BLOCK),
            columns(16, BLOCK),
            columns(8, BLOCK),
            pl.BlockSpec((ROWS, 256), lambda g: (0, bc_at)),
            pl.BlockSpec((16, 256), lambda g: (0, bc_at)),
            pl.BlockSpec((8, 256), lambda g: (0, bc_at)),
            whole((ROWS, 256)),
            wide,
            wide,
            wide,
            whole((8, LANES)),
            grouped(STATE),
            grouped(STATE),
            grouped(STATE),
            grouped(STATE),
            wide,
            whole((8 * GROUPS, ROWS)),
            whole((ROWS, 256)),
        ],
        out_specs=(
            columns(ROWS, BLOCK),
            whole((ROWS, 384)),
            columns(16, BLOCK),
            whole((16, 256)),
            columns(16, BLOCK),
            whole((16, 256)),
            columns(8, BLOCK),
            whole((8, 256)),
            whole((8, LANES)),
        ),
        scratch_shapes=[
            pltpu.VMEM((ROWS + 32, BLOCK), F32),
            pltpu.VMEM((ROWS + 32, BLOCK), F32),
            pltpu.VMEM((ROWS, LANES), F32),
            pltpu.VMEM((ROWS, LANES), F32),
            pltpu.VMEM((ROWS, LANES), F32),
            pltpu.VMEM((ROWS, LANES), F32),
            pltpu.VMEM((16, LANES), F32),
            pltpu.VMEM((ROWS, 256), F32),
        ],
        compiler_params=params(),
        cost_estimate=pl.CostEstimate(
            flops=10 * ROWS * STATE * LOCAL, bytes_accessed=7_500_000, transcendentals=800_000
        ),
        name="finish_back",
    )(
        info, xa, dxi, dy, mixed, halo, cpar, mixed, halo, cpar, bca, cum, dt, rate, hpar,
        lam, hin, s0, own1, u, gsum, dbc,
    )


def gate_in_back_body(weight, info, dz, *rest):
    refs = len(weight.arrays)
    w_refs, (out_ref, buffer, sems) = rest[:refs], rest[refs:]
    weight.start(w_refs, info, buffer, sems)
    for b in range(4):
        rows = weight.wait(w_refs, info, b, buffer, sems)
        out_ref[:, rows] = dot_nt(dz[...], buffer[rows, :])


def gate_in_back(info, dz, weight):
    return pl.pallas_call(
        functools.partial(gate_in_back_body, weight),
        out_shape=shape((ROWS, WIDTH)),
        in_specs=[SMEM, whole((ROWS, LOCAL))] + weight.specs(),
        out_specs=whole((ROWS, WIDTH)),
        scratch_shapes=weight.scratch(),
        compiler_params=params(),
        cost_estimate=pl.CostEstimate(
            flops=2 * ROWS * WIDTH * LOCAL, bytes_accessed=7_000_000, transcendentals=0
        ),
        name="gate_in_back",
    )(info, dz, *weight.arrays)


def patch_body(dmx, dmbc, tailx, tailbc, edge, token, dxc_ref):
    dxc_ref[:, :LOCAL] = dmx[...]
    dxc_ref[:, LOCAL:] = dmbc[...]
    late = edge[...].astype(F32)
    dxc_ref[ROWS - 16 :, :LOCAL] = (tailx[...] + late[:, :LOCAL]).astype(BF16)
    dxc_ref[ROWS - 16 :, LOCAL:MIXED] = (tailbc[...] + late[:, LOCAL:]).astype(BF16)


def patch(dmx, dmbc, tailx, tailbc, edge, token):
    arrays = (dmx, dmbc, tailx, tailbc, edge)
    return pl.pallas_call(
        patch_body,
        out_shape=shape((ROWS, PACKED), BF16),
        in_specs=[whole(v.shape) for v in arrays] + [ANYWHERE],
        out_specs=whole((ROWS, PACKED)),
        compiler_params=params(),
        cost_estimate=pl.CostEstimate(flops=100_000, bytes_accessed=2_000_000, transcendentals=0),
        name="patch",
    )(*arrays, token)


def mixed_back_body(weight, tokens, info, dxc, part, h_ref, *rest):
    refs = len(weight.arrays)
    w_refs, (out_ref, dgain_ref, buffer, sems) = rest[:refs], rest[refs + tokens :]
    weight.start(w_refs, info, buffer, sems)
    h = h_ref[...].astype(F32)
    scale = lax.rsqrt(jnp.mean(h * h, axis=1, keepdims=True) + EPSILON)
    for b in range(4):
        rows = weight.wait(w_refs, info, b, buffer, sems)
        d_norm = part[:, rows] + dot_nt(dxc[...], buffer[rows, :])
        out_ref[:, rows] = d_norm
        total = jnp.sum(d_norm * h_ref[:, rows].astype(F32) * scale, axis=0, keepdims=True)
        dgain_ref[:, rows] = jnp.broadcast_to(total, (8, SHARD))


def mixed_back(info, dxc, part, h, weight, tokens):
    return pl.pallas_call(
        functools.partial(mixed_back_body, weight, len(tokens)),
        out_shape=(shape((ROWS, WIDTH)), shape((8, WIDTH))),
        in_specs=[SMEM, whole((ROWS, PACKED)), whole((ROWS, WIDTH)), whole((ROWS, WIDTH))]
        + weight.specs()
        + [ANYWHERE] * len(tokens),
        out_specs=(whole((ROWS, WIDTH)), whole((8, WIDTH))),
        scratch_shapes=weight.scratch(),
        compiler_params=params(),
        cost_estimate=pl.CostEstimate(
            flops=2 * ROWS * WIDTH * PACKED, bytes_accessed=9_000_000, transcendentals=0
        ),
        name="mixed_back",
    )(info, dxc, part, h, *weight.arrays, *tokens)


def norm_back_body(own, came, h_ref, cot, gain, token, dh_ref, low_ref):
    h = h_ref[...].astype(F32)
    scale = lax.rsqrt(jnp.mean(h * h, axis=1, keepdims=True) + EPSILON)
    d_norm = own[...] + came[...]
    inner = jnp.mean(d_norm * gain[...] * h, axis=1, keepdims=True) * scale * scale * scale
    dh = cot[...].astype(F32) + scale * d_norm * gain[...] - h * inner
    dh_ref[...] = dh
    low_ref[...] = dh.astype(BF16)


def norm_back(own, came, h, cot, gain, token):
    rows = pl.BlockSpec((HALF // 2, WIDTH), lambda i: (i, 0))
    return pl.pallas_call(
        norm_back_body,
        grid=(4,),
        out_shape=(shape((ROWS, WIDTH)), shape((ROWS, WIDTH), BF16)),
        in_specs=[rows] * 4 + [whole((1, WIDTH)), ANYWHERE],
        out_specs=(rows, rows),
        compiler_params=params(),
        cost_estimate=pl.CostEstimate(flops=3_000_000, bytes_accessed=8_000_000, transcendentals=0),
        name="norm_back",
    )(own, came, h, cot, gain, token)


def z_shift(r):
    return "dp", [(z, (z + r) % 4) for z in range(4)]


def y_shift(r):
    return "ctx", [(j, (j + 4 * r) % 16) for j in range(16)]


def x_shift(r):
    return "ctx", [(j, j - j % 4 + (j + r) % 4) for j in range(16)]


SHIFTS = {"z": z_shift, "y": y_shift, "x": x_shift}


def send(value, axis, r):
    name, pairs = SHIFTS[axis](r % 4)
    return lax.ppermute(value, name, pairs)


def swapped(value):
    return lax.ppermute(value, "section", [(0, 1), (1, 0)])


def nothing_body(*refs):
    refs[-1][...] = jnp.zeros((8, LANES), jnp.int32)


def after(values, place):
    nothing = pl.pallas_call(
        nothing_body,
        out_shape=shape((8, LANES), jnp.int32),
        in_specs=[ANYWHERE] * len(values),
        out_specs=whole((8, LANES)),
        compiler_params=params(),
        cost_estimate=pl.CostEstimate(flops=0, bytes_accessed=4096, transcendentals=0),
        name="after",
    )(*values)[0, 0]
    return {axis: n + nothing for axis, n in place.items()}


def fetched(mine, came, layer, section, place):
    rows = SHARD // 2

    def piece(source, side, axis):
        return lax.dynamic_slice_in_dim(source, side * rows + place[axis] * PIECE, PIECE, 0)

    parts = [
        jnp.where(section == layer, piece(mine, side, axis), piece(came, side, axis))
        for side, axis in enumerate("xy")
    ]
    if mine.shape[0] == TALL:
        parts.append(jnp.where(section == layer, mine[SHARD:], came[SHARD:]))
    return jnp.concatenate(parts)


def pieces(mine, came, got, late):
    out = [mine, came]
    for side, axis in enumerate("xy"):
        rows = slice(side * PIECE, (side + 1) * PIECE)
        stack = jnp.concatenate(
            [lax.dynamic_slice_in_dim(g, rows.start + late, PIECE, 0) for g in got[1:]]
        )
        out += [stack] + [send(stack, axis, -r) for r in range(1, 4)]
    return out


def summed(terms):
    a, b, c, d = (t.astype(F32) for t in terms)
    return (a + c) + (b + d)


def arrived(terms, axis):
    return [terms[0]] + [send(terms[r], axis, r) for r in range(1, 4)]


def terms_body(axis, width, info, source, other, *rest):
    small, outs, total = rest[:-5], rest[-5:-1], rest[-1]
    total[...] = dot(source[...], other[...])
    count = 96 if axis == "y" else 24
    for r in range(4):
        first = lax.rem(info[11 if axis == "y" else 12] + r, 4) * count
        starts = [z * SHARD for z in range(4)]
        if axis == "x":
            starts = [start + y * 96 for start in starts for y in range(4)]
        parts = [total[pl.ds(pl.multiple_of(start + first, 8), count), :] for start in starts]
        outs[r][:SHARD, :] = jnp.concatenate(parts, axis=0).astype(BF16)
        for ref in small:
            outs[r][SHARD:, :] = ref[...]


def terms(info, axis, source, other, small=()):
    width = other.shape[1]
    rows = SHARD + sum(v.shape[0] for v in small)
    arrays = (source, other, *small)
    return pl.pallas_call(
        functools.partial(terms_body, axis, width),
        out_shape=[shape((rows, width), BF16)] * 4,
        in_specs=[SMEM] + [whole(v.shape) for v in arrays],
        out_specs=[whole((rows, width))] * 4,
        scratch_shapes=[pltpu.VMEM((4 * SHARD, width), F32)],
        compiler_params=params(),
        cost_estimate=pl.CostEstimate(
            flops=8 * SHARD * ROWS * width, bytes_accessed=5_000_000, transcendentals=0
        ),
        name="terms",
    )(info, *arrays)


def fold_body(slot, counts, outer, inner, rest_rows, info, *rest):
    refs, outs, total = rest[: sum(counts)], rest[sum(counts) + 1 : -1], rest[-1]
    column = 0
    for count in counts:
        arrays, refs = refs[:count], refs[count:]
        cols = slice(column, column + arrays[0].shape[1])
        total[:, cols] = summed([a[...] for a in arrays]) if count == 4 else arrays[0][...].astype(F32)
        column = cols.stop
    for r in range(4):
        first = lax.rem(info[slot] + r, 4) * inner
        parts = [
            total[pl.ds(pl.multiple_of(n * 4 * inner + first, 8), inner), :] for n in range(outer)
        ]
        if rest_rows:
            parts.append(total[4 * outer * inner :, :])
        outs[r][...] = jnp.concatenate(parts, axis=0).astype(BF16)


def fold(info, axis, groups, outer, inner, token):
    slot = 10 + "zyx".index(axis)
    arrays = [a for group in groups for a in group]
    rows, width = arrays[0].shape[0], sum(group[0].shape[1] for group in groups)
    more = rows - 4 * outer * inner
    out = shape((outer * inner + more, width), BF16)
    counts = [len(group) for group in groups]
    return pl.pallas_call(
        functools.partial(fold_body, slot, counts, outer, inner, more),
        out_shape=[out] * 4,
        in_specs=[SMEM] + [whole(a.shape) for a in arrays] + [ANYWHERE],
        out_specs=[whole(out.shape)] * 4,
        scratch_shapes=[pltpu.VMEM((rows, width), F32)],
        compiler_params=params(),
        cost_estimate=pl.CostEstimate(flops=2_000_000, bytes_accessed=8_000_000, transcendentals=0),
        name="fold",
    )(info, *arrays, token)


def last_fold_body(info, *rest):
    left, right, outs, total = rest[:4], rest[4:8], rest[9:13], rest[13]
    width = left[0].shape[1]
    rows = 96 + SMALL // 2
    total[:96, :width] = summed([a[...] for a in left])
    total[:96, width:] = summed([a[:96, :] for a in right])
    total[96:, :width] = summed([a[96:rows, :width] for a in right])
    total[96:, width:] = summed([a[rows:, :] for a in right])
    for r in range(4):
        first = pl.multiple_of(lax.rem(info[10] + r, 4) * 24, 8)
        parts = [total[pl.ds(first, 24), :], total[96:, :]]
        outs[r][...] = jnp.concatenate(parts, axis=0).astype(BF16)


def last_fold(info, left, right, token):
    width = left[0].shape[1] + right[0].shape[1]
    out = shape((24 + SMALL // 2, width), BF16)
    arrays = (*left, *right)
    return pl.pallas_call(
        last_fold_body,
        out_shape=[out] * 4,
        in_specs=[SMEM] + [whole(a.shape) for a in arrays] + [ANYWHERE],
        out_specs=[whole(out.shape)] * 4,
        scratch_shapes=[pltpu.VMEM((96 + SMALL // 2, width), F32)],
        compiler_params=params(),
        cost_estimate=pl.CostEstimate(flops=500_000, bytes_accessed=2_000_000, transcendentals=0),
        name="last_fold",
    )(info, *arrays, token)


PARITY = [[j for j in range(16) if j % 2 == e] for e in range(2)]
NEIGHBOURS = [(j, j ^ 1) for j in range(16)]


def exchange(value):
    return lax.all_to_all(value, "ctx", 0, 0, axis_index_groups=PARITY)


def halo_shift(value, step):
    pairs = [(j, j + 2 * step) for j in range(16) if 0 <= j + 2 * step < 16]
    return lax.ppermute(value, "ctx", pairs)


def halves(values, section):
    grid = values.reshape(values.shape[0], GROUPS, 2, -1)
    size = values.shape[1] // 2
    return [
        lax.dynamic_index_in_dim(grid, i, 2, False).reshape(-1, size)
        for i in (section, 1 - section)
    ]


def turns(low, high):
    rows = low.shape[0]
    parts = [v.reshape(rows, GROUPS, 1, -1) for v in (low, high)]
    return jnp.concatenate(parts, axis=2).reshape(rows, -1)


def pick_x_body(info, x_ref, dt_ref, *rest):
    smalls, outs, small = rest[:7], rest[7:9], rest[9]
    small[...] = jnp.zeros((16, PACKED), F32)
    row = 0
    for ref in smalls[:4]:
        count, width = ref.shape
        small[row : row + count, :width] = ref[...].astype(F32)
        row += count
    for ref in smalls[4:]:
        left = ref[...]
        for _ in range(3):
            part = left.astype(BF16).astype(F32)
            small[row : row + 1, :HEADS] = part
            left = left - part
            row += 1
    head, lane = row_of((HEADS, LANES)), lane_of((HEADS, LANES))
    for out, side in zip(outs, (info[0], 1 - info[0]), strict=True):
        for d in range(GROUPS):
            cols = pl.ds(pl.multiple_of((2 * d + side) * BLOCK, LANES), BLOCK)
            out[:SHARD, d * BLOCK : (d + 1) * BLOCK] = x_ref[:, cols]
        out[:SHARD, LOCAL:MIXED] = x_ref[:, INNER:]
        here = (head // OWN == 2 * (lane // 8) + side) & (head % OWN == lane % 8)
        out[:SHARD, MIXED:] = dot(dt_ref[...], here.astype(BF16)).astype(BF16)
        out[SHARD:, :] = small[...].astype(BF16)


def pick_x(section, x, dt, smalls):
    return pl.pallas_call(
        pick_x_body,
        out_shape=[shape((TALL, PACKED), BF16)] * 2,
        in_specs=[SMEM, whole((SHARD, CONV_CH)), whole((SHARD, HEADS))]
        + [whole(v.shape) for v in smalls],
        out_specs=[whole((TALL, PACKED))] * 2,
        scratch_shapes=[pltpu.VMEM((16, PACKED), F32)],
        compiler_params=params(),
        cost_estimate=pl.CostEstimate(flops=0, bytes_accessed=6_000_000, transcendentals=0),
        name="pick_x",
    )(section, x, dt, *smalls)


def unpack_body(count, info, *rest):
    refs, (cpar, gain_one, gain_two, hpar, held, full, sems) = rest[:count], rest[count:]
    copies = []
    for n in range(4):
        if count == 4:
            source, to = refs[n].at[pl.ds(2 * PIECE, 16)], lax.rem(info[10] + n, 4)
        else:
            source, to = refs[0].at[pl.ds(n * TALL + SHARD, 16)], n
        copies.append(pltpu.make_async_copy(source, held.at[to], sems.at[n]))
    for c in copies:
        c.start()
    for c in copies:
        c.wait()
    section = info[13]
    half_cols = pl.ds(pl.multiple_of(section * BLOCK, LANES), BLOCK)
    for z in range(4):
        values = held[z].astype(F32)
        full[:, z * 832 : (z + 1) * 832] = values[:8, :832]
        gain_one[:, z * SHARD : (z + 1) * SHARD] = values[5:6, :SHARD]
        gain_two[:, z * BLOCK : (z + 1) * BLOCK] = held[z, :, half_cols].astype(F32)[6:7]
    for d in range(GROUPS):
        cols = pl.ds(pl.multiple_of((2 * d + section) * BLOCK, LANES), BLOCK)
        cpar[:, d * BLOCK : (d + 1) * BLOCK] = full[:, cols]
    cpar[:, LOCAL:] = full[:, INNER:]
    values = held[0, :, :LANES].astype(F32)
    heads = [values[n : n + 1] + values[n + 1 : n + 2] + values[n + 2 : n + 3] for n in (7, 10, 13)]
    heads = jnp.concatenate(heads + [jnp.zeros((5, LANES), F32)], axis=0)
    head, lane = row_of((LANES, LANES)), lane_of((LANES, LANES))
    here = (head // OWN == 2 * (lane // 8) + section) & (head % OWN == lane % 8)
    hpar[...] = exact_dot(heads, here.astype(F32))


def unpack(info, arrays):
    shapes = ((8, MIXED), (1, WIDTH), (1, LOCAL), (8, LANES))
    return pl.pallas_call(
        functools.partial(unpack_body, len(arrays)),
        out_shape=[shape(dims) for dims in shapes],
        in_specs=[SMEM] + [ANYWHERE] * len(arrays),
        out_specs=[whole(dims) for dims in shapes],
        scratch_shapes=[
            pltpu.VMEM((4, 16, PACKED), BF16),
            pltpu.VMEM((8, CONV_CH), F32),
            pltpu.SemaphoreType.DMA((4,)),
        ],
        compiler_params=params(),
        cost_estimate=pl.CostEstimate(flops=0, bytes_accessed=400_000, transcendentals=0),
        name="unpack",
    )(info, *arrays)


def pick_zo_body(info, z_ref, o_ref, token, *outs):
    for out, side in zip(outs, (info[0], 1 - info[0]), strict=True):
        for d in range(GROUPS):
            cols = pl.ds(pl.multiple_of((2 * d + side) * BLOCK, LANES), BLOCK)
            out[:, d * BLOCK : (d + 1) * BLOCK] = z_ref[:, cols]
        rows = pl.ds(pl.multiple_of(side * SHARD, SHARD), SHARD)
        out[:, LOCAL:] = o_ref[rows, :]


def pick_zo(section, z, o, token):
    return pl.pallas_call(
        pick_zo_body,
        out_shape=[shape((SHARD, LOCAL + WIDTH), BF16)] * 2,
        in_specs=[SMEM, whole((SHARD, INNER)), whole((2 * SHARD, WIDTH)), ANYWHERE],
        out_specs=[whole((SHARD, LOCAL + WIDTH))] * 2,
        compiler_params=params(),
        cost_estimate=pl.CostEstimate(flops=0, bytes_accessed=9_000_000, transcendentals=0),
        name="pick_zo",
    )(section, z, o, token)


def head_lanes(values):
    rows = values.shape[0]
    grid = jnp.pad(values.reshape(rows, GROUPS, OWN), ((0, 0), (0, 0), (0, 8 - OWN)))
    return jnp.pad(grid.reshape(rows, 8 * GROUPS), ((0, 0), (0, LANES - 8 * GROUPS)))


def lanes_heads(values):
    rows = values.shape[0]
    return values[:, : 8 * GROUPS].reshape(rows, GROUPS, 8)[:, :, :OWN].reshape(rows, -1)


def on_device(
    boundary,
    lengths,
    norm_gain,
    w_z,
    w_xbc,
    w_dt,
    conv_weight,
    conv_bias,
    dt_bias,
    a_log,
    d_skip,
    gate_gain,
    w_out,
):
    section = lax.axis_index("section")
    group = lax.axis_index("dp")
    ctx = lax.axis_index("ctx")
    place = {"z": group, "y": ctx // 4, "x": ctx % 4}
    micro = ctx % 2
    chunk = ctx // 2

    def ordered(mine, came):
        return jnp.where(section == 0, mine, came), jnp.where(section == 0, came, mine)

    own_rows = lax.dynamic_index_in_dim(boundary[0], micro, 0, False)
    other_rows = lax.dynamic_index_in_dim(boundary[0], 1 - micro, 0, False)
    came = lax.ppermute(other_rows, "ctx", NEIGHBOURS)
    block = jnp.where(
        micro == 0, jnp.concatenate([own_rows, came]), jnp.concatenate([came, own_rows])
    )
    hidden, cotangent = ordered(block, swapped(block))

    pair = lengths[group, micro]
    padded = (pair[0] + SPAN - 1) // SPAN * SPAN
    offset = chunk * ROWS
    begin = jnp.where(offset >= padded, padded, 0)
    length = jnp.where(offset >= padded, pair[1], pair[0])
    live = jnp.clip(length - (offset - begin), 0, ROWS)
    offsets = jnp.arange(CHUNKS, dtype=jnp.int32) * ROWS
    keeps = ((offsets != 0) & (offsets != padded)).astype(jnp.int32)
    keep = (offset != 0) & (offset != padded)
    at = [place["z"], place["y"], place["x"], section]
    info = jnp.concatenate(
        [jnp.stack([live, keep]).astype(jnp.int32), keeps, jnp.stack(at).astype(jnp.int32)]
    )

    def forward(h, layer):
        cpar, hpar = cpars[layer], hpars[layer]
        normed, mixed, rate = in_proj(
            info, h, gains_one[layer], weights_x[layer], []
        )
        halo = halo_shift(mixed[ROWS - 16 :], 1)
        gate = gate_proj(info, normed, weights_z[layer], [] if layer else ready)
        xa, bca, cum, dt, s0, msg = state_call(info, mixed, halo, cpar, rate, hpar)
        came = exchange(msg)
        y_in = inside_call(xa, bca, cum, dt, hpar)
        hin = exchange(scan_call(info, came, False, y_in)).reshape(GROUPS, STATE, BLOCK)
        y, part = out_proj(
            info, y_in, bca, cum, hin, s0, gate, gains_two[layer], weights_o[layer]
        )
        result, branch, scale = join(info, h, part, swapped(part), F32 if layer else BF16)
        saved = (h, normed, mixed, halo, rate, gate, xa, bca, cum, dt, s0, msg, hin, y, branch, scale)
        return result, saved

    def backward(cot, saved, layer, higher, tokens):
        h, normed, mixed, halo, rate, gate, xa, bca, cum, dt, s0, msg, hin, y, branch, scale = saved
        cpar, hpar = cpars[layer], hpars[layer]
        bg, dy, dz, normed_two, d_gain_two = gate_back(
            info, cot, y, gate, gains_two[layer], branch, scale, weights_o[layer]
        )
        own1, msg_back = own_grad(dy, bca, cum, msg)
        came = exchange(msg_back)
        normed_two_t, normed_t = normed_two.T, normed.T

        def first_stage(value):
            return lax.psum_scatter(value, "dp", tiled=True)

        grad_o, grad_z = dot(normed_two_t, bg).astype(BF16), dot(normed_t, dz).astype(BF16)
        sums = [first_stage(grad_o), first_stage(grad_z)]
        dxi, d_skips, gsum, u, dbc = inside_back(dy, xa, bca, cum, dt, hpar)
        part = gate_in_back(info, dz, weights_z[layer])
        lam = exchange(scan_call(info, came, True, part, grad_o, grad_z, *tokens)).reshape(GROUPS, STATE, BLOCK)
        dmx, dmbc, tailx, tailbc, edgex, edgebc, d_parx, d_parbc, d_heads = finish_call(
            info, xa, dxi, dy, mixed, halo, cpar, bca, cum, dt, rate, hpar, lam, hin, s0, own1, u, gsum, dbc
        )
        edge = halo_shift(jnp.concatenate([edgex, edgebc], axis=1), -1)
        token = d_heads
        if layer == 0:
            higher_rows, higher = higher
            higher = arrived(fold(info, "y", [[v] for v in higher], 1, 96, d_heads), "y")
            token = higher[0]
        dxc = patch(dmx, dmbc, tailx, tailbc, edge, token)
        middle = 7 * LANES
        left, deadline = [], []
        if layer == 0:
            left = terms(info, "y", normed_t, dxc[:, :middle])
            deadline = [left[0]]
        part, d_gain_one = mixed_back(info, dxc, part, h, weights_x[layer], deadline)
        grad_x = dot(normed_t, dxc).astype(BF16) if layer == 1 else dxc
        dh, dh_low = norm_back(part, swapped(part), h, cot, gains_one[layer], grad_x)

        d_skip_row = jnp.sum(d_skips[0:1].reshape(1, 4 * OWN, HEADDIM), axis=2)
        rows = jnp.where(jnp.arange(8)[:, None] == 5, d_gain_two, d_parx)
        rows = jnp.concatenate([rows, d_parbc], axis=1)
        more = jnp.concatenate(
            [
                d_gain_one[:1],
                jnp.pad(d_heads[:2], ((0, 0), (0, WIDTH - LANES))),
                jnp.pad(head_lanes(d_skip_row), ((0, 4), (0, WIDTH - LANES))),
            ]
        )
        rows = jnp.concatenate([rows, jnp.pad(more, ((0, 0), (0, 2 * STATE)))])
        if layer == 1:
            return dh, dh_low, sums + [first_stage(grad_x)], rows

        rows = jnp.concatenate([rows, higher_rows]).astype(BF16)
        small = jnp.concatenate([rows[:, : MIXED // 2], rows[:, MIXED // 2 :]])
        small = jnp.pad(small, ((0, 0), (0, LANES)))
        left = arrived(left, "y")
        right = arrived(terms(info, "x", normed_t, dxc[:, middle:], (small,)), "x")
        left = fold(info, "x", [left], 4, 24, dh_low)
        right = fold(info, "y", [right], 4, 24, dh_low)
        higher = arrived(fold(info, "x", [higher], 1, 24, left[0]), "x")
        token = right[0]
        left, right = arrived(left, "x"), arrived(right, "y")
        sum_x = summed(arrived(last_fold(info, left, right, higher[0]), "z"))
        rows = jnp.concatenate(
            [sum_x[24:, : MIXED // 2], sum_x[24:, middle : middle + MIXED // 2]], axis=1
        )
        return dh, [higher, sums, token], sum_x[:24], rows

    at = section.reshape(1).astype(jnp.int32)
    smalls = (conv_weight[0], conv_bias, norm_gain, gate_gain, dt_bias, a_log, d_skip)
    mine_x, other_x = pick_x(at, w_xbc[0], w_dt[0], smalls)
    came_x = swapped(other_x)
    mine_zo, other_zo = pick_zo(at, w_z[0], w_out[0], mine_x)
    came_zo = swapped(other_zo)
    first = fetched(mine_x, came_x, 0, section, after([hidden], place))
    got = [first] + [send(first, "z", -r) for r in range(1, 4)]
    small_low = got
    low_x = pieces(mine_x, came_x, got, 0)
    got = lax.all_gather(fetched(mine_zo, came_zo, 0, section, after(got[1:], place)), "dp")
    late = after(low_x[3:6] + low_x[7:10], place)["z"]
    got = [None] + [lax.dynamic_index_in_dim(got, (late + r) % 4, 0, False) for r in range(1, 4)]
    low_zo = pieces(mine_zo, came_zo, got, 0)
    high_x = [lax.all_gather(jnp.where(section == 1, mine_x, came_x), "dp", tiled=True)]
    high_zo = [lax.all_gather(jnp.where(section == 1, mine_zo, came_zo), "dp", tiled=True)]
    ready = low_zo[3:6] + low_zo[7:10]
    weights_x = [Weight(v, n, PACKED) for n, v in enumerate((low_x, high_x))]
    weights_z = [Weight(v, n, LOCAL) for n, v in enumerate((low_zo, high_zo))]
    weights_o = [Weight(v, n, WIDTH, LOCAL) for n, v in enumerate((low_zo, high_zo))]

    unpacked = [unpack(info, v) for v in (small_low, high_x)]
    cpars, gains_one, gains_two, hpars = zip(*unpacked, strict=True)

    def returned(rows, layer):
        pairs = [(layer * 16 + a, layer * 16 + b) for a, b in NEIGHBOURS]
        other = lax.ppermute(
            jnp.where(micro == 0, rows[HALF:], rows[:HALF]), ("section", "ctx"), pairs
        )
        mine = jnp.where(micro == 0, rows[:HALF], rows[HALF:])
        return jnp.where(micro == 0, jnp.stack([mine, other]), jnp.stack([other, mine]))

    middle, saved_low = forward(hidden, 0)
    out_high, saved_high = forward(middle, 1)
    top_high = returned(out_high, 1)
    _, back, higher, rows = backward(cotangent, saved_high, 1, None, [top_high])
    dh_low, (higher, lower, token), low_x, rows = backward(
        back, saved_low, 0, (rows, higher), []
    )

    high_o, high_z, high_x = jnp.split(summed(higher), (WIDTH, WIDTH + LOCAL), axis=1)
    lower = fold(info, "x", [[v] for v in lower], 4, 24, token)
    lower = fold(info, "y", [arrived(lower, "x")], 1, 24, token)
    low_o, low_z = jnp.split(summed(arrived(lower, "y")), 2, axis=1)

    own, given = ordered(rows[:16], rows[16:])
    rows_0, rows_1 = ordered(own, swapped(given))
    wide = jnp.concatenate(
        [turns(rows_0[:8, :LOCAL], rows_1[:8, :LOCAL]), rows_0[:8, LOCAL:] + rows_1[:8, LOCAL:]],
        axis=1,
    )
    head_rows = turns(lanes_heads(rows_0[9:12, :LANES]), lanes_heads(rows_1[9:12, :LANES]))
    index = group * 16 + ctx
    d_conv = lax.dynamic_slice(wide, (0, index * 52), (5, 52))
    d_gain_two = lax.dynamic_slice(wide, (5, index * 48), (1, 48))
    d_gain_one = lax.dynamic_slice(rows_0[8:9] + rows_1[8:9], (0, index * 24), (1, 24))

    own, given = ordered(
        jnp.concatenate([low_z, low_x], axis=1), jnp.concatenate([high_z, high_x], axis=1)
    )
    first, second = ordered(own, swapped(given))
    sum_z = turns(first[:, :LOCAL], second[:, :LOCAL])
    at_x, at_bc, at_dt = LOCAL, LOCAL + LOCAL, LOCAL + MIXED
    sum_x = turns(first[:, at_x:at_bc], second[:, at_x:at_bc])
    sum_bc = first[:, at_bc:at_dt] + second[:, at_bc:at_dt]
    sum_dt = turns(lanes_heads(first[:, at_dt:]), lanes_heads(second[:, at_dt:]))

    trips = []
    for flip in range(2):
        pairs = [
            (c * 16 + j, (flip ^ (j % 2)) * 16 + 8 * c + j // 2) for c in range(2) for j in range(16)
        ]
        value = jnp.where(micro == flip, low_o, high_o)
        trips.append(lax.ppermute(value, ("section", "ctx"), pairs))
    sum_o = jnp.concatenate(ordered(*trips))

    top = jnp.where(section == 0, returned(dh_low, 0), top_high)
    return (
        top[None],
        d_gain_one,
        sum_z[None],
        jnp.concatenate([sum_x, sum_bc], axis=1)[None],
        sum_dt[None],
        d_conv[None, :4],
        d_conv[4:5],
        head_rows[0:1],
        head_rows[1:2],
        head_rows[2:3],
        d_gain_two,
        sum_o[None],
    )


def solution(mesh):
    in_specs = (
        P("section", None, ("dp", "ctx"), None),
        P(),
        P("section", "dp"),
        P("section", "dp", None),
        P("section", "dp", None),
        P("section", "dp", None),
        P("section", None, "dp"),
        P("section", "dp"),
        P("section", None),
        P("section", None),
        P("section", None),
        P("section", "dp"),
        P("section", "dp", None),
    )
    out_specs = (
        P("section", None, ("dp", "ctx"), None),
        P("section", ("dp", "ctx")),
        P("section", ("dp", "ctx"), None),
        P("section", ("dp", "ctx"), None),
        P("section", ("dp", "ctx"), None),
        P("section", None, ("dp", "ctx")),
        P("section", ("dp", "ctx")),
        P("section", None),
        P("section", None),
        P("section", None),
        P("section", ("dp", "ctx")),
        P("section", ("dp", "ctx"), None),
    )
    return jax.shard_map(
        on_device, mesh=mesh, in_specs=in_specs, out_specs=out_specs, check_vma=False
    )
```

```python
import functools

import jax
import jax.numpy as jnp
from jax import lax
from jax.experimental import pallas as pl
from jax.experimental.pallas import tpu as pltpu
from jax.sharding import PartitionSpec as P

HEADS = 48
HEADDIM = 64
STATE = 128
KERNEL = 4
SPAN = 256
MICRO = 2
WIDTH = 1536
INNER = 3072
CONV_CH = 3328
LANES = 128
CHUNKS = 8
GROUPS = 4
OWN = 6
BLOCK = OWN * HEADDIM
LOCAL = GROUPS * BLOCK
MIXED = LOCAL + 2 * STATE
PACKED = MIXED + LANES
ROWS = 256
HALF = 128
SHARD = 384
TALL = SHARD + 16
PIECE = 48
STATE_HALF = STATE // 2
MESSAGE = STATE_HALF + 16
SMALL = 32
EPSILON = 1e-05
PRECISE = lax.Precision.HIGHEST
F32 = jnp.float32
BF16 = jnp.bfloat16
VMEM_LIMIT = 56 * 1024 * 1024


def params(**more):
    return pltpu.CompilerParams(vmem_limit_bytes=VMEM_LIMIT, **more)


def whole(shape):
    return pl.BlockSpec(shape, lambda *_: (0,) * len(shape))


def columns(rows, width):
    return pl.BlockSpec((rows, width), lambda g: (0, g))


def grouped(rows):
    return pl.BlockSpec((1, rows, BLOCK), lambda g: (g, 0, 0))


MESSAGES = pl.BlockSpec((2, MESSAGE, BLOCK), lambda g: (g, 0, 0))
SMEM = pl.BlockSpec(memory_space=pltpu.SMEM)
ANYWHERE = pl.BlockSpec(memory_space=pl.ANY)


def shape(dims, kind=F32):
    return jax.ShapeDtypeStruct(dims, kind)


def dot(a, b):
    return jnp.dot(a, b, preferred_element_type=F32)


def dot_nt(a, b):
    return lax.dot_general(a, b, (((1,), (1,)), ((), ())), preferred_element_type=F32)


def exact_dot(a, b):
    return jnp.dot(a, b, precision=PRECISE, preferred_element_type=F32)


def lane_of(dims):
    return lax.broadcasted_iota(jnp.int32, dims, len(dims) - 1)


def row_of(dims):
    return lax.broadcasted_iota(jnp.int32, dims, len(dims) - 2)


def sigmoid(v):
    return 1.0 / (1.0 + jnp.exp(-v))


def softplus(v):
    return jnp.maximum(v, 0.0) + jnp.log1p(jnp.exp(-jnp.abs(v)))


def rolled(values, g):
    return pltpu.roll(values, lax.rem(LANES - 8 * g, LANES), axis=1)


def pair_lanes(values, p):
    low = lane_of((values.shape[0], LANES)) < HEADDIM
    return jnp.where(low, values[:, 2 * p : 2 * p + 1], values[:, 2 * p + 1 : 2 * p + 2])


def spread(values):
    return jnp.concatenate([pair_lanes(values, p) for p in range(OWN // 2)], axis=1)


def head_sum_matrix(g):
    head = row_of((BLOCK, LANES)) // HEADDIM
    return (lane_of((BLOCK, LANES)) == head + 8 * g).astype(BF16)


def lower_triangle(strict=False):
    i, j = row_of((HALF, HALF)), lane_of((HALF, HALF))
    return ((i > j) if strict else (i >= j)).astype(F32)


def usable_rows(info):
    return (row_of((ROWS, 1)) < info[0]).astype(F32)


def half(values, q):
    return values[q * HALF : (q + 1) * HALF]


class Weight:
    def __init__(self, arrays, layer, width, first=0):
        self.arrays = arrays
        self.stride = arrays[0].shape[0] // 4
        self.layer = layer
        self.width = width
        self.columns = pl.ds(first, width)

    def block(self, info, b):
        return lax.rem(info[10] + b, 4) * SHARD

    def parts(self, refs, info, b):
        start = self.block(info, b)
        if len(refs) == 1:
            there = pl.multiple_of(start // SHARD * self.stride, 16)
            return [(refs[0].at[pl.ds(there, SHARD)], start, SHARD)]
        out = []
        for side in range(2):
            mine = info[12 - side]
            for step in range(4):
                source = refs[2 + 4 * side + step].at[pl.ds((b - 1) * PIECE, PIECE)]
                row = start + side * (SHARD // 2) + lax.rem(mine + step, 4) * PIECE
                out.append((source, row, PIECE))
        return out

    def copies(self, refs, info, b, buffer, sems):
        return [
            pltpu.make_async_copy(
                source.at[:, self.columns],
                buffer.at[pl.ds(pl.multiple_of(row, 16), count)],
                sems.at[b, n],
            )
            for n, (source, row, count) in enumerate(self.parts(refs, info, b))
        ]

    def own_copy(self, source, info, buffer, sems):
        rows = pl.ds(pl.multiple_of(self.block(info, 0), SHARD), SHARD)
        source = source.at[pl.ds(0, SHARD), self.columns]
        return pltpu.make_async_copy(source, buffer.at[rows], sems.at[0, 0])

    def start(self, refs, info, buffer, sems):
        whole_array = len(refs) == 1
        if not whole_array:
            for n in range(2):

                @pl.when((info[13] == self.layer) == (n == 0))
                def _(n=n):
                    self.own_copy(refs[n], info, buffer, sems).start()

        for b in range(0 if whole_array else 1, 4):
            for c in self.copies(refs, info, b, buffer, sems):
                c.start()

    def wait(self, refs, info, b, buffer, sems):
        if b == 0 and len(refs) > 1:
            self.own_copy(refs[0], info, buffer, sems).wait()
        else:
            for c in self.copies(refs, info, b, buffer, sems):
                c.wait()
        return pl.ds(pl.multiple_of(self.block(info, b), SHARD), SHARD)

    def specs(self):
        return [ANYWHERE] * len(self.arrays)

    def scratch(self):
        return [pltpu.VMEM((4 * SHARD, self.width), BF16), pltpu.SemaphoreType.DMA((4, 8))]

    def product(self, refs, info, left, buffer, sems, total):
        for b in range(4):
            self.wait(refs, info, b, buffer, sems)
        step = 512 if self.width % 512 == 0 else 640
        for at in range(0, self.width, step):
            total[:, at : at + step] = dot(left[...], buffer[:, at : at + step])


def in_proj_body(weight, tokens, info, h_ref, gain_ref, *rest):
    refs = len(weight.arrays)
    w_refs, rest = rest[:refs], rest[refs + tokens :]
    (normed_ref, mixed_ref, rate_ref, buffer, sems, total) = rest
    weight.start(w_refs, info, buffer, sems)
    h = h_ref[...].astype(F32)
    scale = lax.rsqrt(jnp.mean(h * h, axis=1, keepdims=True) + EPSILON)
    normed_ref[...] = (h * scale * gain_ref[...]).astype(BF16)
    weight.product(w_refs, info, normed_ref, buffer, sems, total)
    mixed_ref[...] = total[:, :MIXED].astype(BF16)
    rate_ref[...] = total[:, MIXED:]


def in_proj(info, h, gain, weight, tokens):
    return pl.pallas_call(
        functools.partial(in_proj_body, weight, len(tokens)),
        out_shape=(shape((ROWS, WIDTH), BF16), shape((ROWS, MIXED), BF16), shape((ROWS, LANES))),
        in_specs=[SMEM, whole((ROWS, WIDTH)), whole((1, WIDTH))]
        + weight.specs()
        + [ANYWHERE] * len(tokens),
        out_specs=(whole((ROWS, WIDTH)), whole((ROWS, MIXED)), whole((ROWS, LANES))),
        scratch_shapes=weight.scratch() + [pltpu.VMEM((ROWS, PACKED), F32)],
        compiler_params=params(),
        cost_estimate=pl.CostEstimate(
            flops=2 * ROWS * WIDTH * PACKED, bytes_accessed=8_000_000, transcendentals=0
        ),
        name="in_proj",
    )(info, h, gain, *weight.arrays, *tokens)


def gate_proj_body(weight, tokens, info, normed_ref, *rest):
    refs = len(weight.arrays)
    w_refs, (gate_ref, buffer, sems) = rest[:refs], rest[refs + tokens :]
    weight.start(w_refs, info, buffer, sems)
    weight.product(w_refs, info, normed_ref, buffer, sems, gate_ref)


def gate_proj(info, normed, weight, tokens):
    return pl.pallas_call(
        functools.partial(gate_proj_body, weight, len(tokens)),
        out_shape=shape((ROWS, LOCAL)),
        in_specs=[SMEM, whole((ROWS, WIDTH))] + weight.specs() + [ANYWHERE] * len(tokens),
        out_specs=whole((ROWS, LOCAL)),
        scratch_shapes=weight.scratch(),
        compiler_params=params(),
        cost_estimate=pl.CostEstimate(
            flops=2 * ROWS * WIDTH * LOCAL, bytes_accessed=7_000_000, transcendentals=0
        ),
        name="gate_proj",
    )(info, normed, *weight.arrays, *tokens)


def conv_sum_of(values, halo, cpar, keep, ext):
    width = values.shape[1]
    ext[0:16, :width] = halo.astype(F32) * keep
    ext[16 : 16 + ROWS, :width] = values.astype(F32)
    total = cpar[4:5, :]
    for k in range(KERNEL):
        total = total + cpar[k : k + 1, :] * ext[13 + k : 13 + k + ROWS, :width]
    return total


def state_body(
    info, mixed, halo, cpar, bc, halo_bc, cpar_bc, rate, hpar,
    xa_ref, bca_ref, cum_ref, dt_ref, s0_ref, msg_ref, ext, bt, tail,
):
    g = pl.program_id(0)
    keep = info[1].astype(F32)

    @pl.when(g == 0)
    def _():
        total = conv_sum_of(bc[...], halo_bc[...], cpar_bc[...], keep, ext)
        active = total * sigmoid(total)
        bca_ref[...] = active
        bt[...] = active[:, :STATE].T.astype(BF16)
        dt = usable_rows(info) * softplus(rate[...] + hpar[0:1, :])
        log_decay = dt * -jnp.exp(hpar[1:2, :])
        dt_ref[...] = dt
        tri = lower_triangle()
        for q in range(2):
            rows = pl.ds(q * HALF, HALF)
            cum = exact_dot(tri, half(log_decay, q))
            cum_ref[rows, :] = cum
            tail[rows, :] = jnp.exp(cum[HALF - 1 :, :] - cum) * half(dt, q)

    total = conv_sum_of(mixed[...], halo[...], cpar[...], keep, ext)
    xa = total * sigmoid(total)
    xa_ref[...] = xa
    weighted = (xa * spread(rolled(tail[...], g))).astype(BF16)
    ends = rolled(cum_ref[...], g)
    end0, end1 = ends[HALF - 1 : HALF], ends[ROWS - 1 : ROWS]
    s0 = dot(bt[:, :HALF], half(weighted, 0))
    s1 = dot(bt[:, HALF:], half(weighted, 1))
    s0_ref[0] = s0
    state = (spread(jnp.exp(end1)) * s0 + s1).astype(BF16)
    damp = spread(jnp.exp(end0 + end1))
    high = damp.astype(BF16)
    low = (damp - high.astype(F32)).astype(BF16)
    row = row_of((16, BLOCK))
    damps = jnp.where(row == 0, high.astype(F32), low.astype(F32)).astype(BF16)
    for r in range(2):
        msg_ref[r, :STATE_HALF, :] = state[r * STATE_HALF : (r + 1) * STATE_HALF]
        msg_ref[r, STATE_HALF:, :] = damps


def state_call(info, mixed, halo, cpar, rate, hpar):
    bc_at = LOCAL // 256
    return pl.pallas_call(
        state_body,
        grid=(GROUPS,),
        out_shape=(
            shape((ROWS, LOCAL)),
            shape((ROWS, 256)),
            shape((ROWS, LANES)),
            shape((ROWS, LANES)),
            shape((GROUPS, STATE, BLOCK)),
            shape((CHUNKS, MESSAGE, BLOCK), BF16),
        ),
        in_specs=[
            SMEM,
            columns(ROWS, BLOCK),
            columns(16, BLOCK),
            columns(8, BLOCK),
            pl.BlockSpec((ROWS, 256), lambda g: (0, bc_at)),
            pl.BlockSpec((16, 256), lambda g: (0, bc_at)),
            pl.BlockSpec((8, 256), lambda g: (0, bc_at)),
            whole((ROWS, LANES)),
            whole((8, LANES)),
        ],
        out_specs=(
            columns(ROWS, BLOCK),
            whole((ROWS, 256)),
            whole((ROWS, LANES)),
            whole((ROWS, LANES)),
            grouped(STATE),
            MESSAGES,
        ),
        scratch_shapes=[
            pltpu.VMEM((ROWS + 32, BLOCK), F32),
            pltpu.VMEM((STATE, ROWS), BF16),
            pltpu.VMEM((ROWS, LANES), F32),
        ],
        compiler_params=params(),
        cost_estimate=pl.CostEstimate(
            flops=2 * ROWS * STATE * LOCAL, bytes_accessed=4_500_000, transcendentals=400_000
        ),
        name="conv_state",
    )(info, mixed, halo, cpar, mixed, halo, cpar, rate, hpar)


def inside_body(xa, bca, cum, dt, hpar, y_ref, cum_t, scores):
    g = pl.program_id(0)

    @pl.when(g == 0)
    def _():
        tri = lower_triangle()
        for q in range(2):
            b, c = half(bca[:, :STATE], q).astype(BF16), half(bca[:, STATE:], q).astype(BF16)
            scores[q] = dot_nt(c, b) * tri
            cum_t[:, q * HALF : (q + 1) * HALF] = half(cum[...], q).T

    cols = rolled(cum[...], g)
    rows = cum_t[pl.ds(pl.multiple_of(8 * g, 8), 8), :]
    steps = rolled(dt[...], g)
    skips = rolled(hpar[...], g)[2:3, :]
    low = lane_of((HALF, LANES)) < HEADDIM
    for q in range(2):
        for p in range(OWN // 2):
            lanes = slice(p * LANES, (p + 1) * LANES)
            x = xa[q * HALF : (q + 1) * HALF, lanes]
            xdt = x * pair_lanes(half(steps, q), p)
            both = jnp.concatenate([jnp.where(low, xdt, 0.0), jnp.where(low, 0.0, xdt)], axis=0)
            mats = []
            for i in (2 * p, 2 * p + 1):
                gap = half(cols, q)[:, i : i + 1] - rows[i : i + 1, q * HALF : (q + 1) * HALF]
                mats.append((jnp.exp(jnp.minimum(gap, 0.0)) * scores[q]).astype(BF16))
            y = dot(jnp.concatenate(mats, axis=1), both.astype(BF16))
            y_ref[q * HALF : (q + 1) * HALF, lanes] = y + x * pair_lanes(skips, p)


def inside_call(xa, bca, cum, dt, hpar):
    return pl.pallas_call(
        inside_body,
        grid=(GROUPS,),
        out_shape=shape((ROWS, LOCAL)),
        in_specs=[
            columns(ROWS, BLOCK),
            whole((ROWS, 256)),
            whole((ROWS, LANES)),
            whole((ROWS, LANES)),
            whole((8, LANES)),
        ],
        out_specs=columns(ROWS, BLOCK),
        scratch_shapes=[pltpu.VMEM((LANES, ROWS), F32), pltpu.VMEM((2, HALF, HALF), F32)],
        compiler_params=params(),
        cost_estimate=pl.CostEstimate(
            flops=2 * HEADS * HALF * HALF * LANES, bytes_accessed=3_300_000, transcendentals=800_000
        ),
        name="inside",
    )(xa, bca, cum, dt, hpar)


def scan_body(backward, info, msg, *rest):
    out_ref = rest[-1]
    carry = jnp.zeros((STATE_HALF, BLOCK), F32)
    for k in reversed(range(CHUNKS)) if backward else range(CHUNKS):
        keep = info[2 + k].astype(F32)
        if not backward:
            carry = carry * keep
        out_ref[k] = carry.astype(BF16)
        damps = msg[k, STATE_HALF:, :].astype(F32)
        carry = (damps[0:1] + damps[1:2]) * carry + msg[k, :STATE_HALF, :].astype(F32)
        if backward:
            carry = carry * keep


def scan_call(info, msg, backward, *tokens):
    return pl.pallas_call(
        functools.partial(scan_body, backward),
        out_shape=shape((CHUNKS, STATE_HALF, BLOCK), BF16),
        in_specs=[SMEM, whole((CHUNKS, MESSAGE, BLOCK))] + [ANYWHERE] * len(tokens),
        out_specs=whole((CHUNKS, STATE_HALF, BLOCK)),
        compiler_params=params(),
        name="chunk_scan",
    )(info, msg, *tokens)


def out_proj_body(weight, info, y_in, bca, cum, hin, s0, gate, gain, *rest):
    refs = len(weight.arrays)
    w_refs, (y_ref, part_ref, buffer, sems, sums, gained) = rest[:refs], rest[refs:]
    weight.start(w_refs, info, buffer, sems)
    c_all = bca[:, STATE:].astype(BF16)
    grow = jnp.exp(cum[...])
    sums[...] = jnp.zeros((ROWS, LANES), F32)

    def group(g, _):
        lanes = pl.ds(pl.multiple_of(g * BLOCK, LANES), BLOCK)
        factor = rolled(grow, g)
        first = hin[g]
        second = spread(factor[HALF - 1 : HALF]) * first.astype(F32) + s0[g]
        carried = jnp.concatenate(
            [dot(half(c_all, 0), first), dot(half(c_all, 1), second.astype(BF16))], axis=0
        )
        y = y_in[:, lanes] + spread(factor) * carried
        y_ref[:, lanes] = y
        z = gate[:, lanes]
        gated = y * z * sigmoid(z)
        square = gated * gated
        sums[...] += sum(square[:, i * LANES : (i + 1) * LANES] for i in range(BLOCK // LANES))
        gained[:, lanes] = (gated * gain[:, lanes]).astype(BF16)
        return 0

    lax.fori_loop(0, GROUPS, group, 0)
    part_ref[:, WIDTH:] = sums[...]
    weight.product(w_refs, info, gained, buffer, sems, part_ref)


def out_proj(info, y_in, bca, cum, hin, s0, gate, gain, weight):
    return pl.pallas_call(
        functools.partial(out_proj_body, weight),
        out_shape=(shape((ROWS, LOCAL)), shape((ROWS, WIDTH + LANES))),
        in_specs=[
            SMEM,
            whole((ROWS, LOCAL)),
            whole((ROWS, 256)),
            whole((ROWS, LANES)),
            whole((GROUPS, STATE, BLOCK)),
            whole((GROUPS, STATE, BLOCK)),
            whole((ROWS, LOCAL)),
            whole((1, LOCAL)),
        ]
        + weight.specs(),
        out_specs=(whole((ROWS, LOCAL)), whole((ROWS, WIDTH + LANES))),
        scratch_shapes=weight.scratch()
        + [pltpu.VMEM((ROWS, LANES), F32), pltpu.VMEM((ROWS, LOCAL), BF16)],
        compiler_params=params(),
        cost_estimate=pl.CostEstimate(
            flops=2 * ROWS * WIDTH * LOCAL, bytes_accessed=13_000_000, transcendentals=800_000
        ),
        name="out_proj",
    )(info, y_in, bca, cum, hin, s0, gate, gain, *weight.arrays)


def join_body(info, h_ref, own, came, res_ref, branch_ref, scale_ref):
    squares = jnp.sum(own[:, WIDTH:] + came[:, WIDTH:], axis=1, keepdims=True)
    scale = lax.rsqrt(squares / INNER + EPSILON)
    branch = scale * (own[:, :WIDTH] + came[:, :WIDTH])
    branch_ref[...] = branch.astype(BF16)
    scale_ref[...] = jnp.broadcast_to(scale, (HALF // 2, LANES))
    first = pl.program_id(0) * (HALF // 2)
    usable = (row_of((HALF // 2, 1)) + first < info[0]).astype(F32)
    result = h_ref[...].astype(F32) + usable * branch
    res_ref[...] = result.astype(res_ref.dtype)


def join(info, h, own, came, kind):
    def rows(width):
        return pl.BlockSpec((HALF // 2, width), lambda i: (i, 0))

    return pl.pallas_call(
        join_body,
        grid=(4,),
        out_shape=(shape((ROWS, WIDTH), kind), shape((ROWS, WIDTH), BF16), shape((ROWS, LANES))),
        in_specs=[SMEM, rows(WIDTH), rows(WIDTH + LANES), rows(WIDTH + LANES)],
        out_specs=(rows(WIDTH), rows(WIDTH), rows(LANES)),
        compiler_params=params(),
        cost_estimate=pl.CostEstimate(flops=2_000_000, bytes_accessed=8_000_000, transcendentals=0),
        name="join",
    )(info, h, own, came)


def gate_back_body(weight, info, cot, y, gate, gain, branch, scale_ref, *rest):
    refs = len(weight.arrays)
    w_refs, rest = rest[:refs], rest[refs:]
    bg_ref, dy_ref, dz_ref, grad_ref, dgain_ref, buffer, sems, inner_ref = rest
    b = pl.program_id(0)
    scale = scale_ref[:, :1]

    @pl.when(b == 0)
    def _():
        weight.start(w_refs, info, buffer, sems)
        bg = (usable_rows(info) * cot[...].astype(F32)).astype(BF16)
        bg_ref[...] = bg
        inner = jnp.sum(bg.astype(F32) * branch[...].astype(F32), axis=1, keepdims=True)
        inner_ref[...] = jnp.broadcast_to(inner * scale * scale / INNER, (ROWS, LANES))
        for n in range(4):
            weight.wait(w_refs, info, n, buffer, sems)

    inner = inner_ref[:, :1]
    bg = bg_ref[...]
    d_norms = dot_nt(bg, buffer[pl.ds(pl.multiple_of(b * SHARD, SHARD), SHARD), :])
    norms = []
    for i in range(SHARD // LANES):
        lanes = slice(i * LANES, (i + 1) * LANES)
        z = gate[:, lanes]
        sig = sigmoid(z)
        silu = z * sig
        y_here = y[:, lanes]
        gated = y_here * silu
        d_norm = d_norms[:, lanes]
        gained = scale * gain[:, lanes]
        norms.append((gated * gained).astype(BF16))
        d_gated = d_norm * gained - gated * inner
        total = jnp.sum(d_norm * gated * scale, axis=0, keepdims=True)
        dgain_ref[:, lanes] = jnp.broadcast_to(total, (8, LANES))
        dy_ref[:, lanes] = (d_gated * silu).astype(BF16)
        dz_ref[:, lanes] = (d_gated * y_here * sig * (1.0 + z * (1.0 - sig))).astype(BF16)
    norm = jnp.concatenate(norms, axis=1)
    grad_ref[...] = dot(norm.T, bg).astype(BF16) if grad_ref.shape[1] == WIDTH else norm.T


def gate_back(info, cot, y, gate, gain, branch, scale, weight, with_grad):
    wide, local = whole((ROWS, WIDTH)), columns(ROWS, SHARD)
    grad_width = WIDTH if with_grad else ROWS
    return pl.pallas_call(
        functools.partial(gate_back_body, weight),
        grid=(4,),
        out_shape=(
            shape((ROWS, WIDTH), BF16),
            shape((ROWS, LOCAL), BF16),
            shape((ROWS, LOCAL), BF16),
            shape((LOCAL, grad_width), BF16),
            shape((8, LOCAL)),
        ),
        in_specs=[SMEM, wide, local, local, columns(1, SHARD), wide, whole((ROWS, LANES))]
        + weight.specs(),
        out_specs=(
            wide,
            local,
            local,
            pl.BlockSpec((SHARD, grad_width), lambda b: (b, 0)),
            columns(8, SHARD),
        ),
        scratch_shapes=weight.scratch() + [pltpu.VMEM((ROWS, LANES), F32)],
        compiler_params=params(),
        cost_estimate=pl.CostEstimate(
            flops=4 * ROWS * WIDTH * LOCAL, bytes_accessed=17_000_000, transcendentals=800_000
        ),
        name="gate_back",
    )(info, cot, y, gate, gain, branch, scale, *weight.arrays)


def own_grad_body(dy, bca, cum, msg_in, dz, normed, own1_ref, msg_ref, grad_ref, ct, grow):
    g = pl.program_id(0)
    grad_ref[...] = dot(normed[...].T, dz[...]).astype(BF16)

    @pl.when(g == 0)
    def _():
        ct[...] = bca[:, STATE:].T.astype(BF16)
        grow[...] = jnp.exp(cum[...])

    factor = rolled(grow[...], g)
    weighted = (dy[...].astype(F32) * spread(factor)).astype(BF16)
    own0 = dot(ct[:, :HALF], half(weighted, 0))
    own1 = dot(ct[:, HALF:], half(weighted, 1))
    own1_ref[0] = own1
    grad = (spread(factor[HALF - 1 : HALF]) * own1 + own0).astype(BF16)
    for r in range(2):
        msg_ref[r, :STATE_HALF, :] = grad[r * STATE_HALF : (r + 1) * STATE_HALF]
        msg_ref[r, STATE_HALF:, :] = msg_in[r, STATE_HALF:, :]


def own_grad(dy, bca, cum, msg, dz, normed):
    return pl.pallas_call(
        own_grad_body,
        grid=(GROUPS,),
        out_shape=(
            shape((GROUPS, STATE, BLOCK)),
            shape((CHUNKS, MESSAGE, BLOCK), BF16),
            shape((WIDTH, LOCAL), BF16),
        ),
        in_specs=[
            columns(ROWS, BLOCK),
            whole((ROWS, 256)),
            whole((ROWS, LANES)),
            MESSAGES,
            whole((ROWS, LOCAL)),
            columns(ROWS, SHARD),
        ],
        out_specs=(grouped(STATE), MESSAGES, pl.BlockSpec((SHARD, LOCAL), lambda b: (b, 0))),
        scratch_shapes=[pltpu.VMEM((STATE, ROWS), BF16), pltpu.VMEM((ROWS, LANES), F32)],
        compiler_params=params(),
        cost_estimate=pl.CostEstimate(
            flops=2 * ROWS * WIDTH * LOCAL, bytes_accessed=8_000_000, transcendentals=0
        ),
        name="own_grad",
    )(dy, bca, cum, msg, dz, normed)


def inside_back_body(
    dy, xa, bca, cum, dt, hpar,
    dx_ref, dskip_ref, gsum_ref, u_ref, dbc_ref, cum_t, scores, dscores,
):
    g = pl.program_id(0)

    @pl.when(g == 0)
    def _():
        tri = lower_triangle()
        for q in range(2):
            b, c = half(bca[:, :STATE], q).astype(BF16), half(bca[:, STATE:], q).astype(BF16)
            scores[q] = dot_nt(b, c) * tri.T
            cum_t[:, q * HALF : (q + 1) * HALF] = half(cum[...], q).T
        dscores[...] = jnp.zeros((2, HALF, HALF), F32)
        u_ref[...] = jnp.zeros((ROWS, LANES), F32)

    cols = rolled(cum[...], g)
    rows = cum_t[pl.ds(pl.multiple_of(8 * g, 8), 8), :]
    steps = rolled(dt[...], g)
    skips = rolled(hpar[...], g)[2:3, :]
    low = lane_of((HALF, LANES)) < HEADDIM
    lane = lane_of((HALF, LANES))
    gsum_ref[...] = jnp.zeros((8, ROWS), F32)
    for q in range(2):
        here = slice(q * HALF, (q + 1) * HALF)
        u_here = u_ref[here, :]
        for p in range(OWN // 2):
            lanes = slice(p * LANES, (p + 1) * LANES)
            dy_pair = dy[here, lanes]
            x = xa[here, lanes]
            zero = jnp.zeros_like(dy_pair)
            both = jnp.concatenate(
                [jnp.where(low, dy_pair, zero), jnp.where(low, zero, dy_pair)], axis=0
            )
            dw = dot_nt(x.astype(BF16), both)
            mats = []
            for n, i in enumerate((2 * p, 2 * p + 1)):
                gap = rows[i : i + 1, here] - half(cols, q)[:, i : i + 1]
                decay = jnp.exp(jnp.minimum(gap, 0.0))
                step = half(steps, q)[:, i : i + 1]
                weight = decay * scores[q]
                mats.append(weight.astype(BF16))
                dw_here = dw[:, n * HALF : (n + 1) * HALF]
                dscores[q] += decay * dw_here * step
                direct = weight * dw_here
                total = jnp.sum(direct, axis=1, keepdims=True)
                u_here = jnp.where(lane == 8 * g + i, total, u_here)
                gsum_ref[i : i + 1, here] = jnp.sum(direct * step, axis=0, keepdims=True)
            dx = dot(jnp.concatenate(mats, axis=1), both)
            dy_wide = dy_pair.astype(F32)
            dx_ref[here, lanes] = dx * pair_lanes(half(steps, q), p) + dy_wide * pair_lanes(skips, p)
            skip_sum = jnp.sum(dy_wide * x, axis=0, keepdims=True)
            if q == 0:
                dskip_ref[:, lanes] = jnp.broadcast_to(skip_sum, (8, LANES))
            else:
                dskip_ref[:, lanes] += skip_sum
        u_ref[here, :] = u_here

    @pl.when(g == GROUPS - 1)
    def _():
        tri = lower_triangle()
        for q in range(2):
            b, c = half(bca[:, :STATE], q).astype(BF16), half(bca[:, STATE:], q).astype(BF16)
            ds_t = dscores[q] * tri.T
            dbc_ref[q * HALF : (q + 1) * HALF, :STATE] = dot(ds_t.astype(BF16), c)
            dbc_ref[q * HALF : (q + 1) * HALF, STATE:] = dot(ds_t.T.astype(BF16), b)


def inside_back(dy, xa, bca, cum, dt, hpar):
    return pl.pallas_call(
        inside_back_body,
        grid=(GROUPS,),
        out_shape=(
            shape((ROWS, LOCAL)),
            shape((8, LOCAL)),
            shape((8 * GROUPS, ROWS)),
            shape((ROWS, LANES)),
            shape((ROWS, 256)),
        ),
        in_specs=[
            columns(ROWS, BLOCK),
            columns(ROWS, BLOCK),
            whole((ROWS, 256)),
            whole((ROWS, LANES)),
            whole((ROWS, LANES)),
            whole((8, LANES)),
        ],
        out_specs=(
            columns(ROWS, BLOCK),
            columns(8, BLOCK),
            pl.BlockSpec((8, ROWS), lambda g: (g, 0)),
            whole((ROWS, LANES)),
            whole((ROWS, 256)),
        ),
        scratch_shapes=[
            pltpu.VMEM((LANES, ROWS), F32),
            pltpu.VMEM((2, HALF, HALF), F32),
            pltpu.VMEM((2, HALF, HALF), F32),
        ],
        compiler_params=params(),
        cost_estimate=pl.CostEstimate(
            flops=4 * HEADS * HALF * HALF * LANES, bytes_accessed=4_500_000, transcendentals=800_000
        ),
        name="inside_back",
    )(dy, xa, bca, cum, dt, hpar)


def conv_back(d_active, values, halo, cpar, keep, ext, ext_d):
    width = values.shape[1]
    total = conv_sum_of(values, halo, cpar, keep, ext)
    sig = sigmoid(total)
    d_sum = d_active * sig * (1.0 + total * (1.0 - sig))
    ext_d[0:16, :width] = jnp.zeros((16, width), F32)
    ext_d[16 : 16 + ROWS, :width] = d_sum
    ext_d[16 + ROWS :, :width] = jnp.zeros((16, width), F32)
    d_in = jnp.zeros((ROWS + 16, width), F32)
    for k in range(KERNEL):
        d_in = d_in + cpar[k : k + 1, :] * ext_d[3 - k : 3 - k + ROWS + 16, :width]
    row = row_of((8, width))
    d_par = jnp.where(row == 4, jnp.sum(d_sum, axis=0, keepdims=True), 0.0)
    for k in range(KERNEL):
        tap = jnp.sum(d_sum * ext[13 + k : 13 + k + ROWS, :width], axis=0, keepdims=True)
        d_par = jnp.where(row == k, tap, d_par)
    return d_in, d_par


def finish_body(
    info, xa, dxi, dy, mixed, halo, cpar, bc, halo_bc, cpar_bc, bca, cum, dt, rate, hpar, lam, hin, s0, own1, u, gsum, dbc,
    dmx_ref, dmbc_ref, tailx_ref, tailbc_ref, edgex_ref, edgebc_ref, dcx_ref, dcbc_ref, dhead_ref,
    ext, ext_d, grow, tail, v_sum, q_sum, end_sum, dbc_sum,
):
    g = pl.program_id(0)
    keep = info[1].astype(F32)

    @pl.when(g == 0)
    def _():
        grow[...] = jnp.exp(cum[...])
        for q in range(2):
            here = half(cum[...], q)
            tail[q * HALF : (q + 1) * HALF, :] = jnp.exp(here[HALF - 1 :, :] - here)
        v_sum[...] = jnp.zeros((ROWS, LANES), F32)
        q_sum[...] = jnp.zeros((ROWS, LANES), F32)
        end_sum[...] = jnp.zeros((16, LANES), F32)
        dbc_sum[...] = dbc[...]

    sums = head_sum_matrix(g)
    factor = rolled(grow[...], g)
    tails = rolled(tail[...], g)
    steps = rolled(dt[...], g)
    ends = [spread(factor[HALF - 1 : HALF]), spread(factor[ROWS - 1 : ROWS])]
    lam1 = lam[0].astype(F32)
    lams = [ends[1] * lam1 + own1[0], lam1]
    first = hin[0].astype(F32)
    states = [first, ends[0] * first + s0[0]]
    d_x = []
    for q in range(2):
        here = slice(q * HALF, (q + 1) * HALF)
        b, c = bca[here, :STATE].astype(BF16), bca[here, STATE:].astype(BF16)
        lam_q, state_q = lams[q].astype(BF16), states[q].astype(BF16)
        tail_wide = spread(half(tails, q))
        tail_step = tail_wide * spread(half(steps, q))
        x, dy_q = xa[here, :], dy[here, :].astype(F32)
        lb = dot(b, lam_q) * tail_wide
        d_x.append(dxi[here, :] + lb * spread(half(steps, q)))
        v_sum[here, :] += dot((x * lb).astype(BF16), sums)
        grow_wide = spread(half(factor, q))
        dy_grow = (dy_q * grow_wide).astype(BF16)
        carried = dot(c, state_q)
        q_sum[here, :] += dot((dy_q * grow_wide * carried).astype(BF16), sums)
        dbc_sum[here, :STATE] += dot_nt((x * tail_step).astype(BF16), lam_q)
        dbc_sum[here, STATE:] += dot_nt(dy_grow, state_q)
        last = jnp.sum(lams[q] * states[q], axis=0, keepdims=True) * ends[q]
        high = last.astype(BF16).astype(F32)
        both = jnp.where(row_of((16, BLOCK)) == 0, high, last - high).astype(BF16)
        both = dot(both, sums)
        end_sum[8 * q : 8 * q + 8, :] += both[0:1] + both[1:2]
    d_in, d_par = conv_back(
        jnp.concatenate(d_x, axis=0), mixed[...], halo[...], cpar[...], keep, ext, ext_d
    )
    dmx_ref[...] = d_in[16:].astype(BF16)
    tailx_ref[...] = d_in[ROWS:]
    edgex_ref[...] = (d_in[:16] * keep).astype(BF16)
    dcx_ref[...] = d_par

    @pl.when(g == GROUPS - 1)
    def _():
        d_bc, d_par_bc = conv_back(
            dbc_sum[...], bc[...], halo_bc[...], cpar_bc[...], keep, ext, ext_d
        )
        dmbc_ref[:, :256] = d_bc[16:].astype(BF16)
        tailbc_ref[...] = d_bc[ROWS:]
        edgebc_ref[...] = (d_bc[:16] * keep).astype(BF16)
        dcbc_ref[...] = d_par_bc
        rates = -jnp.exp(hpar[1:2, :])
        logit = rate[...] + hpar[0:1, :]
        upper = lower_triangle().T
        before = lower_triangle(True)
        d_bias = jnp.zeros((1, LANES), F32)
        d_log = jnp.zeros((1, LANES), F32)
        usable = usable_rows(info)
        for q in range(2):
            here = slice(q * HALF, (q + 1) * HALF)
            step = dt[here, :]
            gs = gsum[...][:, here].T
            gs = jnp.concatenate([gs, jnp.zeros((HALF, LANES - 8 * GROUPS), F32)], axis=1)
            d_decay = exact_dot(upper, gs - step * u[here, :] + q_sum[here, :])
            d_decay = d_decay + exact_dot(before, step * v_sum[here, :])
            d_decay = d_decay + end_sum[8 * q : 8 * q + 1, :]
            d_step = u[here, :] + v_sum[here, :] + rates * d_decay
            d_rate = half(usable, q) * d_step * sigmoid(half(logit, q))
            d_bias += jnp.sum(d_rate, axis=0, keepdims=True)
            d_log += jnp.sum(d_decay * step * rates, axis=0, keepdims=True)
            dmbc_ref[here, 256:] = d_rate.astype(BF16)
        row = row_of((8, LANES))
        dhead_ref[...] = jnp.where(row == 0, d_bias, jnp.where(row == 1, d_log, 0.0))


def finish_call(
    info, xa, dxi, dy, mixed, halo, cpar, bca, cum, dt, rate, hpar, lam, hin, s0, own1, u, gsum, dbc
):
    bc_at = LOCAL // 256
    wide = whole((ROWS, LANES))
    return pl.pallas_call(
        finish_body,
        grid=(GROUPS,),
        out_shape=(
            shape((ROWS, LOCAL), BF16),
            shape((ROWS, 384), BF16),
            shape((16, LOCAL)),
            shape((16, 256)),
            shape((16, LOCAL), BF16),
            shape((16, 256), BF16),
            shape((8, LOCAL)),
            shape((8, 256)),
            shape((8, LANES)),
        ),
        in_specs=[
            SMEM,
            columns(ROWS, BLOCK),
            columns(ROWS, BLOCK),
            columns(ROWS, BLOCK),
            columns(ROWS, BLOCK),
            columns(16, BLOCK),
            columns(8, BLOCK),
            pl.BlockSpec((ROWS, 256), lambda g: (0, bc_at)),
            pl.BlockSpec((16, 256), lambda g: (0, bc_at)),
            pl.BlockSpec((8, 256), lambda g: (0, bc_at)),
            whole((ROWS, 256)),
            wide,
            wide,
            wide,
            whole((8, LANES)),
            grouped(STATE),
            grouped(STATE),
            grouped(STATE),
            grouped(STATE),
            wide,
            whole((8 * GROUPS, ROWS)),
            whole((ROWS, 256)),
        ],
        out_specs=(
            columns(ROWS, BLOCK),
            whole((ROWS, 384)),
            columns(16, BLOCK),
            whole((16, 256)),
            columns(16, BLOCK),
            whole((16, 256)),
            columns(8, BLOCK),
            whole((8, 256)),
            whole((8, LANES)),
        ),
        scratch_shapes=[
            pltpu.VMEM((ROWS + 32, BLOCK), F32),
            pltpu.VMEM((ROWS + 32, BLOCK), F32),
            pltpu.VMEM((ROWS, LANES), F32),
            pltpu.VMEM((ROWS, LANES), F32),
            pltpu.VMEM((ROWS, LANES), F32),
            pltpu.VMEM((ROWS, LANES), F32),
            pltpu.VMEM((16, LANES), F32),
            pltpu.VMEM((ROWS, 256), F32),
        ],
        compiler_params=params(),
        cost_estimate=pl.CostEstimate(
            flops=10 * ROWS * STATE * LOCAL, bytes_accessed=7_500_000, transcendentals=800_000
        ),
        name="finish_back",
    )(
        info, xa, dxi, dy, mixed, halo, cpar, mixed, halo, cpar, bca, cum, dt, rate, hpar,
        lam, hin, s0, own1, u, gsum, dbc,
    )


def gate_in_back_body(weight, info, dz, token, *rest):
    refs = len(weight.arrays)
    w_refs, (out_ref, buffer, sems) = rest[:refs], rest[refs:]

    @pl.when(pl.program_id(0) == 0)
    def _():
        weight.start(w_refs, info, buffer, sems)
        for n in range(4):
            weight.wait(w_refs, info, n, buffer, sems)

    rows = pl.ds(pl.multiple_of(pl.program_id(0) * SHARD, SHARD), SHARD)
    out_ref[...] = dot_nt(dz[...], buffer[rows, :])


def gate_in_back(info, dz, weight, token):
    return pl.pallas_call(
        functools.partial(gate_in_back_body, weight),
        grid=(4,),
        out_shape=shape((ROWS, WIDTH)),
        in_specs=[SMEM, whole((ROWS, LOCAL)), ANYWHERE] + weight.specs(),
        out_specs=columns(ROWS, SHARD),
        scratch_shapes=weight.scratch(),
        compiler_params=params(),
        cost_estimate=pl.CostEstimate(
            flops=2 * ROWS * WIDTH * LOCAL, bytes_accessed=7_000_000, transcendentals=0
        ),
        name="gate_in_back",
    )(info, dz, token, *weight.arrays)


def patch_body(dmx, dmbc, tailx, tailbc, edge, token, dxc_ref):
    dxc_ref[:, :LOCAL] = dmx[...]
    dxc_ref[:, LOCAL:] = dmbc[...]
    late = edge[...].astype(F32)
    dxc_ref[ROWS - 16 :, :LOCAL] = (tailx[...] + late[:, :LOCAL]).astype(BF16)
    dxc_ref[ROWS - 16 :, LOCAL:MIXED] = (tailbc[...] + late[:, LOCAL:]).astype(BF16)


def patch(dmx, dmbc, tailx, tailbc, edge, token):
    arrays = (dmx, dmbc, tailx, tailbc, edge)
    return pl.pallas_call(
        patch_body,
        out_shape=shape((ROWS, PACKED), BF16),
        in_specs=[whole(v.shape) for v in arrays] + [ANYWHERE],
        out_specs=whole((ROWS, PACKED)),
        compiler_params=params(),
        cost_estimate=pl.CostEstimate(flops=100_000, bytes_accessed=2_000_000, transcendentals=0),
        name="patch",
    )(*arrays, token)


def mixed_back_body(weight, tokens, info, dxc, part, h_ref, normed, *rest):
    refs = len(weight.arrays)
    w_refs, rest = rest[:refs], rest[refs + tokens :]
    (out_ref, dgain_ref, *grad_ref), (buffer, sems, scale_ref) = rest[:-3], rest[-3:]
    b = pl.program_id(0)
    block = pl.ds(pl.multiple_of(b * SHARD, SHARD), SHARD)

    @pl.when(b == 0)
    def _():
        weight.start(w_refs, info, buffer, sems)
        h = h_ref[...].astype(F32)
        scale = lax.rsqrt(jnp.mean(h * h, axis=1, keepdims=True) + EPSILON)
        scale_ref[...] = jnp.broadcast_to(scale, (ROWS, LANES))

    for ref in grad_ref:
        ref[...] = dot(normed[...].T, dxc[...]).astype(BF16)

    @pl.when(b == 0)
    def _():
        for n in range(4):
            weight.wait(w_refs, info, n, buffer, sems)

    d_norm = part[...] + dot_nt(dxc[...], buffer[block, :])
    out_ref[...] = d_norm
    total = jnp.sum(d_norm * h_ref[:, block].astype(F32) * scale_ref[:, :1], axis=0, keepdims=True)
    dgain_ref[...] = jnp.broadcast_to(total, (8, SHARD))


def mixed_back(info, dxc, part, h, normed, weight, with_grad, tokens):
    wide, local = whole((ROWS, WIDTH)), columns(ROWS, SHARD)
    outs = [shape((ROWS, WIDTH)), shape((8, WIDTH))]
    specs = [local, columns(8, SHARD)]
    if with_grad:
        outs.append(shape((WIDTH, PACKED), BF16))
        specs.append(pl.BlockSpec((SHARD, PACKED), lambda b: (b, 0)))
    return pl.pallas_call(
        functools.partial(mixed_back_body, weight, len(tokens)),
        grid=(4,),
        out_shape=outs,
        in_specs=[SMEM, whole((ROWS, PACKED)), local, wide, local]
        + weight.specs()
        + [ANYWHERE] * len(tokens),
        out_specs=specs,
        scratch_shapes=weight.scratch() + [pltpu.VMEM((ROWS, LANES), F32)],
        compiler_params=params(),
        cost_estimate=pl.CostEstimate(
            flops=4 * ROWS * WIDTH * PACKED, bytes_accessed=14_000_000, transcendentals=0
        ),
        name="mixed_back",
    )(info, dxc, part, h, normed, *weight.arrays, *tokens)


def norm_back_body(own, came, h_ref, cot, gain, dh_ref, low_ref):
    h = h_ref[...].astype(F32)
    scale = lax.rsqrt(jnp.mean(h * h, axis=1, keepdims=True) + EPSILON)
    d_norm = own[...] + came[...]
    inner = jnp.mean(d_norm * gain[...] * h, axis=1, keepdims=True) * scale * scale * scale
    dh = cot[...].astype(F32) + scale * d_norm * gain[...] - h * inner
    dh_ref[...] = dh
    low_ref[...] = dh.astype(BF16)


def norm_back(own, came, h, cot, gain):
    rows = pl.BlockSpec((HALF // 2, WIDTH), lambda i: (i, 0))
    return pl.pallas_call(
        norm_back_body,
        grid=(4,),
        out_shape=(shape((ROWS, WIDTH)), shape((ROWS, WIDTH), BF16)),
        in_specs=[rows] * 4 + [whole((1, WIDTH))],
        out_specs=(rows, rows),
        compiler_params=params(),
        cost_estimate=pl.CostEstimate(flops=3_000_000, bytes_accessed=8_000_000, transcendentals=0),
        name="norm_back",
    )(own, came, h, cot, gain)


def z_shift(r):
    return "dp", [(z, (z + r) % 4) for z in range(4)]


def y_shift(r):
    return "ctx", [(j, (j + 4 * r) % 16) for j in range(16)]


def x_shift(r):
    return "ctx", [(j, j - j % 4 + (j + r) % 4) for j in range(16)]


SHIFTS = {"z": z_shift, "y": y_shift, "x": x_shift}


def send(value, axis, r):
    name, pairs = SHIFTS[axis](r % 4)
    return lax.ppermute(value, name, pairs)


def swapped(value):
    return lax.ppermute(value, "section", [(0, 1), (1, 0)])


def nothing_body(*refs):
    refs[-1][...] = jnp.zeros((8, LANES), jnp.int32)


def after(values, place):
    nothing = pl.pallas_call(
        nothing_body,
        out_shape=shape((8, LANES), jnp.int32),
        in_specs=[ANYWHERE] * len(values),
        out_specs=whole((8, LANES)),
        compiler_params=params(),
        cost_estimate=pl.CostEstimate(flops=0, bytes_accessed=4096, transcendentals=0),
        name="after",
    )(*values)[0, 0]
    return {axis: n + nothing for axis, n in place.items()}


def fetched(mine, came, layer, section, place):
    rows = SHARD // 2

    def piece(source, side, axis):
        return lax.dynamic_slice_in_dim(source, side * rows + place[axis] * PIECE, PIECE, 0)

    parts = [
        jnp.where(section == layer, piece(mine, side, axis), piece(came, side, axis))
        for side, axis in enumerate("xy")
    ]
    if mine.shape[0] == TALL:
        parts.append(jnp.where(section == layer, mine[SHARD:], came[SHARD:]))
    return jnp.concatenate(parts)


def pieces(mine, came, got, late):
    out = [mine, came]
    for side, axis in enumerate("xy"):
        rows = slice(side * PIECE, (side + 1) * PIECE)
        stack = jnp.concatenate(
            [lax.dynamic_slice_in_dim(g, rows.start + late, PIECE, 0) for g in got[1:]]
        )
        out += [stack] + [send(stack, axis, -r) for r in range(1, 4)]
    return out


def summed(terms):
    a, b, c, d = (t.astype(F32) for t in terms)
    return (a + c) + (b + d)


def arrived(terms, axis):
    return [terms[0]] + [send(terms[r], axis, r) for r in range(1, 4)]


def terms_body(axis, cuts, stacked, info, *rest):
    factors, rest = rest[: 2 * len(cuts)], rest[2 * len(cuts) :]
    small, outs, total = rest[:-2] if stacked else rest[:-5], rest[-5:-1], rest[-1]
    column = 0
    for n, cols in enumerate(cuts):
        there = slice(column, column + cols.stop - cols.start)
        total[:, there] = dot(factors[2 * n][...], factors[2 * n + 1][:, cols])
        column = there.stop
    count = 96 if axis == "y" else 24
    starts = [z * SHARD for z in range(4)]
    if axis == "x":
        starts = [start + y * 96 for start in starts for y in range(4)]
    for r in range(4):
        first = r * count
        if not stacked:
            first = lax.rem(info[11 if axis == "y" else 12] + r, 4) * count
        parts = [total[pl.ds(pl.multiple_of(start + first, 8), count), :] for start in starts]
        out = rest[-2].at[r] if stacked else outs[r]
        out[:SHARD, :] = jnp.concatenate(parts, axis=0).astype(BF16)
        for ref in small:
            out[SHARD:, :] = ref[...]


def four(dims, stacked):
    if stacked:
        return shape((4, *dims), BF16), whole((4, *dims))
    return [shape(dims, BF16)] * 4, [whole(dims)] * 4


def terms(info, axis, products, small=(), stacked=False):
    cuts = [cols for _, _, cols in products]
    width = sum(cols.stop - cols.start for cols in cuts)
    rows = SHARD + sum(v.shape[0] for v in small)
    arrays = [v for left, right, _ in products for v in (left, right)] + list(small)
    outs, specs = four((rows, width), stacked)
    return pl.pallas_call(
        functools.partial(terms_body, axis, cuts, stacked),
        out_shape=outs,
        in_specs=[SMEM] + [whole(v.shape) for v in arrays],
        out_specs=specs,
        scratch_shapes=[pltpu.VMEM((4 * SHARD, width), F32)],
        compiler_params=params(),
        cost_estimate=pl.CostEstimate(
            flops=8 * SHARD * ROWS * width, bytes_accessed=8_000_000, transcendentals=0
        ),
        name="terms",
    )(info, *arrays)


def fold_body(slot, counts, outer, inner, rest_rows, stacked, info, *rest):
    refs, outs, total = rest[: sum(counts)], rest[sum(counts) + 1 : -1], rest[-1]
    column = 0
    for count in counts:
        arrays, refs = refs[:count], refs[count:]
        cols = slice(column, column + arrays[0].shape[-1])
        if count == 4:
            total[:, cols] = summed([a[...] for a in arrays])
        elif len(arrays[0].shape) == 3:
            total[:, cols] = summed([arrays[0][n] for n in range(4)])
        else:
            total[:, cols] = arrays[0][...].astype(F32)
        column = cols.stop
    for r in range(4):
        first = r * inner if stacked else lax.rem(info[slot] + r, 4) * inner
        parts = [
            total[pl.ds(pl.multiple_of(n * 4 * inner + first, 8), inner), :] for n in range(outer)
        ]
        if rest_rows:
            parts.append(total[4 * outer * inner :, :])
        out = outs[0].at[r] if stacked else outs[r]
        out[...] = jnp.concatenate(parts, axis=0).astype(BF16)


def fold(info, axis, groups, outer, inner, token, stacked=False):
    slot = 10 + "zyx".index(axis)
    arrays = [a for group in groups for a in group]
    rows, width = arrays[0].shape[-2], sum(group[0].shape[-1] for group in groups)
    more = rows - 4 * outer * inner
    outs, specs = four((outer * inner + more, width), stacked)
    counts = [len(group) for group in groups]
    return pl.pallas_call(
        functools.partial(fold_body, slot, counts, outer, inner, more, stacked),
        out_shape=outs,
        in_specs=[SMEM] + [whole(a.shape) for a in arrays] + [ANYWHERE],
        out_specs=specs,
        scratch_shapes=[pltpu.VMEM((rows, width), F32)],
        compiler_params=params(),
        cost_estimate=pl.CostEstimate(flops=2_000_000, bytes_accessed=8_000_000, transcendentals=0),
        name="fold",
    )(info, *arrays, token)


def last_fold_body(info, *rest):
    left, right, outs, total = rest[:4], rest[4:8], rest[9:13], rest[13]
    width = left[0].shape[1]
    total[:96, :width] = summed([a[...] for a in left])
    total[96:, :width] = jnp.zeros((SMALL, width), F32)
    total[:, width:] = summed([a[...] for a in right])
    for r in range(4):
        first = pl.multiple_of(lax.rem(info[10] + r, 4) * 24, 8)
        parts = [total[pl.ds(first, 24), :], total[96:, :]]
        outs[r][...] = jnp.concatenate(parts, axis=0).astype(BF16)


def last_fold(info, left, right, token):
    width = left[0].shape[1] + right[0].shape[1]
    out = shape((24 + SMALL, width), BF16)
    arrays = (*left, *right)
    return pl.pallas_call(
        last_fold_body,
        out_shape=[out] * 4,
        in_specs=[SMEM] + [whole(a.shape) for a in arrays] + [ANYWHERE],
        out_specs=[whole(out.shape)] * 4,
        scratch_shapes=[pltpu.VMEM((96 + SMALL, width), F32)],
        compiler_params=params(),
        cost_estimate=pl.CostEstimate(flops=500_000, bytes_accessed=2_000_000, transcendentals=0),
        name="last_fold",
    )(info, *arrays, token)


PARITY = [[j for j in range(16) if j % 2 == e] for e in range(2)]
NEIGHBOURS = [(j, j ^ 1) for j in range(16)]
GROUPS_OF = {
    "y": [[4 * y + x for y in range(4)] for x in range(4)],
    "x": [[4 * y + x for x in range(4)] for y in range(4)],
}


def traded(value, axis):
    return lax.all_to_all(value, "ctx", 0, 0, axis_index_groups=GROUPS_OF[axis])


def exchange(value):
    return lax.all_to_all(value, "ctx", 0, 0, axis_index_groups=PARITY)


def halo_shift(value, step):
    pairs = [(j, j + 2 * step) for j in range(16) if 0 <= j + 2 * step < 16]
    return lax.ppermute(value, "ctx", pairs)


def halves(values, section):
    grid = values.reshape(values.shape[0], GROUPS, 2, -1)
    size = values.shape[1] // 2
    return [
        lax.dynamic_index_in_dim(grid, i, 2, False).reshape(-1, size)
        for i in (section, 1 - section)
    ]


def turns(low, high):
    rows = low.shape[0]
    parts = [v.reshape(rows, GROUPS, 1, -1) for v in (low, high)]
    return jnp.concatenate(parts, axis=2).reshape(rows, -1)


def pick_x_body(info, x_ref, dt_ref, *rest):
    smalls, outs, small = rest[:7], rest[7:9], rest[9]
    small[...] = jnp.zeros((16, PACKED), F32)
    row = 0
    for ref in smalls[:4]:
        count, width = ref.shape
        small[row : row + count, :width] = ref[...].astype(F32)
        row += count
    for ref in smalls[4:]:
        left = ref[...]
        for _ in range(3):
            part = left.astype(BF16).astype(F32)
            small[row : row + 1, :HEADS] = part
            left = left - part
            row += 1
    head, lane = row_of((HEADS, LANES)), lane_of((HEADS, LANES))
    for out, side in zip(outs, (info[0], 1 - info[0]), strict=True):
        for d in range(GROUPS):
            cols = pl.ds(pl.multiple_of((2 * d + side) * BLOCK, LANES), BLOCK)
            out[:SHARD, d * BLOCK : (d + 1) * BLOCK] = x_ref[:, cols]
        out[:SHARD, LOCAL:MIXED] = x_ref[:, INNER:]
        here = (head // OWN == 2 * (lane // 8) + side) & (head % OWN == lane % 8)
        out[:SHARD, MIXED:] = dot(dt_ref[...], here.astype(BF16)).astype(BF16)
        out[SHARD:, :] = small[...].astype(BF16)


def pick_x(section, x, dt, smalls):
    return pl.pallas_call(
        pick_x_body,
        out_shape=[shape((TALL, PACKED), BF16)] * 2,
        in_specs=[SMEM, whole((SHARD, CONV_CH)), whole((SHARD, HEADS))]
        + [whole(v.shape) for v in smalls],
        out_specs=[whole((TALL, PACKED))] * 2,
        scratch_shapes=[pltpu.VMEM((16, PACKED), F32)],
        compiler_params=params(),
        cost_estimate=pl.CostEstimate(flops=0, bytes_accessed=6_000_000, transcendentals=0),
        name="pick_x",
    )(section, x, dt, *smalls)


def unpack_body(count, info, *rest):
    refs, (cpar, gain_one, gain_two, hpar, held, full, sems) = rest[:count], rest[count:]
    copies = []
    for n in range(4):
        if count == 4:
            source, to = refs[n].at[pl.ds(2 * PIECE, 16)], lax.rem(info[10] + n, 4)
        else:
            source, to = refs[0].at[pl.ds(n * TALL + SHARD, 16)], n
        copies.append(pltpu.make_async_copy(source, held.at[to], sems.at[n]))
    for c in copies:
        c.start()
    for c in copies:
        c.wait()
    section = info[13]
    half_cols = pl.ds(pl.multiple_of(section * BLOCK, LANES), BLOCK)
    for z in range(4):
        values = held[z].astype(F32)
        full[:, z * 832 : (z + 1) * 832] = values[:8, :832]
        gain_one[:, z * SHARD : (z + 1) * SHARD] = values[5:6, :SHARD]
        gain_two[:, z * BLOCK : (z + 1) * BLOCK] = held[z, :, half_cols].astype(F32)[6:7]
    for d in range(GROUPS):
        cols = pl.ds(pl.multiple_of((2 * d + section) * BLOCK, LANES), BLOCK)
        cpar[:, d * BLOCK : (d + 1) * BLOCK] = full[:, cols]
    cpar[:, LOCAL:] = full[:, INNER:]
    values = held[0, :, :LANES].astype(F32)
    heads = [values[n : n + 1] + values[n + 1 : n + 2] + values[n + 2 : n + 3] for n in (7, 10, 13)]
    heads = jnp.concatenate(heads + [jnp.zeros((5, LANES), F32)], axis=0)
    head, lane = row_of((LANES, LANES)), lane_of((LANES, LANES))
    here = (head // OWN == 2 * (lane // 8) + section) & (head % OWN == lane % 8)
    hpar[...] = exact_dot(heads, here.astype(F32))


def unpack(info, arrays):
    shapes = ((8, MIXED), (1, WIDTH), (1, LOCAL), (8, LANES))
    return pl.pallas_call(
        functools.partial(unpack_body, len(arrays)),
        out_shape=[shape(dims) for dims in shapes],
        in_specs=[SMEM] + [ANYWHERE] * len(arrays),
        out_specs=[whole(dims) for dims in shapes],
        scratch_shapes=[
            pltpu.VMEM((4, 16, PACKED), BF16),
            pltpu.VMEM((8, CONV_CH), F32),
            pltpu.SemaphoreType.DMA((4,)),
        ],
        compiler_params=params(),
        cost_estimate=pl.CostEstimate(flops=0, bytes_accessed=400_000, transcendentals=0),
        name="unpack",
    )(info, *arrays)


def pick_zo_body(info, z_ref, o_ref, token, *outs):
    for out, side in zip(outs, (info[0], 1 - info[0]), strict=True):
        for d in range(GROUPS):
            cols = pl.ds(pl.multiple_of((2 * d + side) * BLOCK, LANES), BLOCK)
            out[:, d * BLOCK : (d + 1) * BLOCK] = z_ref[:, cols]
        rows = pl.ds(pl.multiple_of(side * SHARD, SHARD), SHARD)
        out[:, LOCAL:] = o_ref[rows, :]


def pick_zo(section, z, o, token):
    return pl.pallas_call(
        pick_zo_body,
        out_shape=[shape((SHARD, LOCAL + WIDTH), BF16)] * 2,
        in_specs=[SMEM, whole((SHARD, INNER)), whole((2 * SHARD, WIDTH)), ANYWHERE],
        out_specs=[whole((SHARD, LOCAL + WIDTH))] * 2,
        compiler_params=params(),
        cost_estimate=pl.CostEstimate(flops=0, bytes_accessed=9_000_000, transcendentals=0),
        name="pick_zo",
    )(section, z, o, token)


def head_lanes(values):
    rows = values.shape[0]
    grid = jnp.pad(values.reshape(rows, GROUPS, OWN), ((0, 0), (0, 0), (0, 8 - OWN)))
    return jnp.pad(grid.reshape(rows, 8 * GROUPS), ((0, 0), (0, LANES - 8 * GROUPS)))


def lanes_heads(values):
    rows = values.shape[0]
    return values[:, : 8 * GROUPS].reshape(rows, GROUPS, 8)[:, :, :OWN].reshape(rows, -1)


def on_device(
    boundary,
    lengths,
    norm_gain,
    w_z,
    w_xbc,
    w_dt,
    conv_weight,
    conv_bias,
    dt_bias,
    a_log,
    d_skip,
    gate_gain,
    w_out,
):
    section = lax.axis_index("section")
    group = lax.axis_index("dp")
    ctx = lax.axis_index("ctx")
    place = {"z": group, "y": ctx // 4, "x": ctx % 4}
    micro = ctx % 2
    chunk = ctx // 2

    def ordered(mine, came):
        return jnp.where(section == 0, mine, came), jnp.where(section == 0, came, mine)

    own_rows = lax.dynamic_index_in_dim(boundary[0], micro, 0, False)
    other_rows = lax.dynamic_index_in_dim(boundary[0], 1 - micro, 0, False)
    came = lax.ppermute(other_rows, "ctx", NEIGHBOURS)
    block = jnp.where(
        micro == 0, jnp.concatenate([own_rows, came]), jnp.concatenate([came, own_rows])
    )
    hidden, cotangent = ordered(block, swapped(block))

    pair = lengths[group, micro]
    padded = (pair[0] + SPAN - 1) // SPAN * SPAN
    offset = chunk * ROWS
    begin = jnp.where(offset >= padded, padded, 0)
    length = jnp.where(offset >= padded, pair[1], pair[0])
    live = jnp.clip(length - (offset - begin), 0, ROWS)
    offsets = jnp.arange(CHUNKS, dtype=jnp.int32) * ROWS
    keeps = ((offsets != 0) & (offsets != padded)).astype(jnp.int32)
    keep = (offset != 0) & (offset != padded)
    at = [place["z"], place["y"], place["x"], section]
    info = jnp.concatenate(
        [jnp.stack([live, keep]).astype(jnp.int32), keeps, jnp.stack(at).astype(jnp.int32)]
    )

    def forward(h, layer):
        cpar, hpar = cpars[layer], hpars[layer]
        normed, mixed, rate = in_proj(
            info, h, gains_one[layer], weights_x[layer], []
        )
        halo = halo_shift(mixed[ROWS - 16 :], 1)
        gate = gate_proj(info, normed, weights_z[layer], [] if layer else ready)
        xa, bca, cum, dt, s0, msg = state_call(info, mixed, halo, cpar, rate, hpar)
        came = exchange(msg)
        y_in = inside_call(xa, bca, cum, dt, hpar)
        hin = exchange(scan_call(info, came, False, y_in)).reshape(GROUPS, STATE, BLOCK)
        y, part = out_proj(
            info, y_in, bca, cum, hin, s0, gate, gains_two[layer], weights_o[layer]
        )
        result, branch, scale = join(info, h, part, swapped(part), F32 if layer else BF16)
        saved = (h, normed, mixed, halo, rate, gate, xa, bca, cum, dt, s0, msg, hin, y, branch, scale)
        return result, saved

    def backward(cot, saved, layer, higher, tokens):
        h, normed, mixed, halo, rate, gate, xa, bca, cum, dt, s0, msg, hin, y, branch, scale = saved
        cpar, hpar = cpars[layer], hpars[layer]

        def first_stage(value):
            return lax.psum_scatter(value, "dp", tiled=True)

        bg, dy, dz, grad_o, d_gain_two = gate_back(
            info, cot, y, gate, gains_two[layer], branch, scale, weights_o[layer], layer == 1
        )
        own1, msg_back, grad_z = own_grad(dy, bca, cum, msg, dz, normed)
        sums = [first_stage(grad_z)] + ([first_stage(grad_o)] if layer else [])
        came = exchange(msg_back)
        dxi, d_skips, gsum, u, dbc = inside_back(dy, xa, bca, cum, dt, hpar)
        part = gate_in_back(info, dz, weights_z[layer], msg_back)
        lam = exchange(scan_call(info, came, True, part, *tokens)).reshape(GROUPS, STATE, BLOCK)
        dmx, dmbc, tailx, tailbc, edgex, edgebc, d_parx, d_parbc, d_heads = finish_call(
            info, xa, dxi, dy, mixed, halo, cpar, bca, cum, dt, rate, hpar, lam, hin, s0, own1, u, gsum, dbc
        )
        edge = halo_shift(jnp.concatenate([edgex, edgebc], axis=1), -1)
        dxc = patch(dmx, dmbc, tailx, tailbc, edge, d_heads)
        middle = 7 * LANES
        if layer == 0:
            higher_rows, higher = higher
            normed_t = normed.T
            cuts = [(normed_t, dxc, slice(0, middle)), (grad_o, bg, slice(0, WIDTH // 2))]
            left = terms(info, "y", cuts, (), True)
            part, d_gain_one = mixed_back(
                info, dxc, part, h, normed, weights_x[layer], False, [left, *higher]
            )
        else:
            part, d_gain_one, grad_x = mixed_back(
                info, dxc, part, h, normed, weights_x[layer], True, []
            )
        dh, dh_low = norm_back(part, swapped(part), h, cot, gains_one[layer])
        d_skip_row = jnp.sum(d_skips[0:1].reshape(1, 4 * OWN, HEADDIM), axis=2)
        rows = jnp.where(jnp.arange(8)[:, None] == 5, d_gain_two, d_parx)
        rows = jnp.concatenate([rows, d_parbc], axis=1)
        more = jnp.concatenate(
            [
                d_gain_one[:1],
                jnp.pad(d_heads[:2], ((0, 0), (0, WIDTH - LANES))),
                jnp.pad(head_lanes(d_skip_row), ((0, 4), (0, WIDTH - LANES))),
            ]
        )
        rows = jnp.concatenate([rows, jnp.pad(more, ((0, 0), (0, 2 * STATE)))])
        if layer == 1:
            return dh, dh_low, sums + [first_stage(grad_x)], rows

        rows = jnp.concatenate([rows, higher_rows]).astype(BF16)
        cuts = [(normed_t, dxc, slice(middle, PACKED)), (grad_o, bg, slice(WIDTH // 2, WIDTH))]
        right = arrived(terms(info, "x", cuts, (rows,)), "x")
        tall = fold(info, "y", [[v] for v in higher + sums], 1, 96, dh_low, True)
        left = fold(info, "x", [[traded(left, "y")]], 4, 24, tall)
        right = fold(info, "y", [right], 4, 24, dh_low)
        tall = fold(info, "x", [[traded(tall, "y")]], 1, 24, right[0])
        left, right = arrived(left, "x"), arrived(right, "y")
        final = summed(arrived(last_fold(info, left, right, tall[0]), "z"))
        left, right = left[0].shape[1], right[0].shape[1]
        rows = final[24:, left:]
        final = final[:24]
        sum_x = jnp.concatenate(
            [final[:, :middle], final[:, left : left + PACKED - middle]], axis=1
        )
        sum_o = jnp.concatenate([final[:, middle:left], final[:, left + PACKED - middle :]], axis=1)
        return dh, [arrived(tall, "x"), sum_o], sum_x, rows

    at = section.reshape(1).astype(jnp.int32)
    smalls = (conv_weight[0], conv_bias, norm_gain, gate_gain, dt_bias, a_log, d_skip)
    mine_x, other_x = pick_x(at, w_xbc[0], w_dt[0], smalls)
    came_x = swapped(other_x)
    mine_zo, other_zo = pick_zo(at, w_z[0], w_out[0], mine_x)
    came_zo = swapped(other_zo)
    first = fetched(mine_x, came_x, 0, section, after([hidden], place))
    got = [first] + [send(first, "z", -r) for r in range(1, 4)]
    small_low = got
    low_x = pieces(mine_x, came_x, got, 0)
    got = lax.all_gather(fetched(mine_zo, came_zo, 0, section, after(got[1:], place)), "dp")
    late = after(low_x[3:6] + low_x[7:10], place)["z"]
    got = [None] + [lax.dynamic_index_in_dim(got, (late + r) % 4, 0, False) for r in range(1, 4)]
    low_zo = pieces(mine_zo, came_zo, got, 0)
    high_x = [lax.all_gather(jnp.where(section == 1, mine_x, came_x), "dp", tiled=True)]
    high_zo = [lax.all_gather(jnp.where(section == 1, mine_zo, came_zo), "dp", tiled=True)]
    ready = low_zo[3:6] + low_zo[7:10]
    weights_x = [Weight(v, n, PACKED) for n, v in enumerate((low_x, high_x))]
    weights_z = [Weight(v, n, LOCAL) for n, v in enumerate((low_zo, high_zo))]
    weights_o = [Weight(v, n, WIDTH, LOCAL) for n, v in enumerate((low_zo, high_zo))]

    unpacked = [unpack(info, v) for v in (small_low, high_x)]
    cpars, gains_one, gains_two, hpars = zip(*unpacked, strict=True)

    def returned(rows, layer):
        pairs = [(layer * 16 + a, layer * 16 + b) for a, b in NEIGHBOURS]
        other, mine = (
            lax.dynamic_slice_in_dim(rows, n * HALF, HALF, 0) for n in (1 - micro, micro)
        )
        other = lax.ppermute(other, ("section", "ctx"), pairs)
        return jnp.where(micro == 0, jnp.stack([mine, other]), jnp.stack([other, mine]))

    middle, saved_low = forward(hidden, 0)
    out_high, saved_high = forward(middle, 1)
    top_high = returned(out_high, 1)
    _, back, higher, rows = backward(cotangent, saved_high, 1, None, [top_high])
    dh_low, (tall, low_o), low_x, rows = backward(back, saved_low, 0, (rows, higher), [])
    at = (LOCAL, LOCAL + WIDTH, LOCAL + WIDTH + PACKED)
    high_z, high_o, high_x, low_z = jnp.split(summed(tall), at, axis=1)

    own, given = ordered(rows[:16], rows[16:])
    rows_0, rows_1 = ordered(own, swapped(given))
    wide = jnp.concatenate(
        [turns(rows_0[:8, :LOCAL], rows_1[:8, :LOCAL]), rows_0[:8, LOCAL:] + rows_1[:8, LOCAL:]],
        axis=1,
    )
    head_rows = turns(lanes_heads(rows_0[9:12, :LANES]), lanes_heads(rows_1[9:12, :LANES]))
    index = group * 16 + ctx
    d_conv = lax.dynamic_slice(wide, (0, index * 52), (5, 52))
    d_gain_two = lax.dynamic_slice(wide, (5, index * 48), (1, 48))
    d_gain_one = lax.dynamic_slice(rows_0[8:9] + rows_1[8:9], (0, index * 24), (1, 24))

    own, given = ordered(
        jnp.concatenate([low_z, low_x], axis=1), jnp.concatenate([high_z, high_x], axis=1)
    )
    first, second = ordered(own, swapped(given))
    sum_z = turns(first[:, :LOCAL], second[:, :LOCAL])
    at_x, at_bc, at_dt = LOCAL, LOCAL + LOCAL, LOCAL + MIXED
    sum_x = turns(first[:, at_x:at_bc], second[:, at_x:at_bc])
    sum_bc = first[:, at_bc:at_dt] + second[:, at_bc:at_dt]
    sum_dt = turns(lanes_heads(first[:, at_dt:]), lanes_heads(second[:, at_dt:]))

    trips = []
    for flip in range(2):
        pairs = [
            (c * 16 + j, (flip ^ (j % 2)) * 16 + 8 * c + j // 2) for c in range(2) for j in range(16)
        ]
        value = jnp.where(micro == flip, low_o, high_o)
        trips.append(lax.ppermute(value, ("section", "ctx"), pairs))
    sum_o = jnp.concatenate(ordered(*trips))

    top = jnp.where(section == 0, returned(dh_low, 0), top_high)
    return (
        top[None],
        d_gain_one,
        sum_z[None],
        jnp.concatenate([sum_x, sum_bc], axis=1)[None],
        sum_dt[None],
        d_conv[None, :4],
        d_conv[4:5],
        head_rows[0:1],
        head_rows[1:2],
        head_rows[2:3],
        d_gain_two,
        sum_o[None],
    )


def solution(mesh):
    in_specs = (
        P("section", None, ("dp", "ctx"), None),
        P(),
        P("section", "dp"),
        P("section", "dp", None),
        P("section", "dp", None),
        P("section", "dp", None),
        P("section", None, "dp"),
        P("section", "dp"),
        P("section", None),
        P("section", None),
        P("section", None),
        P("section", "dp"),
        P("section", "dp", None),
    )
    out_specs = (
        P("section", None, ("dp", "ctx"), None),
        P("section", ("dp", "ctx")),
        P("section", ("dp", "ctx"), None),
        P("section", ("dp", "ctx"), None),
        P("section", ("dp", "ctx"), None),
        P("section", None, ("dp", "ctx")),
        P("section", ("dp", "ctx")),
        P("section", None),
        P("section", None),
        P("section", None),
        P("section", ("dp", "ctx")),
        P("section", ("dp", "ctx"), None),
    )
    return jax.shard_map(
        on_device, mesh=mesh, in_specs=in_specs, out_specs=out_specs, check_vma=False
    )
```

```python
import functools

import jax
import jax.numpy as jnp
from jax import lax
from jax.experimental import pallas as pl
from jax.experimental.pallas import tpu as pltpu
from jax.sharding import PartitionSpec as P

HEADS = 48
HEADDIM = 64
STATE = 128
KERNEL = 4
SPAN = 256
MICRO = 2
WIDTH = 1536
INNER = 3072
CONV_CH = 3328
LANES = 128
CHUNKS = 8
GROUPS = 4
OWN = 6
BLOCK = OWN * HEADDIM
LOCAL = GROUPS * BLOCK
MIXED = LOCAL + 2 * STATE
PACKED = MIXED + LANES
ROWS = 256
HALF = 128
SHARD = 384
TALL = SHARD + 16
PIECE = 48
STATE_HALF = STATE // 2
MESSAGE = STATE_HALF + 16
SMALL = 32
EPSILON = 1e-05
PRECISE = lax.Precision.HIGHEST
F32 = jnp.float32
BF16 = jnp.bfloat16
VMEM_LIMIT = 56 * 1024 * 1024


def params(**more):
    return pltpu.CompilerParams(vmem_limit_bytes=VMEM_LIMIT, **more)


def whole(shape):
    return pl.BlockSpec(shape, lambda *_: (0,) * len(shape))


def columns(rows, width):
    return pl.BlockSpec((rows, width), lambda g: (0, g))


def grouped(rows):
    return pl.BlockSpec((1, rows, BLOCK), lambda g: (g, 0, 0))


MESSAGES = pl.BlockSpec((2, MESSAGE, BLOCK), lambda g: (g, 0, 0))
SMEM = pl.BlockSpec(memory_space=pltpu.SMEM)
ANYWHERE = pl.BlockSpec(memory_space=pl.ANY)


def shape(dims, kind=F32):
    return jax.ShapeDtypeStruct(dims, kind)


def dot(a, b):
    return jnp.dot(a, b, preferred_element_type=F32)


def dot_nt(a, b):
    return lax.dot_general(a, b, (((1,), (1,)), ((), ())), preferred_element_type=F32)


def exact_dot(a, b):
    return jnp.dot(a, b, precision=PRECISE, preferred_element_type=F32)


def lane_of(dims):
    return lax.broadcasted_iota(jnp.int32, dims, len(dims) - 1)


def row_of(dims):
    return lax.broadcasted_iota(jnp.int32, dims, len(dims) - 2)


def sigmoid(v):
    return 1.0 / (1.0 + jnp.exp(-v))


def softplus(v):
    return jnp.maximum(v, 0.0) + jnp.log1p(jnp.exp(-jnp.abs(v)))


def rolled(values, g):
    return pltpu.roll(values, lax.rem(LANES - 8 * g, LANES), axis=1)


def pair_lanes(values, p):
    low = lane_of((values.shape[0], LANES)) < HEADDIM
    return jnp.where(low, values[:, 2 * p : 2 * p + 1], values[:, 2 * p + 1 : 2 * p + 2])


def spread(values):
    return jnp.concatenate([pair_lanes(values, p) for p in range(OWN // 2)], axis=1)


def head_sum_matrix(g):
    head = row_of((BLOCK, LANES)) // HEADDIM
    return (lane_of((BLOCK, LANES)) == head + 8 * g).astype(BF16)


def lower_triangle(strict=False):
    i, j = row_of((HALF, HALF)), lane_of((HALF, HALF))
    return ((i > j) if strict else (i >= j)).astype(F32)


def usable_rows(info):
    return (row_of((ROWS, 1)) < info[0]).astype(F32)


def half(values, q):
    return values[q * HALF : (q + 1) * HALF]


class Weight:
    def __init__(self, arrays, layer, width, first=0):
        self.arrays = arrays
        self.stride = arrays[0].shape[0] // 4
        self.layer = layer
        self.width = width
        self.columns = pl.ds(first, width)

    def block(self, info, b):
        return lax.rem(info[10] + b, 4) * SHARD

    def parts(self, refs, info, b):
        start = self.block(info, b)
        if len(refs) == 1:
            there = pl.multiple_of(start // SHARD * self.stride, 16)
            return [(refs[0].at[pl.ds(there, SHARD)], start, SHARD)]
        out = []
        for side in range(2):
            mine = info[12 - side]
            for step in range(4):
                source = refs[2 + 4 * side + step].at[pl.ds((b - 1) * PIECE, PIECE)]
                row = start + side * (SHARD // 2) + lax.rem(mine + step, 4) * PIECE
                out.append((source, row, PIECE))
        return out

    def copies(self, refs, info, b, buffer, sems):
        return [
            pltpu.make_async_copy(
                source.at[:, self.columns],
                buffer.at[pl.ds(pl.multiple_of(row, 16), count)],
                sems.at[b, n],
            )
            for n, (source, row, count) in enumerate(self.parts(refs, info, b))
        ]

    def own_copy(self, source, info, buffer, sems):
        rows = pl.ds(pl.multiple_of(self.block(info, 0), SHARD), SHARD)
        source = source.at[pl.ds(0, SHARD), self.columns]
        return pltpu.make_async_copy(source, buffer.at[rows], sems.at[0, 0])

    def start(self, refs, info, buffer, sems):
        whole_array = len(refs) == 1
        if not whole_array:
            for n in range(2):

                @pl.when((info[13] == self.layer) == (n == 0))
                def _(n=n):
                    self.own_copy(refs[n], info, buffer, sems).start()

        for b in range(0 if whole_array else 1, 4):
            for c in self.copies(refs, info, b, buffer, sems):
                c.start()

    def wait(self, refs, info, b, buffer, sems):
        if b == 0 and len(refs) > 1:
            self.own_copy(refs[0], info, buffer, sems).wait()
        else:
            for c in self.copies(refs, info, b, buffer, sems):
                c.wait()
        return pl.ds(pl.multiple_of(self.block(info, b), SHARD), SHARD)

    def specs(self):
        return [ANYWHERE] * len(self.arrays)

    def scratch(self):
        return [pltpu.VMEM((4 * SHARD, self.width), BF16), pltpu.SemaphoreType.DMA((4, 8))]

    def product(self, refs, info, left, buffer, sems, total):
        for b in range(4):
            self.wait(refs, info, b, buffer, sems)
        step = 512 if self.width % 512 == 0 else 640
        for at in range(0, self.width, step):
            total[:, at : at + step] = dot(left[...], buffer[:, at : at + step])


def in_proj_body(weight, tokens, info, h_ref, gain_ref, *rest):
    refs = len(weight.arrays)
    w_refs, rest = rest[:refs], rest[refs + tokens :]
    (normed_ref, mixed_ref, rate_ref, buffer, sems, total) = rest
    weight.start(w_refs, info, buffer, sems)
    h = h_ref[...].astype(F32)
    scale = lax.rsqrt(jnp.mean(h * h, axis=1, keepdims=True) + EPSILON)
    normed_ref[...] = (h * scale * gain_ref[...]).astype(BF16)
    weight.product(w_refs, info, normed_ref, buffer, sems, total)
    mixed_ref[...] = total[:, :MIXED].astype(BF16)
    rate_ref[...] = total[:, MIXED:]


def in_proj(info, h, gain, weight, tokens):
    return pl.pallas_call(
        functools.partial(in_proj_body, weight, len(tokens)),
        out_shape=(shape((ROWS, WIDTH), BF16), shape((ROWS, MIXED), BF16), shape((ROWS, LANES))),
        in_specs=[SMEM, whole((ROWS, WIDTH)), whole((1, WIDTH))]
        + weight.specs()
        + [ANYWHERE] * len(tokens),
        out_specs=(whole((ROWS, WIDTH)), whole((ROWS, MIXED)), whole((ROWS, LANES))),
        scratch_shapes=weight.scratch() + [pltpu.VMEM((ROWS, PACKED), F32)],
        compiler_params=params(),
        cost_estimate=pl.CostEstimate(
            flops=2 * ROWS * WIDTH * PACKED, bytes_accessed=8_000_000, transcendentals=0
        ),
        name="in_proj",
    )(info, h, gain, *weight.arrays, *tokens)


def gate_proj_body(weight, tokens, info, normed_ref, *rest):
    refs = len(weight.arrays)
    w_refs, (gate_ref, buffer, sems) = rest[:refs], rest[refs + tokens :]
    weight.start(w_refs, info, buffer, sems)
    weight.product(w_refs, info, normed_ref, buffer, sems, gate_ref)


def gate_proj(info, normed, weight, tokens):
    return pl.pallas_call(
        functools.partial(gate_proj_body, weight, len(tokens)),
        out_shape=shape((ROWS, LOCAL)),
        in_specs=[SMEM, whole((ROWS, WIDTH))] + weight.specs() + [ANYWHERE] * len(tokens),
        out_specs=whole((ROWS, LOCAL)),
        scratch_shapes=weight.scratch(),
        compiler_params=params(),
        cost_estimate=pl.CostEstimate(
            flops=2 * ROWS * WIDTH * LOCAL, bytes_accessed=7_000_000, transcendentals=0
        ),
        name="gate_proj",
    )(info, normed, *weight.arrays, *tokens)


def conv_sum_of(values, halo, cpar, keep, ext):
    width = values.shape[1]
    ext[0:16, :width] = halo.astype(F32) * keep
    ext[16 : 16 + ROWS, :width] = values.astype(F32)
    total = cpar[4:5, :]
    for k in range(KERNEL):
        total = total + cpar[k : k + 1, :] * ext[13 + k : 13 + k + ROWS, :width]
    return total


def state_body(
    info, mixed, halo, cpar, bc, halo_bc, cpar_bc, rate, hpar,
    xa_ref, bca_ref, cum_ref, dt_ref, s0_ref, msg_ref, ext, bt, tail,
):
    g = pl.program_id(0)
    keep = info[1].astype(F32)

    @pl.when(g == 0)
    def _():
        total = conv_sum_of(bc[...], halo_bc[...], cpar_bc[...], keep, ext)
        active = total * sigmoid(total)
        bca_ref[...] = active
        bt[...] = active[:, :STATE].T.astype(BF16)
        dt = usable_rows(info) * softplus(rate[...] + hpar[0:1, :])
        log_decay = dt * -jnp.exp(hpar[1:2, :])
        dt_ref[...] = dt
        tri = lower_triangle()
        for q in range(2):
            rows = pl.ds(q * HALF, HALF)
            cum = exact_dot(tri, half(log_decay, q))
            cum_ref[rows, :] = cum
            tail[rows, :] = jnp.exp(cum[HALF - 1 :, :] - cum) * half(dt, q)

    total = conv_sum_of(mixed[...], halo[...], cpar[...], keep, ext)
    xa = total * sigmoid(total)
    xa_ref[...] = xa
    weighted = (xa * spread(rolled(tail[...], g))).astype(BF16)
    ends = rolled(cum_ref[...], g)
    end0, end1 = ends[HALF - 1 : HALF], ends[ROWS - 1 : ROWS]
    s0 = dot(bt[:, :HALF], half(weighted, 0))
    s1 = dot(bt[:, HALF:], half(weighted, 1))
    s0_ref[0] = s0
    state = (spread(jnp.exp(end1)) * s0 + s1).astype(BF16)
    damp = spread(jnp.exp(end0 + end1))
    high = damp.astype(BF16)
    low = (damp - high.astype(F32)).astype(BF16)
    row = row_of((16, BLOCK))
    damps = jnp.where(row == 0, high.astype(F32), low.astype(F32)).astype(BF16)
    for r in range(2):
        msg_ref[r, :STATE_HALF, :] = state[r * STATE_HALF : (r + 1) * STATE_HALF]
        msg_ref[r, STATE_HALF:, :] = damps


def state_call(info, mixed, halo, cpar, rate, hpar):
    bc_at = LOCAL // 256
    return pl.pallas_call(
        state_body,
        grid=(GROUPS,),
        out_shape=(
            shape((ROWS, LOCAL)),
            shape((ROWS, 256)),
            shape((ROWS, LANES)),
            shape((ROWS, LANES)),
            shape((GROUPS, STATE, BLOCK)),
            shape((CHUNKS, MESSAGE, BLOCK), BF16),
        ),
        in_specs=[
            SMEM,
            columns(ROWS, BLOCK),
            columns(16, BLOCK),
            columns(8, BLOCK),
            pl.BlockSpec((ROWS, 256), lambda g: (0, bc_at)),
            pl.BlockSpec((16, 256), lambda g: (0, bc_at)),
            pl.BlockSpec((8, 256), lambda g: (0, bc_at)),
            whole((ROWS, LANES)),
            whole((8, LANES)),
        ],
        out_specs=(
            columns(ROWS, BLOCK),
            whole((ROWS, 256)),
            whole((ROWS, LANES)),
            whole((ROWS, LANES)),
            grouped(STATE),
            MESSAGES,
        ),
        scratch_shapes=[
            pltpu.VMEM((ROWS + 32, BLOCK), F32),
            pltpu.VMEM((STATE, ROWS), BF16),
            pltpu.VMEM((ROWS, LANES), F32),
        ],
        compiler_params=params(),
        cost_estimate=pl.CostEstimate(
            flops=2 * ROWS * STATE * LOCAL, bytes_accessed=4_500_000, transcendentals=400_000
        ),
        name="conv_state",
    )(info, mixed, halo, cpar, mixed, halo, cpar, rate, hpar)


def inside_body(xa, bca, cum, dt, hpar, y_ref, cum_t, scores):
    g = pl.program_id(0)

    @pl.when(g == 0)
    def _():
        tri = lower_triangle()
        for q in range(2):
            b, c = half(bca[:, :STATE], q).astype(BF16), half(bca[:, STATE:], q).astype(BF16)
            scores[q] = dot_nt(c, b) * tri
            cum_t[:, q * HALF : (q + 1) * HALF] = half(cum[...], q).T

    cols = rolled(cum[...], g)
    rows = cum_t[pl.ds(pl.multiple_of(8 * g, 8), 8), :]
    steps = rolled(dt[...], g)
    skips = rolled(hpar[...], g)[2:3, :]
    low = lane_of((HALF, LANES)) < HEADDIM
    for q in range(2):
        for p in range(OWN // 2):
            lanes = slice(p * LANES, (p + 1) * LANES)
            x = xa[q * HALF : (q + 1) * HALF, lanes]
            xdt = x * pair_lanes(half(steps, q), p)
            both = jnp.concatenate([jnp.where(low, xdt, 0.0), jnp.where(low, 0.0, xdt)], axis=0)
            mats = []
            for i in (2 * p, 2 * p + 1):
                gap = half(cols, q)[:, i : i + 1] - rows[i : i + 1, q * HALF : (q + 1) * HALF]
                mats.append((jnp.exp(jnp.minimum(gap, 0.0)) * scores[q]).astype(BF16))
            y = dot(jnp.concatenate(mats, axis=1), both.astype(BF16))
            y_ref[q * HALF : (q + 1) * HALF, lanes] = y + x * pair_lanes(skips, p)


def inside_call(xa, bca, cum, dt, hpar):
    return pl.pallas_call(
        inside_body,
        grid=(GROUPS,),
        out_shape=shape((ROWS, LOCAL)),
        in_specs=[
            columns(ROWS, BLOCK),
            whole((ROWS, 256)),
            whole((ROWS, LANES)),
            whole((ROWS, LANES)),
            whole((8, LANES)),
        ],
        out_specs=columns(ROWS, BLOCK),
        scratch_shapes=[pltpu.VMEM((LANES, ROWS), F32), pltpu.VMEM((2, HALF, HALF), F32)],
        compiler_params=params(),
        cost_estimate=pl.CostEstimate(
            flops=2 * HEADS * HALF * HALF * LANES, bytes_accessed=3_300_000, transcendentals=800_000
        ),
        name="inside",
    )(xa, bca, cum, dt, hpar)


def scan_body(backward, info, msg, *rest):
    out_ref = rest[-1]
    carry = jnp.zeros((STATE_HALF, BLOCK), F32)
    for k in reversed(range(CHUNKS)) if backward else range(CHUNKS):
        keep = info[2 + k].astype(F32)
        if not backward:
            carry = carry * keep
        out_ref[k] = carry.astype(BF16)
        damps = msg[k, STATE_HALF:, :].astype(F32)
        carry = (damps[0:1] + damps[1:2]) * carry + msg[k, :STATE_HALF, :].astype(F32)
        if backward:
            carry = carry * keep


def scan_call(info, msg, backward, *tokens):
    return pl.pallas_call(
        functools.partial(scan_body, backward),
        out_shape=shape((CHUNKS, STATE_HALF, BLOCK), BF16),
        in_specs=[SMEM, whole((CHUNKS, MESSAGE, BLOCK))] + [ANYWHERE] * len(tokens),
        out_specs=whole((CHUNKS, STATE_HALF, BLOCK)),
        compiler_params=params(),
        name="chunk_scan",
    )(info, msg, *tokens)


def out_proj_body(weight, info, y_in, bca, cum, hin, s0, gate, gain, *rest):
    refs = len(weight.arrays)
    w_refs, (y_ref, part_ref, buffer, sems, sums, gained) = rest[:refs], rest[refs:]
    weight.start(w_refs, info, buffer, sems)
    c_all = bca[:, STATE:].astype(BF16)
    grow = jnp.exp(cum[...])
    sums[...] = jnp.zeros((ROWS, LANES), F32)

    def group(g, _):
        lanes = pl.ds(pl.multiple_of(g * BLOCK, LANES), BLOCK)
        factor = rolled(grow, g)
        first = hin[g]
        second = spread(factor[HALF - 1 : HALF]) * first.astype(F32) + s0[g]
        carried = jnp.concatenate(
            [dot(half(c_all, 0), first), dot(half(c_all, 1), second.astype(BF16))], axis=0
        )
        y = y_in[:, lanes] + spread(factor) * carried
        y_ref[:, lanes] = y
        z = gate[:, lanes]
        gated = y * z * sigmoid(z)
        square = gated * gated
        sums[...] += sum(square[:, i * LANES : (i + 1) * LANES] for i in range(BLOCK // LANES))
        gained[:, lanes] = (gated * gain[:, lanes]).astype(BF16)
        return 0

    lax.fori_loop(0, GROUPS, group, 0)
    part_ref[:, WIDTH:] = sums[...]
    weight.product(w_refs, info, gained, buffer, sems, part_ref)


def out_proj(info, y_in, bca, cum, hin, s0, gate, gain, weight):
    return pl.pallas_call(
        functools.partial(out_proj_body, weight),
        out_shape=(shape((ROWS, LOCAL)), shape((ROWS, WIDTH + LANES))),
        in_specs=[
            SMEM,
            whole((ROWS, LOCAL)),
            whole((ROWS, 256)),
            whole((ROWS, LANES)),
            whole((GROUPS, STATE, BLOCK)),
            whole((GROUPS, STATE, BLOCK)),
            whole((ROWS, LOCAL)),
            whole((1, LOCAL)),
        ]
        + weight.specs(),
        out_specs=(whole((ROWS, LOCAL)), whole((ROWS, WIDTH + LANES))),
        scratch_shapes=weight.scratch()
        + [pltpu.VMEM((ROWS, LANES), F32), pltpu.VMEM((ROWS, LOCAL), BF16)],
        compiler_params=params(),
        cost_estimate=pl.CostEstimate(
            flops=2 * ROWS * WIDTH * LOCAL, bytes_accessed=13_000_000, transcendentals=800_000
        ),
        name="out_proj",
    )(info, y_in, bca, cum, hin, s0, gate, gain, *weight.arrays)


def join_body(info, h_ref, own, came, res_ref, branch_ref, scale_ref):
    squares = jnp.sum(own[:, WIDTH:] + came[:, WIDTH:], axis=1, keepdims=True)
    scale = lax.rsqrt(squares / INNER + EPSILON)
    branch = scale * (own[:, :WIDTH] + came[:, :WIDTH])
    branch_ref[...] = branch.astype(BF16)
    scale_ref[...] = jnp.broadcast_to(scale, (HALF // 2, LANES))
    first = pl.program_id(0) * (HALF // 2)
    usable = (row_of((HALF // 2, 1)) + first < info[0]).astype(F32)
    result = h_ref[...].astype(F32) + usable * branch
    res_ref[...] = result.astype(res_ref.dtype)


def join(info, h, own, came, kind):
    def rows(width):
        return pl.BlockSpec((HALF // 2, width), lambda i: (i, 0))

    return pl.pallas_call(
        join_body,
        grid=(4,),
        out_shape=(shape((ROWS, WIDTH), kind), shape((ROWS, WIDTH), BF16), shape((ROWS, LANES))),
        in_specs=[SMEM, rows(WIDTH), rows(WIDTH + LANES), rows(WIDTH + LANES)],
        out_specs=(rows(WIDTH), rows(WIDTH), rows(LANES)),
        compiler_params=params(),
        cost_estimate=pl.CostEstimate(flops=2_000_000, bytes_accessed=8_000_000, transcendentals=0),
        name="join",
    )(info, h, own, came)


def gate_back_body(weight, info, cot, y, gate, gain, branch, scale_ref, *rest):
    refs = len(weight.arrays)
    w_refs, rest = rest[:refs], rest[refs:]
    bg_ref, dy_ref, dz_ref, grad_ref, dgain_ref, buffer, sems, inner_ref = rest
    b = pl.program_id(0)
    scale = scale_ref[:, :1]

    @pl.when(b == 0)
    def _():
        weight.start(w_refs, info, buffer, sems)
        bg = (usable_rows(info) * cot[...].astype(F32)).astype(BF16)
        bg_ref[...] = bg
        inner = jnp.sum(bg.astype(F32) * branch[...].astype(F32), axis=1, keepdims=True)
        inner_ref[...] = jnp.broadcast_to(inner * scale * scale / INNER, (ROWS, LANES))
        for n in range(4):
            weight.wait(w_refs, info, n, buffer, sems)

    inner = inner_ref[:, :1]
    bg = bg_ref[...]
    d_norms = dot_nt(bg, buffer[pl.ds(pl.multiple_of(b * SHARD, SHARD), SHARD), :])
    norms = []
    for i in range(SHARD // LANES):
        lanes = slice(i * LANES, (i + 1) * LANES)
        z = gate[:, lanes]
        sig = sigmoid(z)
        silu = z * sig
        y_here = y[:, lanes]
        gated = y_here * silu
        d_norm = d_norms[:, lanes]
        gained = scale * gain[:, lanes]
        norms.append((gated * gained).astype(BF16))
        d_gated = d_norm * gained - gated * inner
        total = jnp.sum(d_norm * gated * scale, axis=0, keepdims=True)
        dgain_ref[:, lanes] = jnp.broadcast_to(total, (8, LANES))
        dy_ref[:, lanes] = (d_gated * silu).astype(BF16)
        dz_ref[:, lanes] = (d_gated * y_here * sig * (1.0 + z * (1.0 - sig))).astype(BF16)
    norm = jnp.concatenate(norms, axis=1)
    grad_ref[...] = dot(norm.T, bg).astype(BF16) if grad_ref.shape[1] == WIDTH else norm.T


def gate_back(info, cot, y, gate, gain, branch, scale, weight, with_grad):
    wide, local = whole((ROWS, WIDTH)), columns(ROWS, SHARD)
    grad_width = WIDTH if with_grad else ROWS
    return pl.pallas_call(
        functools.partial(gate_back_body, weight),
        grid=(4,),
        out_shape=(
            shape((ROWS, WIDTH), BF16),
            shape((ROWS, LOCAL), BF16),
            shape((ROWS, LOCAL), BF16),
            shape((LOCAL, grad_width), BF16),
            shape((8, LOCAL)),
        ),
        in_specs=[SMEM, wide, local, local, columns(1, SHARD), wide, whole((ROWS, LANES))]
        + weight.specs(),
        out_specs=(
            wide,
            local,
            local,
            pl.BlockSpec((SHARD, grad_width), lambda b: (b, 0)),
            columns(8, SHARD),
        ),
        scratch_shapes=weight.scratch() + [pltpu.VMEM((ROWS, LANES), F32)],
        compiler_params=params(),
        cost_estimate=pl.CostEstimate(
            flops=4 * ROWS * WIDTH * LOCAL, bytes_accessed=17_000_000, transcendentals=800_000
        ),
        name="gate_back",
    )(info, cot, y, gate, gain, branch, scale, *weight.arrays)


def own_grad_body(dy, bca, cum, msg_in, dz, normed, own1_ref, msg_ref, grad_ref, ct, grow):
    g = pl.program_id(0)
    grad_ref[...] = dot(normed[...].T, dz[...]).astype(BF16)

    @pl.when(g == 0)
    def _():
        ct[...] = bca[:, STATE:].T.astype(BF16)
        grow[...] = jnp.exp(cum[...])

    factor = rolled(grow[...], g)
    weighted = (dy[...].astype(F32) * spread(factor)).astype(BF16)
    own0 = dot(ct[:, :HALF], half(weighted, 0))
    own1 = dot(ct[:, HALF:], half(weighted, 1))
    own1_ref[0] = own1
    grad = (spread(factor[HALF - 1 : HALF]) * own1 + own0).astype(BF16)
    for r in range(2):
        msg_ref[r, :STATE_HALF, :] = grad[r * STATE_HALF : (r + 1) * STATE_HALF]
        msg_ref[r, STATE_HALF:, :] = msg_in[r, STATE_HALF:, :]


def own_grad(dy, bca, cum, msg, dz, normed):
    return pl.pallas_call(
        own_grad_body,
        grid=(GROUPS,),
        out_shape=(
            shape((GROUPS, STATE, BLOCK)),
            shape((CHUNKS, MESSAGE, BLOCK), BF16),
            shape((WIDTH, LOCAL), BF16),
        ),
        in_specs=[
            columns(ROWS, BLOCK),
            whole((ROWS, 256)),
            whole((ROWS, LANES)),
            MESSAGES,
            whole((ROWS, LOCAL)),
            columns(ROWS, SHARD),
        ],
        out_specs=(grouped(STATE), MESSAGES, pl.BlockSpec((SHARD, LOCAL), lambda b: (b, 0))),
        scratch_shapes=[pltpu.VMEM((STATE, ROWS), BF16), pltpu.VMEM((ROWS, LANES), F32)],
        compiler_params=params(),
        cost_estimate=pl.CostEstimate(
            flops=2 * ROWS * WIDTH * LOCAL, bytes_accessed=8_000_000, transcendentals=0
        ),
        name="own_grad",
    )(dy, bca, cum, msg, dz, normed)


def inside_back_body(
    dy, xa, bca, cum, dt, hpar,
    dx_ref, dskip_ref, gsum_ref, u_ref, dbc_ref, cum_t, scores, dscores,
):
    g = pl.program_id(0)

    @pl.when(g == 0)
    def _():
        tri = lower_triangle()
        for q in range(2):
            b, c = half(bca[:, :STATE], q).astype(BF16), half(bca[:, STATE:], q).astype(BF16)
            scores[q] = dot_nt(b, c) * tri.T
            cum_t[:, q * HALF : (q + 1) * HALF] = half(cum[...], q).T
        dscores[...] = jnp.zeros((2, HALF, HALF), F32)
        u_ref[...] = jnp.zeros((ROWS, LANES), F32)

    cols = rolled(cum[...], g)
    rows = cum_t[pl.ds(pl.multiple_of(8 * g, 8), 8), :]
    steps = rolled(dt[...], g)
    skips = rolled(hpar[...], g)[2:3, :]
    low = lane_of((HALF, LANES)) < HEADDIM
    lane = lane_of((HALF, LANES))
    gsum_ref[...] = jnp.zeros((8, ROWS), F32)
    for q in range(2):
        here = slice(q * HALF, (q + 1) * HALF)
        u_here = u_ref[here, :]
        for p in range(OWN // 2):
            lanes = slice(p * LANES, (p + 1) * LANES)
            dy_pair = dy[here, lanes]
            x = xa[here, lanes]
            zero = jnp.zeros_like(dy_pair)
            both = jnp.concatenate(
                [jnp.where(low, dy_pair, zero), jnp.where(low, zero, dy_pair)], axis=0
            )
            dw = dot_nt(x.astype(BF16), both)
            mats = []
            for n, i in enumerate((2 * p, 2 * p + 1)):
                gap = rows[i : i + 1, here] - half(cols, q)[:, i : i + 1]
                decay = jnp.exp(jnp.minimum(gap, 0.0))
                step = half(steps, q)[:, i : i + 1]
                weight = decay * scores[q]
                mats.append(weight.astype(BF16))
                dw_here = dw[:, n * HALF : (n + 1) * HALF]
                dscores[q] += decay * dw_here * step
                direct = weight * dw_here
                total = jnp.sum(direct, axis=1, keepdims=True)
                u_here = jnp.where(lane == 8 * g + i, total, u_here)
                gsum_ref[i : i + 1, here] = jnp.sum(direct * step, axis=0, keepdims=True)
            dx = dot(jnp.concatenate(mats, axis=1), both)
            dy_wide = dy_pair.astype(F32)
            dx_ref[here, lanes] = dx * pair_lanes(half(steps, q), p) + dy_wide * pair_lanes(skips, p)
            skip_sum = jnp.sum(dy_wide * x, axis=0, keepdims=True)
            if q == 0:
                dskip_ref[:, lanes] = jnp.broadcast_to(skip_sum, (8, LANES))
            else:
                dskip_ref[:, lanes] += skip_sum
        u_ref[here, :] = u_here

    @pl.when(g == GROUPS - 1)
    def _():
        tri = lower_triangle()
        for q in range(2):
            b, c = half(bca[:, :STATE], q).astype(BF16), half(bca[:, STATE:], q).astype(BF16)
            ds_t = dscores[q] * tri.T
            dbc_ref[q * HALF : (q + 1) * HALF, :STATE] = dot(ds_t.astype(BF16), c)
            dbc_ref[q * HALF : (q + 1) * HALF, STATE:] = dot(ds_t.T.astype(BF16), b)


def inside_back(dy, xa, bca, cum, dt, hpar):
    return pl.pallas_call(
        inside_back_body,
        grid=(GROUPS,),
        out_shape=(
            shape((ROWS, LOCAL)),
            shape((8, LOCAL)),
            shape((8 * GROUPS, ROWS)),
            shape((ROWS, LANES)),
            shape((ROWS, 256)),
        ),
        in_specs=[
            columns(ROWS, BLOCK),
            columns(ROWS, BLOCK),
            whole((ROWS, 256)),
            whole((ROWS, LANES)),
            whole((ROWS, LANES)),
            whole((8, LANES)),
        ],
        out_specs=(
            columns(ROWS, BLOCK),
            columns(8, BLOCK),
            pl.BlockSpec((8, ROWS), lambda g: (g, 0)),
            whole((ROWS, LANES)),
            whole((ROWS, 256)),
        ),
        scratch_shapes=[
            pltpu.VMEM((LANES, ROWS), F32),
            pltpu.VMEM((2, HALF, HALF), F32),
            pltpu.VMEM((2, HALF, HALF), F32),
        ],
        compiler_params=params(),
        cost_estimate=pl.CostEstimate(
            flops=4 * HEADS * HALF * HALF * LANES, bytes_accessed=4_500_000, transcendentals=800_000
        ),
        name="inside_back",
    )(dy, xa, bca, cum, dt, hpar)


def conv_back(d_active, values, halo, cpar, keep, ext, ext_d):
    width = values.shape[1]
    total = conv_sum_of(values, halo, cpar, keep, ext)
    sig = sigmoid(total)
    d_sum = d_active * sig * (1.0 + total * (1.0 - sig))
    ext_d[0:16, :width] = jnp.zeros((16, width), F32)
    ext_d[16 : 16 + ROWS, :width] = d_sum
    ext_d[16 + ROWS :, :width] = jnp.zeros((16, width), F32)
    d_in = jnp.zeros((ROWS + 16, width), F32)
    for k in range(KERNEL):
        d_in = d_in + cpar[k : k + 1, :] * ext_d[3 - k : 3 - k + ROWS + 16, :width]
    row = row_of((8, width))
    d_par = jnp.where(row == 4, jnp.sum(d_sum, axis=0, keepdims=True), 0.0)
    for k in range(KERNEL):
        tap = jnp.sum(d_sum * ext[13 + k : 13 + k + ROWS, :width], axis=0, keepdims=True)
        d_par = jnp.where(row == k, tap, d_par)
    return d_in, d_par


def finish_body(
    info, xa, dxi, dy, mixed, halo, cpar, bc, halo_bc, cpar_bc, bca, cum, dt, rate, hpar, lam, hin, s0, own1, u, gsum, dbc,
    dmx_ref, dmbc_ref, tailx_ref, tailbc_ref, edgex_ref, edgebc_ref, dcx_ref, dcbc_ref, dhead_ref,
    ext, ext_d, grow, tail, v_sum, q_sum, end_sum, dbc_sum,
):
    g = pl.program_id(0)
    keep = info[1].astype(F32)

    @pl.when(g == 0)
    def _():
        grow[...] = jnp.exp(cum[...])
        for q in range(2):
            here = half(cum[...], q)
            tail[q * HALF : (q + 1) * HALF, :] = jnp.exp(here[HALF - 1 :, :] - here)
        v_sum[...] = jnp.zeros((ROWS, LANES), F32)
        q_sum[...] = jnp.zeros((ROWS, LANES), F32)
        end_sum[...] = jnp.zeros((16, LANES), F32)
        dbc_sum[...] = dbc[...]

    sums = head_sum_matrix(g)
    factor = rolled(grow[...], g)
    tails = rolled(tail[...], g)
    steps = rolled(dt[...], g)
    ends = [spread(factor[HALF - 1 : HALF]), spread(factor[ROWS - 1 : ROWS])]
    lam1 = lam[0].astype(F32)
    lams = [ends[1] * lam1 + own1[0], lam1]
    first = hin[0].astype(F32)
    states = [first, ends[0] * first + s0[0]]
    d_x = []
    for q in range(2):
        here = slice(q * HALF, (q + 1) * HALF)
        b, c = bca[here, :STATE].astype(BF16), bca[here, STATE:].astype(BF16)
        lam_q, state_q = lams[q].astype(BF16), states[q].astype(BF16)
        tail_wide = spread(half(tails, q))
        tail_step = tail_wide * spread(half(steps, q))
        x, dy_q = xa[here, :], dy[here, :].astype(F32)
        lb = dot(b, lam_q) * tail_wide
        d_x.append(dxi[here, :] + lb * spread(half(steps, q)))
        v_sum[here, :] += dot((x * lb).astype(BF16), sums)
        grow_wide = spread(half(factor, q))
        dy_grow = (dy_q * grow_wide).astype(BF16)
        carried = dot(c, state_q)
        q_sum[here, :] += dot((dy_q * grow_wide * carried).astype(BF16), sums)
        dbc_sum[here, :STATE] += dot_nt((x * tail_step).astype(BF16), lam_q)
        dbc_sum[here, STATE:] += dot_nt(dy_grow, state_q)
        last = jnp.sum(lams[q] * states[q], axis=0, keepdims=True) * ends[q]
        high = last.astype(BF16).astype(F32)
        both = jnp.where(row_of((16, BLOCK)) == 0, high, last - high).astype(BF16)
        both = dot(both, sums)
        end_sum[8 * q : 8 * q + 8, :] += both[0:1] + both[1:2]
    d_in, d_par = conv_back(
        jnp.concatenate(d_x, axis=0), mixed[...], halo[...], cpar[...], keep, ext, ext_d
    )
    dmx_ref[...] = d_in[16:].astype(BF16)
    tailx_ref[...] = d_in[ROWS:]
    edgex_ref[...] = (d_in[:16] * keep).astype(BF16)
    dcx_ref[...] = d_par

    @pl.when(g == GROUPS - 1)
    def _():
        d_bc, d_par_bc = conv_back(
            dbc_sum[...], bc[...], halo_bc[...], cpar_bc[...], keep, ext, ext_d
        )
        dmbc_ref[:, :256] = d_bc[16:].astype(BF16)
        tailbc_ref[...] = d_bc[ROWS:]
        edgebc_ref[...] = (d_bc[:16] * keep).astype(BF16)
        dcbc_ref[...] = d_par_bc
        rates = -jnp.exp(hpar[1:2, :])
        logit = rate[...] + hpar[0:1, :]
        upper = lower_triangle().T
        before = lower_triangle(True)
        d_bias = jnp.zeros((1, LANES), F32)
        d_log = jnp.zeros((1, LANES), F32)
        usable = usable_rows(info)
        for q in range(2):
            here = slice(q * HALF, (q + 1) * HALF)
            step = dt[here, :]
            gs = gsum[...][:, here].T
            gs = jnp.concatenate([gs, jnp.zeros((HALF, LANES - 8 * GROUPS), F32)], axis=1)
            d_decay = exact_dot(upper, gs - step * u[here, :] + q_sum[here, :])
            d_decay = d_decay + exact_dot(before, step * v_sum[here, :])
            d_decay = d_decay + end_sum[8 * q : 8 * q + 1, :]
            d_step = u[here, :] + v_sum[here, :] + rates * d_decay
            d_rate = half(usable, q) * d_step * sigmoid(half(logit, q))
            d_bias += jnp.sum(d_rate, axis=0, keepdims=True)
            d_log += jnp.sum(d_decay * step * rates, axis=0, keepdims=True)
            dmbc_ref[here, 256:] = d_rate.astype(BF16)
        row = row_of((8, LANES))
        dhead_ref[...] = jnp.where(row == 0, d_bias, jnp.where(row == 1, d_log, 0.0))


def finish_call(
    info, xa, dxi, dy, mixed, halo, cpar, bca, cum, dt, rate, hpar, lam, hin, s0, own1, u, gsum, dbc
):
    bc_at = LOCAL // 256
    wide = whole((ROWS, LANES))
    return pl.pallas_call(
        finish_body,
        grid=(GROUPS,),
        out_shape=(
            shape((ROWS, LOCAL), BF16),
            shape((ROWS, 384), BF16),
            shape((16, LOCAL)),
            shape((16, 256)),
            shape((16, LOCAL), BF16),
            shape((16, 256), BF16),
            shape((8, LOCAL)),
            shape((8, 256)),
            shape((8, LANES)),
        ),
        in_specs=[
            SMEM,
            columns(ROWS, BLOCK),
            columns(ROWS, BLOCK),
            columns(ROWS, BLOCK),
            columns(ROWS, BLOCK),
            columns(16, BLOCK),
            columns(8, BLOCK),
            pl.BlockSpec((ROWS, 256), lambda g: (0, bc_at)),
            pl.BlockSpec((16, 256), lambda g: (0, bc_at)),
            pl.BlockSpec((8, 256), lambda g: (0, bc_at)),
            whole((ROWS, 256)),
            wide,
            wide,
            wide,
            whole((8, LANES)),
            grouped(STATE),
            grouped(STATE),
            grouped(STATE),
            grouped(STATE),
            wide,
            whole((8 * GROUPS, ROWS)),
            whole((ROWS, 256)),
        ],
        out_specs=(
            columns(ROWS, BLOCK),
            whole((ROWS, 384)),
            columns(16, BLOCK),
            whole((16, 256)),
            columns(16, BLOCK),
            whole((16, 256)),
            columns(8, BLOCK),
            whole((8, 256)),
            whole((8, LANES)),
        ),
        scratch_shapes=[
            pltpu.VMEM((ROWS + 32, BLOCK), F32),
            pltpu.VMEM((ROWS + 32, BLOCK), F32),
            pltpu.VMEM((ROWS, LANES), F32),
            pltpu.VMEM((ROWS, LANES), F32),
            pltpu.VMEM((ROWS, LANES), F32),
            pltpu.VMEM((ROWS, LANES), F32),
            pltpu.VMEM((16, LANES), F32),
            pltpu.VMEM((ROWS, 256), F32),
        ],
        compiler_params=params(),
        cost_estimate=pl.CostEstimate(
            flops=10 * ROWS * STATE * LOCAL, bytes_accessed=7_500_000, transcendentals=800_000
        ),
        name="finish_back",
    )(
        info, xa, dxi, dy, mixed, halo, cpar, mixed, halo, cpar, bca, cum, dt, rate, hpar,
        lam, hin, s0, own1, u, gsum, dbc,
    )


def gate_in_back_body(weight, info, dz, token, *rest):
    refs = len(weight.arrays)
    w_refs, (out_ref, buffer, sems) = rest[:refs], rest[refs:]

    @pl.when(pl.program_id(0) == 0)
    def _():
        weight.start(w_refs, info, buffer, sems)
        for n in range(4):
            weight.wait(w_refs, info, n, buffer, sems)

    rows = pl.ds(pl.multiple_of(pl.program_id(0) * SHARD, SHARD), SHARD)
    out_ref[...] = dot_nt(dz[...], buffer[rows, :])


def gate_in_back(info, dz, weight, token):
    return pl.pallas_call(
        functools.partial(gate_in_back_body, weight),
        grid=(4,),
        out_shape=shape((ROWS, WIDTH)),
        in_specs=[SMEM, whole((ROWS, LOCAL)), ANYWHERE] + weight.specs(),
        out_specs=columns(ROWS, SHARD),
        scratch_shapes=weight.scratch(),
        compiler_params=params(),
        cost_estimate=pl.CostEstimate(
            flops=2 * ROWS * WIDTH * LOCAL, bytes_accessed=7_000_000, transcendentals=0
        ),
        name="gate_in_back",
    )(info, dz, token, *weight.arrays)


def patch_body(dmx, dmbc, tailx, tailbc, edge, token, dxc_ref):
    dxc_ref[:, :LOCAL] = dmx[...]
    dxc_ref[:, LOCAL:] = dmbc[...]
    late = edge[...].astype(F32)
    dxc_ref[ROWS - 16 :, :LOCAL] = (tailx[...] + late[:, :LOCAL]).astype(BF16)
    dxc_ref[ROWS - 16 :, LOCAL:MIXED] = (tailbc[...] + late[:, LOCAL:]).astype(BF16)


def patch(dmx, dmbc, tailx, tailbc, edge, token):
    arrays = (dmx, dmbc, tailx, tailbc, edge)
    return pl.pallas_call(
        patch_body,
        out_shape=shape((ROWS, PACKED), BF16),
        in_specs=[whole(v.shape) for v in arrays] + [ANYWHERE],
        out_specs=whole((ROWS, PACKED)),
        compiler_params=params(),
        cost_estimate=pl.CostEstimate(flops=100_000, bytes_accessed=2_000_000, transcendentals=0),
        name="patch",
    )(*arrays, token)


def mixed_back_body(weight, tokens, info, dxc, part, h_ref, normed, *rest):
    refs = len(weight.arrays)
    w_refs, rest = rest[:refs], rest[refs + tokens :]
    (out_ref, dgain_ref, *grad_ref), (buffer, sems, scale_ref) = rest[:-3], rest[-3:]
    b = pl.program_id(0)
    block = pl.ds(pl.multiple_of(b * SHARD, SHARD), SHARD)

    @pl.when(b == 0)
    def _():
        weight.start(w_refs, info, buffer, sems)
        h = h_ref[...].astype(F32)
        scale = lax.rsqrt(jnp.mean(h * h, axis=1, keepdims=True) + EPSILON)
        scale_ref[...] = jnp.broadcast_to(scale, (ROWS, LANES))

    for ref in grad_ref:
        ref[...] = dot(normed[...].T, dxc[...]).astype(BF16)

    @pl.when(b == 0)
    def _():
        for n in range(4):
            weight.wait(w_refs, info, n, buffer, sems)

    d_norm = part[...] + dot_nt(dxc[...], buffer[block, :])
    out_ref[...] = d_norm
    total = jnp.sum(d_norm * h_ref[:, block].astype(F32) * scale_ref[:, :1], axis=0, keepdims=True)
    dgain_ref[...] = jnp.broadcast_to(total, (8, SHARD))


def mixed_back(info, dxc, part, h, normed, weight, with_grad, tokens):
    wide, local = whole((ROWS, WIDTH)), columns(ROWS, SHARD)
    outs = [shape((ROWS, WIDTH)), shape((8, WIDTH))]
    specs = [local, columns(8, SHARD)]
    if with_grad:
        outs.append(shape((WIDTH, PACKED), BF16))
        specs.append(pl.BlockSpec((SHARD, PACKED), lambda b: (b, 0)))
    return pl.pallas_call(
        functools.partial(mixed_back_body, weight, len(tokens)),
        grid=(4,),
        out_shape=outs,
        in_specs=[SMEM, whole((ROWS, PACKED)), local, wide, local]
        + weight.specs()
        + [ANYWHERE] * len(tokens),
        out_specs=specs,
        scratch_shapes=weight.scratch() + [pltpu.VMEM((ROWS, LANES), F32)],
        compiler_params=params(),
        cost_estimate=pl.CostEstimate(
            flops=4 * ROWS * WIDTH * PACKED, bytes_accessed=14_000_000, transcendentals=0
        ),
        name="mixed_back",
    )(info, dxc, part, h, normed, *weight.arrays, *tokens)


def norm_back_body(own, came, h_ref, cot, gain, dh_ref, low_ref):
    h = h_ref[...].astype(F32)
    scale = lax.rsqrt(jnp.mean(h * h, axis=1, keepdims=True) + EPSILON)
    d_norm = own[...] + came[...]
    inner = jnp.mean(d_norm * gain[...] * h, axis=1, keepdims=True) * scale * scale * scale
    dh = cot[...].astype(F32) + scale * d_norm * gain[...] - h * inner
    dh_ref[...] = dh
    low_ref[...] = dh.astype(BF16)


def norm_back(own, came, h, cot, gain):
    rows = pl.BlockSpec((HALF // 2, WIDTH), lambda i: (i, 0))
    return pl.pallas_call(
        norm_back_body,
        grid=(4,),
        out_shape=(shape((ROWS, WIDTH)), shape((ROWS, WIDTH), BF16)),
        in_specs=[rows] * 4 + [whole((1, WIDTH))],
        out_specs=(rows, rows),
        compiler_params=params(),
        cost_estimate=pl.CostEstimate(flops=3_000_000, bytes_accessed=8_000_000, transcendentals=0),
        name="norm_back",
    )(own, came, h, cot, gain)


def z_shift(r):
    return "dp", [(z, (z + r) % 4) for z in range(4)]


def y_shift(r):
    return "ctx", [(j, (j + 4 * r) % 16) for j in range(16)]


def x_shift(r):
    return "ctx", [(j, j - j % 4 + (j + r) % 4) for j in range(16)]


SHIFTS = {"z": z_shift, "y": y_shift, "x": x_shift}


def send(value, axis, r):
    name, pairs = SHIFTS[axis](r % 4)
    return lax.ppermute(value, name, pairs)


def swapped(value):
    return lax.ppermute(value, "section", [(0, 1), (1, 0)])


def nothing_body(*refs):
    refs[-1][...] = jnp.zeros((8, LANES), jnp.int32)


def after(values, place):
    nothing = pl.pallas_call(
        nothing_body,
        out_shape=shape((8, LANES), jnp.int32),
        in_specs=[ANYWHERE] * len(values),
        out_specs=whole((8, LANES)),
        compiler_params=params(),
        cost_estimate=pl.CostEstimate(flops=0, bytes_accessed=4096, transcendentals=0),
        name="after",
    )(*values)[0, 0]
    return {axis: n + nothing for axis, n in place.items()}


def fetched(mine, came, layer, section, place):
    rows = SHARD // 2

    def piece(source, side, axis):
        return lax.dynamic_slice_in_dim(source, side * rows + place[axis] * PIECE, PIECE, 0)

    parts = [
        jnp.where(section == layer, piece(mine, side, axis), piece(came, side, axis))
        for side, axis in enumerate("xy")
    ]
    if mine.shape[0] == TALL:
        parts.append(jnp.where(section == layer, mine[SHARD:], came[SHARD:]))
    return jnp.concatenate(parts)


def pieces(mine, came, got, late):
    out = [mine, came]
    for side, axis in enumerate("xy"):
        rows = slice(side * PIECE, (side + 1) * PIECE)
        stack = jnp.concatenate(
            [lax.dynamic_slice_in_dim(g, rows.start + late, PIECE, 0) for g in got[1:]]
        )
        out += [stack] + [send(stack, axis, -r) for r in range(1, 4)]
    return out


def summed(terms):
    a, b, c, d = (t.astype(F32) for t in terms)
    return (a + c) + (b + d)


def arrived(terms, axis):
    return [terms[0]] + [send(terms[r], axis, r) for r in range(1, 4)]


def terms_body(axis, cuts, stacked, info, *rest):
    factors, rest = rest[: 2 * len(cuts)], rest[2 * len(cuts) :]
    small, outs, total = rest[:-2] if stacked else rest[:-5], rest[-5:-1], rest[-1]
    column = 0
    for n, cols in enumerate(cuts):
        there = slice(column, column + cols.stop - cols.start)
        total[:, there] = dot(factors[2 * n][...], factors[2 * n + 1][:, cols])
        column = there.stop
    count = 96 if axis == "y" else 24
    starts = [z * SHARD for z in range(4)]
    if axis == "x":
        starts = [start + y * 96 for start in starts for y in range(4)]
    for r in range(4):
        first = r * count
        if not stacked:
            first = lax.rem(info[11 if axis == "y" else 12] + r, 4) * count
        parts = [total[pl.ds(pl.multiple_of(start + first, 8), count), :] for start in starts]
        out = rest[-2].at[r] if stacked else outs[r]
        out[:SHARD, :] = jnp.concatenate(parts, axis=0).astype(BF16)
        for ref in small:
            out[SHARD:, :] = ref[...]


def four(dims, stacked):
    if stacked:
        return shape((4, *dims), BF16), whole((4, *dims))
    return [shape(dims, BF16)] * 4, [whole(dims)] * 4


def terms(info, axis, products, small=(), stacked=False):
    cuts = [cols for _, _, cols in products]
    width = sum(cols.stop - cols.start for cols in cuts)
    rows = SHARD + sum(v.shape[0] for v in small)
    arrays = [v for left, right, _ in products for v in (left, right)] + list(small)
    outs, specs = four((rows, width), stacked)
    return pl.pallas_call(
        functools.partial(terms_body, axis, cuts, stacked),
        out_shape=outs,
        in_specs=[SMEM] + [whole(v.shape) for v in arrays],
        out_specs=specs,
        scratch_shapes=[pltpu.VMEM((4 * SHARD, width), F32)],
        compiler_params=params(),
        cost_estimate=pl.CostEstimate(
            flops=8 * SHARD * ROWS * width, bytes_accessed=8_000_000, transcendentals=0
        ),
        name="terms",
    )(info, *arrays)


def fold_body(slot, counts, outer, inner, rest_rows, stacked, info, *rest):
    refs, outs, total = rest[: sum(counts)], rest[sum(counts) + 1 : -1], rest[-1]
    column = 0
    for count in counts:
        arrays, refs = refs[:count], refs[count:]
        cols = slice(column, column + arrays[0].shape[-1])
        if count == 4:
            total[:, cols] = summed([a[...] for a in arrays])
        elif len(arrays[0].shape) == 3:
            total[:, cols] = summed([arrays[0][n] for n in range(4)])
        else:
            total[:, cols] = arrays[0][...].astype(F32)
        column = cols.stop
    for r in range(4):
        first = r * inner if stacked else lax.rem(info[slot] + r, 4) * inner
        parts = [
            total[pl.ds(pl.multiple_of(n * 4 * inner + first, 8), inner), :] for n in range(outer)
        ]
        if rest_rows:
            parts.append(total[4 * outer * inner :, :])
        out = outs[0].at[r] if stacked else outs[r]
        out[...] = jnp.concatenate(parts, axis=0).astype(BF16)


def fold(info, axis, groups, outer, inner, token, stacked=False):
    slot = 10 + "zyx".index(axis)
    arrays = [a for group in groups for a in group]
    rows, width = arrays[0].shape[-2], sum(group[0].shape[-1] for group in groups)
    more = rows - 4 * outer * inner
    outs, specs = four((outer * inner + more, width), stacked)
    counts = [len(group) for group in groups]
    return pl.pallas_call(
        functools.partial(fold_body, slot, counts, outer, inner, more, stacked),
        out_shape=outs,
        in_specs=[SMEM] + [whole(a.shape) for a in arrays] + [ANYWHERE],
        out_specs=specs,
        scratch_shapes=[pltpu.VMEM((rows, width), F32)],
        compiler_params=params(),
        cost_estimate=pl.CostEstimate(flops=2_000_000, bytes_accessed=8_000_000, transcendentals=0),
        name="fold",
    )(info, *arrays, token)


def last_fold_body(info, *rest):
    left, right, outs, total = rest[:4], rest[4:8], rest[9:13], rest[13]
    width = left[0].shape[1]
    total[:96, :width] = summed([a[...] for a in left])
    total[96:, :width] = jnp.zeros((SMALL, width), F32)
    total[:, width:] = summed([a[...] for a in right])
    for r in range(4):
        first = pl.multiple_of(lax.rem(info[10] + r, 4) * 24, 8)
        parts = [total[pl.ds(first, 24), :], total[96:, :]]
        outs[r][...] = jnp.concatenate(parts, axis=0).astype(BF16)


def last_fold(info, left, right, token):
    width = left[0].shape[1] + right[0].shape[1]
    out = shape((24 + SMALL, width), BF16)
    arrays = (*left, *right)
    return pl.pallas_call(
        last_fold_body,
        out_shape=[out] * 4,
        in_specs=[SMEM] + [whole(a.shape) for a in arrays] + [ANYWHERE],
        out_specs=[whole(out.shape)] * 4,
        scratch_shapes=[pltpu.VMEM((96 + SMALL, width), F32)],
        compiler_params=params(),
        cost_estimate=pl.CostEstimate(flops=500_000, bytes_accessed=2_000_000, transcendentals=0),
        name="last_fold",
    )(info, *arrays, token)


PARITY = [[j for j in range(16) if j % 2 == e] for e in range(2)]
NEIGHBOURS = [(j, j ^ 1) for j in range(16)]
GROUPS_OF = {
    "y": [[4 * y + x for y in range(4)] for x in range(4)],
    "x": [[4 * y + x for x in range(4)] for y in range(4)],
}


def traded(value, axis):
    return lax.all_to_all(value, "ctx", 0, 0, axis_index_groups=GROUPS_OF[axis])


def exchange(value):
    return lax.all_to_all(value, "ctx", 0, 0, axis_index_groups=PARITY)


def halo_shift(value, step):
    pairs = [(j, j + 2 * step) for j in range(16) if 0 <= j + 2 * step < 16]
    return lax.ppermute(value, "ctx", pairs)


def halves(values, section):
    grid = values.reshape(values.shape[0], GROUPS, 2, -1)
    size = values.shape[1] // 2
    return [
        lax.dynamic_index_in_dim(grid, i, 2, False).reshape(-1, size)
        for i in (section, 1 - section)
    ]


def turns(low, high):
    rows = low.shape[0]
    parts = [v.reshape(rows, GROUPS, 1, -1) for v in (low, high)]
    return jnp.concatenate(parts, axis=2).reshape(rows, -1)


def pick_x_body(info, x_ref, dt_ref, *rest):
    smalls, outs, small = rest[:7], rest[7:9], rest[9]
    small[...] = jnp.zeros((16, PACKED), F32)
    row = 0
    for ref in smalls[:4]:
        count, width = ref.shape
        small[row : row + count, :width] = ref[...].astype(F32)
        row += count
    for ref in smalls[4:]:
        left = ref[...]
        for _ in range(3):
            part = left.astype(BF16).astype(F32)
            small[row : row + 1, :HEADS] = part
            left = left - part
            row += 1
    head, lane = row_of((HEADS, LANES)), lane_of((HEADS, LANES))
    for out, side in zip(outs, (info[0], 1 - info[0]), strict=True):
        for d in range(GROUPS):
            cols = pl.ds(pl.multiple_of((2 * d + side) * BLOCK, LANES), BLOCK)
            out[:SHARD, d * BLOCK : (d + 1) * BLOCK] = x_ref[:, cols]
        out[:SHARD, LOCAL:MIXED] = x_ref[:, INNER:]
        here = (head // OWN == 2 * (lane // 8) + side) & (head % OWN == lane % 8)
        out[:SHARD, MIXED:] = dot(dt_ref[...], here.astype(BF16)).astype(BF16)
        out[SHARD:, :] = small[...].astype(BF16)


def pick_x(section, x, dt, smalls):
    return pl.pallas_call(
        pick_x_body,
        out_shape=[shape((TALL, PACKED), BF16)] * 2,
        in_specs=[SMEM, whole((SHARD, CONV_CH)), whole((SHARD, HEADS))]
        + [whole(v.shape) for v in smalls],
        out_specs=[whole((TALL, PACKED))] * 2,
        scratch_shapes=[pltpu.VMEM((16, PACKED), F32)],
        compiler_params=params(),
        cost_estimate=pl.CostEstimate(flops=0, bytes_accessed=6_000_000, transcendentals=0),
        name="pick_x",
    )(section, x, dt, *smalls)


def unpack_body(count, info, *rest):
    refs, (cpar, gain_one, gain_two, hpar, held, full, sems) = rest[:count], rest[count:]
    copies = []
    for n in range(4):
        if count == 4:
            source, to = refs[n].at[pl.ds(2 * PIECE, 16)], lax.rem(info[10] + n, 4)
        else:
            source, to = refs[0].at[pl.ds(n * TALL + SHARD, 16)], n
        copies.append(pltpu.make_async_copy(source, held.at[to], sems.at[n]))
    for c in copies:
        c.start()
    for c in copies:
        c.wait()
    section = info[13]
    half_cols = pl.ds(pl.multiple_of(section * BLOCK, LANES), BLOCK)
    for z in range(4):
        values = held[z].astype(F32)
        full[:, z * 832 : (z + 1) * 832] = values[:8, :832]
        gain_one[:, z * SHARD : (z + 1) * SHARD] = values[5:6, :SHARD]
        gain_two[:, z * BLOCK : (z + 1) * BLOCK] = held[z, :, half_cols].astype(F32)[6:7]
    for d in range(GROUPS):
        cols = pl.ds(pl.multiple_of((2 * d + section) * BLOCK, LANES), BLOCK)
        cpar[:, d * BLOCK : (d + 1) * BLOCK] = full[:, cols]
    cpar[:, LOCAL:] = full[:, INNER:]
    values = held[0, :, :LANES].astype(F32)
    heads = [values[n : n + 1] + values[n + 1 : n + 2] + values[n + 2 : n + 3] for n in (7, 10, 13)]
    heads = jnp.concatenate(heads + [jnp.zeros((5, LANES), F32)], axis=0)
    head, lane = row_of((LANES, LANES)), lane_of((LANES, LANES))
    here = (head // OWN == 2 * (lane // 8) + section) & (head % OWN == lane % 8)
    hpar[...] = exact_dot(heads, here.astype(F32))


def unpack(info, arrays):
    shapes = ((8, MIXED), (1, WIDTH), (1, LOCAL), (8, LANES))
    return pl.pallas_call(
        functools.partial(unpack_body, len(arrays)),
        out_shape=[shape(dims) for dims in shapes],
        in_specs=[SMEM] + [ANYWHERE] * len(arrays),
        out_specs=[whole(dims) for dims in shapes],
        scratch_shapes=[
            pltpu.VMEM((4, 16, PACKED), BF16),
            pltpu.VMEM((8, CONV_CH), F32),
            pltpu.SemaphoreType.DMA((4,)),
        ],
        compiler_params=params(),
        cost_estimate=pl.CostEstimate(flops=0, bytes_accessed=400_000, transcendentals=0),
        name="unpack",
    )(info, *arrays)


def pick_zo_body(info, z_ref, o_ref, token, *outs):
    for out, side in zip(outs, (info[0], 1 - info[0]), strict=True):
        for d in range(GROUPS):
            cols = pl.ds(pl.multiple_of((2 * d + side) * BLOCK, LANES), BLOCK)
            out[:, d * BLOCK : (d + 1) * BLOCK] = z_ref[:, cols]
        rows = pl.ds(pl.multiple_of(side * SHARD, SHARD), SHARD)
        out[:, LOCAL:] = o_ref[rows, :]


def pick_zo(section, z, o, token):
    return pl.pallas_call(
        pick_zo_body,
        out_shape=[shape((SHARD, LOCAL + WIDTH), BF16)] * 2,
        in_specs=[SMEM, whole((SHARD, INNER)), whole((2 * SHARD, WIDTH)), ANYWHERE],
        out_specs=[whole((SHARD, LOCAL + WIDTH))] * 2,
        compiler_params=params(),
        cost_estimate=pl.CostEstimate(flops=0, bytes_accessed=9_000_000, transcendentals=0),
        name="pick_zo",
    )(section, z, o, token)


def head_lanes(values):
    rows = values.shape[0]
    grid = jnp.pad(values.reshape(rows, GROUPS, OWN), ((0, 0), (0, 0), (0, 8 - OWN)))
    return jnp.pad(grid.reshape(rows, 8 * GROUPS), ((0, 0), (0, LANES - 8 * GROUPS)))


def lanes_heads(values):
    rows = values.shape[0]
    return values[:, : 8 * GROUPS].reshape(rows, GROUPS, 8)[:, :, :OWN].reshape(rows, -1)


def on_device(
    boundary,
    lengths,
    norm_gain,
    w_z,
    w_xbc,
    w_dt,
    conv_weight,
    conv_bias,
    dt_bias,
    a_log,
    d_skip,
    gate_gain,
    w_out,
):
    section = lax.axis_index("section")
    group = lax.axis_index("dp")
    ctx = lax.axis_index("ctx")
    place = {"z": group, "y": ctx // 4, "x": ctx % 4}
    micro = ctx % 2
    chunk = ctx // 2

    def ordered(mine, came):
        return jnp.where(section == 0, mine, came), jnp.where(section == 0, came, mine)

    own_rows = lax.dynamic_index_in_dim(boundary[0], micro, 0, False)
    other_rows = lax.dynamic_index_in_dim(boundary[0], 1 - micro, 0, False)
    came = lax.ppermute(other_rows, "ctx", NEIGHBOURS)
    block = jnp.where(
        micro == 0, jnp.concatenate([own_rows, came]), jnp.concatenate([came, own_rows])
    )
    hidden, cotangent = ordered(block, swapped(block))

    pair = lengths[group, micro]
    padded = (pair[0] + SPAN - 1) // SPAN * SPAN
    offset = chunk * ROWS
    begin = jnp.where(offset >= padded, padded, 0)
    length = jnp.where(offset >= padded, pair[1], pair[0])
    live = jnp.clip(length - (offset - begin), 0, ROWS)
    offsets = jnp.arange(CHUNKS, dtype=jnp.int32) * ROWS
    keeps = ((offsets != 0) & (offsets != padded)).astype(jnp.int32)
    keep = (offset != 0) & (offset != padded)
    at = [place["z"], place["y"], place["x"], section]
    info = jnp.concatenate(
        [jnp.stack([live, keep]).astype(jnp.int32), keeps, jnp.stack(at).astype(jnp.int32)]
    )

    def forward(h, layer):
        cpar, hpar = cpars[layer], hpars[layer]
        normed, mixed, rate = in_proj(
            info, h, gains_one[layer], weights_x[layer], []
        )
        halo = halo_shift(mixed[ROWS - 16 :], 1)
        gate = gate_proj(info, normed, weights_z[layer], [] if layer else ready)
        xa, bca, cum, dt, s0, msg = state_call(info, mixed, halo, cpar, rate, hpar)
        came = exchange(msg)
        y_in = inside_call(xa, bca, cum, dt, hpar)
        hin = exchange(scan_call(info, came, False, y_in, *([] if layer else cpars[1:]))).reshape(GROUPS, STATE, BLOCK)
        y, part = out_proj(
            info, y_in, bca, cum, hin, s0, gate, gains_two[layer], weights_o[layer]
        )
        result, branch, scale = join(info, h, part, swapped(part), F32 if layer else BF16)
        saved = (h, normed, mixed, halo, rate, gate, xa, bca, cum, dt, s0, msg, hin, y, branch, scale)
        return result, saved

    def backward(cot, saved, layer, higher, tokens):
        h, normed, mixed, halo, rate, gate, xa, bca, cum, dt, s0, msg, hin, y, branch, scale = saved
        cpar, hpar = cpars[layer], hpars[layer]

        def first_stage(value):
            return lax.psum_scatter(value, "dp", tiled=True)

        bg, dy, dz, grad_o, d_gain_two = gate_back(
            info, cot, y, gate, gains_two[layer], branch, scale, weights_o[layer], layer == 1
        )
        own1, msg_back, grad_z = own_grad(dy, bca, cum, msg, dz, normed)
        sums = [first_stage(grad_z)] + ([first_stage(grad_o)] if layer else [])
        came = exchange(msg_back)
        dxi, d_skips, gsum, u, dbc = inside_back(dy, xa, bca, cum, dt, hpar)
        part = gate_in_back(info, dz, weights_z[layer], msg_back)
        lam = exchange(scan_call(info, came, True, part)).reshape(GROUPS, STATE, BLOCK)
        dmx, dmbc, tailx, tailbc, edgex, edgebc, d_parx, d_parbc, d_heads = finish_call(
            info, xa, dxi, dy, mixed, halo, cpar, bca, cum, dt, rate, hpar, lam, hin, s0, own1, u, gsum, dbc
        )
        edge = halo_shift(jnp.concatenate([edgex, edgebc], axis=1), -1)
        dxc = patch(dmx, dmbc, tailx, tailbc, edge, *tokens)
        middle = 7 * LANES
        if layer == 0:
            higher_rows, higher = higher
            normed_t = normed.T
            cuts = [(normed_t, dxc, slice(0, middle)), (grad_o, bg, slice(0, WIDTH // 2))]
            left = terms(info, "y", cuts, (), True)
            part, d_gain_one = mixed_back(
                info, dxc, part, h, normed, weights_x[layer], False, [left, *higher]
            )
        else:
            part, d_gain_one, grad_x = mixed_back(
                info, dxc, part, h, normed, weights_x[layer], True, []
            )
        dh, dh_low = norm_back(part, swapped(part), h, cot, gains_one[layer])
        d_skip_row = jnp.sum(d_skips[0:1].reshape(1, 4 * OWN, HEADDIM), axis=2)
        rows = jnp.where(jnp.arange(8)[:, None] == 5, d_gain_two, d_parx)
        rows = jnp.concatenate([rows, d_parbc], axis=1)
        more = jnp.concatenate(
            [
                d_gain_one[:1],
                jnp.pad(d_heads[:2], ((0, 0), (0, WIDTH - LANES))),
                jnp.pad(head_lanes(d_skip_row), ((0, 4), (0, WIDTH - LANES))),
            ]
        )
        rows = jnp.concatenate([rows, jnp.pad(more, ((0, 0), (0, 2 * STATE)))])
        if layer == 1:
            return dh, dh_low, sums + [first_stage(grad_x)], rows

        rows = jnp.concatenate([rows, higher_rows]).astype(BF16)
        cuts = [(normed_t, dxc, slice(middle, PACKED)), (grad_o, bg, slice(WIDTH // 2, WIDTH))]
        right = terms(info, "x", cuts, (rows,))
        tall = fold(info, "y", [[v] for v in higher + sums], 1, 96, right[0], True)
        right = arrived(right, "x")
        left = fold(info, "x", [[traded(left, "y")]], 4, 24, tall)
        right = fold(info, "y", [right], 4, 24, dh_low)
        tall = fold(info, "x", [[traded(tall, "y")]], 1, 24, right[0])
        left, right = arrived(left, "x"), arrived(right, "y")
        final = summed(arrived(last_fold(info, left, right, tall[0]), "z"))
        left, right = left[0].shape[1], right[0].shape[1]
        rows = final[24:, left:]
        final = final[:24]
        sum_x = jnp.concatenate(
            [final[:, :middle], final[:, left : left + PACKED - middle]], axis=1
        )
        sum_o = jnp.concatenate([final[:, middle:left], final[:, left + PACKED - middle :]], axis=1)
        return dh, [arrived(tall, "x"), sum_o], sum_x, rows

    at = section.reshape(1).astype(jnp.int32)
    smalls = (conv_weight[0], conv_bias, norm_gain, gate_gain, dt_bias, a_log, d_skip)
    mine_x, other_x = pick_x(at, w_xbc[0], w_dt[0], smalls)
    came_x = swapped(other_x)
    mine_zo, other_zo = pick_zo(at, w_z[0], w_out[0], mine_x)
    came_zo = swapped(other_zo)
    first = fetched(mine_x, came_x, 0, section, after([hidden], place))
    got = [first] + [send(first, "z", -r) for r in range(1, 4)]
    small_low = got
    low_x = pieces(mine_x, came_x, got, 0)
    got = lax.all_gather(fetched(mine_zo, came_zo, 0, section, after(got[1:], place)), "dp")
    late = after(low_x[3:6] + low_x[7:10], place)["z"]
    got = [None] + [lax.dynamic_index_in_dim(got, (late + r) % 4, 0, False) for r in range(1, 4)]
    low_zo = pieces(mine_zo, came_zo, got, 0)
    here = after([low_x[2], low_x[6]], {"section": section})["section"]
    high_x = [lax.all_gather(jnp.where(here == 1, mine_x, came_x), "dp", tiled=True)]
    high_zo = [lax.all_gather(jnp.where(here == 1, mine_zo, came_zo), "dp", tiled=True)]
    ready = low_zo[3:6] + low_zo[7:10]
    weights_x = [Weight(v, n, PACKED) for n, v in enumerate((low_x, high_x))]
    weights_z = [Weight(v, n, LOCAL) for n, v in enumerate((low_zo, high_zo))]
    weights_o = [Weight(v, n, WIDTH, LOCAL) for n, v in enumerate((low_zo, high_zo))]

    unpacked = [unpack(info, v) for v in (small_low, high_x)]
    cpars, gains_one, gains_two, hpars = zip(*unpacked, strict=True)

    def returned(rows, layer):
        pairs = [(layer * 16 + a, layer * 16 + b) for a, b in NEIGHBOURS]
        other, mine = (
            lax.dynamic_slice_in_dim(rows, n * HALF, HALF, 0) for n in (1 - micro, micro)
        )
        other = lax.ppermute(other, ("section", "ctx"), pairs)
        return jnp.where(micro == 0, jnp.stack([mine, other]), jnp.stack([other, mine]))

    middle, saved_low = forward(hidden, 0)
    out_high, saved_high = forward(middle, 1)
    top_high = returned(out_high, 1)
    _, back, higher, rows = backward(cotangent, saved_high, 1, None, [top_high])
    dh_low, (tall, low_o), low_x, rows = backward(back, saved_low, 0, (rows, higher), [rows])
    at = (LOCAL, LOCAL + WIDTH, LOCAL + WIDTH + PACKED)
    high_z, high_o, high_x, low_z = jnp.split(summed(tall), at, axis=1)

    own, given = ordered(rows[:16], rows[16:])
    rows_0, rows_1 = ordered(own, swapped(given))
    wide = jnp.concatenate(
        [turns(rows_0[:8, :LOCAL], rows_1[:8, :LOCAL]), rows_0[:8, LOCAL:] + rows_1[:8, LOCAL:]],
        axis=1,
    )
    head_rows = turns(lanes_heads(rows_0[9:12, :LANES]), lanes_heads(rows_1[9:12, :LANES]))
    index = group * 16 + ctx
    d_conv = lax.dynamic_slice(wide, (0, index * 52), (5, 52))
    d_gain_two = lax.dynamic_slice(wide, (5, index * 48), (1, 48))
    d_gain_one = lax.dynamic_slice(rows_0[8:9] + rows_1[8:9], (0, index * 24), (1, 24))

    own, given = ordered(
        jnp.concatenate([low_z, low_x], axis=1), jnp.concatenate([high_z, high_x], axis=1)
    )
    first, second = ordered(own, swapped(given))
    sum_z = turns(first[:, :LOCAL], second[:, :LOCAL])
    at_x, at_bc, at_dt = LOCAL, LOCAL + LOCAL, LOCAL + MIXED
    sum_x = turns(first[:, at_x:at_bc], second[:, at_x:at_bc])
    sum_bc = first[:, at_bc:at_dt] + second[:, at_bc:at_dt]
    sum_dt = turns(lanes_heads(first[:, at_dt:]), lanes_heads(second[:, at_dt:]))

    trips = []
    for flip in range(2):
        pairs = [
            (c * 16 + j, (flip ^ (j % 2)) * 16 + 8 * c + j // 2) for c in range(2) for j in range(16)
        ]
        value = jnp.where(micro == flip, low_o, high_o)
        trips.append(lax.ppermute(value, ("section", "ctx"), pairs))
    sum_o = jnp.concatenate(ordered(*trips))

    top = jnp.where(section == 0, returned(dh_low, 0), top_high)
    return (
        top[None],
        d_gain_one,
        sum_z[None],
        jnp.concatenate([sum_x, sum_bc], axis=1)[None],
        sum_dt[None],
        d_conv[None, :4],
        d_conv[4:5],
        head_rows[0:1],
        head_rows[1:2],
        head_rows[2:3],
        d_gain_two,
        sum_o[None],
    )


def solution(mesh):
    in_specs = (
        P("section", None, ("dp", "ctx"), None),
        P(),
        P("section", "dp"),
        P("section", "dp", None),
        P("section", "dp", None),
        P("section", "dp", None),
        P("section", None, "dp"),
        P("section", "dp"),
        P("section", None),
        P("section", None),
        P("section", None),
        P("section", "dp"),
        P("section", "dp", None),
    )
    out_specs = (
        P("section", None, ("dp", "ctx"), None),
        P("section", ("dp", "ctx")),
        P("section", ("dp", "ctx"), None),
        P("section", ("dp", "ctx"), None),
        P("section", ("dp", "ctx"), None),
        P("section", None, ("dp", "ctx")),
        P("section", ("dp", "ctx")),
        P("section", None),
        P("section", None),
        P("section", None),
        P("section", ("dp", "ctx")),
        P("section", ("dp", "ctx"), None),
    )
    return jax.shard_map(
        on_device, mesh=mesh, in_specs=in_specs, out_specs=out_specs, check_vma=False
    )
```

```python
import functools

import jax
import jax.numpy as jnp
from jax import lax
from jax.experimental import pallas as pl
from jax.experimental.pallas import tpu as pltpu
from jax.sharding import PartitionSpec as P

HEADS = 48
HEADDIM = 64
STATE = 128
KERNEL = 4
SPAN = 256
MICRO = 2
WIDTH = 1536
INNER = 3072
CONV_CH = 3328
LANES = 128
CHUNKS = 8
GROUPS = 4
OWN = 6
BLOCK = OWN * HEADDIM
LOCAL = GROUPS * BLOCK
MIXED = LOCAL + 2 * STATE
PACKED = MIXED + LANES
ROWS = 256
HALF = 128
SHARD = 384
TALL = SHARD + 16
PIECE = 48
STATE_HALF = STATE // 2
MESSAGE = STATE_HALF + 16
SMALL = 32
EPSILON = 1e-05
PRECISE = lax.Precision.HIGHEST
F32 = jnp.float32
BF16 = jnp.bfloat16
VMEM_LIMIT = 56 * 1024 * 1024


def params(**more):
    return pltpu.CompilerParams(vmem_limit_bytes=VMEM_LIMIT, **more)


def whole(shape):
    return pl.BlockSpec(shape, lambda *_: (0,) * len(shape))


def columns(rows, width):
    return pl.BlockSpec((rows, width), lambda g: (0, g))


def grouped(rows):
    return pl.BlockSpec((1, rows, BLOCK), lambda g: (g, 0, 0))


MESSAGES = pl.BlockSpec((2, MESSAGE, BLOCK), lambda g: (g, 0, 0))
SMEM = pl.BlockSpec(memory_space=pltpu.SMEM)
ANYWHERE = pl.BlockSpec(memory_space=pl.ANY)


def shape(dims, kind=F32):
    return jax.ShapeDtypeStruct(dims, kind)


def dot(a, b):
    return jnp.dot(a, b, preferred_element_type=F32)


def dot_nt(a, b):
    return lax.dot_general(a, b, (((1,), (1,)), ((), ())), preferred_element_type=F32)


def exact_dot(a, b):
    return jnp.dot(a, b, precision=PRECISE, preferred_element_type=F32)


def lane_of(dims):
    return lax.broadcasted_iota(jnp.int32, dims, len(dims) - 1)


def row_of(dims):
    return lax.broadcasted_iota(jnp.int32, dims, len(dims) - 2)


def sigmoid(v):
    return 1.0 / (1.0 + jnp.exp(-v))


def softplus(v):
    return jnp.maximum(v, 0.0) + jnp.log1p(jnp.exp(-jnp.abs(v)))


def rolled(values, g):
    return pltpu.roll(values, lax.rem(LANES - 8 * g, LANES), axis=1)


def pair_lanes(values, p):
    low = lane_of((values.shape[0], LANES)) < HEADDIM
    return jnp.where(low, values[:, 2 * p : 2 * p + 1], values[:, 2 * p + 1 : 2 * p + 2])


def spread(values):
    return jnp.concatenate([pair_lanes(values, p) for p in range(OWN // 2)], axis=1)


def head_sum_matrix(g):
    head = row_of((BLOCK, LANES)) // HEADDIM
    return (lane_of((BLOCK, LANES)) == head + 8 * g).astype(BF16)


def lower_triangle(strict=False):
    i, j = row_of((HALF, HALF)), lane_of((HALF, HALF))
    return ((i > j) if strict else (i >= j)).astype(F32)


def usable_rows(info):
    return (row_of((ROWS, 1)) < info[0]).astype(F32)


def half(values, q):
    return values[q * HALF : (q + 1) * HALF]


class Weight:
    def __init__(self, arrays, layer, width, first=0):
        self.arrays = arrays
        self.stride = arrays[0].shape[0] // 4
        self.layer = layer
        self.width = width
        self.columns = pl.ds(first, width)

    def block(self, info, b):
        return lax.rem(info[10] + b, 4) * SHARD

    def parts(self, refs, info, b):
        start = self.block(info, b)
        if len(refs) == 1:
            there = pl.multiple_of(start // SHARD * self.stride, 16)
            return [(refs[0].at[pl.ds(there, SHARD)], start, SHARD)]
        out = []
        for side in range(2):
            mine = info[12 - side]
            for step in range(4):
                source = refs[2 + 4 * side + step].at[pl.ds((b - 1) * PIECE, PIECE)]
                row = start + side * (SHARD // 2) + lax.rem(mine + step, 4) * PIECE
                out.append((source, row, PIECE))
        return out

    def copies(self, refs, info, b, buffer, sems):
        return [
            pltpu.make_async_copy(
                source.at[:, self.columns],
                buffer.at[pl.ds(pl.multiple_of(row, 16), count)],
                sems.at[b, n],
            )
            for n, (source, row, count) in enumerate(self.parts(refs, info, b))
        ]

    def own_copy(self, source, info, buffer, sems):
        rows = pl.ds(pl.multiple_of(self.block(info, 0), SHARD), SHARD)
        source = source.at[pl.ds(0, SHARD), self.columns]
        return pltpu.make_async_copy(source, buffer.at[rows], sems.at[0, 0])

    def start(self, refs, info, buffer, sems):
        whole_array = len(refs) == 1
        if not whole_array:
            for n in range(2):

                @pl.when((info[13] == self.layer) == (n == 0))
                def _(n=n):
                    self.own_copy(refs[n], info, buffer, sems).start()

        for b in range(0 if whole_array else 1, 4):
            for c in self.copies(refs, info, b, buffer, sems):
                c.start()

    def wait(self, refs, info, b, buffer, sems):
        if b == 0 and len(refs) > 1:
            self.own_copy(refs[0], info, buffer, sems).wait()
        else:
            for c in self.copies(refs, info, b, buffer, sems):
                c.wait()
        return pl.ds(pl.multiple_of(self.block(info, b), SHARD), SHARD)

    def specs(self):
        return [ANYWHERE] * len(self.arrays)

    def scratch(self):
        return [pltpu.VMEM((4 * SHARD, self.width), BF16), pltpu.SemaphoreType.DMA((4, 8))]

    def product(self, refs, info, left, buffer, sems, total):
        for b in range(4):
            self.wait(refs, info, b, buffer, sems)
        step = 512 if self.width % 512 == 0 else 640
        for at in range(0, self.width, step):
            total[:, at : at + step] = dot(left[...], buffer[:, at : at + step])


def in_proj_body(weight, tokens, info, h_ref, gain_ref, *rest):
    refs = len(weight.arrays)
    w_refs, rest = rest[:refs], rest[refs + tokens :]
    (normed_ref, mixed_ref, rate_ref, buffer, sems, total) = rest
    weight.start(w_refs, info, buffer, sems)
    h = h_ref[...].astype(F32)
    scale = lax.rsqrt(jnp.mean(h * h, axis=1, keepdims=True) + EPSILON)
    normed_ref[...] = (h * scale * gain_ref[...]).astype(BF16)
    weight.product(w_refs, info, normed_ref, buffer, sems, total)
    mixed_ref[...] = total[:, :MIXED].astype(BF16)
    rate_ref[...] = total[:, MIXED:]


def in_proj(info, h, gain, weight, tokens):
    return pl.pallas_call(
        functools.partial(in_proj_body, weight, len(tokens)),
        out_shape=(shape((ROWS, WIDTH), BF16), shape((ROWS, MIXED), BF16), shape((ROWS, LANES))),
        in_specs=[SMEM, whole((ROWS, WIDTH)), whole((1, WIDTH))]
        + weight.specs()
        + [ANYWHERE] * len(tokens),
        out_specs=(whole((ROWS, WIDTH)), whole((ROWS, MIXED)), whole((ROWS, LANES))),
        scratch_shapes=weight.scratch() + [pltpu.VMEM((ROWS, PACKED), F32)],
        compiler_params=params(),
        cost_estimate=pl.CostEstimate(
            flops=2 * ROWS * WIDTH * PACKED, bytes_accessed=8_000_000, transcendentals=0
        ),
        name="in_proj",
    )(info, h, gain, *weight.arrays, *tokens)


def gate_proj_body(weight, tokens, info, normed_ref, *rest):
    refs = len(weight.arrays)
    w_refs, (gate_ref, buffer, sems) = rest[:refs], rest[refs + tokens :]
    weight.start(w_refs, info, buffer, sems)
    weight.product(w_refs, info, normed_ref, buffer, sems, gate_ref)


def gate_proj(info, normed, weight, tokens):
    return pl.pallas_call(
        functools.partial(gate_proj_body, weight, len(tokens)),
        out_shape=shape((ROWS, LOCAL)),
        in_specs=[SMEM, whole((ROWS, WIDTH))] + weight.specs() + [ANYWHERE] * len(tokens),
        out_specs=whole((ROWS, LOCAL)),
        scratch_shapes=weight.scratch(),
        compiler_params=params(),
        cost_estimate=pl.CostEstimate(
            flops=2 * ROWS * WIDTH * LOCAL, bytes_accessed=7_000_000, transcendentals=0
        ),
        name="gate_proj",
    )(info, normed, *weight.arrays, *tokens)


def conv_sum_of(values, halo, cpar, keep, ext):
    width = values.shape[1]
    ext[0:16, :width] = halo.astype(F32) * keep
    ext[16 : 16 + ROWS, :width] = values.astype(F32)
    total = cpar[4:5, :]
    for k in range(KERNEL):
        total = total + cpar[k : k + 1, :] * ext[13 + k : 13 + k + ROWS, :width]
    return total


def state_body(
    info, mixed, halo, cpar, bc, halo_bc, cpar_bc, rate, hpar,
    xa_ref, bca_ref, cum_ref, dt_ref, s0_ref, msg_ref, ext, bt, tail,
):
    g = pl.program_id(0)
    keep = info[1].astype(F32)

    @pl.when(g == 0)
    def _():
        total = conv_sum_of(bc[...], halo_bc[...], cpar_bc[...], keep, ext)
        active = total * sigmoid(total)
        bca_ref[...] = active
        bt[...] = active[:, :STATE].T.astype(BF16)
        dt = usable_rows(info) * softplus(rate[...] + hpar[0:1, :])
        log_decay = dt * -jnp.exp(hpar[1:2, :])
        dt_ref[...] = dt
        tri = lower_triangle()
        for q in range(2):
            rows = pl.ds(q * HALF, HALF)
            cum = exact_dot(tri, half(log_decay, q))
            cum_ref[rows, :] = cum
            tail[rows, :] = jnp.exp(cum[HALF - 1 :, :] - cum) * half(dt, q)

    total = conv_sum_of(mixed[...], halo[...], cpar[...], keep, ext)
    xa = total * sigmoid(total)
    xa_ref[...] = xa
    weighted = (xa * spread(rolled(tail[...], g))).astype(BF16)
    ends = rolled(cum_ref[...], g)
    end0, end1 = ends[HALF - 1 : HALF], ends[ROWS - 1 : ROWS]
    s0 = dot(bt[:, :HALF], half(weighted, 0))
    s1 = dot(bt[:, HALF:], half(weighted, 1))
    s0_ref[0] = s0
    state = (spread(jnp.exp(end1)) * s0 + s1).astype(BF16)
    damp = spread(jnp.exp(end0 + end1))
    high = damp.astype(BF16)
    low = (damp - high.astype(F32)).astype(BF16)
    row = row_of((16, BLOCK))
    damps = jnp.where(row == 0, high.astype(F32), low.astype(F32)).astype(BF16)
    for r in range(2):
        msg_ref[r, :STATE_HALF, :] = state[r * STATE_HALF : (r + 1) * STATE_HALF]
        msg_ref[r, STATE_HALF:, :] = damps


def state_call(info, mixed, halo, cpar, rate, hpar):
    bc_at = LOCAL // 256
    return pl.pallas_call(
        state_body,
        grid=(GROUPS,),
        out_shape=(
            shape((ROWS, LOCAL)),
            shape((ROWS, 256)),
            shape((ROWS, LANES)),
            shape((ROWS, LANES)),
            shape((GROUPS, STATE, BLOCK)),
            shape((CHUNKS, MESSAGE, BLOCK), BF16),
        ),
        in_specs=[
            SMEM,
            columns(ROWS, BLOCK),
            columns(16, BLOCK),
            columns(8, BLOCK),
            pl.BlockSpec((ROWS, 256), lambda g: (0, bc_at)),
            pl.BlockSpec((16, 256), lambda g: (0, bc_at)),
            pl.BlockSpec((8, 256), lambda g: (0, bc_at)),
            whole((ROWS, LANES)),
            whole((8, LANES)),
        ],
        out_specs=(
            columns(ROWS, BLOCK),
            whole((ROWS, 256)),
            whole((ROWS, LANES)),
            whole((ROWS, LANES)),
            grouped(STATE),
            MESSAGES,
        ),
        scratch_shapes=[
            pltpu.VMEM((ROWS + 32, BLOCK), F32),
            pltpu.VMEM((STATE, ROWS), BF16),
            pltpu.VMEM((ROWS, LANES), F32),
        ],
        compiler_params=params(),
        cost_estimate=pl.CostEstimate(
            flops=2 * ROWS * STATE * LOCAL, bytes_accessed=4_500_000, transcendentals=400_000
        ),
        name="conv_state",
    )(info, mixed, halo, cpar, mixed, halo, cpar, rate, hpar)


def inside_body(xa, bca, cum, dt, hpar, y_ref, cum_t, scores):
    g = pl.program_id(0)

    @pl.when(g == 0)
    def _():
        tri = lower_triangle()
        for q in range(2):
            b, c = half(bca[:, :STATE], q).astype(BF16), half(bca[:, STATE:], q).astype(BF16)
            scores[q] = dot_nt(c, b) * tri
            cum_t[:, q * HALF : (q + 1) * HALF] = half(cum[...], q).T

    cols = rolled(cum[...], g)
    rows = cum_t[pl.ds(pl.multiple_of(8 * g, 8), 8), :]
    steps = rolled(dt[...], g)
    skips = rolled(hpar[...], g)[2:3, :]
    low = lane_of((HALF, LANES)) < HEADDIM
    for q in range(2):
        for p in range(OWN // 2):
            lanes = slice(p * LANES, (p + 1) * LANES)
            x = xa[q * HALF : (q + 1) * HALF, lanes]
            xdt = x * pair_lanes(half(steps, q), p)
            both = jnp.concatenate([jnp.where(low, xdt, 0.0), jnp.where(low, 0.0, xdt)], axis=0)
            mats = []
            for i in (2 * p, 2 * p + 1):
                gap = half(cols, q)[:, i : i + 1] - rows[i : i + 1, q * HALF : (q + 1) * HALF]
                mats.append((jnp.exp(jnp.minimum(gap, 0.0)) * scores[q]).astype(BF16))
            y = dot(jnp.concatenate(mats, axis=1), both.astype(BF16))
            y_ref[q * HALF : (q + 1) * HALF, lanes] = y + x * pair_lanes(skips, p)


def inside_call(xa, bca, cum, dt, hpar):
    return pl.pallas_call(
        inside_body,
        grid=(GROUPS,),
        out_shape=shape((ROWS, LOCAL)),
        in_specs=[
            columns(ROWS, BLOCK),
            whole((ROWS, 256)),
            whole((ROWS, LANES)),
            whole((ROWS, LANES)),
            whole((8, LANES)),
        ],
        out_specs=columns(ROWS, BLOCK),
        scratch_shapes=[pltpu.VMEM((LANES, ROWS), F32), pltpu.VMEM((2, HALF, HALF), F32)],
        compiler_params=params(),
        cost_estimate=pl.CostEstimate(
            flops=2 * HEADS * HALF * HALF * LANES, bytes_accessed=3_300_000, transcendentals=800_000
        ),
        name="inside",
    )(xa, bca, cum, dt, hpar)


def scan_body(backward, info, msg, *rest):
    out_ref = rest[-1]
    carry = jnp.zeros((STATE_HALF, BLOCK), F32)
    for k in reversed(range(CHUNKS)) if backward else range(CHUNKS):
        keep = info[2 + k].astype(F32)
        if not backward:
            carry = carry * keep
        out_ref[k] = carry.astype(BF16)
        damps = msg[k, STATE_HALF:, :].astype(F32)
        carry = (damps[0:1] + damps[1:2]) * carry + msg[k, :STATE_HALF, :].astype(F32)
        if backward:
            carry = carry * keep


def scan_call(info, msg, backward, *tokens):
    return pl.pallas_call(
        functools.partial(scan_body, backward),
        out_shape=shape((CHUNKS, STATE_HALF, BLOCK), BF16),
        in_specs=[SMEM, whole((CHUNKS, MESSAGE, BLOCK))] + [ANYWHERE] * len(tokens),
        out_specs=whole((CHUNKS, STATE_HALF, BLOCK)),
        compiler_params=params(),
        name="chunk_scan",
    )(info, msg, *tokens)


def out_proj_body(weight, info, y_in, bca, cum, hin, s0, gate, gain, *rest):
    refs = len(weight.arrays)
    w_refs, (y_ref, part_ref, buffer, sems, sums, gained) = rest[:refs], rest[refs:]
    weight.start(w_refs, info, buffer, sems)
    c_all = bca[:, STATE:].astype(BF16)
    grow = jnp.exp(cum[...])
    sums[...] = jnp.zeros((ROWS, LANES), F32)

    def group(g, _):
        lanes = pl.ds(pl.multiple_of(g * BLOCK, LANES), BLOCK)
        factor = rolled(grow, g)
        first = hin[g]
        second = spread(factor[HALF - 1 : HALF]) * first.astype(F32) + s0[g]
        carried = jnp.concatenate(
            [dot(half(c_all, 0), first), dot(half(c_all, 1), second.astype(BF16))], axis=0
        )
        y = y_in[:, lanes] + spread(factor) * carried
        y_ref[:, lanes] = y
        z = gate[:, lanes]
        gated = y * z * sigmoid(z)
        square = gated * gated
        sums[...] += sum(square[:, i * LANES : (i + 1) * LANES] for i in range(BLOCK // LANES))
        gained[:, lanes] = (gated * gain[:, lanes]).astype(BF16)
        return 0

    lax.fori_loop(0, GROUPS, group, 0)
    part_ref[:, WIDTH:] = sums[...]
    weight.product(w_refs, info, gained, buffer, sems, part_ref)


def out_proj(info, y_in, bca, cum, hin, s0, gate, gain, weight):
    return pl.pallas_call(
        functools.partial(out_proj_body, weight),
        out_shape=(shape((ROWS, LOCAL)), shape((ROWS, WIDTH + LANES))),
        in_specs=[
            SMEM,
            whole((ROWS, LOCAL)),
            whole((ROWS, 256)),
            whole((ROWS, LANES)),
            whole((GROUPS, STATE, BLOCK)),
            whole((GROUPS, STATE, BLOCK)),
            whole((ROWS, LOCAL)),
            whole((1, LOCAL)),
        ]
        + weight.specs(),
        out_specs=(whole((ROWS, LOCAL)), whole((ROWS, WIDTH + LANES))),
        scratch_shapes=weight.scratch()
        + [pltpu.VMEM((ROWS, LANES), F32), pltpu.VMEM((ROWS, LOCAL), BF16)],
        compiler_params=params(),
        cost_estimate=pl.CostEstimate(
            flops=2 * ROWS * WIDTH * LOCAL, bytes_accessed=13_000_000, transcendentals=800_000
        ),
        name="out_proj",
    )(info, y_in, bca, cum, hin, s0, gate, gain, *weight.arrays)


def join_body(info, h_ref, own, came, res_ref, branch_ref, scale_ref):
    squares = jnp.sum(own[:, WIDTH:] + came[:, WIDTH:], axis=1, keepdims=True)
    scale = lax.rsqrt(squares / INNER + EPSILON)
    branch = scale * (own[:, :WIDTH] + came[:, :WIDTH])
    branch_ref[...] = branch.astype(BF16)
    scale_ref[...] = jnp.broadcast_to(scale, (HALF // 2, LANES))
    first = pl.program_id(0) * (HALF // 2)
    usable = (row_of((HALF // 2, 1)) + first < info[0]).astype(F32)
    result = h_ref[...].astype(F32) + usable * branch
    res_ref[...] = result.astype(res_ref.dtype)


def join(info, h, own, came, kind):
    def rows(width):
        return pl.BlockSpec((HALF // 2, width), lambda i: (i, 0))

    return pl.pallas_call(
        join_body,
        grid=(4,),
        out_shape=(shape((ROWS, WIDTH), kind), shape((ROWS, WIDTH), BF16), shape((ROWS, LANES))),
        in_specs=[SMEM, rows(WIDTH), rows(WIDTH + LANES), rows(WIDTH + LANES)],
        out_specs=(rows(WIDTH), rows(WIDTH), rows(LANES)),
        compiler_params=params(),
        cost_estimate=pl.CostEstimate(flops=2_000_000, bytes_accessed=8_000_000, transcendentals=0),
        name="join",
    )(info, h, own, came)


def gate_back_body(weight, info, cot, y, gate, gain, branch, scale_ref, *rest):
    refs = len(weight.arrays)
    w_refs, rest = rest[:refs], rest[refs:]
    bg_ref, dy_ref, dz_ref, grad_ref, dgain_ref, buffer, sems, inner_ref = rest
    b = pl.program_id(0)
    scale = scale_ref[:, :1]

    @pl.when(b == 0)
    def _():
        weight.start(w_refs, info, buffer, sems)
        bg = (usable_rows(info) * cot[...].astype(F32)).astype(BF16)
        bg_ref[...] = bg
        inner = jnp.sum(bg.astype(F32) * branch[...].astype(F32), axis=1, keepdims=True)
        inner_ref[...] = jnp.broadcast_to(inner * scale * scale / INNER, (ROWS, LANES))
        for n in range(4):
            weight.wait(w_refs, info, n, buffer, sems)

    inner = inner_ref[:, :1]
    bg = bg_ref[...]
    d_norms = dot_nt(bg, buffer[pl.ds(pl.multiple_of(b * SHARD, SHARD), SHARD), :])
    norms = []
    for i in range(SHARD // LANES):
        lanes = slice(i * LANES, (i + 1) * LANES)
        z = gate[:, lanes]
        sig = sigmoid(z)
        silu = z * sig
        y_here = y[:, lanes]
        gated = y_here * silu
        d_norm = d_norms[:, lanes]
        gained = scale * gain[:, lanes]
        norms.append((gated * gained).astype(BF16))
        d_gated = d_norm * gained - gated * inner
        total = jnp.sum(d_norm * gated * scale, axis=0, keepdims=True)
        dgain_ref[:, lanes] = jnp.broadcast_to(total, (8, LANES))
        dy_ref[:, lanes] = (d_gated * silu).astype(BF16)
        dz_ref[:, lanes] = (d_gated * y_here * sig * (1.0 + z * (1.0 - sig))).astype(BF16)
    norm = jnp.concatenate(norms, axis=1)
    grad_ref[...] = dot(norm.T, bg).astype(BF16) if grad_ref.shape[1] == WIDTH else norm.T


def gate_back(info, cot, y, gate, gain, branch, scale, weight, with_grad):
    wide, local = whole((ROWS, WIDTH)), columns(ROWS, SHARD)
    grad_width = WIDTH if with_grad else ROWS
    return pl.pallas_call(
        functools.partial(gate_back_body, weight),
        grid=(4,),
        out_shape=(
            shape((ROWS, WIDTH), BF16),
            shape((ROWS, LOCAL), BF16),
            shape((ROWS, LOCAL), BF16),
            shape((LOCAL, grad_width), BF16),
            shape((8, LOCAL)),
        ),
        in_specs=[SMEM, wide, local, local, columns(1, SHARD), wide, whole((ROWS, LANES))]
        + weight.specs(),
        out_specs=(
            wide,
            local,
            local,
            pl.BlockSpec((SHARD, grad_width), lambda b: (b, 0)),
            columns(8, SHARD),
        ),
        scratch_shapes=weight.scratch() + [pltpu.VMEM((ROWS, LANES), F32)],
        compiler_params=params(),
        cost_estimate=pl.CostEstimate(
            flops=4 * ROWS * WIDTH * LOCAL, bytes_accessed=17_000_000, transcendentals=800_000
        ),
        name="gate_back",
    )(info, cot, y, gate, gain, branch, scale, *weight.arrays)


def own_grad_body(dy, bca, cum, msg_in, dz, normed, own1_ref, msg_ref, grad_ref, ct, grow):
    g = pl.program_id(0)
    grad_ref[...] = dot(normed[...].T, dz[...]).astype(BF16)

    @pl.when(g == 0)
    def _():
        ct[...] = bca[:, STATE:].T.astype(BF16)
        grow[...] = jnp.exp(cum[...])

    factor = rolled(grow[...], g)
    weighted = (dy[...].astype(F32) * spread(factor)).astype(BF16)
    own0 = dot(ct[:, :HALF], half(weighted, 0))
    own1 = dot(ct[:, HALF:], half(weighted, 1))
    own1_ref[0] = own1
    grad = (spread(factor[HALF - 1 : HALF]) * own1 + own0).astype(BF16)
    for r in range(2):
        msg_ref[r, :STATE_HALF, :] = grad[r * STATE_HALF : (r + 1) * STATE_HALF]
        msg_ref[r, STATE_HALF:, :] = msg_in[r, STATE_HALF:, :]


def own_grad(dy, bca, cum, msg, dz, normed):
    return pl.pallas_call(
        own_grad_body,
        grid=(GROUPS,),
        out_shape=(
            shape((GROUPS, STATE, BLOCK)),
            shape((CHUNKS, MESSAGE, BLOCK), BF16),
            shape((WIDTH, LOCAL), BF16),
        ),
        in_specs=[
            columns(ROWS, BLOCK),
            whole((ROWS, 256)),
            whole((ROWS, LANES)),
            MESSAGES,
            whole((ROWS, LOCAL)),
            columns(ROWS, SHARD),
        ],
        out_specs=(grouped(STATE), MESSAGES, pl.BlockSpec((SHARD, LOCAL), lambda b: (b, 0))),
        scratch_shapes=[pltpu.VMEM((STATE, ROWS), BF16), pltpu.VMEM((ROWS, LANES), F32)],
        compiler_params=params(),
        cost_estimate=pl.CostEstimate(
            flops=2 * ROWS * WIDTH * LOCAL, bytes_accessed=8_000_000, transcendentals=0
        ),
        name="own_grad",
    )(dy, bca, cum, msg, dz, normed)


def inside_back_body(
    dy, xa, bca, cum, dt, hpar,
    dx_ref, dskip_ref, gsum_ref, u_ref, dbc_ref, cum_t, scores, dscores,
):
    g = pl.program_id(0)

    @pl.when(g == 0)
    def _():
        tri = lower_triangle()
        for q in range(2):
            b, c = half(bca[:, :STATE], q).astype(BF16), half(bca[:, STATE:], q).astype(BF16)
            scores[q] = dot_nt(b, c) * tri.T
            cum_t[:, q * HALF : (q + 1) * HALF] = half(cum[...], q).T
        dscores[...] = jnp.zeros((2, HALF, HALF), F32)
        u_ref[...] = jnp.zeros((ROWS, LANES), F32)

    cols = rolled(cum[...], g)
    rows = cum_t[pl.ds(pl.multiple_of(8 * g, 8), 8), :]
    steps = rolled(dt[...], g)
    skips = rolled(hpar[...], g)[2:3, :]
    low = lane_of((HALF, LANES)) < HEADDIM
    lane = lane_of((HALF, LANES))
    gsum_ref[...] = jnp.zeros((8, ROWS), F32)
    for q in range(2):
        here = slice(q * HALF, (q + 1) * HALF)
        u_here = u_ref[here, :]
        for p in range(OWN // 2):
            lanes = slice(p * LANES, (p + 1) * LANES)
            dy_pair = dy[here, lanes]
            x = xa[here, lanes]
            zero = jnp.zeros_like(dy_pair)
            both = jnp.concatenate(
                [jnp.where(low, dy_pair, zero), jnp.where(low, zero, dy_pair)], axis=0
            )
            dw = dot_nt(x.astype(BF16), both)
            mats = []
            for n, i in enumerate((2 * p, 2 * p + 1)):
                gap = rows[i : i + 1, here] - half(cols, q)[:, i : i + 1]
                decay = jnp.exp(jnp.minimum(gap, 0.0))
                step = half(steps, q)[:, i : i + 1]
                weight = decay * scores[q]
                mats.append(weight.astype(BF16))
                dw_here = dw[:, n * HALF : (n + 1) * HALF]
                dscores[q] += decay * dw_here * step
                direct = weight * dw_here
                total = jnp.sum(direct, axis=1, keepdims=True)
                u_here = jnp.where(lane == 8 * g + i, total, u_here)
                gsum_ref[i : i + 1, here] = jnp.sum(direct * step, axis=0, keepdims=True)
            dx = dot(jnp.concatenate(mats, axis=1), both)
            dy_wide = dy_pair.astype(F32)
            dx_ref[here, lanes] = dx * pair_lanes(half(steps, q), p) + dy_wide * pair_lanes(skips, p)
            skip_sum = jnp.sum(dy_wide * x, axis=0, keepdims=True)
            if q == 0:
                dskip_ref[:, lanes] = jnp.broadcast_to(skip_sum, (8, LANES))
            else:
                dskip_ref[:, lanes] += skip_sum
        u_ref[here, :] = u_here

    @pl.when(g == GROUPS - 1)
    def _():
        tri = lower_triangle()
        for q in range(2):
            b, c = half(bca[:, :STATE], q).astype(BF16), half(bca[:, STATE:], q).astype(BF16)
            ds_t = dscores[q] * tri.T
            dbc_ref[q * HALF : (q + 1) * HALF, :STATE] = dot(ds_t.astype(BF16), c)
            dbc_ref[q * HALF : (q + 1) * HALF, STATE:] = dot(ds_t.T.astype(BF16), b)


def inside_back(dy, xa, bca, cum, dt, hpar):
    return pl.pallas_call(
        inside_back_body,
        grid=(GROUPS,),
        out_shape=(
            shape((ROWS, LOCAL)),
            shape((8, LOCAL)),
            shape((8 * GROUPS, ROWS)),
            shape((ROWS, LANES)),
            shape((ROWS, 256)),
        ),
        in_specs=[
            columns(ROWS, BLOCK),
            columns(ROWS, BLOCK),
            whole((ROWS, 256)),
            whole((ROWS, LANES)),
            whole((ROWS, LANES)),
            whole((8, LANES)),
        ],
        out_specs=(
            columns(ROWS, BLOCK),
            columns(8, BLOCK),
            pl.BlockSpec((8, ROWS), lambda g: (g, 0)),
            whole((ROWS, LANES)),
            whole((ROWS, 256)),
        ),
        scratch_shapes=[
            pltpu.VMEM((LANES, ROWS), F32),
            pltpu.VMEM((2, HALF, HALF), F32),
            pltpu.VMEM((2, HALF, HALF), F32),
        ],
        compiler_params=params(),
        cost_estimate=pl.CostEstimate(
            flops=4 * HEADS * HALF * HALF * LANES, bytes_accessed=4_500_000, transcendentals=800_000
        ),
        name="inside_back",
    )(dy, xa, bca, cum, dt, hpar)


def conv_back(d_active, values, halo, cpar, keep, ext, ext_d):
    width = values.shape[1]
    total = conv_sum_of(values, halo, cpar, keep, ext)
    sig = sigmoid(total)
    d_sum = d_active * sig * (1.0 + total * (1.0 - sig))
    ext_d[0:16, :width] = jnp.zeros((16, width), F32)
    ext_d[16 : 16 + ROWS, :width] = d_sum
    ext_d[16 + ROWS :, :width] = jnp.zeros((16, width), F32)
    d_in = jnp.zeros((ROWS + 16, width), F32)
    for k in range(KERNEL):
        d_in = d_in + cpar[k : k + 1, :] * ext_d[3 - k : 3 - k + ROWS + 16, :width]
    row = row_of((8, width))
    d_par = jnp.where(row == 4, jnp.sum(d_sum, axis=0, keepdims=True), 0.0)
    for k in range(KERNEL):
        tap = jnp.sum(d_sum * ext[13 + k : 13 + k + ROWS, :width], axis=0, keepdims=True)
        d_par = jnp.where(row == k, tap, d_par)
    return d_in, d_par


def finish_body(
    info, xa, dxi, dy, mixed, halo, cpar, bc, halo_bc, cpar_bc, bca, cum, dt, rate, hpar, lam, hin, s0, own1, u, gsum, dbc,
    dmx_ref, dmbc_ref, tailx_ref, tailbc_ref, edgex_ref, edgebc_ref, dcx_ref, dcbc_ref, dhead_ref,
    ext, ext_d, grow, tail, v_sum, q_sum, end_sum, dbc_sum,
):
    g = pl.program_id(0)
    keep = info[1].astype(F32)

    @pl.when(g == 0)
    def _():
        grow[...] = jnp.exp(cum[...])
        for q in range(2):
            here = half(cum[...], q)
            tail[q * HALF : (q + 1) * HALF, :] = jnp.exp(here[HALF - 1 :, :] - here)
        v_sum[...] = jnp.zeros((ROWS, LANES), F32)
        q_sum[...] = jnp.zeros((ROWS, LANES), F32)
        end_sum[...] = jnp.zeros((16, LANES), F32)
        dbc_sum[...] = dbc[...]

    sums = head_sum_matrix(g)
    factor = rolled(grow[...], g)
    tails = rolled(tail[...], g)
    steps = rolled(dt[...], g)
    ends = [spread(factor[HALF - 1 : HALF]), spread(factor[ROWS - 1 : ROWS])]
    lam1 = lam[0].astype(F32)
    lams = [ends[1] * lam1 + own1[0], lam1]
    first = hin[0].astype(F32)
    states = [first, ends[0] * first + s0[0]]
    d_x = []
    for q in range(2):
        here = slice(q * HALF, (q + 1) * HALF)
        b, c = bca[here, :STATE].astype(BF16), bca[here, STATE:].astype(BF16)
        lam_q, state_q = lams[q].astype(BF16), states[q].astype(BF16)
        tail_wide = spread(half(tails, q))
        tail_step = tail_wide * spread(half(steps, q))
        x, dy_q = xa[here, :], dy[here, :].astype(F32)
        lb = dot(b, lam_q) * tail_wide
        d_x.append(dxi[here, :] + lb * spread(half(steps, q)))
        v_sum[here, :] += dot((x * lb).astype(BF16), sums)
        grow_wide = spread(half(factor, q))
        dy_grow = (dy_q * grow_wide).astype(BF16)
        carried = dot(c, state_q)
        q_sum[here, :] += dot((dy_q * grow_wide * carried).astype(BF16), sums)
        dbc_sum[here, :STATE] += dot_nt((x * tail_step).astype(BF16), lam_q)
        dbc_sum[here, STATE:] += dot_nt(dy_grow, state_q)
        last = jnp.sum(lams[q] * states[q], axis=0, keepdims=True) * ends[q]
        high = last.astype(BF16).astype(F32)
        both = jnp.where(row_of((16, BLOCK)) == 0, high, last - high).astype(BF16)
        both = dot(both, sums)
        end_sum[8 * q : 8 * q + 8, :] += both[0:1] + both[1:2]
    d_in, d_par = conv_back(
        jnp.concatenate(d_x, axis=0), mixed[...], halo[...], cpar[...], keep, ext, ext_d
    )
    dmx_ref[...] = d_in[16:].astype(BF16)
    tailx_ref[...] = d_in[ROWS:]
    edgex_ref[...] = (d_in[:16] * keep).astype(BF16)
    dcx_ref[...] = d_par

    @pl.when(g == GROUPS - 1)
    def _():
        d_bc, d_par_bc = conv_back(
            dbc_sum[...], bc[...], halo_bc[...], cpar_bc[...], keep, ext, ext_d
        )
        dmbc_ref[:, :256] = d_bc[16:].astype(BF16)
        tailbc_ref[...] = d_bc[ROWS:]
        edgebc_ref[...] = (d_bc[:16] * keep).astype(BF16)
        dcbc_ref[...] = d_par_bc
        rates = -jnp.exp(hpar[1:2, :])
        logit = rate[...] + hpar[0:1, :]
        upper = lower_triangle().T
        before = lower_triangle(True)
        d_bias = jnp.zeros((1, LANES), F32)
        d_log = jnp.zeros((1, LANES), F32)
        usable = usable_rows(info)
        for q in range(2):
            here = slice(q * HALF, (q + 1) * HALF)
            step = dt[here, :]
            gs = gsum[...][:, here].T
            gs = jnp.concatenate([gs, jnp.zeros((HALF, LANES - 8 * GROUPS), F32)], axis=1)
            d_decay = exact_dot(upper, gs - step * u[here, :] + q_sum[here, :])
            d_decay = d_decay + exact_dot(before, step * v_sum[here, :])
            d_decay = d_decay + end_sum[8 * q : 8 * q + 1, :]
            d_step = u[here, :] + v_sum[here, :] + rates * d_decay
            d_rate = half(usable, q) * d_step * sigmoid(half(logit, q))
            d_bias += jnp.sum(d_rate, axis=0, keepdims=True)
            d_log += jnp.sum(d_decay * step * rates, axis=0, keepdims=True)
            dmbc_ref[here, 256:] = d_rate.astype(BF16)
        row = row_of((8, LANES))
        dhead_ref[...] = jnp.where(row == 0, d_bias, jnp.where(row == 1, d_log, 0.0))


def finish_call(
    info, xa, dxi, dy, mixed, halo, cpar, bca, cum, dt, rate, hpar, lam, hin, s0, own1, u, gsum, dbc
):
    bc_at = LOCAL // 256
    wide = whole((ROWS, LANES))
    return pl.pallas_call(
        finish_body,
        grid=(GROUPS,),
        out_shape=(
            shape((ROWS, LOCAL), BF16),
            shape((ROWS, 384), BF16),
            shape((16, LOCAL)),
            shape((16, 256)),
            shape((16, LOCAL), BF16),
            shape((16, 256), BF16),
            shape((8, LOCAL)),
            shape((8, 256)),
            shape((8, LANES)),
        ),
        in_specs=[
            SMEM,
            columns(ROWS, BLOCK),
            columns(ROWS, BLOCK),
            columns(ROWS, BLOCK),
            columns(ROWS, BLOCK),
            columns(16, BLOCK),
            columns(8, BLOCK),
            pl.BlockSpec((ROWS, 256), lambda g: (0, bc_at)),
            pl.BlockSpec((16, 256), lambda g: (0, bc_at)),
            pl.BlockSpec((8, 256), lambda g: (0, bc_at)),
            whole((ROWS, 256)),
            wide,
            wide,
            wide,
            whole((8, LANES)),
            grouped(STATE),
            grouped(STATE),
            grouped(STATE),
            grouped(STATE),
            wide,
            whole((8 * GROUPS, ROWS)),
            whole((ROWS, 256)),
        ],
        out_specs=(
            columns(ROWS, BLOCK),
            whole((ROWS, 384)),
            columns(16, BLOCK),
            whole((16, 256)),
            columns(16, BLOCK),
            whole((16, 256)),
            columns(8, BLOCK),
            whole((8, 256)),
            whole((8, LANES)),
        ),
        scratch_shapes=[
            pltpu.VMEM((ROWS + 32, BLOCK), F32),
            pltpu.VMEM((ROWS + 32, BLOCK), F32),
            pltpu.VMEM((ROWS, LANES), F32),
            pltpu.VMEM((ROWS, LANES), F32),
            pltpu.VMEM((ROWS, LANES), F32),
            pltpu.VMEM((ROWS, LANES), F32),
            pltpu.VMEM((16, LANES), F32),
            pltpu.VMEM((ROWS, 256), F32),
        ],
        compiler_params=params(),
        cost_estimate=pl.CostEstimate(
            flops=10 * ROWS * STATE * LOCAL, bytes_accessed=7_500_000, transcendentals=800_000
        ),
        name="finish_back",
    )(
        info, xa, dxi, dy, mixed, halo, cpar, mixed, halo, cpar, bca, cum, dt, rate, hpar,
        lam, hin, s0, own1, u, gsum, dbc,
    )


def gate_in_back_body(weight, info, dz, token, *rest):
    refs = len(weight.arrays)
    w_refs, (out_ref, buffer, sems) = rest[:refs], rest[refs:]

    @pl.when(pl.program_id(0) == 0)
    def _():
        weight.start(w_refs, info, buffer, sems)
        for n in range(4):
            weight.wait(w_refs, info, n, buffer, sems)

    rows = pl.ds(pl.multiple_of(pl.program_id(0) * SHARD, SHARD), SHARD)
    out_ref[...] = dot_nt(dz[...], buffer[rows, :])


def gate_in_back(info, dz, weight, token):
    return pl.pallas_call(
        functools.partial(gate_in_back_body, weight),
        grid=(4,),
        out_shape=shape((ROWS, WIDTH)),
        in_specs=[SMEM, whole((ROWS, LOCAL)), ANYWHERE] + weight.specs(),
        out_specs=columns(ROWS, SHARD),
        scratch_shapes=weight.scratch(),
        compiler_params=params(),
        cost_estimate=pl.CostEstimate(
            flops=2 * ROWS * WIDTH * LOCAL, bytes_accessed=7_000_000, transcendentals=0
        ),
        name="gate_in_back",
    )(info, dz, token, *weight.arrays)


def patch_body(dmx, dmbc, tailx, tailbc, edge, token, dxc_ref):
    dxc_ref[:, :LOCAL] = dmx[...]
    dxc_ref[:, LOCAL:] = dmbc[...]
    late = edge[...].astype(F32)
    dxc_ref[ROWS - 16 :, :LOCAL] = (tailx[...] + late[:, :LOCAL]).astype(BF16)
    dxc_ref[ROWS - 16 :, LOCAL:MIXED] = (tailbc[...] + late[:, LOCAL:]).astype(BF16)


def patch(dmx, dmbc, tailx, tailbc, edge, token):
    arrays = (dmx, dmbc, tailx, tailbc, edge)
    return pl.pallas_call(
        patch_body,
        out_shape=shape((ROWS, PACKED), BF16),
        in_specs=[whole(v.shape) for v in arrays] + [ANYWHERE],
        out_specs=whole((ROWS, PACKED)),
        compiler_params=params(),
        cost_estimate=pl.CostEstimate(flops=100_000, bytes_accessed=2_000_000, transcendentals=0),
        name="patch",
    )(*arrays, token)


def mixed_back_body(weight, tokens, info, dxc, part, h_ref, normed, *rest):
    refs = len(weight.arrays)
    w_refs, rest = rest[:refs], rest[refs + tokens :]
    (out_ref, dgain_ref, *grad_ref), (buffer, sems, scale_ref) = rest[:-3], rest[-3:]
    b = pl.program_id(0)
    block = pl.ds(pl.multiple_of(b * SHARD, SHARD), SHARD)

    @pl.when(b == 0)
    def _():
        weight.start(w_refs, info, buffer, sems)
        h = h_ref[...].astype(F32)
        scale = lax.rsqrt(jnp.mean(h * h, axis=1, keepdims=True) + EPSILON)
        scale_ref[...] = jnp.broadcast_to(scale, (ROWS, LANES))

    for ref in grad_ref:
        ref[...] = dot(normed[...].T, dxc[...]).astype(BF16)

    @pl.when(b == 0)
    def _():
        for n in range(4):
            weight.wait(w_refs, info, n, buffer, sems)

    d_norm = part[...] + dot_nt(dxc[...], buffer[block, :])
    out_ref[...] = d_norm
    total = jnp.sum(d_norm * h_ref[:, block].astype(F32) * scale_ref[:, :1], axis=0, keepdims=True)
    dgain_ref[...] = jnp.broadcast_to(total, (8, SHARD))


def mixed_back(info, dxc, part, h, normed, weight, with_grad, tokens):
    wide, local = whole((ROWS, WIDTH)), columns(ROWS, SHARD)
    outs = [shape((ROWS, WIDTH)), shape((8, WIDTH))]
    specs = [local, columns(8, SHARD)]
    if with_grad:
        outs.append(shape((WIDTH, PACKED), BF16))
        specs.append(pl.BlockSpec((SHARD, PACKED), lambda b: (b, 0)))
    return pl.pallas_call(
        functools.partial(mixed_back_body, weight, len(tokens)),
        grid=(4,),
        out_shape=outs,
        in_specs=[SMEM, whole((ROWS, PACKED)), local, wide, local]
        + weight.specs()
        + [ANYWHERE] * len(tokens),
        out_specs=specs,
        scratch_shapes=weight.scratch() + [pltpu.VMEM((ROWS, LANES), F32)],
        compiler_params=params(),
        cost_estimate=pl.CostEstimate(
            flops=4 * ROWS * WIDTH * PACKED, bytes_accessed=14_000_000, transcendentals=0
        ),
        name="mixed_back",
    )(info, dxc, part, h, normed, *weight.arrays, *tokens)


def norm_back_body(own, came, h_ref, cot, gain, dh_ref, low_ref):
    h = h_ref[...].astype(F32)
    scale = lax.rsqrt(jnp.mean(h * h, axis=1, keepdims=True) + EPSILON)
    d_norm = own[...] + came[...]
    inner = jnp.mean(d_norm * gain[...] * h, axis=1, keepdims=True) * scale * scale * scale
    dh = cot[...].astype(F32) + scale * d_norm * gain[...] - h * inner
    dh_ref[...] = dh
    low_ref[...] = dh.astype(BF16)


def norm_back(own, came, h, cot, gain):
    rows = pl.BlockSpec((HALF // 2, WIDTH), lambda i: (i, 0))
    return pl.pallas_call(
        norm_back_body,
        grid=(4,),
        out_shape=(shape((ROWS, WIDTH)), shape((ROWS, WIDTH), BF16)),
        in_specs=[rows] * 4 + [whole((1, WIDTH))],
        out_specs=(rows, rows),
        compiler_params=params(),
        cost_estimate=pl.CostEstimate(flops=3_000_000, bytes_accessed=8_000_000, transcendentals=0),
        name="norm_back",
    )(own, came, h, cot, gain)


def z_shift(r):
    return "dp", [(z, (z + r) % 4) for z in range(4)]


def y_shift(r):
    return "ctx", [(j, (j + 4 * r) % 16) for j in range(16)]


def x_shift(r):
    return "ctx", [(j, j - j % 4 + (j + r) % 4) for j in range(16)]


SHIFTS = {"z": z_shift, "y": y_shift, "x": x_shift}


def send(value, axis, r):
    name, pairs = SHIFTS[axis](r % 4)
    return lax.ppermute(value, name, pairs)


def swapped(value):
    return lax.ppermute(value, "section", [(0, 1), (1, 0)])


def nothing_body(*refs):
    refs[-1][...] = jnp.zeros((8, LANES), jnp.int32)


def after(values, place):
    nothing = pl.pallas_call(
        nothing_body,
        out_shape=shape((8, LANES), jnp.int32),
        in_specs=[ANYWHERE] * len(values),
        out_specs=whole((8, LANES)),
        compiler_params=params(),
        cost_estimate=pl.CostEstimate(flops=0, bytes_accessed=4096, transcendentals=0),
        name="after",
    )(*values)[0, 0]
    return {axis: n + nothing for axis, n in place.items()}


def fetched(mine, came, layer, section, place):
    rows = SHARD // 2

    def piece(source, side, axis):
        return lax.dynamic_slice_in_dim(source, side * rows + place[axis] * PIECE, PIECE, 0)

    parts = [
        jnp.where(section == layer, piece(mine, side, axis), piece(came, side, axis))
        for side, axis in enumerate("xy")
    ]
    if mine.shape[0] == TALL:
        parts.append(jnp.where(section == layer, mine[SHARD:], came[SHARD:]))
    return jnp.concatenate(parts)


def pieces(mine, came, got, late):
    out = [mine, came]
    for side, axis in enumerate("xy"):
        rows = slice(side * PIECE, (side + 1) * PIECE)
        stack = jnp.concatenate(
            [lax.dynamic_slice_in_dim(g, rows.start + late, PIECE, 0) for g in got[1:]]
        )
        out += [stack] + [send(stack, axis, -r) for r in range(1, 4)]
    return out


def summed(terms):
    a, b, c, d = (t.astype(F32) for t in terms)
    return (a + c) + (b + d)


def arrived(terms, axis):
    return [terms[0]] + [send(terms[r], axis, r) for r in range(1, 4)]


def terms_body(axis, cuts, stacked, info, *rest):
    factors, rest = rest[: 2 * len(cuts)], rest[2 * len(cuts) :]
    small, outs, total = rest[:-2] if stacked else rest[:-5], rest[-5:-1], rest[-1]
    column = 0
    for n, cols in enumerate(cuts):
        there = slice(column, column + cols.stop - cols.start)
        total[:, there] = dot(factors[2 * n][...], factors[2 * n + 1][:, cols])
        column = there.stop
    count = 96 if axis == "y" else 24
    starts = [z * SHARD for z in range(4)]
    if axis == "x":
        starts = [start + y * 96 for start in starts for y in range(4)]
    for r in range(4):
        first = r * count
        if not stacked:
            first = lax.rem(info[11 if axis == "y" else 12] + r, 4) * count
        parts = [total[pl.ds(pl.multiple_of(start + first, 8), count), :] for start in starts]
        out = rest[-2].at[r] if stacked else outs[r]
        out[:SHARD, :] = jnp.concatenate(parts, axis=0).astype(BF16)
        for ref in small:
            out[SHARD:, :] = ref[...]


def four(dims, stacked):
    if stacked:
        return shape((4, *dims), BF16), whole((4, *dims))
    return [shape(dims, BF16)] * 4, [whole(dims)] * 4


def terms(info, axis, products, small=(), stacked=False):
    cuts = [cols for _, _, cols in products]
    width = sum(cols.stop - cols.start for cols in cuts)
    rows = SHARD + sum(v.shape[0] for v in small)
    arrays = [v for left, right, _ in products for v in (left, right)] + list(small)
    outs, specs = four((rows, width), stacked)
    return pl.pallas_call(
        functools.partial(terms_body, axis, cuts, stacked),
        out_shape=outs,
        in_specs=[SMEM] + [whole(v.shape) for v in arrays],
        out_specs=specs,
        scratch_shapes=[pltpu.VMEM((4 * SHARD, width), F32)],
        compiler_params=params(),
        cost_estimate=pl.CostEstimate(
            flops=8 * SHARD * ROWS * width, bytes_accessed=8_000_000, transcendentals=0
        ),
        name="terms",
    )(info, *arrays)


def fold_body(slot, counts, outer, inner, rest_rows, stacked, info, *rest):
    refs, outs, total = rest[: sum(counts)], rest[sum(counts) + 1 : -1], rest[-1]
    column = 0
    for count in counts:
        arrays, refs = refs[:count], refs[count:]
        cols = slice(column, column + arrays[0].shape[-1])
        if count == 4:
            total[:, cols] = summed([a[...] for a in arrays])
        elif len(arrays[0].shape) == 3:
            total[:, cols] = summed([arrays[0][n] for n in range(4)])
        else:
            total[:, cols] = arrays[0][...].astype(F32)
        column = cols.stop
    for r in range(4):
        first = r * inner if stacked else lax.rem(info[slot] + r, 4) * inner
        parts = [
            total[pl.ds(pl.multiple_of(n * 4 * inner + first, 8), inner), :] for n in range(outer)
        ]
        if rest_rows:
            parts.append(total[4 * outer * inner :, :])
        out = outs[0].at[r] if stacked else outs[r]
        out[...] = jnp.concatenate(parts, axis=0).astype(BF16)


def fold(info, axis, groups, outer, inner, token, stacked=False):
    slot = 10 + "zyx".index(axis)
    arrays = [a for group in groups for a in group]
    rows, width = arrays[0].shape[-2], sum(group[0].shape[-1] for group in groups)
    more = rows - 4 * outer * inner
    outs, specs = four((outer * inner + more, width), stacked)
    counts = [len(group) for group in groups]
    return pl.pallas_call(
        functools.partial(fold_body, slot, counts, outer, inner, more, stacked),
        out_shape=outs,
        in_specs=[SMEM] + [whole(a.shape) for a in arrays] + [ANYWHERE],
        out_specs=specs,
        scratch_shapes=[pltpu.VMEM((rows, width), F32)],
        compiler_params=params(),
        cost_estimate=pl.CostEstimate(flops=2_000_000, bytes_accessed=8_000_000, transcendentals=0),
        name="fold",
    )(info, *arrays, token)


def last_fold_body(info, *rest):
    left, right, outs, total = rest[:4], rest[4:8], rest[9:13], rest[13]
    width = left[0].shape[1]
    total[:96, :width] = summed([a[...] for a in left])
    total[96:, :width] = jnp.zeros((SMALL, width), F32)
    total[:, width:] = summed([a[...] for a in right])
    for r in range(4):
        first = pl.multiple_of(lax.rem(info[10] + r, 4) * 24, 8)
        parts = [total[pl.ds(first, 24), :], total[96:, :]]
        outs[r][...] = jnp.concatenate(parts, axis=0).astype(BF16)


def last_fold(info, left, right, token):
    width = left[0].shape[1] + right[0].shape[1]
    out = shape((24 + SMALL, width), BF16)
    arrays = (*left, *right)
    return pl.pallas_call(
        last_fold_body,
        out_shape=[out] * 4,
        in_specs=[SMEM] + [whole(a.shape) for a in arrays] + [ANYWHERE],
        out_specs=[whole(out.shape)] * 4,
        scratch_shapes=[pltpu.VMEM((96 + SMALL, width), F32)],
        compiler_params=params(),
        cost_estimate=pl.CostEstimate(flops=500_000, bytes_accessed=2_000_000, transcendentals=0),
        name="last_fold",
    )(info, *arrays, token)


PARITY = [[j for j in range(16) if j % 2 == e] for e in range(2)]
NEIGHBOURS = [(j, j ^ 1) for j in range(16)]
GROUPS_OF = {
    "y": [[4 * y + x for y in range(4)] for x in range(4)],
    "x": [[4 * y + x for x in range(4)] for y in range(4)],
}


def traded(value, axis):
    return lax.all_to_all(value, "ctx", 0, 0, axis_index_groups=GROUPS_OF[axis])


def exchange(value):
    return lax.all_to_all(value, "ctx", 0, 0, axis_index_groups=PARITY)


def halo_shift(value, step):
    pairs = [(j, j + 2 * step) for j in range(16) if 0 <= j + 2 * step < 16]
    return lax.ppermute(value, "ctx", pairs)


def halves(values, section):
    grid = values.reshape(values.shape[0], GROUPS, 2, -1)
    size = values.shape[1] // 2
    return [
        lax.dynamic_index_in_dim(grid, i, 2, False).reshape(-1, size)
        for i in (section, 1 - section)
    ]


def turns(low, high):
    rows = low.shape[0]
    parts = [v.reshape(rows, GROUPS, 1, -1) for v in (low, high)]
    return jnp.concatenate(parts, axis=2).reshape(rows, -1)


def pick_x_body(info, x_ref, dt_ref, *rest):
    smalls, outs, small = rest[:7], rest[7:9], rest[9]
    small[...] = jnp.zeros((16, PACKED), F32)
    row = 0
    for ref in smalls[:4]:
        count, width = ref.shape
        small[row : row + count, :width] = ref[...].astype(F32)
        row += count
    for ref in smalls[4:]:
        left = ref[...]
        for _ in range(3):
            part = left.astype(BF16).astype(F32)
            small[row : row + 1, :HEADS] = part
            left = left - part
            row += 1
    head, lane = row_of((HEADS, LANES)), lane_of((HEADS, LANES))
    for out, side in zip(outs, (info[0], 1 - info[0]), strict=True):
        for d in range(GROUPS):
            cols = pl.ds(pl.multiple_of((2 * d + side) * BLOCK, LANES), BLOCK)
            out[:SHARD, d * BLOCK : (d + 1) * BLOCK] = x_ref[:, cols]
        out[:SHARD, LOCAL:MIXED] = x_ref[:, INNER:]
        here = (head // OWN == 2 * (lane // 8) + side) & (head % OWN == lane % 8)
        out[:SHARD, MIXED:] = dot(dt_ref[...], here.astype(BF16)).astype(BF16)
        out[SHARD:, :] = small[...].astype(BF16)


def pick_x(section, x, dt, smalls):
    return pl.pallas_call(
        pick_x_body,
        out_shape=[shape((TALL, PACKED), BF16)] * 2,
        in_specs=[SMEM, whole((SHARD, CONV_CH)), whole((SHARD, HEADS))]
        + [whole(v.shape) for v in smalls],
        out_specs=[whole((TALL, PACKED))] * 2,
        scratch_shapes=[pltpu.VMEM((16, PACKED), F32)],
        compiler_params=params(),
        cost_estimate=pl.CostEstimate(flops=0, bytes_accessed=6_000_000, transcendentals=0),
        name="pick_x",
    )(section, x, dt, *smalls)


def unpack_body(count, info, *rest):
    refs, (cpar, gain_one, gain_two, hpar, held, full, sems) = rest[:count], rest[count:]
    copies = []
    for n in range(4):
        if count == 4:
            source, to = refs[n].at[pl.ds(2 * PIECE, 16)], lax.rem(info[10] + n, 4)
        else:
            source, to = refs[0].at[pl.ds(n * TALL + SHARD, 16)], n
        copies.append(pltpu.make_async_copy(source, held.at[to], sems.at[n]))
    for c in copies:
        c.start()
    for c in copies:
        c.wait()
    section = info[13]
    half_cols = pl.ds(pl.multiple_of(section * BLOCK, LANES), BLOCK)
    for z in range(4):
        values = held[z].astype(F32)
        full[:, z * 832 : (z + 1) * 832] = values[:8, :832]
        gain_one[:, z * SHARD : (z + 1) * SHARD] = values[5:6, :SHARD]
        gain_two[:, z * BLOCK : (z + 1) * BLOCK] = held[z, :, half_cols].astype(F32)[6:7]
    for d in range(GROUPS):
        cols = pl.ds(pl.multiple_of((2 * d + section) * BLOCK, LANES), BLOCK)
        cpar[:, d * BLOCK : (d + 1) * BLOCK] = full[:, cols]
    cpar[:, LOCAL:] = full[:, INNER:]
    values = held[0, :, :LANES].astype(F32)
    heads = [values[n : n + 1] + values[n + 1 : n + 2] + values[n + 2 : n + 3] for n in (7, 10, 13)]
    heads = jnp.concatenate(heads + [jnp.zeros((5, LANES), F32)], axis=0)
    head, lane = row_of((LANES, LANES)), lane_of((LANES, LANES))
    here = (head // OWN == 2 * (lane // 8) + section) & (head % OWN == lane % 8)
    hpar[...] = exact_dot(heads, here.astype(F32))


def unpack(info, arrays):
    shapes = ((8, MIXED), (1, WIDTH), (1, LOCAL), (8, LANES))
    return pl.pallas_call(
        functools.partial(unpack_body, len(arrays)),
        out_shape=[shape(dims) for dims in shapes],
        in_specs=[SMEM] + [ANYWHERE] * len(arrays),
        out_specs=[whole(dims) for dims in shapes],
        scratch_shapes=[
            pltpu.VMEM((4, 16, PACKED), BF16),
            pltpu.VMEM((8, CONV_CH), F32),
            pltpu.SemaphoreType.DMA((4,)),
        ],
        compiler_params=params(),
        cost_estimate=pl.CostEstimate(flops=0, bytes_accessed=400_000, transcendentals=0),
        name="unpack",
    )(info, *arrays)


def pick_zo_body(info, z_ref, o_ref, token, *outs):
    for out, side in zip(outs, (info[0], 1 - info[0]), strict=True):
        for d in range(GROUPS):
            cols = pl.ds(pl.multiple_of((2 * d + side) * BLOCK, LANES), BLOCK)
            out[:, d * BLOCK : (d + 1) * BLOCK] = z_ref[:, cols]
        rows = pl.ds(pl.multiple_of(side * SHARD, SHARD), SHARD)
        out[:, LOCAL:] = o_ref[rows, :]


def pick_zo(section, z, o, token):
    return pl.pallas_call(
        pick_zo_body,
        out_shape=[shape((SHARD, LOCAL + WIDTH), BF16)] * 2,
        in_specs=[SMEM, whole((SHARD, INNER)), whole((2 * SHARD, WIDTH)), ANYWHERE],
        out_specs=[whole((SHARD, LOCAL + WIDTH))] * 2,
        compiler_params=params(),
        cost_estimate=pl.CostEstimate(flops=0, bytes_accessed=9_000_000, transcendentals=0),
        name="pick_zo",
    )(section, z, o, token)


def head_lanes(values):
    rows = values.shape[0]
    grid = jnp.pad(values.reshape(rows, GROUPS, OWN), ((0, 0), (0, 0), (0, 8 - OWN)))
    return jnp.pad(grid.reshape(rows, 8 * GROUPS), ((0, 0), (0, LANES - 8 * GROUPS)))


def lanes_heads(values):
    rows = values.shape[0]
    return values[:, : 8 * GROUPS].reshape(rows, GROUPS, 8)[:, :, :OWN].reshape(rows, -1)


def on_device(
    boundary,
    lengths,
    norm_gain,
    w_z,
    w_xbc,
    w_dt,
    conv_weight,
    conv_bias,
    dt_bias,
    a_log,
    d_skip,
    gate_gain,
    w_out,
):
    section = lax.axis_index("section")
    group = lax.axis_index("dp")
    ctx = lax.axis_index("ctx")
    place = {"z": group, "y": ctx // 4, "x": ctx % 4}
    micro = ctx % 2
    chunk = ctx // 2

    def ordered(mine, came):
        return jnp.where(section == 0, mine, came), jnp.where(section == 0, came, mine)

    own_rows = lax.dynamic_index_in_dim(boundary[0], micro, 0, False)
    other_rows = lax.dynamic_index_in_dim(boundary[0], 1 - micro, 0, False)
    came = lax.ppermute(other_rows, "ctx", NEIGHBOURS)
    block = jnp.where(
        micro == 0, jnp.concatenate([own_rows, came]), jnp.concatenate([came, own_rows])
    )
    hidden, cotangent = ordered(block, swapped(block))

    pair = lengths[group, micro]
    padded = (pair[0] + SPAN - 1) // SPAN * SPAN
    offset = chunk * ROWS
    begin = jnp.where(offset >= padded, padded, 0)
    length = jnp.where(offset >= padded, pair[1], pair[0])
    live = jnp.clip(length - (offset - begin), 0, ROWS)
    offsets = jnp.arange(CHUNKS, dtype=jnp.int32) * ROWS
    keeps = ((offsets != 0) & (offsets != padded)).astype(jnp.int32)
    keep = (offset != 0) & (offset != padded)
    at = [place["z"], place["y"], place["x"], section]
    info = jnp.concatenate(
        [jnp.stack([live, keep]).astype(jnp.int32), keeps, jnp.stack(at).astype(jnp.int32)]
    )

    def forward(h, layer):
        cpar, hpar = cpars[layer], hpars[layer]
        normed, mixed, rate = in_proj(
            info, h, gains_one[layer], weights_x[layer], []
        )
        halo = halo_shift(mixed[ROWS - 16 :], 1)
        gate = gate_proj(info, normed, weights_z[layer], [] if layer else ready)
        xa, bca, cum, dt, s0, msg = state_call(info, mixed, halo, cpar, rate, hpar)
        came = exchange(msg)
        y_in = inside_call(xa, bca, cum, dt, hpar)
        hin = exchange(scan_call(info, came, False, y_in, *([] if layer else cpars[1:]))).reshape(GROUPS, STATE, BLOCK)
        y, part = out_proj(
            info, y_in, bca, cum, hin, s0, gate, gains_two[layer], weights_o[layer]
        )
        result, branch, scale = join(info, h, part, swapped(part), F32 if layer else BF16)
        saved = (h, normed, mixed, halo, rate, gate, xa, bca, cum, dt, s0, msg, hin, y, branch, scale)
        return result, saved

    def backward(cot, saved, layer, higher, tokens):
        h, normed, mixed, halo, rate, gate, xa, bca, cum, dt, s0, msg, hin, y, branch, scale = saved
        cpar, hpar = cpars[layer], hpars[layer]

        def first_stage(value):
            return lax.psum_scatter(value, "dp", tiled=True)

        bg, dy, dz, grad_o, d_gain_two = gate_back(
            info, cot, y, gate, gains_two[layer], branch, scale, weights_o[layer], layer == 1
        )
        own1, msg_back, grad_z = own_grad(dy, bca, cum, msg, dz, normed)
        sums = [first_stage(grad_z)] + ([first_stage(grad_o)] if layer else [])
        came = exchange(msg_back)
        dxi, d_skips, gsum, u, dbc = inside_back(dy, xa, bca, cum, dt, hpar)
        part = gate_in_back(info, dz, weights_z[layer], msg_back)
        lam = exchange(scan_call(info, came, True, part)).reshape(GROUPS, STATE, BLOCK)
        dmx, dmbc, tailx, tailbc, edgex, edgebc, d_parx, d_parbc, d_heads = finish_call(
            info, xa, dxi, dy, mixed, halo, cpar, bca, cum, dt, rate, hpar, lam, hin, s0, own1, u, gsum, dbc
        )
        edge = halo_shift(jnp.concatenate([edgex, edgebc], axis=1), -1)
        dxc = patch(dmx, dmbc, tailx, tailbc, edge, *tokens)
        middle = 7 * LANES
        if layer == 0:
            higher_rows, higher = higher
            normed_t = normed.T
            cuts = [(normed_t, dxc, slice(0, middle)), (grad_o, bg, slice(0, WIDTH // 2))]
            left = terms(info, "y", cuts, (), True)
            part, d_gain_one = mixed_back(
                info, dxc, part, h, normed, weights_x[layer], False, [left, *higher]
            )
        else:
            part, d_gain_one, grad_x = mixed_back(
                info, dxc, part, h, normed, weights_x[layer], True, []
            )
        dh, dh_low = norm_back(part, swapped(part), h, cot, gains_one[layer])
        d_skip_row = jnp.sum(d_skips[0:1].reshape(1, 4 * OWN, HEADDIM), axis=2)
        rows = jnp.where(jnp.arange(8)[:, None] == 5, d_gain_two, d_parx)
        rows = jnp.concatenate([rows, d_parbc], axis=1)
        more = jnp.concatenate(
            [
                d_gain_one[:1],
                jnp.pad(d_heads[:2], ((0, 0), (0, WIDTH - LANES))),
                jnp.pad(head_lanes(d_skip_row), ((0, 4), (0, WIDTH - LANES))),
            ]
        )
        rows = jnp.concatenate([rows, jnp.pad(more, ((0, 0), (0, 2 * STATE)))])
        if layer == 1:
            return dh, dh_low, sums + [first_stage(grad_x)], rows

        rows = jnp.concatenate([rows, higher_rows]).astype(BF16)
        cuts = [(normed_t, dxc, slice(middle, PACKED)), (grad_o, bg, slice(WIDTH // 2, WIDTH))]
        right = arrived(terms(info, "x", cuts, (rows,)), "x")
        tall = fold(info, "y", [[v] for v in higher + sums], 1, 96, right[1], True)
        left = fold(info, "x", [[traded(left, "y")]], 4, 24, tall)
        right = fold(info, "y", [right], 4, 24, dh_low)
        tall = fold(info, "x", [[traded(tall, "y")]], 1, 24, right[0])
        left, right = arrived(left, "x"), arrived(right, "y")
        final = summed(arrived(last_fold(info, left, right, tall[0]), "z"))
        left, right = left[0].shape[1], right[0].shape[1]
        rows = final[24:, left:]
        final = final[:24]
        sum_x = jnp.concatenate(
            [final[:, :middle], final[:, left : left + PACKED - middle]], axis=1
        )
        sum_o = jnp.concatenate([final[:, middle:left], final[:, left + PACKED - middle :]], axis=1)
        return dh, [arrived(tall, "x"), sum_o], sum_x, rows

    at = section.reshape(1).astype(jnp.int32)
    smalls = (conv_weight[0], conv_bias, norm_gain, gate_gain, dt_bias, a_log, d_skip)
    mine_x, other_x = pick_x(at, w_xbc[0], w_dt[0], smalls)
    came_x = swapped(other_x)
    mine_zo, other_zo = pick_zo(at, w_z[0], w_out[0], mine_x)
    came_zo = swapped(other_zo)
    first = fetched(mine_x, came_x, 0, section, after([hidden], place))
    got = [first] + [send(first, "z", -r) for r in range(1, 4)]
    small_low = got
    low_x = pieces(mine_x, came_x, got, 0)
    got = lax.all_gather(fetched(mine_zo, came_zo, 0, section, after(got[1:], place)), "dp")
    late = after(low_x[3:6] + low_x[7:10], place)["z"]
    got = [None] + [lax.dynamic_index_in_dim(got, (late + r) % 4, 0, False) for r in range(1, 4)]
    low_zo = pieces(mine_zo, came_zo, got, 0)
    here = after([low_x[3], low_x[7]], {"section": section})["section"]
    high_x = [lax.all_gather(jnp.where(here == 1, mine_x, came_x), "dp", tiled=True)]
    high_zo = [lax.all_gather(jnp.where(here == 1, mine_zo, came_zo), "dp", tiled=True)]
    ready = low_zo[3:6] + low_zo[7:10]
    weights_x = [Weight(v, n, PACKED) for n, v in enumerate((low_x, high_x))]
    weights_z = [Weight(v, n, LOCAL) for n, v in enumerate((low_zo, high_zo))]
    weights_o = [Weight(v, n, WIDTH, LOCAL) for n, v in enumerate((low_zo, high_zo))]

    unpacked = [unpack(info, v) for v in (small_low, high_x)]
    cpars, gains_one, gains_two, hpars = zip(*unpacked, strict=True)

    def returned(rows, layer):
        pairs = [(layer * 16 + a, layer * 16 + b) for a, b in NEIGHBOURS]
        other, mine = (
            lax.dynamic_slice_in_dim(rows, n * HALF, HALF, 0) for n in (1 - micro, micro)
        )
        other = lax.ppermute(other, ("section", "ctx"), pairs)
        return jnp.where(micro == 0, jnp.stack([mine, other]), jnp.stack([other, mine]))

    middle, saved_low = forward(hidden, 0)
    out_high, saved_high = forward(middle, 1)
    top_high = returned(out_high, 1)
    _, back, higher, rows = backward(cotangent, saved_high, 1, None, [top_high])
    dh_low, (tall, low_o), low_x, rows = backward(back, saved_low, 0, (rows, higher), [rows])
    at = (LOCAL, LOCAL + WIDTH, LOCAL + WIDTH + PACKED)
    high_z, high_o, high_x, low_z = jnp.split(summed(tall), at, axis=1)

    own, given = ordered(rows[:16], rows[16:])
    rows_0, rows_1 = ordered(own, swapped(given))
    wide = jnp.concatenate(
        [turns(rows_0[:8, :LOCAL], rows_1[:8, :LOCAL]), rows_0[:8, LOCAL:] + rows_1[:8, LOCAL:]],
        axis=1,
    )
    head_rows = turns(lanes_heads(rows_0[9:12, :LANES]), lanes_heads(rows_1[9:12, :LANES]))
    index = group * 16 + ctx
    d_conv = lax.dynamic_slice(wide, (0, index * 52), (5, 52))
    d_gain_two = lax.dynamic_slice(wide, (5, index * 48), (1, 48))
    d_gain_one = lax.dynamic_slice(rows_0[8:9] + rows_1[8:9], (0, index * 24), (1, 24))

    own, given = ordered(
        jnp.concatenate([low_z, low_x], axis=1), jnp.concatenate([high_z, high_x], axis=1)
    )
    first, second = ordered(own, swapped(given))
    sum_z = turns(first[:, :LOCAL], second[:, :LOCAL])
    at_x, at_bc, at_dt = LOCAL, LOCAL + LOCAL, LOCAL + MIXED
    sum_x = turns(first[:, at_x:at_bc], second[:, at_x:at_bc])
    sum_bc = first[:, at_bc:at_dt] + second[:, at_bc:at_dt]
    sum_dt = turns(lanes_heads(first[:, at_dt:]), lanes_heads(second[:, at_dt:]))

    trips = []
    for flip in range(2):
        pairs = [
            (c * 16 + j, (flip ^ (j % 2)) * 16 + 8 * c + j // 2) for c in range(2) for j in range(16)
        ]
        value = jnp.where(micro == flip, low_o, high_o)
        trips.append(lax.ppermute(value, ("section", "ctx"), pairs))
    sum_o = jnp.concatenate(ordered(*trips))

    top = jnp.where(section == 0, returned(dh_low, 0), top_high)
    return (
        top[None],
        d_gain_one,
        sum_z[None],
        jnp.concatenate([sum_x, sum_bc], axis=1)[None],
        sum_dt[None],
        d_conv[None, :4],
        d_conv[4:5],
        head_rows[0:1],
        head_rows[1:2],
        head_rows[2:3],
        d_gain_two,
        sum_o[None],
    )


def solution(mesh):
    in_specs = (
        P("section", None, ("dp", "ctx"), None),
        P(),
        P("section", "dp"),
        P("section", "dp", None),
        P("section", "dp", None),
        P("section", "dp", None),
        P("section", None, "dp"),
        P("section", "dp"),
        P("section", None),
        P("section", None),
        P("section", None),
        P("section", "dp"),
        P("section", "dp", None),
    )
    out_specs = (
        P("section", None, ("dp", "ctx"), None),
        P("section", ("dp", "ctx")),
        P("section", ("dp", "ctx"), None),
        P("section", ("dp", "ctx"), None),
        P("section", ("dp", "ctx"), None),
        P("section", None, ("dp", "ctx")),
        P("section", ("dp", "ctx")),
        P("section", None),
        P("section", None),
        P("section", None),
        P("section", ("dp", "ctx")),
        P("section", ("dp", "ctx"), None),
    )
    return jax.shard_map(
        on_device, mesh=mesh, in_specs=in_specs, out_specs=out_specs, check_vma=False
    )
```

```python
import functools

import jax
import jax.numpy as jnp
from jax import lax
from jax.experimental import pallas as pl
from jax.experimental.pallas import tpu as pltpu
from jax.sharding import PartitionSpec as P

HEADS = 48
HEADDIM = 64
STATE = 128
KERNEL = 4
SPAN = 256
MICRO = 2
WIDTH = 1536
INNER = 3072
CONV_CH = 3328
LANES = 128
CHUNKS = 8
GROUPS = 4
OWN = 6
BLOCK = OWN * HEADDIM
LOCAL = GROUPS * BLOCK
MIXED = LOCAL + 2 * STATE
PACKED = MIXED + LANES
ROWS = 256
HALF = 128
SHARD = 384
TALL = SHARD + 16
PIECE = 48
STATE_HALF = STATE // 2
MESSAGE = STATE_HALF + 16
SMALL = 32
EPSILON = 1e-05
PRECISE = lax.Precision.HIGHEST
F32 = jnp.float32
BF16 = jnp.bfloat16
VMEM_LIMIT = 56 * 1024 * 1024


def params(**more):
    return pltpu.CompilerParams(vmem_limit_bytes=VMEM_LIMIT, **more)


def whole(shape):
    return pl.BlockSpec(shape, lambda *_: (0,) * len(shape))


def columns(rows, width):
    return pl.BlockSpec((rows, width), lambda g: (0, g))


def grouped(rows):
    return pl.BlockSpec((1, rows, BLOCK), lambda g: (g, 0, 0))


MESSAGES = pl.BlockSpec((2, MESSAGE, BLOCK), lambda g: (g, 0, 0))
SMEM = pl.BlockSpec(memory_space=pltpu.SMEM)
ANYWHERE = pl.BlockSpec(memory_space=pl.ANY)


def shape(dims, kind=F32):
    return jax.ShapeDtypeStruct(dims, kind)


def dot(a, b):
    return jnp.dot(a, b, preferred_element_type=F32)


def dot_nt(a, b):
    return lax.dot_general(a, b, (((1,), (1,)), ((), ())), preferred_element_type=F32)


def exact_dot(a, b):
    return jnp.dot(a, b, precision=PRECISE, preferred_element_type=F32)


def lane_of(dims):
    return lax.broadcasted_iota(jnp.int32, dims, len(dims) - 1)


def row_of(dims):
    return lax.broadcasted_iota(jnp.int32, dims, len(dims) - 2)


def sigmoid(v):
    return 1.0 / (1.0 + jnp.exp(-v))


def softplus(v):
    return jnp.maximum(v, 0.0) + jnp.log1p(jnp.exp(-jnp.abs(v)))


def rolled(values, g):
    return pltpu.roll(values, lax.rem(LANES - 8 * g, LANES), axis=1)


def pair_lanes(values, p):
    low = lane_of((values.shape[0], LANES)) < HEADDIM
    return jnp.where(low, values[:, 2 * p : 2 * p + 1], values[:, 2 * p + 1 : 2 * p + 2])


def spread(values):
    return jnp.concatenate([pair_lanes(values, p) for p in range(OWN // 2)], axis=1)


def head_sum_matrix(g):
    head = row_of((BLOCK, LANES)) // HEADDIM
    return (lane_of((BLOCK, LANES)) == head + 8 * g).astype(BF16)


def lower_triangle(strict=False):
    i, j = row_of((HALF, HALF)), lane_of((HALF, HALF))
    return ((i > j) if strict else (i >= j)).astype(F32)


def usable_rows(info):
    return (row_of((ROWS, 1)) < info[0]).astype(F32)


def half(values, q):
    return values[q * HALF : (q + 1) * HALF]


class Weight:
    def __init__(self, arrays, layer, width, first=0):
        self.arrays = arrays
        self.stride = arrays[0].shape[0] // 4
        self.layer = layer
        self.width = width
        self.columns = pl.ds(first, width)

    def block(self, info, b):
        return lax.rem(info[10] + b, 4) * SHARD

    def parts(self, refs, info, b):
        start = self.block(info, b)
        if len(refs) == 1:
            there = pl.multiple_of(start // SHARD * self.stride, 16)
            return [(refs[0].at[pl.ds(there, SHARD)], start, SHARD)]
        out = []
        for side in range(2):
            mine = info[12 - side]
            for step in range(4):
                source = refs[2 + 4 * side + step].at[pl.ds((b - 1) * PIECE, PIECE)]
                row = start + side * (SHARD // 2) + lax.rem(mine + step, 4) * PIECE
                out.append((source, row, PIECE))
        return out

    def copies(self, refs, info, b, buffer, sems):
        return [
            pltpu.make_async_copy(
                source.at[:, self.columns],
                buffer.at[pl.ds(pl.multiple_of(row, 16), count)],
                sems.at[b, n],
            )
            for n, (source, row, count) in enumerate(self.parts(refs, info, b))
        ]

    def own_copy(self, source, info, buffer, sems):
        rows = pl.ds(pl.multiple_of(self.block(info, 0), SHARD), SHARD)
        source = source.at[pl.ds(0, SHARD), self.columns]
        return pltpu.make_async_copy(source, buffer.at[rows], sems.at[0, 0])

    def start(self, refs, info, buffer, sems):
        whole_array = len(refs) == 1
        if not whole_array:
            for n in range(2):

                @pl.when((info[13] == self.layer) == (n == 0))
                def _(n=n):
                    self.own_copy(refs[n], info, buffer, sems).start()

        for b in range(0 if whole_array else 1, 4):
            for c in self.copies(refs, info, b, buffer, sems):
                c.start()

    def wait(self, refs, info, b, buffer, sems):
        if b == 0 and len(refs) > 1:
            self.own_copy(refs[0], info, buffer, sems).wait()
        else:
            for c in self.copies(refs, info, b, buffer, sems):
                c.wait()
        return pl.ds(pl.multiple_of(self.block(info, b), SHARD), SHARD)

    def specs(self):
        return [ANYWHERE] * len(self.arrays)

    def scratch(self):
        return [pltpu.VMEM((4 * SHARD, self.width), BF16), pltpu.SemaphoreType.DMA((4, 8))]

    def product(self, refs, info, left, buffer, sems, total):
        for b in range(4):
            self.wait(refs, info, b, buffer, sems)
        step = 512 if self.width % 512 == 0 else 640
        for at in range(0, self.width, step):
            total[:, at : at + step] = dot(left[...], buffer[:, at : at + step])


def in_proj_body(weight, tokens, info, h_ref, gain_ref, *rest):
    refs = len(weight.arrays)
    w_refs, rest = rest[:refs], rest[refs + tokens :]
    (normed_ref, mixed_ref, rate_ref, buffer, sems, total) = rest
    weight.start(w_refs, info, buffer, sems)
    h = h_ref[...].astype(F32)
    scale = lax.rsqrt(jnp.mean(h * h, axis=1, keepdims=True) + EPSILON)
    normed_ref[...] = (h * scale * gain_ref[...]).astype(BF16)
    weight.product(w_refs, info, normed_ref, buffer, sems, total)
    mixed_ref[...] = total[:, :MIXED].astype(BF16)
    rate_ref[...] = total[:, MIXED:]


def in_proj(info, h, gain, weight, tokens):
    return pl.pallas_call(
        functools.partial(in_proj_body, weight, len(tokens)),
        out_shape=(shape((ROWS, WIDTH), BF16), shape((ROWS, MIXED), BF16), shape((ROWS, LANES))),
        in_specs=[SMEM, whole((ROWS, WIDTH)), whole((1, WIDTH))]
        + weight.specs()
        + [ANYWHERE] * len(tokens),
        out_specs=(whole((ROWS, WIDTH)), whole((ROWS, MIXED)), whole((ROWS, LANES))),
        scratch_shapes=weight.scratch() + [pltpu.VMEM((ROWS, PACKED), F32)],
        compiler_params=params(),
        cost_estimate=pl.CostEstimate(
            flops=2 * ROWS * WIDTH * PACKED, bytes_accessed=8_000_000, transcendentals=0
        ),
        name="in_proj",
    )(info, h, gain, *weight.arrays, *tokens)


def gate_proj_body(weight, tokens, info, normed_ref, *rest):
    refs = len(weight.arrays)
    w_refs, (gate_ref, buffer, sems) = rest[:refs], rest[refs + tokens :]
    weight.start(w_refs, info, buffer, sems)
    weight.product(w_refs, info, normed_ref, buffer, sems, gate_ref)


def gate_proj(info, normed, weight, tokens):
    return pl.pallas_call(
        functools.partial(gate_proj_body, weight, len(tokens)),
        out_shape=shape((ROWS, LOCAL)),
        in_specs=[SMEM, whole((ROWS, WIDTH))] + weight.specs() + [ANYWHERE] * len(tokens),
        out_specs=whole((ROWS, LOCAL)),
        scratch_shapes=weight.scratch(),
        compiler_params=params(),
        cost_estimate=pl.CostEstimate(
            flops=2 * ROWS * WIDTH * LOCAL, bytes_accessed=7_000_000, transcendentals=0
        ),
        name="gate_proj",
    )(info, normed, *weight.arrays, *tokens)


def conv_sum_of(values, halo, cpar, keep, ext):
    width = values.shape[1]
    ext[0:16, :width] = halo.astype(F32) * keep
    ext[16 : 16 + ROWS, :width] = values.astype(F32)
    total = cpar[4:5, :]
    for k in range(KERNEL):
        total = total + cpar[k : k + 1, :] * ext[13 + k : 13 + k + ROWS, :width]
    return total


def state_body(
    info, mixed, halo, cpar, bc, halo_bc, cpar_bc, rate, hpar,
    xa_ref, bca_ref, cum_ref, dt_ref, s0_ref, msg_ref, ext, bt, tail,
):
    g = pl.program_id(0)
    keep = info[1].astype(F32)

    @pl.when(g == 0)
    def _():
        total = conv_sum_of(bc[...], halo_bc[...], cpar_bc[...], keep, ext)
        active = total * sigmoid(total)
        bca_ref[...] = active
        bt[...] = active[:, :STATE].T.astype(BF16)
        dt = usable_rows(info) * softplus(rate[...] + hpar[0:1, :])
        log_decay = dt * -jnp.exp(hpar[1:2, :])
        dt_ref[...] = dt
        tri = lower_triangle()
        for q in range(2):
            rows = pl.ds(q * HALF, HALF)
            cum = exact_dot(tri, half(log_decay, q))
            cum_ref[rows, :] = cum
            tail[rows, :] = jnp.exp(cum[HALF - 1 :, :] - cum) * half(dt, q)

    total = conv_sum_of(mixed[...], halo[...], cpar[...], keep, ext)
    xa = total * sigmoid(total)
    xa_ref[...] = xa
    weighted = (xa * spread(rolled(tail[...], g))).astype(BF16)
    ends = rolled(cum_ref[...], g)
    end0, end1 = ends[HALF - 1 : HALF], ends[ROWS - 1 : ROWS]
    s0 = dot(bt[:, :HALF], half(weighted, 0))
    s1 = dot(bt[:, HALF:], half(weighted, 1))
    s0_ref[0] = s0
    state = (spread(jnp.exp(end1)) * s0 + s1).astype(BF16)
    damp = spread(jnp.exp(end0 + end1))
    high = damp.astype(BF16)
    low = (damp - high.astype(F32)).astype(BF16)
    row = row_of((16, BLOCK))
    damps = jnp.where(row == 0, high.astype(F32), low.astype(F32)).astype(BF16)
    for r in range(2):
        msg_ref[r, :STATE_HALF, :] = state[r * STATE_HALF : (r + 1) * STATE_HALF]
        msg_ref[r, STATE_HALF:, :] = damps


def state_call(info, mixed, halo, cpar, rate, hpar):
    bc_at = LOCAL // 256
    return pl.pallas_call(
        state_body,
        grid=(GROUPS,),
        out_shape=(
            shape((ROWS, LOCAL)),
            shape((ROWS, 256)),
            shape((ROWS, LANES)),
            shape((ROWS, LANES)),
            shape((GROUPS, STATE, BLOCK)),
            shape((CHUNKS, MESSAGE, BLOCK), BF16),
        ),
        in_specs=[
            SMEM,
            columns(ROWS, BLOCK),
            columns(16, BLOCK),
            columns(8, BLOCK),
            pl.BlockSpec((ROWS, 256), lambda g: (0, bc_at)),
            pl.BlockSpec((16, 256), lambda g: (0, bc_at)),
            pl.BlockSpec((8, 256), lambda g: (0, bc_at)),
            whole((ROWS, LANES)),
            whole((8, LANES)),
        ],
        out_specs=(
            columns(ROWS, BLOCK),
            whole((ROWS, 256)),
            whole((ROWS, LANES)),
            whole((ROWS, LANES)),
            grouped(STATE),
            MESSAGES,
        ),
        scratch_shapes=[
            pltpu.VMEM((ROWS + 32, BLOCK), F32),
            pltpu.VMEM((STATE, ROWS), BF16),
            pltpu.VMEM((ROWS, LANES), F32),
        ],
        compiler_params=params(),
        cost_estimate=pl.CostEstimate(
            flops=2 * ROWS * STATE * LOCAL, bytes_accessed=4_500_000, transcendentals=400_000
        ),
        name="conv_state",
    )(info, mixed, halo, cpar, mixed, halo, cpar, rate, hpar)


def inside_body(xa, bca, cum, dt, hpar, y_ref, cum_t, scores):
    g = pl.program_id(0)

    @pl.when(g == 0)
    def _():
        tri = lower_triangle()
        for q in range(2):
            b, c = half(bca[:, :STATE], q).astype(BF16), half(bca[:, STATE:], q).astype(BF16)
            scores[q] = dot_nt(c, b) * tri
            cum_t[:, q * HALF : (q + 1) * HALF] = half(cum[...], q).T

    cols = rolled(cum[...], g)
    rows = cum_t[pl.ds(pl.multiple_of(8 * g, 8), 8), :]
    steps = rolled(dt[...], g)
    skips = rolled(hpar[...], g)[2:3, :]
    low = lane_of((HALF, LANES)) < HEADDIM
    for q in range(2):
        for p in range(OWN // 2):
            lanes = slice(p * LANES, (p + 1) * LANES)
            x = xa[q * HALF : (q + 1) * HALF, lanes]
            xdt = x * pair_lanes(half(steps, q), p)
            both = jnp.concatenate([jnp.where(low, xdt, 0.0), jnp.where(low, 0.0, xdt)], axis=0)
            mats = []
            for i in (2 * p, 2 * p + 1):
                gap = half(cols, q)[:, i : i + 1] - rows[i : i + 1, q * HALF : (q + 1) * HALF]
                mats.append((jnp.exp(jnp.minimum(gap, 0.0)) * scores[q]).astype(BF16))
            y = dot(jnp.concatenate(mats, axis=1), both.astype(BF16))
            y_ref[q * HALF : (q + 1) * HALF, lanes] = y + x * pair_lanes(skips, p)


def inside_call(xa, bca, cum, dt, hpar):
    return pl.pallas_call(
        inside_body,
        grid=(GROUPS,),
        out_shape=shape((ROWS, LOCAL)),
        in_specs=[
            columns(ROWS, BLOCK),
            whole((ROWS, 256)),
            whole((ROWS, LANES)),
            whole((ROWS, LANES)),
            whole((8, LANES)),
        ],
        out_specs=columns(ROWS, BLOCK),
        scratch_shapes=[pltpu.VMEM((LANES, ROWS), F32), pltpu.VMEM((2, HALF, HALF), F32)],
        compiler_params=params(),
        cost_estimate=pl.CostEstimate(
            flops=2 * HEADS * HALF * HALF * LANES, bytes_accessed=3_300_000, transcendentals=800_000
        ),
        name="inside",
    )(xa, bca, cum, dt, hpar)


def scan_body(backward, info, msg, *rest):
    out_ref = rest[-1]
    carry = jnp.zeros((STATE_HALF, BLOCK), F32)
    for k in reversed(range(CHUNKS)) if backward else range(CHUNKS):
        keep = info[2 + k].astype(F32)
        if not backward:
            carry = carry * keep
        out_ref[k] = carry.astype(BF16)
        damps = msg[k, STATE_HALF:, :].astype(F32)
        carry = (damps[0:1] + damps[1:2]) * carry + msg[k, :STATE_HALF, :].astype(F32)
        if backward:
            carry = carry * keep


def scan_call(info, msg, backward, *tokens):
    return pl.pallas_call(
        functools.partial(scan_body, backward),
        out_shape=shape((CHUNKS, STATE_HALF, BLOCK), BF16),
        in_specs=[SMEM, whole((CHUNKS, MESSAGE, BLOCK))] + [ANYWHERE] * len(tokens),
        out_specs=whole((CHUNKS, STATE_HALF, BLOCK)),
        compiler_params=params(),
        name="chunk_scan",
    )(info, msg, *tokens)


def out_proj_body(weight, info, y_in, bca, cum, hin, s0, gate, gain, *rest):
    refs = len(weight.arrays)
    w_refs, (y_ref, part_ref, buffer, sems, sums, gained) = rest[:refs], rest[refs:]
    weight.start(w_refs, info, buffer, sems)
    c_all = bca[:, STATE:].astype(BF16)
    grow = jnp.exp(cum[...])
    sums[...] = jnp.zeros((ROWS, LANES), F32)

    def group(g, _):
        lanes = pl.ds(pl.multiple_of(g * BLOCK, LANES), BLOCK)
        factor = rolled(grow, g)
        first = hin[g]
        second = spread(factor[HALF - 1 : HALF]) * first.astype(F32) + s0[g]
        carried = jnp.concatenate(
            [dot(half(c_all, 0), first), dot(half(c_all, 1), second.astype(BF16))], axis=0
        )
        y = y_in[:, lanes] + spread(factor) * carried
        y_ref[:, lanes] = y
        z = gate[:, lanes]
        gated = y * z * sigmoid(z)
        square = gated * gated
        sums[...] += sum(square[:, i * LANES : (i + 1) * LANES] for i in range(BLOCK // LANES))
        gained[:, lanes] = (gated * gain[:, lanes]).astype(BF16)
        return 0

    lax.fori_loop(0, GROUPS, group, 0)
    part_ref[:, WIDTH:] = sums[...]
    weight.product(w_refs, info, gained, buffer, sems, part_ref)


def out_proj(info, y_in, bca, cum, hin, s0, gate, gain, weight):
    return pl.pallas_call(
        functools.partial(out_proj_body, weight),
        out_shape=(shape((ROWS, LOCAL)), shape((ROWS, WIDTH + LANES))),
        in_specs=[
            SMEM,
            whole((ROWS, LOCAL)),
            whole((ROWS, 256)),
            whole((ROWS, LANES)),
            whole((GROUPS, STATE, BLOCK)),
            whole((GROUPS, STATE, BLOCK)),
            whole((ROWS, LOCAL)),
            whole((1, LOCAL)),
        ]
        + weight.specs(),
        out_specs=(whole((ROWS, LOCAL)), whole((ROWS, WIDTH + LANES))),
        scratch_shapes=weight.scratch()
        + [pltpu.VMEM((ROWS, LANES), F32), pltpu.VMEM((ROWS, LOCAL), BF16)],
        compiler_params=params(),
        cost_estimate=pl.CostEstimate(
            flops=2 * ROWS * WIDTH * LOCAL, bytes_accessed=13_000_000, transcendentals=800_000
        ),
        name="out_proj",
    )(info, y_in, bca, cum, hin, s0, gate, gain, *weight.arrays)


def join_body(info, h_ref, own, came, res_ref, branch_ref, scale_ref):
    squares = jnp.sum(own[:, WIDTH:] + came[:, WIDTH:], axis=1, keepdims=True)
    scale = lax.rsqrt(squares / INNER + EPSILON)
    branch = scale * (own[:, :WIDTH] + came[:, :WIDTH])
    branch_ref[...] = branch.astype(BF16)
    scale_ref[...] = jnp.broadcast_to(scale, (HALF // 2, LANES))
    first = pl.program_id(0) * (HALF // 2)
    usable = (row_of((HALF // 2, 1)) + first < info[0]).astype(F32)
    result = h_ref[...].astype(F32) + usable * branch
    res_ref[...] = result.astype(res_ref.dtype)


def join(info, h, own, came, kind):
    def rows(width):
        return pl.BlockSpec((HALF // 2, width), lambda i: (i, 0))

    return pl.pallas_call(
        join_body,
        grid=(4,),
        out_shape=(shape((ROWS, WIDTH), kind), shape((ROWS, WIDTH), BF16), shape((ROWS, LANES))),
        in_specs=[SMEM, rows(WIDTH), rows(WIDTH + LANES), rows(WIDTH + LANES)],
        out_specs=(rows(WIDTH), rows(WIDTH), rows(LANES)),
        compiler_params=params(),
        cost_estimate=pl.CostEstimate(flops=2_000_000, bytes_accessed=8_000_000, transcendentals=0),
        name="join",
    )(info, h, own, came)


def gate_back_body(weight, info, cot, y, gate, gain, branch, scale_ref, *rest):
    refs = len(weight.arrays)
    w_refs, rest = rest[:refs], rest[refs:]
    bg_ref, dy_ref, dz_ref, grad_ref, dgain_ref, buffer, sems, inner_ref = rest
    b = pl.program_id(0)
    scale = scale_ref[:, :1]

    @pl.when(b == 0)
    def _():
        weight.start(w_refs, info, buffer, sems)
        bg = (usable_rows(info) * cot[...].astype(F32)).astype(BF16)
        bg_ref[...] = bg
        inner = jnp.sum(bg.astype(F32) * branch[...].astype(F32), axis=1, keepdims=True)
        inner_ref[...] = jnp.broadcast_to(inner * scale * scale / INNER, (ROWS, LANES))
        for n in range(4):
            weight.wait(w_refs, info, n, buffer, sems)

    inner = inner_ref[:, :1]
    bg = bg_ref[...]
    d_norms = dot_nt(bg, buffer[pl.ds(pl.multiple_of(b * SHARD, SHARD), SHARD), :])
    norms = []
    for i in range(SHARD // LANES):
        lanes = slice(i * LANES, (i + 1) * LANES)
        z = gate[:, lanes]
        sig = sigmoid(z)
        silu = z * sig
        y_here = y[:, lanes]
        gated = y_here * silu
        d_norm = d_norms[:, lanes]
        gained = scale * gain[:, lanes]
        norms.append((gated * gained).astype(BF16))
        d_gated = d_norm * gained - gated * inner
        total = jnp.sum(d_norm * gated * scale, axis=0, keepdims=True)
        dgain_ref[:, lanes] = jnp.broadcast_to(total, (8, LANES))
        dy_ref[:, lanes] = (d_gated * silu).astype(BF16)
        dz_ref[:, lanes] = (d_gated * y_here * sig * (1.0 + z * (1.0 - sig))).astype(BF16)
    norm = jnp.concatenate(norms, axis=1)
    grad_ref[...] = dot(norm.T, bg).astype(BF16) if grad_ref.shape[1] == WIDTH else norm.T


def gate_back(info, cot, y, gate, gain, branch, scale, weight, with_grad):
    wide, local = whole((ROWS, WIDTH)), columns(ROWS, SHARD)
    grad_width = WIDTH if with_grad else ROWS
    return pl.pallas_call(
        functools.partial(gate_back_body, weight),
        grid=(4,),
        out_shape=(
            shape((ROWS, WIDTH), BF16),
            shape((ROWS, LOCAL), BF16),
            shape((ROWS, LOCAL), BF16),
            shape((LOCAL, grad_width), BF16),
            shape((8, LOCAL)),
        ),
        in_specs=[SMEM, wide, local, local, columns(1, SHARD), wide, whole((ROWS, LANES))]
        + weight.specs(),
        out_specs=(
            wide,
            local,
            local,
            pl.BlockSpec((SHARD, grad_width), lambda b: (b, 0)),
            columns(8, SHARD),
        ),
        scratch_shapes=weight.scratch() + [pltpu.VMEM((ROWS, LANES), F32)],
        compiler_params=params(),
        cost_estimate=pl.CostEstimate(
            flops=4 * ROWS * WIDTH * LOCAL, bytes_accessed=17_000_000, transcendentals=800_000
        ),
        name="gate_back",
    )(info, cot, y, gate, gain, branch, scale, *weight.arrays)


def own_grad_body(dy, bca, cum, msg_in, dz, normed, own1_ref, msg_ref, grad_ref, ct, grow):
    g = pl.program_id(0)
    grad_ref[...] = dot(normed[...].T, dz[...]).astype(BF16)

    @pl.when(g == 0)
    def _():
        ct[...] = bca[:, STATE:].T.astype(BF16)
        grow[...] = jnp.exp(cum[...])

    factor = rolled(grow[...], g)
    weighted = (dy[...].astype(F32) * spread(factor)).astype(BF16)
    own0 = dot(ct[:, :HALF], half(weighted, 0))
    own1 = dot(ct[:, HALF:], half(weighted, 1))
    own1_ref[0] = own1
    grad = (spread(factor[HALF - 1 : HALF]) * own1 + own0).astype(BF16)
    for r in range(2):
        msg_ref[r, :STATE_HALF, :] = grad[r * STATE_HALF : (r + 1) * STATE_HALF]
        msg_ref[r, STATE_HALF:, :] = msg_in[r, STATE_HALF:, :]


def own_grad(dy, bca, cum, msg, dz, normed):
    return pl.pallas_call(
        own_grad_body,
        grid=(GROUPS,),
        out_shape=(
            shape((GROUPS, STATE, BLOCK)),
            shape((CHUNKS, MESSAGE, BLOCK), BF16),
            shape((WIDTH, LOCAL), BF16),
        ),
        in_specs=[
            columns(ROWS, BLOCK),
            whole((ROWS, 256)),
            whole((ROWS, LANES)),
            MESSAGES,
            whole((ROWS, LOCAL)),
            columns(ROWS, SHARD),
        ],
        out_specs=(grouped(STATE), MESSAGES, pl.BlockSpec((SHARD, LOCAL), lambda b: (b, 0))),
        scratch_shapes=[pltpu.VMEM((STATE, ROWS), BF16), pltpu.VMEM((ROWS, LANES), F32)],
        compiler_params=params(),
        cost_estimate=pl.CostEstimate(
            flops=2 * ROWS * WIDTH * LOCAL, bytes_accessed=8_000_000, transcendentals=0
        ),
        name="own_grad",
    )(dy, bca, cum, msg, dz, normed)


def inside_back_body(
    dy, xa, bca, cum, dt, hpar,
    dx_ref, dskip_ref, gsum_ref, u_ref, dbc_ref, cum_t, scores, dscores,
):
    g = pl.program_id(0)

    @pl.when(g == 0)
    def _():
        tri = lower_triangle()
        for q in range(2):
            b, c = half(bca[:, :STATE], q).astype(BF16), half(bca[:, STATE:], q).astype(BF16)
            scores[q] = dot_nt(b, c) * tri.T
            cum_t[:, q * HALF : (q + 1) * HALF] = half(cum[...], q).T
        dscores[...] = jnp.zeros((2, HALF, HALF), F32)
        u_ref[...] = jnp.zeros((ROWS, LANES), F32)

    cols = rolled(cum[...], g)
    rows = cum_t[pl.ds(pl.multiple_of(8 * g, 8), 8), :]
    steps = rolled(dt[...], g)
    skips = rolled(hpar[...], g)[2:3, :]
    low = lane_of((HALF, LANES)) < HEADDIM
    lane = lane_of((HALF, LANES))
    gsum_ref[...] = jnp.zeros((8, ROWS), F32)
    for q in range(2):
        here = slice(q * HALF, (q + 1) * HALF)
        u_here = u_ref[here, :]
        for p in range(OWN // 2):
            lanes = slice(p * LANES, (p + 1) * LANES)
            dy_pair = dy[here, lanes]
            x = xa[here, lanes]
            zero = jnp.zeros_like(dy_pair)
            both = jnp.concatenate(
                [jnp.where(low, dy_pair, zero), jnp.where(low, zero, dy_pair)], axis=0
            )
            dw = dot_nt(x.astype(BF16), both)
            mats = []
            for n, i in enumerate((2 * p, 2 * p + 1)):
                gap = rows[i : i + 1, here] - half(cols, q)[:, i : i + 1]
                decay = jnp.exp(jnp.minimum(gap, 0.0))
                step = half(steps, q)[:, i : i + 1]
                weight = decay * scores[q]
                mats.append(weight.astype(BF16))
                dw_here = dw[:, n * HALF : (n + 1) * HALF]
                dscores[q] += decay * dw_here * step
                direct = weight * dw_here
                total = jnp.sum(direct, axis=1, keepdims=True)
                u_here = jnp.where(lane == 8 * g + i, total, u_here)
                gsum_ref[i : i + 1, here] = jnp.sum(direct * step, axis=0, keepdims=True)
            dx = dot(jnp.concatenate(mats, axis=1), both)
            dy_wide = dy_pair.astype(F32)
            dx_ref[here, lanes] = dx * pair_lanes(half(steps, q), p) + dy_wide * pair_lanes(skips, p)
            skip_sum = jnp.sum(dy_wide * x, axis=0, keepdims=True)
            if q == 0:
                dskip_ref[:, lanes] = jnp.broadcast_to(skip_sum, (8, LANES))
            else:
                dskip_ref[:, lanes] += skip_sum
        u_ref[here, :] = u_here

    @pl.when(g == GROUPS - 1)
    def _():
        tri = lower_triangle()
        for q in range(2):
            b, c = half(bca[:, :STATE], q).astype(BF16), half(bca[:, STATE:], q).astype(BF16)
            ds_t = dscores[q] * tri.T
            dbc_ref[q * HALF : (q + 1) * HALF, :STATE] = dot(ds_t.astype(BF16), c)
            dbc_ref[q * HALF : (q + 1) * HALF, STATE:] = dot(ds_t.T.astype(BF16), b)


def inside_back(dy, xa, bca, cum, dt, hpar):
    return pl.pallas_call(
        inside_back_body,
        grid=(GROUPS,),
        out_shape=(
            shape((ROWS, LOCAL)),
            shape((8, LOCAL)),
            shape((8 * GROUPS, ROWS)),
            shape((ROWS, LANES)),
            shape((ROWS, 256)),
        ),
        in_specs=[
            columns(ROWS, BLOCK),
            columns(ROWS, BLOCK),
            whole((ROWS, 256)),
            whole((ROWS, LANES)),
            whole((ROWS, LANES)),
            whole((8, LANES)),
        ],
        out_specs=(
            columns(ROWS, BLOCK),
            columns(8, BLOCK),
            pl.BlockSpec((8, ROWS), lambda g: (g, 0)),
            whole((ROWS, LANES)),
            whole((ROWS, 256)),
        ),
        scratch_shapes=[
            pltpu.VMEM((LANES, ROWS), F32),
            pltpu.VMEM((2, HALF, HALF), F32),
            pltpu.VMEM((2, HALF, HALF), F32),
        ],
        compiler_params=params(),
        cost_estimate=pl.CostEstimate(
            flops=4 * HEADS * HALF * HALF * LANES, bytes_accessed=4_500_000, transcendentals=800_000
        ),
        name="inside_back",
    )(dy, xa, bca, cum, dt, hpar)


def conv_back(d_active, values, halo, cpar, keep, ext, ext_d):
    width = values.shape[1]
    total = conv_sum_of(values, halo, cpar, keep, ext)
    sig = sigmoid(total)
    d_sum = d_active * sig * (1.0 + total * (1.0 - sig))
    ext_d[0:16, :width] = jnp.zeros((16, width), F32)
    ext_d[16 : 16 + ROWS, :width] = d_sum
    ext_d[16 + ROWS :, :width] = jnp.zeros((16, width), F32)
    d_in = jnp.zeros((ROWS + 16, width), F32)
    for k in range(KERNEL):
        d_in = d_in + cpar[k : k + 1, :] * ext_d[3 - k : 3 - k + ROWS + 16, :width]
    row = row_of((8, width))
    d_par = jnp.where(row == 4, jnp.sum(d_sum, axis=0, keepdims=True), 0.0)
    for k in range(KERNEL):
        tap = jnp.sum(d_sum * ext[13 + k : 13 + k + ROWS, :width], axis=0, keepdims=True)
        d_par = jnp.where(row == k, tap, d_par)
    return d_in, d_par


def finish_body(
    info, xa, dxi, dy, mixed, halo, cpar, bc, halo_bc, cpar_bc, bca, cum, dt, rate, hpar, lam, hin, s0, own1, u, gsum, dbc,
    dmx_ref, dmbc_ref, tailx_ref, tailbc_ref, edgex_ref, edgebc_ref, dcx_ref, dcbc_ref, dhead_ref,
    ext, ext_d, grow, tail, v_sum, q_sum, end_sum, dbc_sum,
):
    g = pl.program_id(0)
    keep = info[1].astype(F32)

    @pl.when(g == 0)
    def _():
        grow[...] = jnp.exp(cum[...])
        for q in range(2):
            here = half(cum[...], q)
            tail[q * HALF : (q + 1) * HALF, :] = jnp.exp(here[HALF - 1 :, :] - here)
        v_sum[...] = jnp.zeros((ROWS, LANES), F32)
        q_sum[...] = jnp.zeros((ROWS, LANES), F32)
        end_sum[...] = jnp.zeros((16, LANES), F32)
        dbc_sum[...] = dbc[...]

    sums = head_sum_matrix(g)
    factor = rolled(grow[...], g)
    tails = rolled(tail[...], g)
    steps = rolled(dt[...], g)
    ends = [spread(factor[HALF - 1 : HALF]), spread(factor[ROWS - 1 : ROWS])]
    lam1 = lam[0].astype(F32)
    lams = [ends[1] * lam1 + own1[0], lam1]
    first = hin[0].astype(F32)
    states = [first, ends[0] * first + s0[0]]
    d_x = []
    for q in range(2):
        here = slice(q * HALF, (q + 1) * HALF)
        b, c = bca[here, :STATE].astype(BF16), bca[here, STATE:].astype(BF16)
        lam_q, state_q = lams[q].astype(BF16), states[q].astype(BF16)
        tail_wide = spread(half(tails, q))
        tail_step = tail_wide * spread(half(steps, q))
        x, dy_q = xa[here, :], dy[here, :].astype(F32)
        lb = dot(b, lam_q) * tail_wide
        d_x.append(dxi[here, :] + lb * spread(half(steps, q)))
        v_sum[here, :] += dot((x * lb).astype(BF16), sums)
        grow_wide = spread(half(factor, q))
        dy_grow = (dy_q * grow_wide).astype(BF16)
        carried = dot(c, state_q)
        q_sum[here, :] += dot((dy_q * grow_wide * carried).astype(BF16), sums)
        dbc_sum[here, :STATE] += dot_nt((x * tail_step).astype(BF16), lam_q)
        dbc_sum[here, STATE:] += dot_nt(dy_grow, state_q)
        last = jnp.sum(lams[q] * states[q], axis=0, keepdims=True) * ends[q]
        high = last.astype(BF16).astype(F32)
        both = jnp.where(row_of((16, BLOCK)) == 0, high, last - high).astype(BF16)
        both = dot(both, sums)
        end_sum[8 * q : 8 * q + 8, :] += both[0:1] + both[1:2]
    d_in, d_par = conv_back(
        jnp.concatenate(d_x, axis=0), mixed[...], halo[...], cpar[...], keep, ext, ext_d
    )
    dmx_ref[...] = d_in[16:].astype(BF16)
    tailx_ref[...] = d_in[ROWS:]
    edgex_ref[...] = (d_in[:16] * keep).astype(BF16)
    dcx_ref[...] = d_par

    @pl.when(g == GROUPS - 1)
    def _():
        d_bc, d_par_bc = conv_back(
            dbc_sum[...], bc[...], halo_bc[...], cpar_bc[...], keep, ext, ext_d
        )
        dmbc_ref[:, :256] = d_bc[16:].astype(BF16)
        tailbc_ref[...] = d_bc[ROWS:]
        edgebc_ref[...] = (d_bc[:16] * keep).astype(BF16)
        dcbc_ref[...] = d_par_bc
        rates = -jnp.exp(hpar[1:2, :])
        logit = rate[...] + hpar[0:1, :]
        upper = lower_triangle().T
        before = lower_triangle(True)
        d_bias = jnp.zeros((1, LANES), F32)
        d_log = jnp.zeros((1, LANES), F32)
        usable = usable_rows(info)
        for q in range(2):
            here = slice(q * HALF, (q + 1) * HALF)
            step = dt[here, :]
            gs = gsum[...][:, here].T
            gs = jnp.concatenate([gs, jnp.zeros((HALF, LANES - 8 * GROUPS), F32)], axis=1)
            d_decay = exact_dot(upper, gs - step * u[here, :] + q_sum[here, :])
            d_decay = d_decay + exact_dot(before, step * v_sum[here, :])
            d_decay = d_decay + end_sum[8 * q : 8 * q + 1, :]
            d_step = u[here, :] + v_sum[here, :] + rates * d_decay
            d_rate = half(usable, q) * d_step * sigmoid(half(logit, q))
            d_bias += jnp.sum(d_rate, axis=0, keepdims=True)
            d_log += jnp.sum(d_decay * step * rates, axis=0, keepdims=True)
            dmbc_ref[here, 256:] = d_rate.astype(BF16)
        row = row_of((8, LANES))
        dhead_ref[...] = jnp.where(row == 0, d_bias, jnp.where(row == 1, d_log, 0.0))


def finish_call(
    info, xa, dxi, dy, mixed, halo, cpar, bca, cum, dt, rate, hpar, lam, hin, s0, own1, u, gsum, dbc
):
    bc_at = LOCAL // 256
    wide = whole((ROWS, LANES))
    return pl.pallas_call(
        finish_body,
        grid=(GROUPS,),
        out_shape=(
            shape((ROWS, LOCAL), BF16),
            shape((ROWS, 384), BF16),
            shape((16, LOCAL)),
            shape((16, 256)),
            shape((16, LOCAL), BF16),
            shape((16, 256), BF16),
            shape((8, LOCAL)),
            shape((8, 256)),
            shape((8, LANES)),
        ),
        in_specs=[
            SMEM,
            columns(ROWS, BLOCK),
            columns(ROWS, BLOCK),
            columns(ROWS, BLOCK),
            columns(ROWS, BLOCK),
            columns(16, BLOCK),
            columns(8, BLOCK),
            pl.BlockSpec((ROWS, 256), lambda g: (0, bc_at)),
            pl.BlockSpec((16, 256), lambda g: (0, bc_at)),
            pl.BlockSpec((8, 256), lambda g: (0, bc_at)),
            whole((ROWS, 256)),
            wide,
            wide,
            wide,
            whole((8, LANES)),
            grouped(STATE),
            grouped(STATE),
            grouped(STATE),
            grouped(STATE),
            wide,
            whole((8 * GROUPS, ROWS)),
            whole((ROWS, 256)),
        ],
        out_specs=(
            columns(ROWS, BLOCK),
            whole((ROWS, 384)),
            columns(16, BLOCK),
            whole((16, 256)),
            columns(16, BLOCK),
            whole((16, 256)),
            columns(8, BLOCK),
            whole((8, 256)),
            whole((8, LANES)),
        ),
        scratch_shapes=[
            pltpu.VMEM((ROWS + 32, BLOCK), F32),
            pltpu.VMEM((ROWS + 32, BLOCK), F32),
            pltpu.VMEM((ROWS, LANES), F32),
            pltpu.VMEM((ROWS, LANES), F32),
            pltpu.VMEM((ROWS, LANES), F32),
            pltpu.VMEM((ROWS, LANES), F32),
            pltpu.VMEM((16, LANES), F32),
            pltpu.VMEM((ROWS, 256), F32),
        ],
        compiler_params=params(),
        cost_estimate=pl.CostEstimate(
            flops=10 * ROWS * STATE * LOCAL, bytes_accessed=7_500_000, transcendentals=800_000
        ),
        name="finish_back",
    )(
        info, xa, dxi, dy, mixed, halo, cpar, mixed, halo, cpar, bca, cum, dt, rate, hpar,
        lam, hin, s0, own1, u, gsum, dbc,
    )


def gate_in_back_body(weight, info, dz, token, *rest):
    refs = len(weight.arrays)
    w_refs, (out_ref, buffer, sems) = rest[:refs], rest[refs:]

    @pl.when(pl.program_id(0) == 0)
    def _():
        weight.start(w_refs, info, buffer, sems)
        for n in range(4):
            weight.wait(w_refs, info, n, buffer, sems)

    rows = pl.ds(pl.multiple_of(pl.program_id(0) * SHARD, SHARD), SHARD)
    out_ref[...] = dot_nt(dz[...], buffer[rows, :])


def gate_in_back(info, dz, weight, token):
    return pl.pallas_call(
        functools.partial(gate_in_back_body, weight),
        grid=(4,),
        out_shape=shape((ROWS, WIDTH)),
        in_specs=[SMEM, whole((ROWS, LOCAL)), ANYWHERE] + weight.specs(),
        out_specs=columns(ROWS, SHARD),
        scratch_shapes=weight.scratch(),
        compiler_params=params(),
        cost_estimate=pl.CostEstimate(
            flops=2 * ROWS * WIDTH * LOCAL, bytes_accessed=7_000_000, transcendentals=0
        ),
        name="gate_in_back",
    )(info, dz, token, *weight.arrays)


def patch_body(dmx, dmbc, tailx, tailbc, edge, token, dxc_ref):
    dxc_ref[:, :LOCAL] = dmx[...]
    dxc_ref[:, LOCAL:] = dmbc[...]
    late = edge[...].astype(F32)
    dxc_ref[ROWS - 16 :, :LOCAL] = (tailx[...] + late[:, :LOCAL]).astype(BF16)
    dxc_ref[ROWS - 16 :, LOCAL:MIXED] = (tailbc[...] + late[:, LOCAL:]).astype(BF16)


def patch(dmx, dmbc, tailx, tailbc, edge, token):
    arrays = (dmx, dmbc, tailx, tailbc, edge)
    return pl.pallas_call(
        patch_body,
        out_shape=shape((ROWS, PACKED), BF16),
        in_specs=[whole(v.shape) for v in arrays] + [ANYWHERE],
        out_specs=whole((ROWS, PACKED)),
        compiler_params=params(),
        cost_estimate=pl.CostEstimate(flops=100_000, bytes_accessed=2_000_000, transcendentals=0),
        name="patch",
    )(*arrays, token)


def mixed_back_body(weight, tokens, info, dxc, part, h_ref, normed, *rest):
    refs = len(weight.arrays)
    w_refs, rest = rest[:refs], rest[refs + tokens :]
    (out_ref, dgain_ref, *grad_ref), (buffer, sems, scale_ref) = rest[:-3], rest[-3:]
    b = pl.program_id(0)
    block = pl.ds(pl.multiple_of(b * SHARD, SHARD), SHARD)

    @pl.when(b == 0)
    def _():
        weight.start(w_refs, info, buffer, sems)
        h = h_ref[...].astype(F32)
        scale = lax.rsqrt(jnp.mean(h * h, axis=1, keepdims=True) + EPSILON)
        scale_ref[...] = jnp.broadcast_to(scale, (ROWS, LANES))

    for ref in grad_ref:
        ref[...] = dot(normed[...].T, dxc[...]).astype(BF16)

    @pl.when(b == 0)
    def _():
        for n in range(4):
            weight.wait(w_refs, info, n, buffer, sems)

    d_norm = part[...] + dot_nt(dxc[...], buffer[block, :])
    out_ref[...] = d_norm
    total = jnp.sum(d_norm * h_ref[:, block].astype(F32) * scale_ref[:, :1], axis=0, keepdims=True)
    dgain_ref[...] = jnp.broadcast_to(total, (8, SHARD))


def mixed_back(info, dxc, part, h, normed, weight, with_grad, tokens):
    wide, local = whole((ROWS, WIDTH)), columns(ROWS, SHARD)
    outs = [shape((ROWS, WIDTH)), shape((8, WIDTH))]
    specs = [local, columns(8, SHARD)]
    if with_grad:
        outs.append(shape((WIDTH, PACKED), BF16))
        specs.append(pl.BlockSpec((SHARD, PACKED), lambda b: (b, 0)))
    return pl.pallas_call(
        functools.partial(mixed_back_body, weight, len(tokens)),
        grid=(4,),
        out_shape=outs,
        in_specs=[SMEM, whole((ROWS, PACKED)), local, wide, local]
        + weight.specs()
        + [ANYWHERE] * len(tokens),
        out_specs=specs,
        scratch_shapes=weight.scratch() + [pltpu.VMEM((ROWS, LANES), F32)],
        compiler_params=params(),
        cost_estimate=pl.CostEstimate(
            flops=4 * ROWS * WIDTH * PACKED, bytes_accessed=14_000_000, transcendentals=0
        ),
        name="mixed_back",
    )(info, dxc, part, h, normed, *weight.arrays, *tokens)


def norm_back_body(own, came, h_ref, cot, gain, dh_ref, low_ref):
    h = h_ref[...].astype(F32)
    scale = lax.rsqrt(jnp.mean(h * h, axis=1, keepdims=True) + EPSILON)
    d_norm = own[...] + came[...]
    inner = jnp.mean(d_norm * gain[...] * h, axis=1, keepdims=True) * scale * scale * scale
    dh = cot[...].astype(F32) + scale * d_norm * gain[...] - h * inner
    dh_ref[...] = dh
    low_ref[...] = dh.astype(BF16)


def norm_back(own, came, h, cot, gain):
    rows = pl.BlockSpec((HALF // 2, WIDTH), lambda i: (i, 0))
    return pl.pallas_call(
        norm_back_body,
        grid=(4,),
        out_shape=(shape((ROWS, WIDTH)), shape((ROWS, WIDTH), BF16)),
        in_specs=[rows] * 4 + [whole((1, WIDTH))],
        out_specs=(rows, rows),
        compiler_params=params(),
        cost_estimate=pl.CostEstimate(flops=3_000_000, bytes_accessed=8_000_000, transcendentals=0),
        name="norm_back",
    )(own, came, h, cot, gain)


def z_shift(r):
    return "dp", [(z, (z + r) % 4) for z in range(4)]


def y_shift(r):
    return "ctx", [(j, (j + 4 * r) % 16) for j in range(16)]


def x_shift(r):
    return "ctx", [(j, j - j % 4 + (j + r) % 4) for j in range(16)]


SHIFTS = {"z": z_shift, "y": y_shift, "x": x_shift}


def send(value, axis, r):
    name, pairs = SHIFTS[axis](r % 4)
    return lax.ppermute(value, name, pairs)


def swapped(value):
    return lax.ppermute(value, "section", [(0, 1), (1, 0)])


def nothing_body(*refs):
    refs[-1][...] = jnp.zeros((8, LANES), jnp.int32)


def after(values, place):
    nothing = pl.pallas_call(
        nothing_body,
        out_shape=shape((8, LANES), jnp.int32),
        in_specs=[ANYWHERE] * len(values),
        out_specs=whole((8, LANES)),
        compiler_params=params(),
        cost_estimate=pl.CostEstimate(flops=0, bytes_accessed=4096, transcendentals=0),
        name="after",
    )(*values)[0, 0]
    return {axis: n + nothing for axis, n in place.items()}


def fetched(mine, came, layer, section, place):
    rows = SHARD // 2

    def piece(source, side, axis):
        return lax.dynamic_slice_in_dim(source, side * rows + place[axis] * PIECE, PIECE, 0)

    parts = [
        jnp.where(section == layer, piece(mine, side, axis), piece(came, side, axis))
        for side, axis in enumerate("xy")
    ]
    if mine.shape[0] == TALL:
        parts.append(jnp.where(section == layer, mine[SHARD:], came[SHARD:]))
    return jnp.concatenate(parts)


def pieces(mine, came, got, late):
    out = [mine, came]
    for side, axis in enumerate("xy"):
        rows = slice(side * PIECE, (side + 1) * PIECE)
        stack = jnp.concatenate(
            [lax.dynamic_slice_in_dim(g, rows.start + late, PIECE, 0) for g in got[1:]]
        )
        out += [stack] + [send(stack, axis, -r) for r in range(1, 4)]
    return out


def summed(terms):
    a, b, c, d = (t.astype(F32) for t in terms)
    return (a + c) + (b + d)


def arrived(terms, axis):
    return [terms[0]] + [send(terms[r], axis, r) for r in range(1, 4)]


def terms_body(axis, cuts, stacked, info, *rest):
    factors, rest = rest[: 2 * len(cuts)], rest[2 * len(cuts) :]
    small, outs, total = rest[:-2] if stacked else rest[:-5], rest[-5:-1], rest[-1]
    column = 0
    for n, cols in enumerate(cuts):
        there = slice(column, column + cols.stop - cols.start)
        total[:, there] = dot(factors[2 * n][...], factors[2 * n + 1][:, cols])
        column = there.stop
    count = 96 if axis == "y" else 24
    starts = [z * SHARD for z in range(4)]
    if axis == "x":
        starts = [start + y * 96 for start in starts for y in range(4)]
    for r in range(4):
        first = r * count
        if not stacked:
            first = lax.rem(info[11 if axis == "y" else 12] + r, 4) * count
        parts = [total[pl.ds(pl.multiple_of(start + first, 8), count), :] for start in starts]
        out = rest[-2].at[r] if stacked else outs[r]
        out[:SHARD, :] = jnp.concatenate(parts, axis=0).astype(BF16)
        for ref in small:
            out[SHARD:, :] = ref[...]


def four(dims, stacked):
    if stacked:
        return shape((4, *dims), BF16), whole((4, *dims))
    return [shape(dims, BF16)] * 4, [whole(dims)] * 4


def terms(info, axis, products, small=(), stacked=False):
    cuts = [cols for _, _, cols in products]
    width = sum(cols.stop - cols.start for cols in cuts)
    rows = SHARD + sum(v.shape[0] for v in small)
    arrays = [v for left, right, _ in products for v in (left, right)] + list(small)
    outs, specs = four((rows, width), stacked)
    return pl.pallas_call(
        functools.partial(terms_body, axis, cuts, stacked),
        out_shape=outs,
        in_specs=[SMEM] + [whole(v.shape) for v in arrays],
        out_specs=specs,
        scratch_shapes=[pltpu.VMEM((4 * SHARD, width), F32)],
        compiler_params=params(),
        cost_estimate=pl.CostEstimate(
            flops=8 * SHARD * ROWS * width, bytes_accessed=8_000_000, transcendentals=0
        ),
        name="terms",
    )(info, *arrays)


def fold_body(slot, counts, outer, inner, rest_rows, stacked, info, *rest):
    refs, outs, total = rest[: sum(counts)], rest[-2:-1] if stacked else rest[-5:-1], rest[-1]
    column = 0
    for count in counts:
        arrays, refs = refs[:count], refs[count:]
        cols = slice(column, column + arrays[0].shape[-1])
        if count == 4:
            total[:, cols] = summed([a[...] for a in arrays])
        elif len(arrays[0].shape) == 3:
            total[:, cols] = summed([arrays[0][n] for n in range(4)])
        else:
            total[:, cols] = arrays[0][...].astype(F32)
        column = cols.stop
    for r in range(4):
        first = r * inner if stacked else lax.rem(info[slot] + r, 4) * inner
        parts = [
            total[pl.ds(pl.multiple_of(n * 4 * inner + first, 8), inner), :] for n in range(outer)
        ]
        if rest_rows:
            parts.append(total[4 * outer * inner :, :])
        out = outs[0].at[r] if stacked else outs[r]
        out[...] = jnp.concatenate(parts, axis=0).astype(BF16)


def fold(info, axis, groups, outer, inner, token, stacked=False):
    slot = 10 + "zyx".index(axis)
    arrays = [a for group in groups for a in group]
    tokens = token if isinstance(token, tuple) else (token,)
    rows, width = arrays[0].shape[-2], sum(group[0].shape[-1] for group in groups)
    more = rows - 4 * outer * inner
    outs, specs = four((outer * inner + more, width), stacked)
    counts = [len(group) for group in groups]
    return pl.pallas_call(
        functools.partial(fold_body, slot, counts, outer, inner, more, stacked),
        out_shape=outs,
        in_specs=[SMEM] + [whole(a.shape) for a in arrays] + [ANYWHERE] * len(tokens),
        out_specs=specs,
        scratch_shapes=[pltpu.VMEM((rows, width), F32)],
        compiler_params=params(),
        cost_estimate=pl.CostEstimate(flops=2_000_000, bytes_accessed=8_000_000, transcendentals=0),
        name="fold",
    )(info, *arrays, *tokens)


def last_fold_body(info, *rest):
    left, right, outs, total = rest[:4], rest[4:8], rest[9:13], rest[13]
    width = left[0].shape[1]
    total[:96, :width] = summed([a[...] for a in left])
    total[96:, :width] = jnp.zeros((SMALL, width), F32)
    total[:, width:] = summed([a[...] for a in right])
    for r in range(4):
        first = pl.multiple_of(lax.rem(info[10] + r, 4) * 24, 8)
        parts = [total[pl.ds(first, 24), :], total[96:, :]]
        outs[r][...] = jnp.concatenate(parts, axis=0).astype(BF16)


def last_fold(info, left, right, token):
    width = left[0].shape[1] + right[0].shape[1]
    out = shape((24 + SMALL, width), BF16)
    arrays = (*left, *right)
    return pl.pallas_call(
        last_fold_body,
        out_shape=[out] * 4,
        in_specs=[SMEM] + [whole(a.shape) for a in arrays] + [ANYWHERE],
        out_specs=[whole(out.shape)] * 4,
        scratch_shapes=[pltpu.VMEM((96 + SMALL, width), F32)],
        compiler_params=params(),
        cost_estimate=pl.CostEstimate(flops=500_000, bytes_accessed=2_000_000, transcendentals=0),
        name="last_fold",
    )(info, *arrays, token)


PARITY = [[j for j in range(16) if j % 2 == e] for e in range(2)]
NEIGHBOURS = [(j, j ^ 1) for j in range(16)]
GROUPS_OF = {
    "y": [[4 * y + x for y in range(4)] for x in range(4)],
    "x": [[4 * y + x for x in range(4)] for y in range(4)],
}


def traded(value, axis):
    return lax.all_to_all(value, "ctx", 0, 0, axis_index_groups=GROUPS_OF[axis])


def exchange(value):
    return lax.all_to_all(value, "ctx", 0, 0, axis_index_groups=PARITY)


def halo_shift(value, step):
    pairs = [(j, j + 2 * step) for j in range(16) if 0 <= j + 2 * step < 16]
    return lax.ppermute(value, "ctx", pairs)


def halves(values, section):
    grid = values.reshape(values.shape[0], GROUPS, 2, -1)
    size = values.shape[1] // 2
    return [
        lax.dynamic_index_in_dim(grid, i, 2, False).reshape(-1, size)
        for i in (section, 1 - section)
    ]


def turns(low, high):
    rows = low.shape[0]
    parts = [v.reshape(rows, GROUPS, 1, -1) for v in (low, high)]
    return jnp.concatenate(parts, axis=2).reshape(rows, -1)


def pick_x_body(info, x_ref, dt_ref, *rest):
    smalls, outs, small = rest[:7], rest[7:9], rest[9]
    small[...] = jnp.zeros((16, PACKED), F32)
    row = 0
    for ref in smalls[:4]:
        count, width = ref.shape
        small[row : row + count, :width] = ref[...].astype(F32)
        row += count
    for ref in smalls[4:]:
        left = ref[...]
        for _ in range(3):
            part = left.astype(BF16).astype(F32)
            small[row : row + 1, :HEADS] = part
            left = left - part
            row += 1
    head, lane = row_of((HEADS, LANES)), lane_of((HEADS, LANES))
    for out, side in zip(outs, (info[0], 1 - info[0]), strict=True):
        for d in range(GROUPS):
            cols = pl.ds(pl.multiple_of((2 * d + side) * BLOCK, LANES), BLOCK)
            out[:SHARD, d * BLOCK : (d + 1) * BLOCK] = x_ref[:, cols]
        out[:SHARD, LOCAL:MIXED] = x_ref[:, INNER:]
        here = (head // OWN == 2 * (lane // 8) + side) & (head % OWN == lane % 8)
        out[:SHARD, MIXED:] = dot(dt_ref[...], here.astype(BF16)).astype(BF16)
        out[SHARD:, :] = small[...].astype(BF16)


def pick_x(section, x, dt, smalls):
    return pl.pallas_call(
        pick_x_body,
        out_shape=[shape((TALL, PACKED), BF16)] * 2,
        in_specs=[SMEM, whole((SHARD, CONV_CH)), whole((SHARD, HEADS))]
        + [whole(v.shape) for v in smalls],
        out_specs=[whole((TALL, PACKED))] * 2,
        scratch_shapes=[pltpu.VMEM((16, PACKED), F32)],
        compiler_params=params(),
        cost_estimate=pl.CostEstimate(flops=0, bytes_accessed=6_000_000, transcendentals=0),
        name="pick_x",
    )(section, x, dt, *smalls)


def unpack_body(count, info, *rest):
    refs, (cpar, gain_one, gain_two, hpar, held, full, sems) = rest[:count], rest[count:]
    copies = []
    for n in range(4):
        if count == 4:
            source, to = refs[n].at[pl.ds(2 * PIECE, 16)], lax.rem(info[10] + n, 4)
        else:
            source, to = refs[0].at[pl.ds(n * TALL + SHARD, 16)], n
        copies.append(pltpu.make_async_copy(source, held.at[to], sems.at[n]))
    for c in copies:
        c.start()
    for c in copies:
        c.wait()
    section = info[13]
    half_cols = pl.ds(pl.multiple_of(section * BLOCK, LANES), BLOCK)
    for z in range(4):
        values = held[z].astype(F32)
        full[:, z * 832 : (z + 1) * 832] = values[:8, :832]
        gain_one[:, z * SHARD : (z + 1) * SHARD] = values[5:6, :SHARD]
        gain_two[:, z * BLOCK : (z + 1) * BLOCK] = held[z, :, half_cols].astype(F32)[6:7]
    for d in range(GROUPS):
        cols = pl.ds(pl.multiple_of((2 * d + section) * BLOCK, LANES), BLOCK)
        cpar[:, d * BLOCK : (d + 1) * BLOCK] = full[:, cols]
    cpar[:, LOCAL:] = full[:, INNER:]
    values = held[0, :, :LANES].astype(F32)
    heads = [values[n : n + 1] + values[n + 1 : n + 2] + values[n + 2 : n + 3] for n in (7, 10, 13)]
    heads = jnp.concatenate(heads + [jnp.zeros((5, LANES), F32)], axis=0)
    head, lane = row_of((LANES, LANES)), lane_of((LANES, LANES))
    here = (head // OWN == 2 * (lane // 8) + section) & (head % OWN == lane % 8)
    hpar[...] = exact_dot(heads, here.astype(F32))


def unpack(info, arrays):
    shapes = ((8, MIXED), (1, WIDTH), (1, LOCAL), (8, LANES))
    return pl.pallas_call(
        functools.partial(unpack_body, len(arrays)),
        out_shape=[shape(dims) for dims in shapes],
        in_specs=[SMEM] + [ANYWHERE] * len(arrays),
        out_specs=[whole(dims) for dims in shapes],
        scratch_shapes=[
            pltpu.VMEM((4, 16, PACKED), BF16),
            pltpu.VMEM((8, CONV_CH), F32),
            pltpu.SemaphoreType.DMA((4,)),
        ],
        compiler_params=params(),
        cost_estimate=pl.CostEstimate(flops=0, bytes_accessed=400_000, transcendentals=0),
        name="unpack",
    )(info, *arrays)


def pick_zo_body(info, z_ref, o_ref, token, *outs):
    for out, side in zip(outs, (info[0], 1 - info[0]), strict=True):
        for d in range(GROUPS):
            cols = pl.ds(pl.multiple_of((2 * d + side) * BLOCK, LANES), BLOCK)
            out[:, d * BLOCK : (d + 1) * BLOCK] = z_ref[:, cols]
        rows = pl.ds(pl.multiple_of(side * SHARD, SHARD), SHARD)
        out[:, LOCAL:] = o_ref[rows, :]


def pick_zo(section, z, o, token):
    return pl.pallas_call(
        pick_zo_body,
        out_shape=[shape((SHARD, LOCAL + WIDTH), BF16)] * 2,
        in_specs=[SMEM, whole((SHARD, INNER)), whole((2 * SHARD, WIDTH)), ANYWHERE],
        out_specs=[whole((SHARD, LOCAL + WIDTH))] * 2,
        compiler_params=params(),
        cost_estimate=pl.CostEstimate(flops=0, bytes_accessed=9_000_000, transcendentals=0),
        name="pick_zo",
    )(section, z, o, token)


def head_lanes(values):
    rows = values.shape[0]
    grid = jnp.pad(values.reshape(rows, GROUPS, OWN), ((0, 0), (0, 0), (0, 8 - OWN)))
    return jnp.pad(grid.reshape(rows, 8 * GROUPS), ((0, 0), (0, LANES - 8 * GROUPS)))


def lanes_heads(values):
    rows = values.shape[0]
    return values[:, : 8 * GROUPS].reshape(rows, GROUPS, 8)[:, :, :OWN].reshape(rows, -1)


def on_device(
    boundary,
    lengths,
    norm_gain,
    w_z,
    w_xbc,
    w_dt,
    conv_weight,
    conv_bias,
    dt_bias,
    a_log,
    d_skip,
    gate_gain,
    w_out,
):
    section = lax.axis_index("section")
    group = lax.axis_index("dp")
    ctx = lax.axis_index("ctx")
    place = {"z": group, "y": ctx // 4, "x": ctx % 4}
    micro = ctx % 2
    chunk = ctx // 2

    def ordered(mine, came):
        return jnp.where(section == 0, mine, came), jnp.where(section == 0, came, mine)

    own_rows = lax.dynamic_index_in_dim(boundary[0], micro, 0, False)
    other_rows = lax.dynamic_index_in_dim(boundary[0], 1 - micro, 0, False)
    came = lax.ppermute(other_rows, "ctx", NEIGHBOURS)
    block = jnp.where(
        micro == 0, jnp.concatenate([own_rows, came]), jnp.concatenate([came, own_rows])
    )
    hidden, cotangent = ordered(block, swapped(block))

    pair = lengths[group, micro]
    padded = (pair[0] + SPAN - 1) // SPAN * SPAN
    offset = chunk * ROWS
    begin = jnp.where(offset >= padded, padded, 0)
    length = jnp.where(offset >= padded, pair[1], pair[0])
    live = jnp.clip(length - (offset - begin), 0, ROWS)
    offsets = jnp.arange(CHUNKS, dtype=jnp.int32) * ROWS
    keeps = ((offsets != 0) & (offsets != padded)).astype(jnp.int32)
    keep = (offset != 0) & (offset != padded)
    at = [place["z"], place["y"], place["x"], section]
    info = jnp.concatenate(
        [jnp.stack([live, keep]).astype(jnp.int32), keeps, jnp.stack(at).astype(jnp.int32)]
    )

    def forward(h, layer):
        cpar, hpar = cpars[layer], hpars[layer]
        normed, mixed, rate = in_proj(
            info, h, gains_one[layer], weights_x[layer], []
        )
        halo = halo_shift(mixed[ROWS - 16 :], 1)
        gate = gate_proj(info, normed, weights_z[layer], [] if layer else ready)
        xa, bca, cum, dt, s0, msg = state_call(info, mixed, halo, cpar, rate, hpar)
        came = exchange(msg)
        y_in = inside_call(xa, bca, cum, dt, hpar)
        hin = exchange(scan_call(info, came, False, y_in, *([] if layer else cpars[1:]))).reshape(GROUPS, STATE, BLOCK)
        y, part = out_proj(
            info, y_in, bca, cum, hin, s0, gate, gains_two[layer], weights_o[layer]
        )
        result, branch, scale = join(info, h, part, swapped(part), F32 if layer else BF16)
        saved = (h, normed, mixed, halo, rate, gate, xa, bca, cum, dt, s0, msg, hin, y, branch, scale)
        return result, saved

    def backward(cot, saved, layer, higher, tokens):
        h, normed, mixed, halo, rate, gate, xa, bca, cum, dt, s0, msg, hin, y, branch, scale = saved
        cpar, hpar = cpars[layer], hpars[layer]

        def first_stage(value):
            return lax.psum_scatter(value, "dp", tiled=True)

        bg, dy, dz, grad_o, d_gain_two = gate_back(
            info, cot, y, gate, gains_two[layer], branch, scale, weights_o[layer], layer == 1
        )
        own1, msg_back, grad_z = own_grad(dy, bca, cum, msg, dz, normed)
        sums = [first_stage(grad_z)] + ([first_stage(grad_o)] if layer else [])
        came = exchange(msg_back)
        dxi, d_skips, gsum, u, dbc = inside_back(dy, xa, bca, cum, dt, hpar)
        part = gate_in_back(info, dz, weights_z[layer], msg_back)
        lam = exchange(scan_call(info, came, True, part)).reshape(GROUPS, STATE, BLOCK)
        dmx, dmbc, tailx, tailbc, edgex, edgebc, d_parx, d_parbc, d_heads = finish_call(
            info, xa, dxi, dy, mixed, halo, cpar, bca, cum, dt, rate, hpar, lam, hin, s0, own1, u, gsum, dbc
        )
        edge = halo_shift(jnp.concatenate([edgex, edgebc], axis=1), -1)
        dxc = patch(dmx, dmbc, tailx, tailbc, edge, *tokens)
        middle = 7 * LANES
        if layer == 0:
            higher_rows, higher = higher
            normed_t = normed.T
            cuts = [(normed_t, dxc, slice(0, middle)), (grad_o, bg, slice(0, WIDTH // 2))]
            left = terms(info, "y", cuts, (), True)
            part, d_gain_one = mixed_back(
                info, dxc, part, h, normed, weights_x[layer], False, [left, *higher]
            )
        else:
            part, d_gain_one, grad_x = mixed_back(
                info, dxc, part, h, normed, weights_x[layer], True, []
            )
        dh, dh_low = norm_back(part, swapped(part), h, cot, gains_one[layer])
        d_skip_row = jnp.sum(d_skips[0:1].reshape(1, 4 * OWN, HEADDIM), axis=2)
        rows = jnp.where(jnp.arange(8)[:, None] == 5, d_gain_two, d_parx)
        rows = jnp.concatenate([rows, d_parbc], axis=1)
        more = jnp.concatenate(
            [
                d_gain_one[:1],
                jnp.pad(d_heads[:2], ((0, 0), (0, WIDTH - LANES))),
                jnp.pad(head_lanes(d_skip_row), ((0, 4), (0, WIDTH - LANES))),
            ]
        )
        rows = jnp.concatenate([rows, jnp.pad(more, ((0, 0), (0, 2 * STATE)))])
        if layer == 1:
            return dh, dh_low, sums + [first_stage(grad_x)], rows

        rows = jnp.concatenate([rows, higher_rows]).astype(BF16)
        cuts = [(normed_t, dxc, slice(middle, PACKED)), (grad_o, bg, slice(WIDTH // 2, WIDTH))]
        right = arrived(terms(info, "x", cuts, (rows,)), "x")
        near = (right[1], right[3])
        tall = fold(info, "y", [[v] for v in higher + sums], 1, 96, near, True)
        left = fold(info, "x", [[traded(left, "y")]], 4, 24, tall)
        right = fold(info, "y", [right], 4, 24, dh_low)
        tall = fold(info, "x", [[traded(tall, "y")]], 1, 24, right[0])
        left, right = arrived(left, "x"), arrived(right, "y")
        final = summed(arrived(last_fold(info, left, right, tall[0]), "z"))
        left, right = left[0].shape[1], right[0].shape[1]
        rows = final[24:, left:]
        final = final[:24]
        sum_x = jnp.concatenate(
            [final[:, :middle], final[:, left : left + PACKED - middle]], axis=1
        )
        sum_o = jnp.concatenate([final[:, middle:left], final[:, left + PACKED - middle :]], axis=1)
        return dh, [arrived(tall, "x"), sum_o], sum_x, rows

    at = section.reshape(1).astype(jnp.int32)
    smalls = (conv_weight[0], conv_bias, norm_gain, gate_gain, dt_bias, a_log, d_skip)
    mine_x, other_x = pick_x(at, w_xbc[0], w_dt[0], smalls)
    came_x = swapped(other_x)
    mine_zo, other_zo = pick_zo(at, w_z[0], w_out[0], mine_x)
    came_zo = swapped(other_zo)
    first = fetched(mine_x, came_x, 0, section, after([hidden], place))
    got = [first] + [send(first, "z", -r) for r in range(1, 4)]
    small_low = got
    low_x = pieces(mine_x, came_x, got, 0)
    got = lax.all_gather(fetched(mine_zo, came_zo, 0, section, after(got[1:], place)), "dp")
    late = after(low_x[3:6] + low_x[7:10], place)["z"]
    got = [None] + [lax.dynamic_index_in_dim(got, (late + r) % 4, 0, False) for r in range(1, 4)]
    low_zo = pieces(mine_zo, came_zo, got, 0)
    here = after([low_x[2], low_x[6]], {"section": section})["section"]
    high_x = [lax.all_gather(jnp.where(here == 1, mine_x, came_x), "dp", tiled=True)]
    high_zo = [lax.all_gather(jnp.where(here == 1, mine_zo, came_zo), "dp", tiled=True)]
    ready = low_zo[3:6] + low_zo[7:10]
    weights_x = [Weight(v, n, PACKED) for n, v in enumerate((low_x, high_x))]
    weights_z = [Weight(v, n, LOCAL) for n, v in enumerate((low_zo, high_zo))]
    weights_o = [Weight(v, n, WIDTH, LOCAL) for n, v in enumerate((low_zo, high_zo))]

    unpacked = [unpack(info, v) for v in (small_low, high_x)]
    cpars, gains_one, gains_two, hpars = zip(*unpacked, strict=True)

    def returned(rows, layer):
        pairs = [(layer * 16 + a, layer * 16 + b) for a, b in NEIGHBOURS]
        other, mine = (
            lax.dynamic_slice_in_dim(rows, n * HALF, HALF, 0) for n in (1 - micro, micro)
        )
        other = lax.ppermute(other, ("section", "ctx"), pairs)
        return jnp.where(micro == 0, jnp.stack([mine, other]), jnp.stack([other, mine]))

    middle, saved_low = forward(hidden, 0)
    out_high, saved_high = forward(middle, 1)
    top_high = returned(out_high, 1)
    _, back, higher, rows = backward(cotangent, saved_high, 1, None, [top_high])
    dh_low, (tall, low_o), low_x, rows = backward(back, saved_low, 0, (rows, higher), [rows])
    at = (LOCAL, LOCAL + WIDTH, LOCAL + WIDTH + PACKED)
    high_z, high_o, high_x, low_z = jnp.split(summed(tall), at, axis=1)

    own, given = ordered(rows[:16], rows[16:])
    rows_0, rows_1 = ordered(own, swapped(given))
    wide = jnp.concatenate(
        [turns(rows_0[:8, :LOCAL], rows_1[:8, :LOCAL]), rows_0[:8, LOCAL:] + rows_1[:8, LOCAL:]],
        axis=1,
    )
    head_rows = turns(lanes_heads(rows_0[9:12, :LANES]), lanes_heads(rows_1[9:12, :LANES]))
    index = group * 16 + ctx
    d_conv = lax.dynamic_slice(wide, (0, index * 52), (5, 52))
    d_gain_two = lax.dynamic_slice(wide, (5, index * 48), (1, 48))
    d_gain_one = lax.dynamic_slice(rows_0[8:9] + rows_1[8:9], (0, index * 24), (1, 24))

    own, given = ordered(
        jnp.concatenate([low_z, low_x], axis=1), jnp.concatenate([high_z, high_x], axis=1)
    )
    first, second = ordered(own, swapped(given))
    sum_z = turns(first[:, :LOCAL], second[:, :LOCAL])
    at_x, at_bc, at_dt = LOCAL, LOCAL + LOCAL, LOCAL + MIXED
    sum_x = turns(first[:, at_x:at_bc], second[:, at_x:at_bc])
    sum_bc = first[:, at_bc:at_dt] + second[:, at_bc:at_dt]
    sum_dt = turns(lanes_heads(first[:, at_dt:]), lanes_heads(second[:, at_dt:]))

    trips = []
    for flip in range(2):
        pairs = [
            (c * 16 + j, (flip ^ (j % 2)) * 16 + 8 * c + j // 2) for c in range(2) for j in range(16)
        ]
        value = jnp.where(micro == flip, low_o, high_o)
        trips.append(lax.ppermute(value, ("section", "ctx"), pairs))
    sum_o = jnp.concatenate(ordered(*trips))

    top = jnp.where(section == 0, returned(dh_low, 0), top_high)
    return (
        top[None],
        d_gain_one,
        sum_z[None],
        jnp.concatenate([sum_x, sum_bc], axis=1)[None],
        sum_dt[None],
        d_conv[None, :4],
        d_conv[4:5],
        head_rows[0:1],
        head_rows[1:2],
        head_rows[2:3],
        d_gain_two,
        sum_o[None],
    )


def solution(mesh):
    in_specs = (
        P("section", None, ("dp", "ctx"), None),
        P(),
        P("section", "dp"),
        P("section", "dp", None),
        P("section", "dp", None),
        P("section", "dp", None),
        P("section", None, "dp"),
        P("section", "dp"),
        P("section", None),
        P("section", None),
        P("section", None),
        P("section", "dp"),
        P("section", "dp", None),
    )
    out_specs = (
        P("section", None, ("dp", "ctx"), None),
        P("section", ("dp", "ctx")),
        P("section", ("dp", "ctx"), None),
        P("section", ("dp", "ctx"), None),
        P("section", ("dp", "ctx"), None),
        P("section", None, ("dp", "ctx")),
        P("section", ("dp", "ctx")),
        P("section", None),
        P("section", None),
        P("section", None),
        P("section", ("dp", "ctx")),
        P("section", ("dp", "ctx"), None),
    )
    return jax.shard_map(
        on_device, mesh=mesh, in_specs=in_specs, out_specs=out_specs, check_vma=False
    )
```

```python
import functools

import jax
import jax.numpy as jnp
from jax import lax
from jax.experimental import pallas as pl
from jax.experimental.pallas import tpu as pltpu
from jax.sharding import PartitionSpec as P

HEADS = 48
HEADDIM = 64
STATE = 128
KERNEL = 4
SPAN = 256
MICRO = 2
WIDTH = 1536
INNER = 3072
CONV_CH = 3328
LANES = 128
CHUNKS = 8
GROUPS = 4
OWN = 6
BLOCK = OWN * HEADDIM
LOCAL = GROUPS * BLOCK
MIXED = LOCAL + 2 * STATE
PACKED = MIXED + LANES
ROWS = 256
HALF = 128
SHARD = 384
TALL = SHARD + 16
PIECE = 48
STATE_HALF = STATE // 2
MESSAGE = STATE_HALF + 16
SMALL = 32
EPSILON = 1e-05
PRECISE = lax.Precision.HIGHEST
F32 = jnp.float32
BF16 = jnp.bfloat16
VMEM_LIMIT = 56 * 1024 * 1024


def params(**more):
    return pltpu.CompilerParams(vmem_limit_bytes=VMEM_LIMIT, **more)


def whole(shape):
    return pl.BlockSpec(shape, lambda *_: (0,) * len(shape))


def columns(rows, width):
    return pl.BlockSpec((rows, width), lambda g: (0, g))


def grouped(rows):
    return pl.BlockSpec((1, rows, BLOCK), lambda g: (g, 0, 0))


MESSAGES = pl.BlockSpec((2, MESSAGE, BLOCK), lambda g: (g, 0, 0))
SMEM = pl.BlockSpec(memory_space=pltpu.SMEM)
ANYWHERE = pl.BlockSpec(memory_space=pl.ANY)


def shape(dims, kind=F32):
    return jax.ShapeDtypeStruct(dims, kind)


def dot(a, b):
    return jnp.dot(a, b, preferred_element_type=F32)


def dot_nt(a, b):
    return lax.dot_general(a, b, (((1,), (1,)), ((), ())), preferred_element_type=F32)


def exact_dot(a, b):
    return jnp.dot(a, b, precision=PRECISE, preferred_element_type=F32)


def lane_of(dims):
    return lax.broadcasted_iota(jnp.int32, dims, len(dims) - 1)


def row_of(dims):
    return lax.broadcasted_iota(jnp.int32, dims, len(dims) - 2)


def sigmoid(v):
    return 1.0 / (1.0 + jnp.exp(-v))


def softplus(v):
    return jnp.maximum(v, 0.0) + jnp.log1p(jnp.exp(-jnp.abs(v)))


def rolled(values, g):
    return pltpu.roll(values, lax.rem(LANES - 8 * g, LANES), axis=1)


def pair_lanes(values, p):
    low = lane_of((values.shape[0], LANES)) < HEADDIM
    return jnp.where(low, values[:, 2 * p : 2 * p + 1], values[:, 2 * p + 1 : 2 * p + 2])


def spread(values):
    return jnp.concatenate([pair_lanes(values, p) for p in range(OWN // 2)], axis=1)


def head_sum_matrix(g):
    head = row_of((BLOCK, LANES)) // HEADDIM
    return (lane_of((BLOCK, LANES)) == head + 8 * g).astype(BF16)


def lower_triangle(strict=False):
    i, j = row_of((HALF, HALF)), lane_of((HALF, HALF))
    return ((i > j) if strict else (i >= j)).astype(F32)


def usable_rows(info):
    return (row_of((ROWS, 1)) < info[0]).astype(F32)


def half(values, q):
    return values[q * HALF : (q + 1) * HALF]


class Weight:
    def __init__(self, arrays, layer, width, first=0):
        self.arrays = arrays
        self.stride = arrays[0].shape[0] // 4
        self.layer = layer
        self.width = width
        self.columns = pl.ds(first, width)

    def block(self, info, b):
        return lax.rem(info[10] + b, 4) * SHARD

    def parts(self, refs, info, b):
        start = self.block(info, b)
        if len(refs) == 1:
            there = pl.multiple_of(start // SHARD * self.stride, 16)
            return [(refs[0].at[pl.ds(there, SHARD)], start, SHARD)]
        out = []
        for side in range(2):
            mine = info[12 - side]
            for step in range(4):
                source = refs[2 + 4 * side + step].at[pl.ds((b - 1) * PIECE, PIECE)]
                row = start + side * (SHARD // 2) + lax.rem(mine + step, 4) * PIECE
                out.append((source, row, PIECE))
        return out

    def copies(self, refs, info, b, buffer, sems):
        return [
            pltpu.make_async_copy(
                source.at[:, self.columns],
                buffer.at[pl.ds(pl.multiple_of(row, 16), count)],
                sems.at[b, n],
            )
            for n, (source, row, count) in enumerate(self.parts(refs, info, b))
        ]

    def own_copy(self, source, info, buffer, sems):
        rows = pl.ds(pl.multiple_of(self.block(info, 0), SHARD), SHARD)
        source = source.at[pl.ds(0, SHARD), self.columns]
        return pltpu.make_async_copy(source, buffer.at[rows], sems.at[0, 0])

    def start(self, refs, info, buffer, sems):
        whole_array = len(refs) == 1
        if not whole_array:
            for n in range(2):

                @pl.when((info[13] == self.layer) == (n == 0))
                def _(n=n):
                    self.own_copy(refs[n], info, buffer, sems).start()

        for b in range(0 if whole_array else 1, 4):
            for c in self.copies(refs, info, b, buffer, sems):
                c.start()

    def wait(self, refs, info, b, buffer, sems):
        if b == 0 and len(refs) > 1:
            self.own_copy(refs[0], info, buffer, sems).wait()
        else:
            for c in self.copies(refs, info, b, buffer, sems):
                c.wait()
        return pl.ds(pl.multiple_of(self.block(info, b), SHARD), SHARD)

    def specs(self):
        return [ANYWHERE] * len(self.arrays)

    def scratch(self):
        return [pltpu.VMEM((4 * SHARD, self.width), BF16), pltpu.SemaphoreType.DMA((4, 8))]

    def product(self, refs, info, left, buffer, sems, total):
        for b in range(4):
            self.wait(refs, info, b, buffer, sems)
        step = 512 if self.width % 512 == 0 else 640
        for at in range(0, self.width, step):
            value = dot(left[...], buffer[:, at : at + step])
            total[:, at : at + step] = value.astype(total.dtype)


def in_proj_body(weight, tokens, info, h_ref, gain_ref, *rest):
    refs = len(weight.arrays)
    w_refs, rest = rest[:refs], rest[refs + tokens :]
    (normed_ref, mixed_ref, rate_ref, buffer, sems, total) = rest
    weight.start(w_refs, info, buffer, sems)
    h = h_ref[...].astype(F32)
    scale = lax.rsqrt(jnp.mean(h * h, axis=1, keepdims=True) + EPSILON)
    normed_ref[...] = (h * scale * gain_ref[...]).astype(BF16)
    weight.product(w_refs, info, normed_ref, buffer, sems, total)
    mixed_ref[...] = total[:, :MIXED].astype(BF16)
    rate_ref[...] = total[:, MIXED:]


def in_proj(info, h, gain, weight, tokens):
    return pl.pallas_call(
        functools.partial(in_proj_body, weight, len(tokens)),
        out_shape=(shape((ROWS, WIDTH), BF16), shape((ROWS, MIXED), BF16), shape((ROWS, LANES))),
        in_specs=[SMEM, whole((ROWS, WIDTH)), whole((1, WIDTH))]
        + weight.specs()
        + [ANYWHERE] * len(tokens),
        out_specs=(whole((ROWS, WIDTH)), whole((ROWS, MIXED)), whole((ROWS, LANES))),
        scratch_shapes=weight.scratch() + [pltpu.VMEM((ROWS, PACKED), F32)],
        compiler_params=params(),
        cost_estimate=pl.CostEstimate(
            flops=2 * ROWS * WIDTH * PACKED, bytes_accessed=8_000_000, transcendentals=0
        ),
        name="in_proj",
    )(info, h, gain, *weight.arrays, *tokens)


def gate_proj_body(weight, tokens, info, normed_ref, *rest):
    refs = len(weight.arrays)
    w_refs, (gate_ref, buffer, sems) = rest[:refs], rest[refs + tokens :]
    weight.start(w_refs, info, buffer, sems)
    weight.product(w_refs, info, normed_ref, buffer, sems, gate_ref)


def gate_proj(info, normed, weight, tokens):
    return pl.pallas_call(
        functools.partial(gate_proj_body, weight, len(tokens)),
        out_shape=shape((ROWS, LOCAL)),
        in_specs=[SMEM, whole((ROWS, WIDTH))] + weight.specs() + [ANYWHERE] * len(tokens),
        out_specs=whole((ROWS, LOCAL)),
        scratch_shapes=weight.scratch(),
        compiler_params=params(),
        cost_estimate=pl.CostEstimate(
            flops=2 * ROWS * WIDTH * LOCAL, bytes_accessed=7_000_000, transcendentals=0
        ),
        name="gate_proj",
    )(info, normed, *weight.arrays, *tokens)


def conv_sum_of(values, halo, cpar, keep, ext):
    width = values.shape[1]
    ext[0:16, :width] = halo.astype(F32) * keep
    ext[16 : 16 + ROWS, :width] = values.astype(F32)
    total = cpar[4:5, :]
    for k in range(KERNEL):
        total = total + cpar[k : k + 1, :] * ext[13 + k : 13 + k + ROWS, :width]
    return total


def state_body(
    info, mixed, halo, cpar, bc, halo_bc, cpar_bc, rate, hpar,
    xa_ref, bca_ref, cum_ref, dt_ref, s0_ref, msg_ref, ext, bt, tail,
):
    g = pl.program_id(0)
    keep = info[1].astype(F32)

    @pl.when(g == 0)
    def _():
        total = conv_sum_of(bc[...], halo_bc[...], cpar_bc[...], keep, ext)
        active = total * sigmoid(total)
        bca_ref[...] = active
        bt[...] = active[:, :STATE].T.astype(BF16)
        dt = usable_rows(info) * softplus(rate[...] + hpar[0:1, :])
        log_decay = dt * -jnp.exp(hpar[1:2, :])
        dt_ref[...] = dt
        tri = lower_triangle()
        for q in range(2):
            rows = pl.ds(q * HALF, HALF)
            cum = exact_dot(tri, half(log_decay, q))
            cum_ref[rows, :] = cum
            tail[rows, :] = jnp.exp(cum[HALF - 1 :, :] - cum) * half(dt, q)

    total = conv_sum_of(mixed[...], halo[...], cpar[...], keep, ext)
    xa = total * sigmoid(total)
    xa_ref[...] = xa
    weighted = (xa * spread(rolled(tail[...], g))).astype(BF16)
    ends = rolled(cum_ref[...], g)
    end0, end1 = ends[HALF - 1 : HALF], ends[ROWS - 1 : ROWS]
    s0 = dot(bt[:, :HALF], half(weighted, 0))
    s1 = dot(bt[:, HALF:], half(weighted, 1))
    s0_ref[0] = s0
    state = (spread(jnp.exp(end1)) * s0 + s1).astype(BF16)
    damp = spread(jnp.exp(end0 + end1))
    high = damp.astype(BF16)
    low = (damp - high.astype(F32)).astype(BF16)
    row = row_of((16, BLOCK))
    damps = jnp.where(row == 0, high.astype(F32), low.astype(F32)).astype(BF16)
    for r in range(2):
        msg_ref[r, :STATE_HALF, :] = state[r * STATE_HALF : (r + 1) * STATE_HALF]
        msg_ref[r, STATE_HALF:, :] = damps


def state_call(info, mixed, halo, cpar, rate, hpar):
    bc_at = LOCAL // 256
    return pl.pallas_call(
        state_body,
        grid=(GROUPS,),
        out_shape=(
            shape((ROWS, LOCAL)),
            shape((ROWS, 256)),
            shape((ROWS, LANES)),
            shape((ROWS, LANES)),
            shape((GROUPS, STATE, BLOCK)),
            shape((CHUNKS, MESSAGE, BLOCK), BF16),
        ),
        in_specs=[
            SMEM,
            columns(ROWS, BLOCK),
            columns(16, BLOCK),
            columns(8, BLOCK),
            pl.BlockSpec((ROWS, 256), lambda g: (0, bc_at)),
            pl.BlockSpec((16, 256), lambda g: (0, bc_at)),
            pl.BlockSpec((8, 256), lambda g: (0, bc_at)),
            whole((ROWS, LANES)),
            whole((8, LANES)),
        ],
        out_specs=(
            columns(ROWS, BLOCK),
            whole((ROWS, 256)),
            whole((ROWS, LANES)),
            whole((ROWS, LANES)),
            grouped(STATE),
            MESSAGES,
        ),
        scratch_shapes=[
            pltpu.VMEM((ROWS + 32, BLOCK), F32),
            pltpu.VMEM((STATE, ROWS), BF16),
            pltpu.VMEM((ROWS, LANES), F32),
        ],
        compiler_params=params(),
        cost_estimate=pl.CostEstimate(
            flops=2 * ROWS * STATE * LOCAL, bytes_accessed=4_500_000, transcendentals=400_000
        ),
        name="conv_state",
    )(info, mixed, halo, cpar, mixed, halo, cpar, rate, hpar)


def inside_body(xa, bca, cum, dt, hpar, y_ref, cum_t, scores):
    g = pl.program_id(0)

    @pl.when(g == 0)
    def _():
        tri = lower_triangle()
        for q in range(2):
            b, c = half(bca[:, :STATE], q).astype(BF16), half(bca[:, STATE:], q).astype(BF16)
            scores[q] = dot_nt(c, b) * tri
            cum_t[:, q * HALF : (q + 1) * HALF] = half(cum[...], q).T

    cols = rolled(cum[...], g)
    rows = cum_t[pl.ds(pl.multiple_of(8 * g, 8), 8), :]
    steps = rolled(dt[...], g)
    skips = rolled(hpar[...], g)[2:3, :]
    low = lane_of((HALF, LANES)) < HEADDIM
    for q in range(2):
        for p in range(OWN // 2):
            lanes = slice(p * LANES, (p + 1) * LANES)
            x = xa[q * HALF : (q + 1) * HALF, lanes]
            xdt = x * pair_lanes(half(steps, q), p)
            both = jnp.concatenate([jnp.where(low, xdt, 0.0), jnp.where(low, 0.0, xdt)], axis=0)
            mats = []
            for i in (2 * p, 2 * p + 1):
                gap = half(cols, q)[:, i : i + 1] - rows[i : i + 1, q * HALF : (q + 1) * HALF]
                mats.append((jnp.exp(jnp.minimum(gap, 0.0)) * scores[q]).astype(BF16))
            y = dot(jnp.concatenate(mats, axis=1), both.astype(BF16))
            y_ref[q * HALF : (q + 1) * HALF, lanes] = y + x * pair_lanes(skips, p)


def inside_call(xa, bca, cum, dt, hpar):
    return pl.pallas_call(
        inside_body,
        grid=(GROUPS,),
        out_shape=shape((ROWS, LOCAL)),
        in_specs=[
            columns(ROWS, BLOCK),
            whole((ROWS, 256)),
            whole((ROWS, LANES)),
            whole((ROWS, LANES)),
            whole((8, LANES)),
        ],
        out_specs=columns(ROWS, BLOCK),
        scratch_shapes=[pltpu.VMEM((LANES, ROWS), F32), pltpu.VMEM((2, HALF, HALF), F32)],
        compiler_params=params(),
        cost_estimate=pl.CostEstimate(
            flops=2 * HEADS * HALF * HALF * LANES, bytes_accessed=3_300_000, transcendentals=800_000
        ),
        name="inside",
    )(xa, bca, cum, dt, hpar)


def scan_body(backward, info, msg, *rest):
    out_ref = rest[-1]
    carry = jnp.zeros((STATE_HALF, BLOCK), F32)
    for k in reversed(range(CHUNKS)) if backward else range(CHUNKS):
        keep = info[2 + k].astype(F32)
        if not backward:
            carry = carry * keep
        out_ref[k] = carry.astype(BF16)
        damps = msg[k, STATE_HALF:, :].astype(F32)
        carry = (damps[0:1] + damps[1:2]) * carry + msg[k, :STATE_HALF, :].astype(F32)
        if backward:
            carry = carry * keep


def scan_call(info, msg, backward, *tokens):
    return pl.pallas_call(
        functools.partial(scan_body, backward),
        out_shape=shape((CHUNKS, STATE_HALF, BLOCK), BF16),
        in_specs=[SMEM, whole((CHUNKS, MESSAGE, BLOCK))] + [ANYWHERE] * len(tokens),
        out_specs=whole((CHUNKS, STATE_HALF, BLOCK)),
        compiler_params=params(),
        name="chunk_scan",
    )(info, msg, *tokens)


def out_proj_body(weight, info, y_in, bca, cum, hin, s0, gate, gain, *rest):
    refs = len(weight.arrays)
    w_refs, (y_ref, part_ref, buffer, sems, sums, gained) = rest[:refs], rest[refs:]
    weight.start(w_refs, info, buffer, sems)
    c_all = bca[:, STATE:].astype(BF16)
    grow = jnp.exp(cum[...])
    sums[...] = jnp.zeros((ROWS, LANES), F32)

    def group(g, _):
        lanes = pl.ds(pl.multiple_of(g * BLOCK, LANES), BLOCK)
        factor = rolled(grow, g)
        first = hin[g]
        second = spread(factor[HALF - 1 : HALF]) * first.astype(F32) + s0[g]
        carried = jnp.concatenate(
            [dot(half(c_all, 0), first), dot(half(c_all, 1), second.astype(BF16))], axis=0
        )
        y = y_in[:, lanes] + spread(factor) * carried
        y_ref[:, lanes] = y
        z = gate[:, lanes]
        gated = y * z * sigmoid(z)
        square = gated * gated
        sums[...] += sum(square[:, i * LANES : (i + 1) * LANES] for i in range(BLOCK // LANES))
        gained[:, lanes] = (gated * gain[:, lanes]).astype(BF16)
        return 0

    lax.fori_loop(0, GROUPS, group, 0)
    part_ref[:, WIDTH:] = sums[...].astype(BF16)
    weight.product(w_refs, info, gained, buffer, sems, part_ref)


def out_proj(info, y_in, bca, cum, hin, s0, gate, gain, weight):
    return pl.pallas_call(
        functools.partial(out_proj_body, weight),
        out_shape=(shape((ROWS, LOCAL)), shape((ROWS, WIDTH + LANES), BF16)),
        in_specs=[
            SMEM,
            whole((ROWS, LOCAL)),
            whole((ROWS, 256)),
            whole((ROWS, LANES)),
            whole((GROUPS, STATE, BLOCK)),
            whole((GROUPS, STATE, BLOCK)),
            whole((ROWS, LOCAL)),
            whole((1, LOCAL)),
        ]
        + weight.specs(),
        out_specs=(whole((ROWS, LOCAL)), whole((ROWS, WIDTH + LANES))),
        scratch_shapes=weight.scratch()
        + [pltpu.VMEM((ROWS, LANES), F32), pltpu.VMEM((ROWS, LOCAL), BF16)],
        compiler_params=params(),
        cost_estimate=pl.CostEstimate(
            flops=2 * ROWS * WIDTH * LOCAL, bytes_accessed=13_000_000, transcendentals=800_000
        ),
        name="out_proj",
    )(info, y_in, bca, cum, hin, s0, gate, gain, *weight.arrays)


def join_body(info, h_ref, own, came, res_ref, branch_ref, scale_ref):
    both = own[...].astype(F32) + came[...].astype(F32)
    squares = jnp.sum(both[:, WIDTH:], axis=1, keepdims=True)
    scale = lax.rsqrt(squares / INNER + EPSILON)
    branch = scale * both[:, :WIDTH]
    branch_ref[...] = branch.astype(BF16)
    scale_ref[...] = jnp.broadcast_to(scale, (HALF // 2, LANES))
    first = pl.program_id(0) * (HALF // 2)
    usable = (row_of((HALF // 2, 1)) + first < info[0]).astype(F32)
    result = h_ref[...].astype(F32) + usable * branch
    res_ref[...] = result.astype(res_ref.dtype)


def join(info, h, own, came, kind):
    def rows(width):
        return pl.BlockSpec((HALF // 2, width), lambda i: (i, 0))

    return pl.pallas_call(
        join_body,
        grid=(4,),
        out_shape=(shape((ROWS, WIDTH), kind), shape((ROWS, WIDTH), BF16), shape((ROWS, LANES))),
        in_specs=[SMEM, rows(WIDTH), rows(WIDTH + LANES), rows(WIDTH + LANES)],
        out_specs=(rows(WIDTH), rows(WIDTH), rows(LANES)),
        compiler_params=params(),
        cost_estimate=pl.CostEstimate(flops=2_000_000, bytes_accessed=8_000_000, transcendentals=0),
        name="join",
    )(info, h, own, came)


def gate_back_body(weight, info, cot, y, gate, gain, branch, scale_ref, *rest):
    refs = len(weight.arrays)
    w_refs, rest = rest[:refs], rest[refs:]
    bg_ref, dy_ref, dz_ref, grad_ref, dgain_ref, buffer, sems, inner_ref = rest
    b = pl.program_id(0)
    scale = scale_ref[:, :1]

    @pl.when(b == 0)
    def _():
        weight.start(w_refs, info, buffer, sems)
        bg = (usable_rows(info) * cot[...].astype(F32)).astype(BF16)
        bg_ref[...] = bg
        inner = jnp.sum(bg.astype(F32) * branch[...].astype(F32), axis=1, keepdims=True)
        inner_ref[...] = jnp.broadcast_to(inner * scale * scale / INNER, (ROWS, LANES))
        for n in range(4):
            weight.wait(w_refs, info, n, buffer, sems)

    inner = inner_ref[:, :1]
    bg = bg_ref[...]
    d_norms = dot_nt(bg, buffer[pl.ds(pl.multiple_of(b * SHARD, SHARD), SHARD), :])
    norms = []
    for i in range(SHARD // LANES):
        lanes = slice(i * LANES, (i + 1) * LANES)
        z = gate[:, lanes]
        sig = sigmoid(z)
        silu = z * sig
        y_here = y[:, lanes]
        gated = y_here * silu
        d_norm = d_norms[:, lanes]
        gained = scale * gain[:, lanes]
        norms.append((gated * gained).astype(BF16))
        d_gated = d_norm * gained - gated * inner
        total = jnp.sum(d_norm * gated * scale, axis=0, keepdims=True)
        dgain_ref[:, lanes] = jnp.broadcast_to(total, (8, LANES))
        dy_ref[:, lanes] = (d_gated * silu).astype(BF16)
        dz_ref[:, lanes] = (d_gated * y_here * sig * (1.0 + z * (1.0 - sig))).astype(BF16)
    norm = jnp.concatenate(norms, axis=1)
    grad_ref[...] = dot(norm.T, bg).astype(BF16) if grad_ref.shape[1] == WIDTH else norm.T


def gate_back(info, cot, y, gate, gain, branch, scale, weight, with_grad):
    wide, local = whole((ROWS, WIDTH)), columns(ROWS, SHARD)
    grad_width = WIDTH if with_grad else ROWS
    return pl.pallas_call(
        functools.partial(gate_back_body, weight),
        grid=(4,),
        out_shape=(
            shape((ROWS, WIDTH), BF16),
            shape((ROWS, LOCAL), BF16),
            shape((ROWS, LOCAL), BF16),
            shape((LOCAL, grad_width), BF16),
            shape((8, LOCAL)),
        ),
        in_specs=[SMEM, wide, local, local, columns(1, SHARD), wide, whole((ROWS, LANES))]
        + weight.specs(),
        out_specs=(
            wide,
            local,
            local,
            pl.BlockSpec((SHARD, grad_width), lambda b: (b, 0)),
            columns(8, SHARD),
        ),
        scratch_shapes=weight.scratch() + [pltpu.VMEM((ROWS, LANES), F32)],
        compiler_params=params(),
        cost_estimate=pl.CostEstimate(
            flops=4 * ROWS * WIDTH * LOCAL, bytes_accessed=17_000_000, transcendentals=800_000
        ),
        name="gate_back",
    )(info, cot, y, gate, gain, branch, scale, *weight.arrays)


def own_grad_body(dy, bca, cum, msg_in, dz, normed, own1_ref, msg_ref, grad_ref, ct, grow):
    g = pl.program_id(0)
    grad_ref[...] = dot(normed[...].T, dz[...]).astype(BF16)

    @pl.when(g == 0)
    def _():
        ct[...] = bca[:, STATE:].T.astype(BF16)
        grow[...] = jnp.exp(cum[...])

    factor = rolled(grow[...], g)
    weighted = (dy[...].astype(F32) * spread(factor)).astype(BF16)
    own0 = dot(ct[:, :HALF], half(weighted, 0))
    own1 = dot(ct[:, HALF:], half(weighted, 1))
    own1_ref[0] = own1
    grad = (spread(factor[HALF - 1 : HALF]) * own1 + own0).astype(BF16)
    for r in range(2):
        msg_ref[r, :STATE_HALF, :] = grad[r * STATE_HALF : (r + 1) * STATE_HALF]
        msg_ref[r, STATE_HALF:, :] = msg_in[r, STATE_HALF:, :]


def own_grad(dy, bca, cum, msg, dz, normed):
    return pl.pallas_call(
        own_grad_body,
        grid=(GROUPS,),
        out_shape=(
            shape((GROUPS, STATE, BLOCK)),
            shape((CHUNKS, MESSAGE, BLOCK), BF16),
            shape((WIDTH, LOCAL), BF16),
        ),
        in_specs=[
            columns(ROWS, BLOCK),
            whole((ROWS, 256)),
            whole((ROWS, LANES)),
            MESSAGES,
            whole((ROWS, LOCAL)),
            columns(ROWS, SHARD),
        ],
        out_specs=(grouped(STATE), MESSAGES, pl.BlockSpec((SHARD, LOCAL), lambda b: (b, 0))),
        scratch_shapes=[pltpu.VMEM((STATE, ROWS), BF16), pltpu.VMEM((ROWS, LANES), F32)],
        compiler_params=params(),
        cost_estimate=pl.CostEstimate(
            flops=2 * ROWS * WIDTH * LOCAL, bytes_accessed=8_000_000, transcendentals=0
        ),
        name="own_grad",
    )(dy, bca, cum, msg, dz, normed)


def inside_back_body(
    dy, xa, bca, cum, dt, hpar,
    dx_ref, dskip_ref, gsum_ref, u_ref, dbc_ref, cum_t, scores, dscores,
):
    g = pl.program_id(0)

    @pl.when(g == 0)
    def _():
        tri = lower_triangle()
        for q in range(2):
            b, c = half(bca[:, :STATE], q).astype(BF16), half(bca[:, STATE:], q).astype(BF16)
            scores[q] = dot_nt(b, c) * tri.T
            cum_t[:, q * HALF : (q + 1) * HALF] = half(cum[...], q).T
        dscores[...] = jnp.zeros((2, HALF, HALF), F32)
        u_ref[...] = jnp.zeros((ROWS, LANES), F32)

    cols = rolled(cum[...], g)
    rows = cum_t[pl.ds(pl.multiple_of(8 * g, 8), 8), :]
    steps = rolled(dt[...], g)
    skips = rolled(hpar[...], g)[2:3, :]
    low = lane_of((HALF, LANES)) < HEADDIM
    lane = lane_of((HALF, LANES))
    gsum_ref[...] = jnp.zeros((8, ROWS), F32)
    for q in range(2):
        here = slice(q * HALF, (q + 1) * HALF)
        u_here = u_ref[here, :]
        for p in range(OWN // 2):
            lanes = slice(p * LANES, (p + 1) * LANES)
            dy_pair = dy[here, lanes]
            x = xa[here, lanes]
            zero = jnp.zeros_like(dy_pair)
            both = jnp.concatenate(
                [jnp.where(low, dy_pair, zero), jnp.where(low, zero, dy_pair)], axis=0
            )
            dw = dot_nt(x.astype(BF16), both)
            mats = []
            for n, i in enumerate((2 * p, 2 * p + 1)):
                gap = rows[i : i + 1, here] - half(cols, q)[:, i : i + 1]
                decay = jnp.exp(jnp.minimum(gap, 0.0))
                step = half(steps, q)[:, i : i + 1]
                weight = decay * scores[q]
                mats.append(weight.astype(BF16))
                dw_here = dw[:, n * HALF : (n + 1) * HALF]
                dscores[q] += decay * dw_here * step
                direct = weight * dw_here
                total = jnp.sum(direct, axis=1, keepdims=True)
                u_here = jnp.where(lane == 8 * g + i, total, u_here)
                gsum_ref[i : i + 1, here] = jnp.sum(direct * step, axis=0, keepdims=True)
            dx = dot(jnp.concatenate(mats, axis=1), both)
            dy_wide = dy_pair.astype(F32)
            dx_ref[here, lanes] = dx * pair_lanes(half(steps, q), p) + dy_wide * pair_lanes(skips, p)
            skip_sum = jnp.sum(dy_wide * x, axis=0, keepdims=True)
            if q == 0:
                dskip_ref[:, lanes] = jnp.broadcast_to(skip_sum, (8, LANES))
            else:
                dskip_ref[:, lanes] += skip_sum
        u_ref[here, :] = u_here

    @pl.when(g == GROUPS - 1)
    def _():
        tri = lower_triangle()
        for q in range(2):
            b, c = half(bca[:, :STATE], q).astype(BF16), half(bca[:, STATE:], q).astype(BF16)
            ds_t = dscores[q] * tri.T
            dbc_ref[q * HALF : (q + 1) * HALF, :STATE] = dot(ds_t.astype(BF16), c)
            dbc_ref[q * HALF : (q + 1) * HALF, STATE:] = dot(ds_t.T.astype(BF16), b)


def inside_back(dy, xa, bca, cum, dt, hpar):
    return pl.pallas_call(
        inside_back_body,
        grid=(GROUPS,),
        out_shape=(
            shape((ROWS, LOCAL)),
            shape((8, LOCAL)),
            shape((8 * GROUPS, ROWS)),
            shape((ROWS, LANES)),
            shape((ROWS, 256)),
        ),
        in_specs=[
            columns(ROWS, BLOCK),
            columns(ROWS, BLOCK),
            whole((ROWS, 256)),
            whole((ROWS, LANES)),
            whole((ROWS, LANES)),
            whole((8, LANES)),
        ],
        out_specs=(
            columns(ROWS, BLOCK),
            columns(8, BLOCK),
            pl.BlockSpec((8, ROWS), lambda g: (g, 0)),
            whole((ROWS, LANES)),
            whole((ROWS, 256)),
        ),
        scratch_shapes=[
            pltpu.VMEM((LANES, ROWS), F32),
            pltpu.VMEM((2, HALF, HALF), F32),
            pltpu.VMEM((2, HALF, HALF), F32),
        ],
        compiler_params=params(),
        cost_estimate=pl.CostEstimate(
            flops=4 * HEADS * HALF * HALF * LANES, bytes_accessed=4_500_000, transcendentals=800_000
        ),
        name="inside_back",
    )(dy, xa, bca, cum, dt, hpar)


def conv_back(d_active, values, halo, cpar, keep, ext, ext_d):
    width = values.shape[1]
    total = conv_sum_of(values, halo, cpar, keep, ext)
    sig = sigmoid(total)
    d_sum = d_active * sig * (1.0 + total * (1.0 - sig))
    ext_d[0:16, :width] = jnp.zeros((16, width), F32)
    ext_d[16 : 16 + ROWS, :width] = d_sum
    ext_d[16 + ROWS :, :width] = jnp.zeros((16, width), F32)
    d_in = jnp.zeros((ROWS + 16, width), F32)
    for k in range(KERNEL):
        d_in = d_in + cpar[k : k + 1, :] * ext_d[3 - k : 3 - k + ROWS + 16, :width]
    row = row_of((8, width))
    d_par = jnp.where(row == 4, jnp.sum(d_sum, axis=0, keepdims=True), 0.0)
    for k in range(KERNEL):
        tap = jnp.sum(d_sum * ext[13 + k : 13 + k + ROWS, :width], axis=0, keepdims=True)
        d_par = jnp.where(row == k, tap, d_par)
    return d_in, d_par


def finish_body(
    info, xa, dxi, dy, mixed, halo, cpar, bc, halo_bc, cpar_bc, bca, cum, dt, rate, hpar, lam, hin, s0, own1, u, gsum, dbc,
    dmx_ref, dmbc_ref, tailx_ref, tailbc_ref, edgex_ref, edgebc_ref, dcx_ref, dcbc_ref, dhead_ref,
    ext, ext_d, grow, tail, v_sum, q_sum, end_sum, dbc_sum,
):
    g = pl.program_id(0)
    keep = info[1].astype(F32)

    @pl.when(g == 0)
    def _():
        grow[...] = jnp.exp(cum[...])
        for q in range(2):
            here = half(cum[...], q)
            tail[q * HALF : (q + 1) * HALF, :] = jnp.exp(here[HALF - 1 :, :] - here)
        v_sum[...] = jnp.zeros((ROWS, LANES), F32)
        q_sum[...] = jnp.zeros((ROWS, LANES), F32)
        end_sum[...] = jnp.zeros((16, LANES), F32)
        dbc_sum[...] = dbc[...]

    sums = head_sum_matrix(g)
    factor = rolled(grow[...], g)
    tails = rolled(tail[...], g)
    steps = rolled(dt[...], g)
    ends = [spread(factor[HALF - 1 : HALF]), spread(factor[ROWS - 1 : ROWS])]
    lam1 = lam[0].astype(F32)
    lams = [ends[1] * lam1 + own1[0], lam1]
    first = hin[0].astype(F32)
    states = [first, ends[0] * first + s0[0]]
    d_x = []
    for q in range(2):
        here = slice(q * HALF, (q + 1) * HALF)
        b, c = bca[here, :STATE].astype(BF16), bca[here, STATE:].astype(BF16)
        lam_q, state_q = lams[q].astype(BF16), states[q].astype(BF16)
        tail_wide = spread(half(tails, q))
        tail_step = tail_wide * spread(half(steps, q))
        x, dy_q = xa[here, :], dy[here, :].astype(F32)
        lb = dot(b, lam_q) * tail_wide
        d_x.append(dxi[here, :] + lb * spread(half(steps, q)))
        v_sum[here, :] += dot((x * lb).astype(BF16), sums)
        grow_wide = spread(half(factor, q))
        dy_grow = (dy_q * grow_wide).astype(BF16)
        carried = dot(c, state_q)
        q_sum[here, :] += dot((dy_q * grow_wide * carried).astype(BF16), sums)
        dbc_sum[here, :STATE] += dot_nt((x * tail_step).astype(BF16), lam_q)
        dbc_sum[here, STATE:] += dot_nt(dy_grow, state_q)
        last = jnp.sum(lams[q] * states[q], axis=0, keepdims=True) * ends[q]
        high = last.astype(BF16).astype(F32)
        both = jnp.where(row_of((16, BLOCK)) == 0, high, last - high).astype(BF16)
        both = dot(both, sums)
        end_sum[8 * q : 8 * q + 8, :] += both[0:1] + both[1:2]
    d_in, d_par = conv_back(
        jnp.concatenate(d_x, axis=0), mixed[...], halo[...], cpar[...], keep, ext, ext_d
    )
    dmx_ref[...] = d_in[16:].astype(BF16)
    tailx_ref[...] = d_in[ROWS:]
    edgex_ref[...] = (d_in[:16] * keep).astype(BF16)
    dcx_ref[...] = d_par

    @pl.when(g == GROUPS - 1)
    def _():
        d_bc, d_par_bc = conv_back(
            dbc_sum[...], bc[...], halo_bc[...], cpar_bc[...], keep, ext, ext_d
        )
        dmbc_ref[:, :256] = d_bc[16:].astype(BF16)
        tailbc_ref[...] = d_bc[ROWS:]
        edgebc_ref[...] = (d_bc[:16] * keep).astype(BF16)
        dcbc_ref[...] = d_par_bc
        rates = -jnp.exp(hpar[1:2, :])
        logit = rate[...] + hpar[0:1, :]
        upper = lower_triangle().T
        before = lower_triangle(True)
        d_bias = jnp.zeros((1, LANES), F32)
        d_log = jnp.zeros((1, LANES), F32)
        usable = usable_rows(info)
        for q in range(2):
            here = slice(q * HALF, (q + 1) * HALF)
            step = dt[here, :]
            gs = gsum[...][:, here].T
            gs = jnp.concatenate([gs, jnp.zeros((HALF, LANES - 8 * GROUPS), F32)], axis=1)
            d_decay = exact_dot(upper, gs - step * u[here, :] + q_sum[here, :])
            d_decay = d_decay + exact_dot(before, step * v_sum[here, :])
            d_decay = d_decay + end_sum[8 * q : 8 * q + 1, :]
            d_step = u[here, :] + v_sum[here, :] + rates * d_decay
            d_rate = half(usable, q) * d_step * sigmoid(half(logit, q))
            d_bias += jnp.sum(d_rate, axis=0, keepdims=True)
            d_log += jnp.sum(d_decay * step * rates, axis=0, keepdims=True)
            dmbc_ref[here, 256:] = d_rate.astype(BF16)
        row = row_of((8, LANES))
        dhead_ref[...] = jnp.where(row == 0, d_bias, jnp.where(row == 1, d_log, 0.0))


def finish_call(
    info, xa, dxi, dy, mixed, halo, cpar, bca, cum, dt, rate, hpar, lam, hin, s0, own1, u, gsum, dbc
):
    bc_at = LOCAL // 256
    wide = whole((ROWS, LANES))
    return pl.pallas_call(
        finish_body,
        grid=(GROUPS,),
        out_shape=(
            shape((ROWS, LOCAL), BF16),
            shape((ROWS, 384), BF16),
            shape((16, LOCAL)),
            shape((16, 256)),
            shape((16, LOCAL), BF16),
            shape((16, 256), BF16),
            shape((8, LOCAL)),
            shape((8, 256)),
            shape((8, LANES)),
        ),
        in_specs=[
            SMEM,
            columns(ROWS, BLOCK),
            columns(ROWS, BLOCK),
            columns(ROWS, BLOCK),
            columns(ROWS, BLOCK),
            columns(16, BLOCK),
            columns(8, BLOCK),
            pl.BlockSpec((ROWS, 256), lambda g: (0, bc_at)),
            pl.BlockSpec((16, 256), lambda g: (0, bc_at)),
            pl.BlockSpec((8, 256), lambda g: (0, bc_at)),
            whole((ROWS, 256)),
            wide,
            wide,
            wide,
            whole((8, LANES)),
            grouped(STATE),
            grouped(STATE),
            grouped(STATE),
            grouped(STATE),
            wide,
            whole((8 * GROUPS, ROWS)),
            whole((ROWS, 256)),
        ],
        out_specs=(
            columns(ROWS, BLOCK),
            whole((ROWS, 384)),
            columns(16, BLOCK),
            whole((16, 256)),
            columns(16, BLOCK),
            whole((16, 256)),
            columns(8, BLOCK),
            whole((8, 256)),
            whole((8, LANES)),
        ),
        scratch_shapes=[
            pltpu.VMEM((ROWS + 32, BLOCK), F32),
            pltpu.VMEM((ROWS + 32, BLOCK), F32),
            pltpu.VMEM((ROWS, LANES), F32),
            pltpu.VMEM((ROWS, LANES), F32),
            pltpu.VMEM((ROWS, LANES), F32),
            pltpu.VMEM((ROWS, LANES), F32),
            pltpu.VMEM((16, LANES), F32),
            pltpu.VMEM((ROWS, 256), F32),
        ],
        compiler_params=params(),
        cost_estimate=pl.CostEstimate(
            flops=10 * ROWS * STATE * LOCAL, bytes_accessed=7_500_000, transcendentals=800_000
        ),
        name="finish_back",
    )(
        info, xa, dxi, dy, mixed, halo, cpar, mixed, halo, cpar, bca, cum, dt, rate, hpar,
        lam, hin, s0, own1, u, gsum, dbc,
    )


def gate_in_back_body(weight, info, dz, token, *rest):
    refs = len(weight.arrays)
    w_refs, (out_ref, buffer, sems) = rest[:refs], rest[refs:]

    @pl.when(pl.program_id(0) == 0)
    def _():
        weight.start(w_refs, info, buffer, sems)
        for n in range(4):
            weight.wait(w_refs, info, n, buffer, sems)

    rows = pl.ds(pl.multiple_of(pl.program_id(0) * SHARD, SHARD), SHARD)
    out_ref[...] = dot_nt(dz[...], buffer[rows, :])


def gate_in_back(info, dz, weight, token):
    return pl.pallas_call(
        functools.partial(gate_in_back_body, weight),
        grid=(4,),
        out_shape=shape((ROWS, WIDTH)),
        in_specs=[SMEM, whole((ROWS, LOCAL)), ANYWHERE] + weight.specs(),
        out_specs=columns(ROWS, SHARD),
        scratch_shapes=weight.scratch(),
        compiler_params=params(),
        cost_estimate=pl.CostEstimate(
            flops=2 * ROWS * WIDTH * LOCAL, bytes_accessed=7_000_000, transcendentals=0
        ),
        name="gate_in_back",
    )(info, dz, token, *weight.arrays)


def patch_body(dmx, dmbc, tailx, tailbc, edge, token, dxc_ref):
    dxc_ref[:, :LOCAL] = dmx[...]
    dxc_ref[:, LOCAL:] = dmbc[...]
    late = edge[...].astype(F32)
    dxc_ref[ROWS - 16 :, :LOCAL] = (tailx[...] + late[:, :LOCAL]).astype(BF16)
    dxc_ref[ROWS - 16 :, LOCAL:MIXED] = (tailbc[...] + late[:, LOCAL:]).astype(BF16)


def patch(dmx, dmbc, tailx, tailbc, edge, token):
    arrays = (dmx, dmbc, tailx, tailbc, edge)
    return pl.pallas_call(
        patch_body,
        out_shape=shape((ROWS, PACKED), BF16),
        in_specs=[whole(v.shape) for v in arrays] + [ANYWHERE],
        out_specs=whole((ROWS, PACKED)),
        compiler_params=params(),
        cost_estimate=pl.CostEstimate(flops=100_000, bytes_accessed=2_000_000, transcendentals=0),
        name="patch",
    )(*arrays, token)


def mixed_back_body(weight, tokens, info, dxc, part, h_ref, normed, *rest):
    refs = len(weight.arrays)
    w_refs, rest = rest[:refs], rest[refs + tokens :]
    (out_ref, dgain_ref, *grad_ref), (buffer, sems, scale_ref) = rest[:-3], rest[-3:]
    b = pl.program_id(0)
    block = pl.ds(pl.multiple_of(b * SHARD, SHARD), SHARD)

    @pl.when(b == 0)
    def _():
        weight.start(w_refs, info, buffer, sems)
        h = h_ref[...].astype(F32)
        scale = lax.rsqrt(jnp.mean(h * h, axis=1, keepdims=True) + EPSILON)
        scale_ref[...] = jnp.broadcast_to(scale, (ROWS, LANES))

    for ref in grad_ref:
        ref[...] = dot(normed[...].T, dxc[...]).astype(BF16)

    @pl.when(b == 0)
    def _():
        for n in range(4):
            weight.wait(w_refs, info, n, buffer, sems)

    d_norm = part[...] + dot_nt(dxc[...], buffer[block, :])
    out_ref[...] = d_norm.astype(BF16)
    total = jnp.sum(d_norm * h_ref[:, block].astype(F32) * scale_ref[:, :1], axis=0, keepdims=True)
    dgain_ref[...] = jnp.broadcast_to(total, (8, SHARD))


def mixed_back(info, dxc, part, h, normed, weight, with_grad, tokens):
    wide, local = whole((ROWS, WIDTH)), columns(ROWS, SHARD)
    outs = [shape((ROWS, WIDTH), BF16), shape((8, WIDTH))]
    specs = [local, columns(8, SHARD)]
    if with_grad:
        outs.append(shape((WIDTH, PACKED), BF16))
        specs.append(pl.BlockSpec((SHARD, PACKED), lambda b: (b, 0)))
    return pl.pallas_call(
        functools.partial(mixed_back_body, weight, len(tokens)),
        grid=(4,),
        out_shape=outs,
        in_specs=[SMEM, whole((ROWS, PACKED)), local, wide, local]
        + weight.specs()
        + [ANYWHERE] * len(tokens),
        out_specs=specs,
        scratch_shapes=weight.scratch() + [pltpu.VMEM((ROWS, LANES), F32)],
        compiler_params=params(),
        cost_estimate=pl.CostEstimate(
            flops=4 * ROWS * WIDTH * PACKED, bytes_accessed=14_000_000, transcendentals=0
        ),
        name="mixed_back",
    )(info, dxc, part, h, normed, *weight.arrays, *tokens)


def norm_back_body(own, came, h_ref, cot, gain, dh_ref, low_ref):
    h = h_ref[...].astype(F32)
    scale = lax.rsqrt(jnp.mean(h * h, axis=1, keepdims=True) + EPSILON)
    d_norm = own[...].astype(F32) + came[...].astype(F32)
    inner = jnp.mean(d_norm * gain[...] * h, axis=1, keepdims=True) * scale * scale * scale
    dh = cot[...].astype(F32) + scale * d_norm * gain[...] - h * inner
    dh_ref[...] = dh
    low_ref[...] = dh.astype(BF16)


def norm_back(own, came, h, cot, gain):
    rows = pl.BlockSpec((HALF // 2, WIDTH), lambda i: (i, 0))
    return pl.pallas_call(
        norm_back_body,
        grid=(4,),
        out_shape=(shape((ROWS, WIDTH)), shape((ROWS, WIDTH), BF16)),
        in_specs=[rows] * 4 + [whole((1, WIDTH))],
        out_specs=(rows, rows),
        compiler_params=params(),
        cost_estimate=pl.CostEstimate(flops=3_000_000, bytes_accessed=8_000_000, transcendentals=0),
        name="norm_back",
    )(own, came, h, cot, gain)


def z_shift(r):
    return "dp", [(z, (z + r) % 4) for z in range(4)]


def y_shift(r):
    return "ctx", [(j, (j + 4 * r) % 16) for j in range(16)]


def x_shift(r):
    return "ctx", [(j, j - j % 4 + (j + r) % 4) for j in range(16)]


SHIFTS = {"z": z_shift, "y": y_shift, "x": x_shift}


def send(value, axis, r):
    name, pairs = SHIFTS[axis](r % 4)
    return lax.ppermute(value, name, pairs)


def swapped(value):
    return lax.ppermute(value, "section", [(0, 1), (1, 0)])


def nothing_body(*refs):
    refs[-1][...] = jnp.zeros((8, LANES), jnp.int32)


def after(values, place):
    nothing = pl.pallas_call(
        nothing_body,
        out_shape=shape((8, LANES), jnp.int32),
        in_specs=[ANYWHERE] * len(values),
        out_specs=whole((8, LANES)),
        compiler_params=params(),
        cost_estimate=pl.CostEstimate(flops=0, bytes_accessed=4096, transcendentals=0),
        name="after",
    )(*values)[0, 0]
    return {axis: n + nothing for axis, n in place.items()}


def fetched(mine, came, layer, section, place):
    rows = SHARD // 2

    def piece(source, side, axis):
        return lax.dynamic_slice_in_dim(source, side * rows + place[axis] * PIECE, PIECE, 0)

    parts = [
        jnp.where(section == layer, piece(mine, side, axis), piece(came, side, axis))
        for side, axis in enumerate("xy")
    ]
    if mine.shape[0] == TALL:
        parts.append(jnp.where(section == layer, mine[SHARD:], came[SHARD:]))
    return jnp.concatenate(parts)


def pieces(mine, came, got, late):
    out = [mine, came]
    for side, axis in enumerate("xy"):
        rows = slice(side * PIECE, (side + 1) * PIECE)
        stack = jnp.concatenate(
            [lax.dynamic_slice_in_dim(g, rows.start + late, PIECE, 0) for g in got[1:]]
        )
        out += [stack] + [send(stack, axis, -r) for r in range(1, 4)]
    return out


def summed(terms):
    a, b, c, d = (t.astype(F32) for t in terms)
    return (a + c) + (b + d)


def arrived(terms, axis):
    return [terms[0]] + [send(terms[r], axis, r) for r in range(1, 4)]


def terms_body(axis, cuts, stacked, info, *rest):
    factors, rest = rest[: 2 * len(cuts)], rest[2 * len(cuts) :]
    small, outs, total = rest[:-2] if stacked else rest[:-5], rest[-5:-1], rest[-1]
    column = 0
    for n, cols in enumerate(cuts):
        there = slice(column, column + cols.stop - cols.start)
        total[:, there] = dot(factors[2 * n][...], factors[2 * n + 1][:, cols])
        column = there.stop
    count = 96 if axis == "y" else 24
    starts = [z * SHARD for z in range(4)]
    if axis == "x":
        starts = [start + y * 96 for start in starts for y in range(4)]
    for r in range(4):
        first = r * count
        if not stacked:
            first = lax.rem(info[11 if axis == "y" else 12] + r, 4) * count
        parts = [total[pl.ds(pl.multiple_of(start + first, 8), count), :] for start in starts]
        out = rest[-2].at[r] if stacked else outs[r]
        out[:SHARD, :] = jnp.concatenate(parts, axis=0).astype(BF16)
        for ref in small:
            out[SHARD:, :] = ref[...]


def four(dims, stacked):
    if stacked:
        return shape((4, *dims), BF16), whole((4, *dims))
    return [shape(dims, BF16)] * 4, [whole(dims)] * 4


def terms(info, axis, products, small=(), stacked=False):
    cuts = [cols for _, _, cols in products]
    width = sum(cols.stop - cols.start for cols in cuts)
    rows = SHARD + sum(v.shape[0] for v in small)
    arrays = [v for left, right, _ in products for v in (left, right)] + list(small)
    outs, specs = four((rows, width), stacked)
    return pl.pallas_call(
        functools.partial(terms_body, axis, cuts, stacked),
        out_shape=outs,
        in_specs=[SMEM] + [whole(v.shape) for v in arrays],
        out_specs=specs,
        scratch_shapes=[pltpu.VMEM((4 * SHARD, width), F32)],
        compiler_params=params(),
        cost_estimate=pl.CostEstimate(
            flops=8 * SHARD * ROWS * width, bytes_accessed=8_000_000, transcendentals=0
        ),
        name="terms",
    )(info, *arrays)


def fold_body(slot, counts, outer, inner, rest_rows, stacked, info, *rest):
    refs, outs, total = rest[: sum(counts)], rest[-2:-1] if stacked else rest[-5:-1], rest[-1]
    column = 0
    for count in counts:
        arrays, refs = refs[:count], refs[count:]
        cols = slice(column, column + arrays[0].shape[-1])
        if count == 4:
            total[:, cols] = summed([a[...] for a in arrays])
        elif len(arrays[0].shape) == 3:
            total[:, cols] = summed([arrays[0][n] for n in range(4)])
        else:
            total[:, cols] = arrays[0][...].astype(F32)
        column = cols.stop
    for r in range(4):
        first = r * inner if stacked else lax.rem(info[slot] + r, 4) * inner
        parts = [
            total[pl.ds(pl.multiple_of(n * 4 * inner + first, 8), inner), :] for n in range(outer)
        ]
        if rest_rows:
            parts.append(total[4 * outer * inner :, :])
        out = outs[0].at[r] if stacked else outs[r]
        out[...] = jnp.concatenate(parts, axis=0).astype(BF16)


def fold(info, axis, groups, outer, inner, token, stacked=False):
    slot = 10 + "zyx".index(axis)
    arrays = [a for group in groups for a in group]
    tokens = token if isinstance(token, tuple) else (token,)
    rows, width = arrays[0].shape[-2], sum(group[0].shape[-1] for group in groups)
    more = rows - 4 * outer * inner
    outs, specs = four((outer * inner + more, width), stacked)
    counts = [len(group) for group in groups]
    return pl.pallas_call(
        functools.partial(fold_body, slot, counts, outer, inner, more, stacked),
        out_shape=outs,
        in_specs=[SMEM] + [whole(a.shape) for a in arrays] + [ANYWHERE] * len(tokens),
        out_specs=specs,
        scratch_shapes=[pltpu.VMEM((rows, width), F32)],
        compiler_params=params(),
        cost_estimate=pl.CostEstimate(flops=2_000_000, bytes_accessed=8_000_000, transcendentals=0),
        name="fold",
    )(info, *arrays, *tokens)


def last_fold_body(info, *rest):
    left, right, outs, total = rest[:4], rest[4:8], rest[9:13], rest[13]
    width = left[0].shape[1]
    total[:96, :width] = summed([a[...] for a in left])
    total[96:, :width] = jnp.zeros((SMALL, width), F32)
    total[:, width:] = summed([a[...] for a in right])
    for r in range(4):
        first = pl.multiple_of(lax.rem(info[10] + r, 4) * 24, 8)
        parts = [total[pl.ds(first, 24), :], total[96:, :]]
        outs[r][...] = jnp.concatenate(parts, axis=0).astype(BF16)


def last_fold(info, left, right, token):
    width = left[0].shape[1] + right[0].shape[1]
    out = shape((24 + SMALL, width), BF16)
    arrays = (*left, *right)
    return pl.pallas_call(
        last_fold_body,
        out_shape=[out] * 4,
        in_specs=[SMEM] + [whole(a.shape) for a in arrays] + [ANYWHERE],
        out_specs=[whole(out.shape)] * 4,
        scratch_shapes=[pltpu.VMEM((96 + SMALL, width), F32)],
        compiler_params=params(),
        cost_estimate=pl.CostEstimate(flops=500_000, bytes_accessed=2_000_000, transcendentals=0),
        name="last_fold",
    )(info, *arrays, token)


PARITY = [[j for j in range(16) if j % 2 == e] for e in range(2)]
NEIGHBOURS = [(j, j ^ 1) for j in range(16)]
GROUPS_OF = {
    "y": [[4 * y + x for y in range(4)] for x in range(4)],
    "x": [[4 * y + x for x in range(4)] for y in range(4)],
}


def traded(value, axis):
    return lax.all_to_all(value, "ctx", 0, 0, axis_index_groups=GROUPS_OF[axis])


def exchange(value):
    return lax.all_to_all(value, "ctx", 0, 0, axis_index_groups=PARITY)


def halo_shift(value, step):
    pairs = [(j, j + 2 * step) for j in range(16) if 0 <= j + 2 * step < 16]
    return lax.ppermute(value, "ctx", pairs)


def halves(values, section):
    grid = values.reshape(values.shape[0], GROUPS, 2, -1)
    size = values.shape[1] // 2
    return [
        lax.dynamic_index_in_dim(grid, i, 2, False).reshape(-1, size)
        for i in (section, 1 - section)
    ]


def turns(low, high):
    rows = low.shape[0]
    parts = [v.reshape(rows, GROUPS, 1, -1) for v in (low, high)]
    return jnp.concatenate(parts, axis=2).reshape(rows, -1)


def pick_x_body(info, x_ref, dt_ref, *rest):
    smalls, outs, small = rest[:7], rest[7:9], rest[9]
    small[...] = jnp.zeros((16, PACKED), F32)
    row = 0
    for ref in smalls[:4]:
        count, width = ref.shape
        small[row : row + count, :width] = ref[...].astype(F32)
        row += count
    for ref in smalls[4:]:
        left = ref[...]
        for _ in range(3):
            part = left.astype(BF16).astype(F32)
            small[row : row + 1, :HEADS] = part
            left = left - part
            row += 1
    head, lane = row_of((HEADS, LANES)), lane_of((HEADS, LANES))
    for out, side in zip(outs, (info[0], 1 - info[0]), strict=True):
        for d in range(GROUPS):
            cols = pl.ds(pl.multiple_of((2 * d + side) * BLOCK, LANES), BLOCK)
            out[:SHARD, d * BLOCK : (d + 1) * BLOCK] = x_ref[:, cols]
        out[:SHARD, LOCAL:MIXED] = x_ref[:, INNER:]
        here = (head // OWN == 2 * (lane // 8) + side) & (head % OWN == lane % 8)
        out[:SHARD, MIXED:] = dot(dt_ref[...], here.astype(BF16)).astype(BF16)
        out[SHARD:, :] = small[...].astype(BF16)


def pick_x(section, x, dt, smalls):
    return pl.pallas_call(
        pick_x_body,
        out_shape=[shape((TALL, PACKED), BF16)] * 2,
        in_specs=[SMEM, whole((SHARD, CONV_CH)), whole((SHARD, HEADS))]
        + [whole(v.shape) for v in smalls],
        out_specs=[whole((TALL, PACKED))] * 2,
        scratch_shapes=[pltpu.VMEM((16, PACKED), F32)],
        compiler_params=params(),
        cost_estimate=pl.CostEstimate(flops=0, bytes_accessed=6_000_000, transcendentals=0),
        name="pick_x",
    )(section, x, dt, *smalls)


def unpack_body(count, info, *rest):
    refs, (cpar, gain_one, gain_two, hpar, held, full, sems) = rest[:count], rest[count:]
    copies = []
    for n in range(4):
        if count == 4:
            source, to = refs[n].at[pl.ds(2 * PIECE, 16)], lax.rem(info[10] + n, 4)
        else:
            source, to = refs[0].at[pl.ds(n * TALL + SHARD, 16)], n
        copies.append(pltpu.make_async_copy(source, held.at[to], sems.at[n]))
    for c in copies:
        c.start()
    for c in copies:
        c.wait()
    section = info[13]
    half_cols = pl.ds(pl.multiple_of(section * BLOCK, LANES), BLOCK)
    for z in range(4):
        values = held[z].astype(F32)
        full[:, z * 832 : (z + 1) * 832] = values[:8, :832]
        gain_one[:, z * SHARD : (z + 1) * SHARD] = values[5:6, :SHARD]
        gain_two[:, z * BLOCK : (z + 1) * BLOCK] = held[z, :, half_cols].astype(F32)[6:7]
    for d in range(GROUPS):
        cols = pl.ds(pl.multiple_of((2 * d + section) * BLOCK, LANES), BLOCK)
        cpar[:, d * BLOCK : (d + 1) * BLOCK] = full[:, cols]
    cpar[:, LOCAL:] = full[:, INNER:]
    values = held[0, :, :LANES].astype(F32)
    heads = [values[n : n + 1] + values[n + 1 : n + 2] + values[n + 2 : n + 3] for n in (7, 10, 13)]
    heads = jnp.concatenate(heads + [jnp.zeros((5, LANES), F32)], axis=0)
    head, lane = row_of((LANES, LANES)), lane_of((LANES, LANES))
    here = (head // OWN == 2 * (lane // 8) + section) & (head % OWN == lane % 8)
    hpar[...] = exact_dot(heads, here.astype(F32))


def unpack(info, arrays):
    shapes = ((8, MIXED), (1, WIDTH), (1, LOCAL), (8, LANES))
    return pl.pallas_call(
        functools.partial(unpack_body, len(arrays)),
        out_shape=[shape(dims) for dims in shapes],
        in_specs=[SMEM] + [ANYWHERE] * len(arrays),
        out_specs=[whole(dims) for dims in shapes],
        scratch_shapes=[
            pltpu.VMEM((4, 16, PACKED), BF16),
            pltpu.VMEM((8, CONV_CH), F32),
            pltpu.SemaphoreType.DMA((4,)),
        ],
        compiler_params=params(),
        cost_estimate=pl.CostEstimate(flops=0, bytes_accessed=400_000, transcendentals=0),
        name="unpack",
    )(info, *arrays)


def pick_zo_body(info, z_ref, o_ref, token, *outs):
    for out, side in zip(outs, (info[0], 1 - info[0]), strict=True):
        for d in range(GROUPS):
            cols = pl.ds(pl.multiple_of((2 * d + side) * BLOCK, LANES), BLOCK)
            out[:, d * BLOCK : (d + 1) * BLOCK] = z_ref[:, cols]
        rows = pl.ds(pl.multiple_of(side * SHARD, SHARD), SHARD)
        out[:, LOCAL:] = o_ref[rows, :]


def pick_zo(section, z, o, token):
    return pl.pallas_call(
        pick_zo_body,
        out_shape=[shape((SHARD, LOCAL + WIDTH), BF16)] * 2,
        in_specs=[SMEM, whole((SHARD, INNER)), whole((2 * SHARD, WIDTH)), ANYWHERE],
        out_specs=[whole((SHARD, LOCAL + WIDTH))] * 2,
        compiler_params=params(),
        cost_estimate=pl.CostEstimate(flops=0, bytes_accessed=9_000_000, transcendentals=0),
        name="pick_zo",
    )(section, z, o, token)


def head_lanes(values):
    rows = values.shape[0]
    grid = jnp.pad(values.reshape(rows, GROUPS, OWN), ((0, 0), (0, 0), (0, 8 - OWN)))
    return jnp.pad(grid.reshape(rows, 8 * GROUPS), ((0, 0), (0, LANES - 8 * GROUPS)))


def lanes_heads(values):
    rows = values.shape[0]
    return values[:, : 8 * GROUPS].reshape(rows, GROUPS, 8)[:, :, :OWN].reshape(rows, -1)


def on_device(
    boundary,
    lengths,
    norm_gain,
    w_z,
    w_xbc,
    w_dt,
    conv_weight,
    conv_bias,
    dt_bias,
    a_log,
    d_skip,
    gate_gain,
    w_out,
):
    section = lax.axis_index("section")
    group = lax.axis_index("dp")
    ctx = lax.axis_index("ctx")
    place = {"z": group, "y": ctx // 4, "x": ctx % 4}
    micro = ctx % 2
    chunk = ctx // 2

    def ordered(mine, came):
        return jnp.where(section == 0, mine, came), jnp.where(section == 0, came, mine)

    own_rows = lax.dynamic_index_in_dim(boundary[0], micro, 0, False)
    other_rows = lax.dynamic_index_in_dim(boundary[0], 1 - micro, 0, False)
    came = lax.ppermute(other_rows, "ctx", NEIGHBOURS)
    block = jnp.where(
        micro == 0, jnp.concatenate([own_rows, came]), jnp.concatenate([came, own_rows])
    )
    hidden, cotangent = ordered(block, swapped(block))

    pair = lengths[group, micro]
    padded = (pair[0] + SPAN - 1) // SPAN * SPAN
    offset = chunk * ROWS
    begin = jnp.where(offset >= padded, padded, 0)
    length = jnp.where(offset >= padded, pair[1], pair[0])
    live = jnp.clip(length - (offset - begin), 0, ROWS)
    offsets = jnp.arange(CHUNKS, dtype=jnp.int32) * ROWS
    keeps = ((offsets != 0) & (offsets != padded)).astype(jnp.int32)
    keep = (offset != 0) & (offset != padded)
    at = [place["z"], place["y"], place["x"], section]
    info = jnp.concatenate(
        [jnp.stack([live, keep]).astype(jnp.int32), keeps, jnp.stack(at).astype(jnp.int32)]
    )

    def forward(h, layer):
        cpar, hpar = cpars[layer], hpars[layer]
        normed, mixed, rate = in_proj(
            info, h, gains_one[layer], weights_x[layer], []
        )
        halo = halo_shift(mixed[ROWS - 16 :], 1)
        gate = gate_proj(info, normed, weights_z[layer], [] if layer else ready)
        xa, bca, cum, dt, s0, msg = state_call(info, mixed, halo, cpar, rate, hpar)
        came = exchange(msg)
        y_in = inside_call(xa, bca, cum, dt, hpar)
        hin = exchange(scan_call(info, came, False, y_in, *([] if layer else cpars[1:]))).reshape(GROUPS, STATE, BLOCK)
        y, part = out_proj(
            info, y_in, bca, cum, hin, s0, gate, gains_two[layer], weights_o[layer]
        )
        result, branch, scale = join(info, h, part, swapped(part), F32 if layer else BF16)
        saved = (h, normed, mixed, halo, rate, gate, xa, bca, cum, dt, s0, msg, hin, y, branch, scale)
        return result, saved

    def backward(cot, saved, layer, higher, tokens):
        h, normed, mixed, halo, rate, gate, xa, bca, cum, dt, s0, msg, hin, y, branch, scale = saved
        cpar, hpar = cpars[layer], hpars[layer]

        def first_stage(value):
            return lax.psum_scatter(value, "dp", tiled=True)

        bg, dy, dz, grad_o, d_gain_two = gate_back(
            info, cot, y, gate, gains_two[layer], branch, scale, weights_o[layer], layer == 1
        )
        own1, msg_back, grad_z = own_grad(dy, bca, cum, msg, dz, normed)
        sums = [first_stage(grad_z)] + ([first_stage(grad_o)] if layer else [])
        came = exchange(msg_back)
        dxi, d_skips, gsum, u, dbc = inside_back(dy, xa, bca, cum, dt, hpar)
        part = gate_in_back(info, dz, weights_z[layer], msg_back)
        lam = exchange(scan_call(info, came, True, part)).reshape(GROUPS, STATE, BLOCK)
        dmx, dmbc, tailx, tailbc, edgex, edgebc, d_parx, d_parbc, d_heads = finish_call(
            info, xa, dxi, dy, mixed, halo, cpar, bca, cum, dt, rate, hpar, lam, hin, s0, own1, u, gsum, dbc
        )
        edge = halo_shift(jnp.concatenate([edgex, edgebc], axis=1), -1)
        dxc = patch(dmx, dmbc, tailx, tailbc, edge, *tokens)
        middle = 7 * LANES
        if layer == 0:
            higher_rows, higher = higher
            normed_t = normed.T
            cuts = [(normed_t, dxc, slice(0, middle)), (grad_o, bg, slice(0, WIDTH // 2))]
            left = terms(info, "y", cuts, (), True)
            part, d_gain_one = mixed_back(
                info, dxc, part, h, normed, weights_x[layer], False, [left, *higher]
            )
        else:
            part, d_gain_one, grad_x = mixed_back(
                info, dxc, part, h, normed, weights_x[layer], True, []
            )
        dh, dh_low = norm_back(part, swapped(part), h, cot, gains_one[layer])
        d_skip_row = jnp.sum(d_skips[0:1].reshape(1, 4 * OWN, HEADDIM), axis=2)
        rows = jnp.where(jnp.arange(8)[:, None] == 5, d_gain_two, d_parx)
        rows = jnp.concatenate([rows, d_parbc], axis=1)
        more = jnp.concatenate(
            [
                d_gain_one[:1],
                jnp.pad(d_heads[:2], ((0, 0), (0, WIDTH - LANES))),
                jnp.pad(head_lanes(d_skip_row), ((0, 4), (0, WIDTH - LANES))),
            ]
        )
        rows = jnp.concatenate([rows, jnp.pad(more, ((0, 0), (0, 2 * STATE)))])
        if layer == 1:
            return dh, dh_low, sums + [first_stage(grad_x)], rows

        rows = jnp.concatenate([rows, higher_rows]).astype(BF16)
        cuts = [(normed_t, dxc, slice(middle, PACKED)), (grad_o, bg, slice(WIDTH // 2, WIDTH))]
        right = arrived(terms(info, "x", cuts, (rows,)), "x")
        near = (right[1], right[3])
        tall = fold(info, "y", [[v] for v in higher + sums], 1, 96, near, True)
        left = fold(info, "x", [[traded(left, "y")]], 4, 24, tall)
        right = fold(info, "y", [right], 4, 24, dh_low)
        tall = fold(info, "x", [[traded(tall, "y")]], 1, 24, right[0])
        left, right = arrived(left, "x"), arrived(right, "y")
        final = summed(arrived(last_fold(info, left, right, tall[0]), "z"))
        left, right = left[0].shape[1], right[0].shape[1]
        rows = final[24:, left:]
        final = final[:24]
        sum_x = jnp.concatenate(
            [final[:, :middle], final[:, left : left + PACKED - middle]], axis=1
        )
        sum_o = jnp.concatenate([final[:, middle:left], final[:, left + PACKED - middle :]], axis=1)
        return dh, [arrived(tall, "x"), sum_o], sum_x, rows

    at = section.reshape(1).astype(jnp.int32)
    smalls = (conv_weight[0], conv_bias, norm_gain, gate_gain, dt_bias, a_log, d_skip)
    mine_x, other_x = pick_x(at, w_xbc[0], w_dt[0], smalls)
    came_x = swapped(other_x)
    mine_zo, other_zo = pick_zo(at, w_z[0], w_out[0], mine_x)
    came_zo = swapped(other_zo)
    first = fetched(mine_x, came_x, 0, section, after([hidden], place))
    got = [first] + [send(first, "z", -r) for r in range(1, 4)]
    small_low = got
    low_x = pieces(mine_x, came_x, got, 0)
    got = lax.all_gather(fetched(mine_zo, came_zo, 0, section, after(got[1:], place)), "dp")
    low_params = unpack(info, small_low)
    late = after([*low_x[3:6], *low_x[7:10], low_params[0]], place)["z"]
    got = [None] + [lax.dynamic_index_in_dim(got, (late + r) % 4, 0, False) for r in range(1, 4)]
    low_zo = pieces(mine_zo, came_zo, got, 0)
    here = after([low_x[2], low_x[6]], {"section": section})["section"]
    high_x = [lax.all_gather(jnp.where(here == 1, mine_x, came_x), "dp", tiled=True)]
    high_zo = [lax.all_gather(jnp.where(here == 1, mine_zo, came_zo), "dp", tiled=True)]
    ready = low_zo[3:6] + low_zo[7:10]
    weights_x = [Weight(v, n, PACKED) for n, v in enumerate((low_x, high_x))]
    weights_z = [Weight(v, n, LOCAL) for n, v in enumerate((low_zo, high_zo))]
    weights_o = [Weight(v, n, WIDTH, LOCAL) for n, v in enumerate((low_zo, high_zo))]

    unpacked = [low_params, unpack(info, high_x)]
    cpars, gains_one, gains_two, hpars = zip(*unpacked, strict=True)

    def returned(rows, layer):
        pairs = [(layer * 16 + a, layer * 16 + b) for a, b in NEIGHBOURS]
        other, mine = (
            lax.dynamic_slice_in_dim(rows, n * HALF, HALF, 0) for n in (1 - micro, micro)
        )
        other = lax.ppermute(other, ("section", "ctx"), pairs)
        return jnp.where(micro == 0, jnp.stack([mine, other]), jnp.stack([other, mine]))

    middle, saved_low = forward(hidden, 0)
    out_high, saved_high = forward(middle, 1)
    top_high = returned(out_high, 1)
    _, back, higher, rows = backward(cotangent, saved_high, 1, None, [top_high])
    dh_low, (tall, low_o), low_x, rows = backward(back, saved_low, 0, (rows, higher), [rows])
    at = (LOCAL, LOCAL + WIDTH, LOCAL + WIDTH + PACKED)
    high_z, high_o, high_x, low_z = jnp.split(summed(tall), at, axis=1)

    own, given = ordered(rows[:16], rows[16:])
    rows_0, rows_1 = ordered(own, swapped(given))
    wide = jnp.concatenate(
        [turns(rows_0[:8, :LOCAL], rows_1[:8, :LOCAL]), rows_0[:8, LOCAL:] + rows_1[:8, LOCAL:]],
        axis=1,
    )
    head_rows = turns(lanes_heads(rows_0[9:12, :LANES]), lanes_heads(rows_1[9:12, :LANES]))
    index = group * 16 + ctx
    d_conv = lax.dynamic_slice(wide, (0, index * 52), (5, 52))
    d_gain_two = lax.dynamic_slice(wide, (5, index * 48), (1, 48))
    d_gain_one = lax.dynamic_slice(rows_0[8:9] + rows_1[8:9], (0, index * 24), (1, 24))

    own, given = ordered(
        jnp.concatenate([low_z, low_x], axis=1), jnp.concatenate([high_z, high_x], axis=1)
    )
    first, second = ordered(own, swapped(given))
    sum_z = turns(first[:, :LOCAL], second[:, :LOCAL])
    at_x, at_bc, at_dt = LOCAL, LOCAL + LOCAL, LOCAL + MIXED
    sum_x = turns(first[:, at_x:at_bc], second[:, at_x:at_bc])
    sum_bc = first[:, at_bc:at_dt] + second[:, at_bc:at_dt]
    sum_dt = turns(lanes_heads(first[:, at_dt:]), lanes_heads(second[:, at_dt:]))

    trips = []
    for flip in range(2):
        pairs = [
            (c * 16 + j, (flip ^ (j % 2)) * 16 + 8 * c + j // 2) for c in range(2) for j in range(16)
        ]
        value = jnp.where(micro == flip, low_o, high_o)
        trips.append(lax.ppermute(value, ("section", "ctx"), pairs))
    sum_o = jnp.concatenate(ordered(*trips))

    top = jnp.where(section == 0, returned(dh_low, 0), top_high)
    return (
        top[None],
        d_gain_one,
        sum_z[None],
        jnp.concatenate([sum_x, sum_bc], axis=1)[None],
        sum_dt[None],
        d_conv[None, :4],
        d_conv[4:5],
        head_rows[0:1],
        head_rows[1:2],
        head_rows[2:3],
        d_gain_two,
        sum_o[None],
    )


def solution(mesh):
    in_specs = (
        P("section", None, ("dp", "ctx"), None),
        P(),
        P("section", "dp"),
        P("section", "dp", None),
        P("section", "dp", None),
        P("section", "dp", None),
        P("section", None, "dp"),
        P("section", "dp"),
        P("section", None),
        P("section", None),
        P("section", None),
        P("section", "dp"),
        P("section", "dp", None),
    )
    out_specs = (
        P("section", None, ("dp", "ctx"), None),
        P("section", ("dp", "ctx")),
        P("section", ("dp", "ctx"), None),
        P("section", ("dp", "ctx"), None),
        P("section", ("dp", "ctx"), None),
        P("section", None, ("dp", "ctx")),
        P("section", ("dp", "ctx")),
        P("section", None),
        P("section", None),
        P("section", None),
        P("section", ("dp", "ctx")),
        P("section", ("dp", "ctx"), None),
    )
    return jax.shard_map(
        on_device, mesh=mesh, in_specs=in_specs, out_specs=out_specs, check_vma=False
    )
```

```python
import functools

import jax
import jax.numpy as jnp
from jax import lax
from jax.experimental import pallas as pl
from jax.experimental.pallas import tpu as pltpu
from jax.sharding import PartitionSpec as P

HEADS = 48
HEADDIM = 64
STATE = 128
KERNEL = 4
SPAN = 256
MICRO = 2
WIDTH = 1536
INNER = 3072
CONV_CH = 3328
LANES = 128
CHUNKS = 8
GROUPS = 4
OWN = 6
BLOCK = OWN * HEADDIM
LOCAL = GROUPS * BLOCK
MIXED = LOCAL + 2 * STATE
PACKED = MIXED + LANES
ROWS = 256
HALF = 128
SHARD = 384
TALL = SHARD + 16
PIECE = 48
STATE_HALF = STATE // 2
MESSAGE = STATE_HALF + 16
SMALL = 32
EPSILON = 1e-05
PRECISE = lax.Precision.HIGHEST
F32 = jnp.float32
BF16 = jnp.bfloat16
VMEM_LIMIT = 56 * 1024 * 1024


def params(**more):
    return pltpu.CompilerParams(vmem_limit_bytes=VMEM_LIMIT, **more)


def whole(shape):
    return pl.BlockSpec(shape, lambda *_: (0,) * len(shape))


def columns(rows, width):
    return pl.BlockSpec((rows, width), lambda g: (0, g))


def grouped(rows):
    return pl.BlockSpec((1, rows, BLOCK), lambda g: (g, 0, 0))


MESSAGES = pl.BlockSpec((2, MESSAGE, BLOCK), lambda g: (g, 0, 0))
SMEM = pl.BlockSpec(memory_space=pltpu.SMEM)
ANYWHERE = pl.BlockSpec(memory_space=pl.ANY)


def shape(dims, kind=F32):
    return jax.ShapeDtypeStruct(dims, kind)


def dot(a, b):
    return jnp.dot(a, b, preferred_element_type=F32)


def dot_nt(a, b):
    return lax.dot_general(a, b, (((1,), (1,)), ((), ())), preferred_element_type=F32)


def exact_dot(a, b):
    return jnp.dot(a, b, precision=PRECISE, preferred_element_type=F32)


def lane_of(dims):
    return lax.broadcasted_iota(jnp.int32, dims, len(dims) - 1)


def row_of(dims):
    return lax.broadcasted_iota(jnp.int32, dims, len(dims) - 2)


def sigmoid(v):
    return 1.0 / (1.0 + jnp.exp(-v))


def softplus(v):
    return jnp.maximum(v, 0.0) + jnp.log1p(jnp.exp(-jnp.abs(v)))


def rolled(values, g):
    return pltpu.roll(values, lax.rem(LANES - 8 * g, LANES), axis=1)


def pair_lanes(values, p):
    low = lane_of((values.shape[0], LANES)) < HEADDIM
    return jnp.where(low, values[:, 2 * p : 2 * p + 1], values[:, 2 * p + 1 : 2 * p + 2])


def spread(values):
    return jnp.concatenate([pair_lanes(values, p) for p in range(OWN // 2)], axis=1)


def head_sum_matrix(g):
    head = row_of((BLOCK, LANES)) // HEADDIM
    return (lane_of((BLOCK, LANES)) == head + 8 * g).astype(BF16)


def lower_triangle(strict=False):
    i, j = row_of((HALF, HALF)), lane_of((HALF, HALF))
    return ((i > j) if strict else (i >= j)).astype(F32)


def usable_rows(info):
    return (row_of((ROWS, 1)) < info[0]).astype(F32)


def half(values, q):
    return values[q * HALF : (q + 1) * HALF]


class Weight:
    def __init__(self, arrays, layer, width, first=0):
        self.arrays = arrays
        self.stride = arrays[0].shape[0] // 4
        self.layer = layer
        self.width = width
        self.columns = pl.ds(first, width)

    def block(self, info, b):
        return lax.rem(info[10] + b, 4) * SHARD

    def parts(self, refs, info, b):
        start = self.block(info, b)
        if len(refs) == 1:
            there = pl.multiple_of(start // SHARD * self.stride, 16)
            return [(refs[0].at[pl.ds(there, SHARD)], start, SHARD)]
        out = []
        for side in range(2):
            mine = info[12 - side]
            for step in range(4):
                source = refs[2 + 4 * side + step].at[pl.ds((b - 1) * PIECE, PIECE)]
                row = start + side * (SHARD // 2) + lax.rem(mine + step, 4) * PIECE
                out.append((source, row, PIECE))
        return out

    def copies(self, refs, info, b, buffer, sems):
        return [
            pltpu.make_async_copy(
                source.at[:, self.columns],
                buffer.at[pl.ds(pl.multiple_of(row, 16), count)],
                sems.at[b, n],
            )
            for n, (source, row, count) in enumerate(self.parts(refs, info, b))
        ]

    def own_copy(self, source, info, buffer, sems):
        rows = pl.ds(pl.multiple_of(self.block(info, 0), SHARD), SHARD)
        source = source.at[pl.ds(0, SHARD), self.columns]
        return pltpu.make_async_copy(source, buffer.at[rows], sems.at[0, 0])

    def start(self, refs, info, buffer, sems):
        whole_array = len(refs) == 1
        if not whole_array:
            for n in range(2):

                @pl.when((info[13] == self.layer) == (n == 0))
                def _(n=n):
                    self.own_copy(refs[n], info, buffer, sems).start()

        for b in range(0 if whole_array else 1, 4):
            for c in self.copies(refs, info, b, buffer, sems):
                c.start()

    def wait(self, refs, info, b, buffer, sems):
        if b == 0 and len(refs) > 1:
            self.own_copy(refs[0], info, buffer, sems).wait()
        else:
            for c in self.copies(refs, info, b, buffer, sems):
                c.wait()
        return pl.ds(pl.multiple_of(self.block(info, b), SHARD), SHARD)

    def specs(self):
        return [ANYWHERE] * len(self.arrays)

    def scratch(self):
        return [pltpu.VMEM((4 * SHARD, self.width), BF16), pltpu.SemaphoreType.DMA((4, 8))]

    def product(self, refs, info, left, buffer, sems, total):
        for b in range(4):
            self.wait(refs, info, b, buffer, sems)
        step = 512 if self.width % 512 == 0 else 640
        for at in range(0, self.width, step):
            value = dot(left[...], buffer[:, at : at + step])
            total[:, at : at + step] = value.astype(total.dtype)


def in_proj_body(weight, tokens, info, h_ref, gain_ref, *rest):
    refs = len(weight.arrays)
    w_refs, rest = rest[:refs], rest[refs + tokens :]
    (normed_ref, mixed_ref, rate_ref, buffer, sems, total) = rest
    weight.start(w_refs, info, buffer, sems)
    h = h_ref[...].astype(F32)
    scale = lax.rsqrt(jnp.mean(h * h, axis=1, keepdims=True) + EPSILON)
    normed_ref[...] = (h * scale * gain_ref[...]).astype(BF16)
    weight.product(w_refs, info, normed_ref, buffer, sems, total)
    mixed_ref[...] = total[:, :MIXED].astype(BF16)
    rate_ref[...] = total[:, MIXED:]


def in_proj(info, h, gain, weight, tokens):
    return pl.pallas_call(
        functools.partial(in_proj_body, weight, len(tokens)),
        out_shape=(shape((ROWS, WIDTH), BF16), shape((ROWS, MIXED), BF16), shape((ROWS, LANES))),
        in_specs=[SMEM, whole((ROWS, WIDTH)), whole((1, WIDTH))]
        + weight.specs()
        + [ANYWHERE] * len(tokens),
        out_specs=(whole((ROWS, WIDTH)), whole((ROWS, MIXED)), whole((ROWS, LANES))),
        scratch_shapes=weight.scratch() + [pltpu.VMEM((ROWS, PACKED), F32)],
        compiler_params=params(),
        cost_estimate=pl.CostEstimate(
            flops=2 * ROWS * WIDTH * PACKED, bytes_accessed=8_000_000, transcendentals=0
        ),
        name="in_proj",
    )(info, h, gain, *weight.arrays, *tokens)


def gate_proj_body(weight, tokens, info, normed_ref, *rest):
    refs = len(weight.arrays)
    w_refs, (gate_ref, buffer, sems) = rest[:refs], rest[refs + tokens :]
    weight.start(w_refs, info, buffer, sems)
    weight.product(w_refs, info, normed_ref, buffer, sems, gate_ref)


def gate_proj(info, normed, weight, tokens):
    return pl.pallas_call(
        functools.partial(gate_proj_body, weight, len(tokens)),
        out_shape=shape((ROWS, LOCAL)),
        in_specs=[SMEM, whole((ROWS, WIDTH))] + weight.specs() + [ANYWHERE] * len(tokens),
        out_specs=whole((ROWS, LOCAL)),
        scratch_shapes=weight.scratch(),
        compiler_params=params(),
        cost_estimate=pl.CostEstimate(
            flops=2 * ROWS * WIDTH * LOCAL, bytes_accessed=7_000_000, transcendentals=0
        ),
        name="gate_proj",
    )(info, normed, *weight.arrays, *tokens)


def conv_sum_of(values, halo, cpar, keep, ext):
    width = values.shape[1]
    ext[0:16, :width] = halo.astype(F32) * keep
    ext[16 : 16 + ROWS, :width] = values.astype(F32)
    total = cpar[4:5, :]
    for k in range(KERNEL):
        total = total + cpar[k : k + 1, :] * ext[13 + k : 13 + k + ROWS, :width]
    return total


def state_body(
    info, mixed, halo, cpar, bc, halo_bc, cpar_bc, rate, hpar,
    xa_ref, bca_ref, cum_ref, dt_ref, s0_ref, msg_ref, ext, bt, tail,
):
    g = pl.program_id(0)
    keep = info[1].astype(F32)

    @pl.when(g == 0)
    def _():
        total = conv_sum_of(bc[...], halo_bc[...], cpar_bc[...], keep, ext)
        active = total * sigmoid(total)
        bca_ref[...] = active
        bt[...] = active[:, :STATE].T.astype(BF16)
        dt = usable_rows(info) * softplus(rate[...] + hpar[0:1, :])
        log_decay = dt * -jnp.exp(hpar[1:2, :])
        dt_ref[...] = dt
        tri = lower_triangle()
        for q in range(2):
            rows = pl.ds(q * HALF, HALF)
            cum = exact_dot(tri, half(log_decay, q))
            cum_ref[rows, :] = cum
            tail[rows, :] = jnp.exp(cum[HALF - 1 :, :] - cum) * half(dt, q)

    total = conv_sum_of(mixed[...], halo[...], cpar[...], keep, ext)
    xa = total * sigmoid(total)
    xa_ref[...] = xa
    weighted = (xa * spread(rolled(tail[...], g))).astype(BF16)
    ends = rolled(cum_ref[...], g)
    end0, end1 = ends[HALF - 1 : HALF], ends[ROWS - 1 : ROWS]
    s0 = dot(bt[:, :HALF], half(weighted, 0))
    s1 = dot(bt[:, HALF:], half(weighted, 1))
    s0_ref[0] = s0
    state = (spread(jnp.exp(end1)) * s0 + s1).astype(BF16)
    damp = spread(jnp.exp(end0 + end1))
    high = damp.astype(BF16)
    low = (damp - high.astype(F32)).astype(BF16)
    row = row_of((16, BLOCK))
    damps = jnp.where(row == 0, high.astype(F32), low.astype(F32)).astype(BF16)
    for r in range(2):
        msg_ref[r, :STATE_HALF, :] = state[r * STATE_HALF : (r + 1) * STATE_HALF]
        msg_ref[r, STATE_HALF:, :] = damps


def state_call(info, mixed, halo, cpar, rate, hpar):
    bc_at = LOCAL // 256
    return pl.pallas_call(
        state_body,
        grid=(GROUPS,),
        out_shape=(
            shape((ROWS, LOCAL)),
            shape((ROWS, 256)),
            shape((ROWS, LANES)),
            shape((ROWS, LANES)),
            shape((GROUPS, STATE, BLOCK)),
            shape((CHUNKS, MESSAGE, BLOCK), BF16),
        ),
        in_specs=[
            SMEM,
            columns(ROWS, BLOCK),
            columns(16, BLOCK),
            columns(8, BLOCK),
            pl.BlockSpec((ROWS, 256), lambda g: (0, bc_at)),
            pl.BlockSpec((16, 256), lambda g: (0, bc_at)),
            pl.BlockSpec((8, 256), lambda g: (0, bc_at)),
            whole((ROWS, LANES)),
            whole((8, LANES)),
        ],
        out_specs=(
            columns(ROWS, BLOCK),
            whole((ROWS, 256)),
            whole((ROWS, LANES)),
            whole((ROWS, LANES)),
            grouped(STATE),
            MESSAGES,
        ),
        scratch_shapes=[
            pltpu.VMEM((ROWS + 32, BLOCK), F32),
            pltpu.VMEM((STATE, ROWS), BF16),
            pltpu.VMEM((ROWS, LANES), F32),
        ],
        compiler_params=params(),
        cost_estimate=pl.CostEstimate(
            flops=2 * ROWS * STATE * LOCAL, bytes_accessed=4_500_000, transcendentals=400_000
        ),
        name="conv_state",
    )(info, mixed, halo, cpar, mixed, halo, cpar, rate, hpar)


def inside_body(xa, bca, cum, dt, hpar, y_ref, cum_t, scores):
    g = pl.program_id(0)

    @pl.when(g == 0)
    def _():
        tri = lower_triangle()
        for q in range(2):
            b, c = half(bca[:, :STATE], q).astype(BF16), half(bca[:, STATE:], q).astype(BF16)
            scores[q] = dot_nt(c, b) * tri
            cum_t[:, q * HALF : (q + 1) * HALF] = half(cum[...], q).T

    cols = rolled(cum[...], g)
    rows = cum_t[pl.ds(pl.multiple_of(8 * g, 8), 8), :]
    steps = rolled(dt[...], g)
    skips = rolled(hpar[...], g)[2:3, :]
    low = lane_of((HALF, LANES)) < HEADDIM
    for q in range(2):
        for p in range(OWN // 2):
            lanes = slice(p * LANES, (p + 1) * LANES)
            x = xa[q * HALF : (q + 1) * HALF, lanes]
            xdt = x * pair_lanes(half(steps, q), p)
            both = jnp.concatenate([jnp.where(low, xdt, 0.0), jnp.where(low, 0.0, xdt)], axis=0)
            mats = []
            for i in (2 * p, 2 * p + 1):
                gap = half(cols, q)[:, i : i + 1] - rows[i : i + 1, q * HALF : (q + 1) * HALF]
                mats.append((jnp.exp(jnp.minimum(gap, 0.0)) * scores[q]).astype(BF16))
            y = dot(jnp.concatenate(mats, axis=1), both.astype(BF16))
            y_ref[q * HALF : (q + 1) * HALF, lanes] = y + x * pair_lanes(skips, p)


def inside_call(xa, bca, cum, dt, hpar):
    return pl.pallas_call(
        inside_body,
        grid=(GROUPS,),
        out_shape=shape((ROWS, LOCAL)),
        in_specs=[
            columns(ROWS, BLOCK),
            whole((ROWS, 256)),
            whole((ROWS, LANES)),
            whole((ROWS, LANES)),
            whole((8, LANES)),
        ],
        out_specs=columns(ROWS, BLOCK),
        scratch_shapes=[pltpu.VMEM((LANES, ROWS), F32), pltpu.VMEM((2, HALF, HALF), F32)],
        compiler_params=params(),
        cost_estimate=pl.CostEstimate(
            flops=2 * HEADS * HALF * HALF * LANES, bytes_accessed=3_300_000, transcendentals=800_000
        ),
        name="inside",
    )(xa, bca, cum, dt, hpar)


def scan_body(backward, info, msg, *rest):
    out_ref = rest[-1]
    carry = jnp.zeros((STATE_HALF, BLOCK), F32)
    for k in reversed(range(CHUNKS)) if backward else range(CHUNKS):
        keep = info[2 + k].astype(F32)
        if not backward:
            carry = carry * keep
        out_ref[k] = carry.astype(BF16)
        damps = msg[k, STATE_HALF:, :].astype(F32)
        carry = (damps[0:1] + damps[1:2]) * carry + msg[k, :STATE_HALF, :].astype(F32)
        if backward:
            carry = carry * keep


def scan_call(info, msg, backward, *tokens):
    return pl.pallas_call(
        functools.partial(scan_body, backward),
        out_shape=shape((CHUNKS, STATE_HALF, BLOCK), BF16),
        in_specs=[SMEM, whole((CHUNKS, MESSAGE, BLOCK))] + [ANYWHERE] * len(tokens),
        out_specs=whole((CHUNKS, STATE_HALF, BLOCK)),
        compiler_params=params(),
        name="chunk_scan",
    )(info, msg, *tokens)


def out_proj_body(weight, info, y_in, bca, cum, hin, s0, gate, gain, *rest):
    refs = len(weight.arrays)
    w_refs, (y_ref, part_ref, buffer, sems, sums, gained) = rest[:refs], rest[refs:]
    weight.start(w_refs, info, buffer, sems)
    c_all = bca[:, STATE:].astype(BF16)
    grow = jnp.exp(cum[...])
    sums[...] = jnp.zeros((ROWS, LANES), F32)

    def group(g, _):
        lanes = pl.ds(pl.multiple_of(g * BLOCK, LANES), BLOCK)
        factor = rolled(grow, g)
        first = hin[g]
        second = spread(factor[HALF - 1 : HALF]) * first.astype(F32) + s0[g]
        carried = jnp.concatenate(
            [dot(half(c_all, 0), first), dot(half(c_all, 1), second.astype(BF16))], axis=0
        )
        y = y_in[:, lanes] + spread(factor) * carried
        y_ref[:, lanes] = y
        z = gate[:, lanes]
        gated = y * z * sigmoid(z)
        square = gated * gated
        sums[...] += sum(square[:, i * LANES : (i + 1) * LANES] for i in range(BLOCK // LANES))
        gained[:, lanes] = (gated * gain[:, lanes]).astype(BF16)
        return 0

    lax.fori_loop(0, GROUPS, group, 0)
    part_ref[:, WIDTH:] = sums[...].astype(BF16)
    weight.product(w_refs, info, gained, buffer, sems, part_ref)


def out_proj(info, y_in, bca, cum, hin, s0, gate, gain, weight):
    return pl.pallas_call(
        functools.partial(out_proj_body, weight),
        out_shape=(shape((ROWS, LOCAL)), shape((ROWS, WIDTH + LANES), BF16)),
        in_specs=[
            SMEM,
            whole((ROWS, LOCAL)),
            whole((ROWS, 256)),
            whole((ROWS, LANES)),
            whole((GROUPS, STATE, BLOCK)),
            whole((GROUPS, STATE, BLOCK)),
            whole((ROWS, LOCAL)),
            whole((1, LOCAL)),
        ]
        + weight.specs(),
        out_specs=(whole((ROWS, LOCAL)), whole((ROWS, WIDTH + LANES))),
        scratch_shapes=weight.scratch()
        + [pltpu.VMEM((ROWS, LANES), F32), pltpu.VMEM((ROWS, LOCAL), BF16)],
        compiler_params=params(),
        cost_estimate=pl.CostEstimate(
            flops=2 * ROWS * WIDTH * LOCAL, bytes_accessed=13_000_000, transcendentals=800_000
        ),
        name="out_proj",
    )(info, y_in, bca, cum, hin, s0, gate, gain, *weight.arrays)


def join_body(info, h_ref, own, came, res_ref, branch_ref, scale_ref):
    both = own[...].astype(F32) + came[...].astype(F32)
    squares = jnp.sum(both[:, WIDTH:], axis=1, keepdims=True)
    scale = lax.rsqrt(squares / INNER + EPSILON)
    branch = scale * both[:, :WIDTH]
    branch_ref[...] = branch.astype(BF16)
    scale_ref[...] = jnp.broadcast_to(scale, (HALF // 2, LANES))
    first = pl.program_id(0) * (HALF // 2)
    usable = (row_of((HALF // 2, 1)) + first < info[0]).astype(F32)
    result = h_ref[...].astype(F32) + usable * branch
    res_ref[...] = result.astype(res_ref.dtype)


def join(info, h, own, came, kind):
    def rows(width):
        return pl.BlockSpec((HALF // 2, width), lambda i: (i, 0))

    return pl.pallas_call(
        join_body,
        grid=(4,),
        out_shape=(shape((ROWS, WIDTH), kind), shape((ROWS, WIDTH), BF16), shape((ROWS, LANES))),
        in_specs=[SMEM, rows(WIDTH), rows(WIDTH + LANES), rows(WIDTH + LANES)],
        out_specs=(rows(WIDTH), rows(WIDTH), rows(LANES)),
        compiler_params=params(),
        cost_estimate=pl.CostEstimate(flops=2_000_000, bytes_accessed=8_000_000, transcendentals=0),
        name="join",
    )(info, h, own, came)


def gate_back_body(weight, info, cot, y, gate, gain, branch, scale_ref, *rest):
    refs = len(weight.arrays)
    w_refs, rest = rest[:refs], rest[refs:]
    bg_ref, dy_ref, dz_ref, grad_ref, dgain_ref, buffer, sems, inner_ref = rest
    b = pl.program_id(0)
    scale = scale_ref[:, :1]

    @pl.when(b == 0)
    def _():
        weight.start(w_refs, info, buffer, sems)
        bg = (usable_rows(info) * cot[...].astype(F32)).astype(BF16)
        bg_ref[...] = bg
        inner = jnp.sum(bg.astype(F32) * branch[...].astype(F32), axis=1, keepdims=True)
        inner_ref[...] = jnp.broadcast_to(inner * scale * scale / INNER, (ROWS, LANES))
        for n in range(4):
            weight.wait(w_refs, info, n, buffer, sems)

    inner = inner_ref[:, :1]
    bg = bg_ref[...]
    d_norms = dot_nt(bg, buffer[pl.ds(pl.multiple_of(b * SHARD, SHARD), SHARD), :])
    norms = []
    for i in range(SHARD // LANES):
        lanes = slice(i * LANES, (i + 1) * LANES)
        z = gate[:, lanes]
        sig = sigmoid(z)
        silu = z * sig
        y_here = y[:, lanes]
        gated = y_here * silu
        d_norm = d_norms[:, lanes]
        gained = scale * gain[:, lanes]
        norms.append((gated * gained).astype(BF16))
        d_gated = d_norm * gained - gated * inner
        total = jnp.sum(d_norm * gated * scale, axis=0, keepdims=True)
        dgain_ref[:, lanes] = jnp.broadcast_to(total, (8, LANES))
        dy_ref[:, lanes] = (d_gated * silu).astype(BF16)
        dz_ref[:, lanes] = (d_gated * y_here * sig * (1.0 + z * (1.0 - sig))).astype(BF16)
    norm = jnp.concatenate(norms, axis=1)
    grad_ref[...] = dot(norm.T, bg).astype(BF16) if grad_ref.shape[1] == WIDTH else norm.T


def gate_back(info, cot, y, gate, gain, branch, scale, weight, with_grad):
    wide, local = whole((ROWS, WIDTH)), columns(ROWS, SHARD)
    grad_width = WIDTH if with_grad else ROWS
    return pl.pallas_call(
        functools.partial(gate_back_body, weight),
        grid=(4,),
        out_shape=(
            shape((ROWS, WIDTH), BF16),
            shape((ROWS, LOCAL), BF16),
            shape((ROWS, LOCAL), BF16),
            shape((LOCAL, grad_width), BF16),
            shape((8, LOCAL)),
        ),
        in_specs=[SMEM, wide, local, local, columns(1, SHARD), wide, whole((ROWS, LANES))]
        + weight.specs(),
        out_specs=(
            wide,
            local,
            local,
            pl.BlockSpec((SHARD, grad_width), lambda b: (b, 0)),
            columns(8, SHARD),
        ),
        scratch_shapes=weight.scratch() + [pltpu.VMEM((ROWS, LANES), F32)],
        compiler_params=params(),
        cost_estimate=pl.CostEstimate(
            flops=4 * ROWS * WIDTH * LOCAL, bytes_accessed=17_000_000, transcendentals=800_000
        ),
        name="gate_back",
    )(info, cot, y, gate, gain, branch, scale, *weight.arrays)


def own_grad_body(dy, bca, cum, msg_in, dz, normed, own1_ref, msg_ref, grad_ref, ct, grow):
    g = pl.program_id(0)
    grad_ref[...] = dot(normed[...].T, dz[...]).astype(BF16)

    @pl.when(g == 0)
    def _():
        ct[...] = bca[:, STATE:].T.astype(BF16)
        grow[...] = jnp.exp(cum[...])

    factor = rolled(grow[...], g)
    weighted = (dy[...].astype(F32) * spread(factor)).astype(BF16)
    own0 = dot(ct[:, :HALF], half(weighted, 0))
    own1 = dot(ct[:, HALF:], half(weighted, 1))
    own1_ref[0] = own1
    grad = (spread(factor[HALF - 1 : HALF]) * own1 + own0).astype(BF16)
    for r in range(2):
        msg_ref[r, :STATE_HALF, :] = grad[r * STATE_HALF : (r + 1) * STATE_HALF]
        msg_ref[r, STATE_HALF:, :] = msg_in[r, STATE_HALF:, :]


def own_grad(dy, bca, cum, msg, dz, normed):
    return pl.pallas_call(
        own_grad_body,
        grid=(GROUPS,),
        out_shape=(
            shape((GROUPS, STATE, BLOCK)),
            shape((CHUNKS, MESSAGE, BLOCK), BF16),
            shape((WIDTH, LOCAL), BF16),
        ),
        in_specs=[
            columns(ROWS, BLOCK),
            whole((ROWS, 256)),
            whole((ROWS, LANES)),
            MESSAGES,
            whole((ROWS, LOCAL)),
            columns(ROWS, SHARD),
        ],
        out_specs=(grouped(STATE), MESSAGES, pl.BlockSpec((SHARD, LOCAL), lambda b: (b, 0))),
        scratch_shapes=[pltpu.VMEM((STATE, ROWS), BF16), pltpu.VMEM((ROWS, LANES), F32)],
        compiler_params=params(),
        cost_estimate=pl.CostEstimate(
            flops=2 * ROWS * WIDTH * LOCAL, bytes_accessed=8_000_000, transcendentals=0
        ),
        name="own_grad",
    )(dy, bca, cum, msg, dz, normed)


def inside_back_body(
    dy, xa, bca, cum, dt, hpar,
    dx_ref, dskip_ref, gsum_ref, u_ref, dbc_ref, cum_t, scores, dscores,
):
    g = pl.program_id(0)

    @pl.when(g == 0)
    def _():
        tri = lower_triangle()
        for q in range(2):
            b, c = half(bca[:, :STATE], q).astype(BF16), half(bca[:, STATE:], q).astype(BF16)
            scores[q] = dot_nt(b, c) * tri.T
            cum_t[:, q * HALF : (q + 1) * HALF] = half(cum[...], q).T
        dscores[...] = jnp.zeros((2, HALF, HALF), F32)
        u_ref[...] = jnp.zeros((ROWS, LANES), F32)

    cols = rolled(cum[...], g)
    rows = cum_t[pl.ds(pl.multiple_of(8 * g, 8), 8), :]
    steps = rolled(dt[...], g)
    skips = rolled(hpar[...], g)[2:3, :]
    low = lane_of((HALF, LANES)) < HEADDIM
    lane = lane_of((HALF, LANES))
    gsum_ref[...] = jnp.zeros((8, ROWS), F32)
    for q in range(2):
        here = slice(q * HALF, (q + 1) * HALF)
        u_here = u_ref[here, :]
        for p in range(OWN // 2):
            lanes = slice(p * LANES, (p + 1) * LANES)
            dy_pair = dy[here, lanes]
            x = xa[here, lanes]
            zero = jnp.zeros_like(dy_pair)
            both = jnp.concatenate(
                [jnp.where(low, dy_pair, zero), jnp.where(low, zero, dy_pair)], axis=0
            )
            dw = dot_nt(x.astype(BF16), both)
            mats = []
            for n, i in enumerate((2 * p, 2 * p + 1)):
                gap = rows[i : i + 1, here] - half(cols, q)[:, i : i + 1]
                decay = jnp.exp(jnp.minimum(gap, 0.0))
                step = half(steps, q)[:, i : i + 1]
                weight = decay * scores[q]
                mats.append(weight.astype(BF16))
                dw_here = dw[:, n * HALF : (n + 1) * HALF]
                dscores[q] += decay * dw_here * step
                direct = weight * dw_here
                total = jnp.sum(direct, axis=1, keepdims=True)
                u_here = jnp.where(lane == 8 * g + i, total, u_here)
                gsum_ref[i : i + 1, here] = jnp.sum(direct * step, axis=0, keepdims=True)
            dx = dot(jnp.concatenate(mats, axis=1), both)
            dy_wide = dy_pair.astype(F32)
            dx_ref[here, lanes] = dx * pair_lanes(half(steps, q), p) + dy_wide * pair_lanes(skips, p)
            skip_sum = jnp.sum(dy_wide * x, axis=0, keepdims=True)
            if q == 0:
                dskip_ref[:, lanes] = jnp.broadcast_to(skip_sum, (8, LANES))
            else:
                dskip_ref[:, lanes] += skip_sum
        u_ref[here, :] = u_here

    @pl.when(g == GROUPS - 1)
    def _():
        tri = lower_triangle()
        for q in range(2):
            b, c = half(bca[:, :STATE], q).astype(BF16), half(bca[:, STATE:], q).astype(BF16)
            ds_t = dscores[q] * tri.T
            dbc_ref[q * HALF : (q + 1) * HALF, :STATE] = dot(ds_t.astype(BF16), c)
            dbc_ref[q * HALF : (q + 1) * HALF, STATE:] = dot(ds_t.T.astype(BF16), b)


def inside_back(dy, xa, bca, cum, dt, hpar):
    return pl.pallas_call(
        inside_back_body,
        grid=(GROUPS,),
        out_shape=(
            shape((ROWS, LOCAL)),
            shape((8, LOCAL)),
            shape((8 * GROUPS, ROWS)),
            shape((ROWS, LANES)),
            shape((ROWS, 256)),
        ),
        in_specs=[
            columns(ROWS, BLOCK),
            columns(ROWS, BLOCK),
            whole((ROWS, 256)),
            whole((ROWS, LANES)),
            whole((ROWS, LANES)),
            whole((8, LANES)),
        ],
        out_specs=(
            columns(ROWS, BLOCK),
            columns(8, BLOCK),
            pl.BlockSpec((8, ROWS), lambda g: (g, 0)),
            whole((ROWS, LANES)),
            whole((ROWS, 256)),
        ),
        scratch_shapes=[
            pltpu.VMEM((LANES, ROWS), F32),
            pltpu.VMEM((2, HALF, HALF), F32),
            pltpu.VMEM((2, HALF, HALF), F32),
        ],
        compiler_params=params(),
        cost_estimate=pl.CostEstimate(
            flops=4 * HEADS * HALF * HALF * LANES, bytes_accessed=4_500_000, transcendentals=800_000
        ),
        name="inside_back",
    )(dy, xa, bca, cum, dt, hpar)


def conv_back(d_active, values, halo, cpar, keep, ext, ext_d):
    width = values.shape[1]
    total = conv_sum_of(values, halo, cpar, keep, ext)
    sig = sigmoid(total)
    d_sum = d_active * sig * (1.0 + total * (1.0 - sig))
    ext_d[0:16, :width] = jnp.zeros((16, width), F32)
    ext_d[16 : 16 + ROWS, :width] = d_sum
    ext_d[16 + ROWS :, :width] = jnp.zeros((16, width), F32)
    d_in = jnp.zeros((ROWS + 16, width), F32)
    for k in range(KERNEL):
        d_in = d_in + cpar[k : k + 1, :] * ext_d[3 - k : 3 - k + ROWS + 16, :width]
    row = row_of((8, width))
    d_par = jnp.where(row == 4, jnp.sum(d_sum, axis=0, keepdims=True), 0.0)
    for k in range(KERNEL):
        tap = jnp.sum(d_sum * ext[13 + k : 13 + k + ROWS, :width], axis=0, keepdims=True)
        d_par = jnp.where(row == k, tap, d_par)
    return d_in, d_par


def finish_body(
    info, xa, dxi, dy, mixed, halo, cpar, bc, halo_bc, cpar_bc, bca, cum, dt, rate, hpar, lam, hin, s0, own1, u, gsum, dbc,
    dmx_ref, dmbc_ref, tailx_ref, tailbc_ref, edgex_ref, edgebc_ref, dcx_ref, dcbc_ref, dhead_ref,
    ext, ext_d, grow, tail, v_sum, q_sum, end_sum, dbc_sum,
):
    g = pl.program_id(0)
    keep = info[1].astype(F32)

    @pl.when(g == 0)
    def _():
        grow[...] = jnp.exp(cum[...])
        for q in range(2):
            here = half(cum[...], q)
            tail[q * HALF : (q + 1) * HALF, :] = jnp.exp(here[HALF - 1 :, :] - here)
        v_sum[...] = jnp.zeros((ROWS, LANES), F32)
        q_sum[...] = jnp.zeros((ROWS, LANES), F32)
        end_sum[...] = jnp.zeros((16, LANES), F32)
        dbc_sum[...] = dbc[...]

    sums = head_sum_matrix(g)
    factor = rolled(grow[...], g)
    tails = rolled(tail[...], g)
    steps = rolled(dt[...], g)
    ends = [spread(factor[HALF - 1 : HALF]), spread(factor[ROWS - 1 : ROWS])]
    lam1 = lam[0].astype(F32)
    lams = [ends[1] * lam1 + own1[0], lam1]
    first = hin[0].astype(F32)
    states = [first, ends[0] * first + s0[0]]
    d_x = []
    for q in range(2):
        here = slice(q * HALF, (q + 1) * HALF)
        b, c = bca[here, :STATE].astype(BF16), bca[here, STATE:].astype(BF16)
        lam_q, state_q = lams[q].astype(BF16), states[q].astype(BF16)
        tail_wide = spread(half(tails, q))
        tail_step = tail_wide * spread(half(steps, q))
        x, dy_q = xa[here, :], dy[here, :].astype(F32)
        lb = dot(b, lam_q) * tail_wide
        d_x.append(dxi[here, :] + lb * spread(half(steps, q)))
        v_sum[here, :] += dot((x * lb).astype(BF16), sums)
        grow_wide = spread(half(factor, q))
        dy_grow = (dy_q * grow_wide).astype(BF16)
        carried = dot(c, state_q)
        q_sum[here, :] += dot((dy_q * grow_wide * carried).astype(BF16), sums)
        dbc_sum[here, :STATE] += dot_nt((x * tail_step).astype(BF16), lam_q)
        dbc_sum[here, STATE:] += dot_nt(dy_grow, state_q)
        last = jnp.sum(lams[q] * states[q], axis=0, keepdims=True) * ends[q]
        high = last.astype(BF16).astype(F32)
        both = jnp.where(row_of((16, BLOCK)) == 0, high, last - high).astype(BF16)
        both = dot(both, sums)
        end_sum[8 * q : 8 * q + 8, :] += both[0:1] + both[1:2]
    d_in, d_par = conv_back(
        jnp.concatenate(d_x, axis=0), mixed[...], halo[...], cpar[...], keep, ext, ext_d
    )
    dmx_ref[...] = d_in[16:].astype(BF16)
    tailx_ref[...] = d_in[ROWS:]
    edgex_ref[...] = (d_in[:16] * keep).astype(BF16)
    dcx_ref[...] = d_par

    @pl.when(g == GROUPS - 1)
    def _():
        d_bc, d_par_bc = conv_back(
            dbc_sum[...], bc[...], halo_bc[...], cpar_bc[...], keep, ext, ext_d
        )
        dmbc_ref[:, :256] = d_bc[16:].astype(BF16)
        tailbc_ref[...] = d_bc[ROWS:]
        edgebc_ref[...] = (d_bc[:16] * keep).astype(BF16)
        dcbc_ref[...] = d_par_bc
        rates = -jnp.exp(hpar[1:2, :])
        logit = rate[...] + hpar[0:1, :]
        upper = lower_triangle().T
        before = lower_triangle(True)
        d_bias = jnp.zeros((1, LANES), F32)
        d_log = jnp.zeros((1, LANES), F32)
        usable = usable_rows(info)
        for q in range(2):
            here = slice(q * HALF, (q + 1) * HALF)
            step = dt[here, :]
            gs = gsum[...][:, here].T
            gs = jnp.concatenate([gs, jnp.zeros((HALF, LANES - 8 * GROUPS), F32)], axis=1)
            d_decay = exact_dot(upper, gs - step * u[here, :] + q_sum[here, :])
            d_decay = d_decay + exact_dot(before, step * v_sum[here, :])
            d_decay = d_decay + end_sum[8 * q : 8 * q + 1, :]
            d_step = u[here, :] + v_sum[here, :] + rates * d_decay
            d_rate = half(usable, q) * d_step * sigmoid(half(logit, q))
            d_bias += jnp.sum(d_rate, axis=0, keepdims=True)
            d_log += jnp.sum(d_decay * step * rates, axis=0, keepdims=True)
            dmbc_ref[here, 256:] = d_rate.astype(BF16)
        row = row_of((8, LANES))
        dhead_ref[...] = jnp.where(row == 0, d_bias, jnp.where(row == 1, d_log, 0.0))


def finish_call(
    info, xa, dxi, dy, mixed, halo, cpar, bca, cum, dt, rate, hpar, lam, hin, s0, own1, u, gsum, dbc
):
    bc_at = LOCAL // 256
    wide = whole((ROWS, LANES))
    return pl.pallas_call(
        finish_body,
        grid=(GROUPS,),
        out_shape=(
            shape((ROWS, LOCAL), BF16),
            shape((ROWS, 384), BF16),
            shape((16, LOCAL)),
            shape((16, 256)),
            shape((16, LOCAL), BF16),
            shape((16, 256), BF16),
            shape((8, LOCAL)),
            shape((8, 256)),
            shape((8, LANES)),
        ),
        in_specs=[
            SMEM,
            columns(ROWS, BLOCK),
            columns(ROWS, BLOCK),
            columns(ROWS, BLOCK),
            columns(ROWS, BLOCK),
            columns(16, BLOCK),
            columns(8, BLOCK),
            pl.BlockSpec((ROWS, 256), lambda g: (0, bc_at)),
            pl.BlockSpec((16, 256), lambda g: (0, bc_at)),
            pl.BlockSpec((8, 256), lambda g: (0, bc_at)),
            whole((ROWS, 256)),
            wide,
            wide,
            wide,
            whole((8, LANES)),
            grouped(STATE),
            grouped(STATE),
            grouped(STATE),
            grouped(STATE),
            wide,
            whole((8 * GROUPS, ROWS)),
            whole((ROWS, 256)),
        ],
        out_specs=(
            columns(ROWS, BLOCK),
            whole((ROWS, 384)),
            columns(16, BLOCK),
            whole((16, 256)),
            columns(16, BLOCK),
            whole((16, 256)),
            columns(8, BLOCK),
            whole((8, 256)),
            whole((8, LANES)),
        ),
        scratch_shapes=[
            pltpu.VMEM((ROWS + 32, BLOCK), F32),
            pltpu.VMEM((ROWS + 32, BLOCK), F32),
            pltpu.VMEM((ROWS, LANES), F32),
            pltpu.VMEM((ROWS, LANES), F32),
            pltpu.VMEM((ROWS, LANES), F32),
            pltpu.VMEM((ROWS, LANES), F32),
            pltpu.VMEM((16, LANES), F32),
            pltpu.VMEM((ROWS, 256), F32),
        ],
        compiler_params=params(),
        cost_estimate=pl.CostEstimate(
            flops=10 * ROWS * STATE * LOCAL, bytes_accessed=7_500_000, transcendentals=800_000
        ),
        name="finish_back",
    )(
        info, xa, dxi, dy, mixed, halo, cpar, mixed, halo, cpar, bca, cum, dt, rate, hpar,
        lam, hin, s0, own1, u, gsum, dbc,
    )


def gate_in_back_body(weight, info, dz, token, *rest):
    refs = len(weight.arrays)
    w_refs, (out_ref, buffer, sems) = rest[:refs], rest[refs:]

    @pl.when(pl.program_id(0) == 0)
    def _():
        weight.start(w_refs, info, buffer, sems)
        for n in range(4):
            weight.wait(w_refs, info, n, buffer, sems)

    rows = pl.ds(pl.multiple_of(pl.program_id(0) * SHARD, SHARD), SHARD)
    out_ref[...] = dot_nt(dz[...], buffer[rows, :])


def gate_in_back(info, dz, weight, token):
    return pl.pallas_call(
        functools.partial(gate_in_back_body, weight),
        grid=(4,),
        out_shape=shape((ROWS, WIDTH)),
        in_specs=[SMEM, whole((ROWS, LOCAL)), ANYWHERE] + weight.specs(),
        out_specs=columns(ROWS, SHARD),
        scratch_shapes=weight.scratch(),
        compiler_params=params(),
        cost_estimate=pl.CostEstimate(
            flops=2 * ROWS * WIDTH * LOCAL, bytes_accessed=7_000_000, transcendentals=0
        ),
        name="gate_in_back",
    )(info, dz, token, *weight.arrays)


def patch_body(dmx, dmbc, tailx, tailbc, edge, token, dxc_ref):
    dxc_ref[:, :LOCAL] = dmx[...]
    dxc_ref[:, LOCAL:] = dmbc[...]
    late = edge[...].astype(F32)
    dxc_ref[ROWS - 16 :, :LOCAL] = (tailx[...] + late[:, :LOCAL]).astype(BF16)
    dxc_ref[ROWS - 16 :, LOCAL:MIXED] = (tailbc[...] + late[:, LOCAL:]).astype(BF16)


def patch(dmx, dmbc, tailx, tailbc, edge, token):
    arrays = (dmx, dmbc, tailx, tailbc, edge)
    return pl.pallas_call(
        patch_body,
        out_shape=shape((ROWS, PACKED), BF16),
        in_specs=[whole(v.shape) for v in arrays] + [ANYWHERE],
        out_specs=whole((ROWS, PACKED)),
        compiler_params=params(),
        cost_estimate=pl.CostEstimate(flops=100_000, bytes_accessed=2_000_000, transcendentals=0),
        name="patch",
    )(*arrays, token)


def mixed_back_body(weight, tokens, info, dxc, part, h_ref, normed, *rest):
    refs = len(weight.arrays)
    w_refs, rest = rest[:refs], rest[refs + tokens :]
    (out_ref, dgain_ref, *grad_ref), (buffer, sems, scale_ref) = rest[:-3], rest[-3:]
    b = pl.program_id(0)
    block = pl.ds(pl.multiple_of(b * SHARD, SHARD), SHARD)

    @pl.when(b == 0)
    def _():
        weight.start(w_refs, info, buffer, sems)
        h = h_ref[...].astype(F32)
        scale = lax.rsqrt(jnp.mean(h * h, axis=1, keepdims=True) + EPSILON)
        scale_ref[...] = jnp.broadcast_to(scale, (ROWS, LANES))

    for ref in grad_ref:
        ref[...] = dot(normed[...].T, dxc[...]).astype(BF16)

    @pl.when(b == 0)
    def _():
        for n in range(4):
            weight.wait(w_refs, info, n, buffer, sems)

    d_norm = part[...] + dot_nt(dxc[...], buffer[block, :])
    out_ref[...] = d_norm.astype(BF16)
    total = jnp.sum(d_norm * h_ref[:, block].astype(F32) * scale_ref[:, :1], axis=0, keepdims=True)
    dgain_ref[...] = jnp.broadcast_to(total, (8, SHARD))


def mixed_back(info, dxc, part, h, normed, weight, with_grad, tokens):
    wide, local = whole((ROWS, WIDTH)), columns(ROWS, SHARD)
    outs = [shape((ROWS, WIDTH), BF16), shape((8, WIDTH))]
    specs = [local, columns(8, SHARD)]
    if with_grad:
        outs.append(shape((WIDTH, PACKED), BF16))
        specs.append(pl.BlockSpec((SHARD, PACKED), lambda b: (b, 0)))
    return pl.pallas_call(
        functools.partial(mixed_back_body, weight, len(tokens)),
        grid=(4,),
        out_shape=outs,
        in_specs=[SMEM, whole((ROWS, PACKED)), local, wide, local]
        + weight.specs()
        + [ANYWHERE] * len(tokens),
        out_specs=specs,
        scratch_shapes=weight.scratch() + [pltpu.VMEM((ROWS, LANES), F32)],
        compiler_params=params(),
        cost_estimate=pl.CostEstimate(
            flops=4 * ROWS * WIDTH * PACKED, bytes_accessed=14_000_000, transcendentals=0
        ),
        name="mixed_back",
    )(info, dxc, part, h, normed, *weight.arrays, *tokens)


def norm_back_body(own, came, h_ref, cot, gain, dh_ref, low_ref):
    h = h_ref[...].astype(F32)
    scale = lax.rsqrt(jnp.mean(h * h, axis=1, keepdims=True) + EPSILON)
    d_norm = own[...].astype(F32) + came[...].astype(F32)
    inner = jnp.mean(d_norm * gain[...] * h, axis=1, keepdims=True) * scale * scale * scale
    dh = cot[...].astype(F32) + scale * d_norm * gain[...] - h * inner
    dh_ref[...] = dh
    low_ref[...] = dh.astype(BF16)


def norm_back(own, came, h, cot, gain):
    rows = pl.BlockSpec((HALF // 2, WIDTH), lambda i: (i, 0))
    return pl.pallas_call(
        norm_back_body,
        grid=(4,),
        out_shape=(shape((ROWS, WIDTH)), shape((ROWS, WIDTH), BF16)),
        in_specs=[rows] * 4 + [whole((1, WIDTH))],
        out_specs=(rows, rows),
        compiler_params=params(),
        cost_estimate=pl.CostEstimate(flops=3_000_000, bytes_accessed=8_000_000, transcendentals=0),
        name="norm_back",
    )(own, came, h, cot, gain)


def z_shift(r):
    return "dp", [(z, (z + r) % 4) for z in range(4)]


def y_shift(r):
    return "ctx", [(j, (j + 4 * r) % 16) for j in range(16)]


def x_shift(r):
    return "ctx", [(j, j - j % 4 + (j + r) % 4) for j in range(16)]


SHIFTS = {"z": z_shift, "y": y_shift, "x": x_shift}


def send(value, axis, r):
    name, pairs = SHIFTS[axis](r % 4)
    return lax.ppermute(value, name, pairs)


def swapped(value):
    return lax.ppermute(value, "section", [(0, 1), (1, 0)])


def nothing_body(*refs):
    refs[-1][0] = jnp.int32(0)


def after(values, place):
    nothing = pl.pallas_call(
        nothing_body,
        out_shape=shape((1,), jnp.int32),
        in_specs=[ANYWHERE] * len(values),
        out_specs=SMEM,
        compiler_params=params(),
        cost_estimate=pl.CostEstimate(flops=0, bytes_accessed=4096, transcendentals=0),
        name="after",
    )(*values)[0]
    return {axis: n + nothing for axis, n in place.items()}


def fetched(mine, came, layer, section, place):
    rows = SHARD // 2

    def piece(source, side, axis):
        return lax.dynamic_slice_in_dim(source, side * rows + place[axis] * PIECE, PIECE, 0)

    parts = [
        jnp.where(section == layer, piece(mine, side, axis), piece(came, side, axis))
        for side, axis in enumerate("xy")
    ]
    if mine.shape[0] == TALL:
        parts.append(jnp.where(section == layer, mine[SHARD:], came[SHARD:]))
    return jnp.concatenate(parts)


def pieces(mine, came, got, late):
    out = [mine, came]
    for side, axis in enumerate("xy"):
        rows = slice(side * PIECE, (side + 1) * PIECE)
        stack = jnp.concatenate(
            [lax.dynamic_slice_in_dim(g, rows.start + late, PIECE, 0) for g in got[1:]]
        )
        out += [stack] + [send(stack, axis, -r) for r in range(1, 4)]
    return out


def summed(terms):
    a, b, c, d = (t.astype(F32) for t in terms)
    return (a + c) + (b + d)


def arrived(terms, axis):
    return [terms[0]] + [send(terms[r], axis, r) for r in range(1, 4)]


def terms_body(axis, cuts, stacked, info, *rest):
    factors, rest = rest[: 2 * len(cuts)], rest[2 * len(cuts) :]
    small, outs, total = rest[:-2] if stacked else rest[:-5], rest[-5:-1], rest[-1]
    column = 0
    for n, cols in enumerate(cuts):
        there = slice(column, column + cols.stop - cols.start)
        total[:, there] = dot(factors[2 * n][...], factors[2 * n + 1][:, cols])
        column = there.stop
    count = 96 if axis == "y" else 24
    starts = [z * SHARD for z in range(4)]
    if axis == "x":
        starts = [start + y * 96 for start in starts for y in range(4)]
    for r in range(4):
        first = r * count
        if not stacked:
            first = lax.rem(info[11 if axis == "y" else 12] + r, 4) * count
        parts = [total[pl.ds(pl.multiple_of(start + first, 8), count), :] for start in starts]
        out = rest[-2].at[r] if stacked else outs[r]
        out[:SHARD, :] = jnp.concatenate(parts, axis=0).astype(BF16)
        for ref in small:
            out[SHARD:, :] = ref[...]


def four(dims, stacked):
    if stacked:
        return shape((4, *dims), BF16), whole((4, *dims))
    return [shape(dims, BF16)] * 4, [whole(dims)] * 4


def terms(info, axis, products, small=(), stacked=False):
    cuts = [cols for _, _, cols in products]
    width = sum(cols.stop - cols.start for cols in cuts)
    rows = SHARD + sum(v.shape[0] for v in small)
    arrays = [v for left, right, _ in products for v in (left, right)] + list(small)
    outs, specs = four((rows, width), stacked)
    return pl.pallas_call(
        functools.partial(terms_body, axis, cuts, stacked),
        out_shape=outs,
        in_specs=[SMEM] + [whole(v.shape) for v in arrays],
        out_specs=specs,
        scratch_shapes=[pltpu.VMEM((4 * SHARD, width), F32)],
        compiler_params=params(),
        cost_estimate=pl.CostEstimate(
            flops=8 * SHARD * ROWS * width, bytes_accessed=8_000_000, transcendentals=0
        ),
        name="terms",
    )(info, *arrays)


def fold_body(slot, counts, outer, inner, rest_rows, stacked, info, *rest):
    refs, outs, total = rest[: sum(counts)], rest[-2:-1] if stacked else rest[-5:-1], rest[-1]
    column = 0
    for count in counts:
        arrays, refs = refs[:count], refs[count:]
        cols = slice(column, column + arrays[0].shape[-1])
        if count == 4:
            total[:, cols] = summed([a[...] for a in arrays])
        elif len(arrays[0].shape) == 3:
            total[:, cols] = summed([arrays[0][n] for n in range(4)])
        else:
            total[:, cols] = arrays[0][...].astype(F32)
        column = cols.stop
    for r in range(4):
        first = r * inner if stacked else lax.rem(info[slot] + r, 4) * inner
        parts = [
            total[pl.ds(pl.multiple_of(n * 4 * inner + first, 8), inner), :] for n in range(outer)
        ]
        if rest_rows:
            parts.append(total[4 * outer * inner :, :])
        out = outs[0].at[r] if stacked else outs[r]
        out[...] = jnp.concatenate(parts, axis=0).astype(BF16)


def fold(info, axis, groups, outer, inner, token, stacked=False):
    slot = 10 + "zyx".index(axis)
    arrays = [a for group in groups for a in group]
    tokens = token if isinstance(token, tuple) else (token,)
    rows, width = arrays[0].shape[-2], sum(group[0].shape[-1] for group in groups)
    more = rows - 4 * outer * inner
    outs, specs = four((outer * inner + more, width), stacked)
    counts = [len(group) for group in groups]
    return pl.pallas_call(
        functools.partial(fold_body, slot, counts, outer, inner, more, stacked),
        out_shape=outs,
        in_specs=[SMEM] + [whole(a.shape) for a in arrays] + [ANYWHERE] * len(tokens),
        out_specs=specs,
        scratch_shapes=[pltpu.VMEM((rows, width), F32)],
        compiler_params=params(),
        cost_estimate=pl.CostEstimate(flops=2_000_000, bytes_accessed=8_000_000, transcendentals=0),
        name="fold",
    )(info, *arrays, *tokens)


def last_fold_body(info, *rest):
    left, right, outs, total = rest[:4], rest[4:8], rest[9:13], rest[13]
    width = left[0].shape[1]
    total[:96, :width] = summed([a[...] for a in left])
    total[96:, :width] = jnp.zeros((SMALL, width), F32)
    total[:, width:] = summed([a[...] for a in right])
    for r in range(4):
        first = pl.multiple_of(lax.rem(info[10] + r, 4) * 24, 8)
        parts = [total[pl.ds(first, 24), :], total[96:, :]]
        outs[r][...] = jnp.concatenate(parts, axis=0).astype(BF16)


def last_fold(info, left, right, token):
    width = left[0].shape[1] + right[0].shape[1]
    out = shape((24 + SMALL, width), BF16)
    arrays = (*left, *right)
    return pl.pallas_call(
        last_fold_body,
        out_shape=[out] * 4,
        in_specs=[SMEM] + [whole(a.shape) for a in arrays] + [ANYWHERE],
        out_specs=[whole(out.shape)] * 4,
        scratch_shapes=[pltpu.VMEM((96 + SMALL, width), F32)],
        compiler_params=params(),
        cost_estimate=pl.CostEstimate(flops=500_000, bytes_accessed=2_000_000, transcendentals=0),
        name="last_fold",
    )(info, *arrays, token)


PARITY = [[j for j in range(16) if j % 2 == e] for e in range(2)]
NEIGHBOURS = [(j, j ^ 1) for j in range(16)]
GROUPS_OF = {
    "y": [[4 * y + x for y in range(4)] for x in range(4)],
    "x": [[4 * y + x for x in range(4)] for y in range(4)],
}


def traded(value, axis):
    return lax.all_to_all(value, "ctx", 0, 0, axis_index_groups=GROUPS_OF[axis])


def exchange(value):
    return lax.all_to_all(value, "ctx", 0, 0, axis_index_groups=PARITY)


def halo_shift(value, step):
    pairs = [(j, j + 2 * step) for j in range(16) if 0 <= j + 2 * step < 16]
    return lax.ppermute(value, "ctx", pairs)


def halves(values, section):
    grid = values.reshape(values.shape[0], GROUPS, 2, -1)
    size = values.shape[1] // 2
    return [
        lax.dynamic_index_in_dim(grid, i, 2, False).reshape(-1, size)
        for i in (section, 1 - section)
    ]


def turns(low, high):
    rows = low.shape[0]
    parts = [v.reshape(rows, GROUPS, 1, -1) for v in (low, high)]
    return jnp.concatenate(parts, axis=2).reshape(rows, -1)


def pick_x_body(info, x_ref, dt_ref, *rest):
    smalls, outs, small = rest[:7], rest[7:9], rest[9]
    small[...] = jnp.zeros((16, PACKED), F32)
    row = 0
    for ref in smalls[:4]:
        count, width = ref.shape
        small[row : row + count, :width] = ref[...].astype(F32)
        row += count
    for ref in smalls[4:]:
        left = ref[...]
        for _ in range(3):
            part = left.astype(BF16).astype(F32)
            small[row : row + 1, :HEADS] = part
            left = left - part
            row += 1
    head, lane = row_of((HEADS, LANES)), lane_of((HEADS, LANES))
    for out, side in zip(outs, (info[0], 1 - info[0]), strict=True):
        for d in range(GROUPS):
            cols = pl.ds(pl.multiple_of((2 * d + side) * BLOCK, LANES), BLOCK)
            out[:SHARD, d * BLOCK : (d + 1) * BLOCK] = x_ref[:, cols]
        out[:SHARD, LOCAL:MIXED] = x_ref[:, INNER:]
        here = (head // OWN == 2 * (lane // 8) + side) & (head % OWN == lane % 8)
        out[:SHARD, MIXED:] = dot(dt_ref[...], here.astype(BF16)).astype(BF16)
        out[SHARD:, :] = small[...].astype(BF16)


def pick_x(section, x, dt, smalls):
    return pl.pallas_call(
        pick_x_body,
        out_shape=[shape((TALL, PACKED), BF16)] * 2,
        in_specs=[SMEM, whole((SHARD, CONV_CH)), whole((SHARD, HEADS))]
        + [whole(v.shape) for v in smalls],
        out_specs=[whole((TALL, PACKED))] * 2,
        scratch_shapes=[pltpu.VMEM((16, PACKED), F32)],
        compiler_params=params(),
        cost_estimate=pl.CostEstimate(flops=0, bytes_accessed=6_000_000, transcendentals=0),
        name="pick_x",
    )(section, x, dt, *smalls)


def unpack_body(count, info, *rest):
    refs, (cpar, gain_one, gain_two, hpar, held, full, sems) = rest[:count], rest[count:]
    copies = []
    for n in range(4):
        if count == 4:
            source, to = refs[n].at[pl.ds(2 * PIECE, 16)], lax.rem(info[10] + n, 4)
        else:
            source, to = refs[0].at[pl.ds(n * TALL + SHARD, 16)], n
        copies.append(pltpu.make_async_copy(source, held.at[to], sems.at[n]))
    for c in copies:
        c.start()
    for c in copies:
        c.wait()
    section = info[13]
    half_cols = pl.ds(pl.multiple_of(section * BLOCK, LANES), BLOCK)
    for z in range(4):
        values = held[z].astype(F32)
        full[:, z * 832 : (z + 1) * 832] = values[:8, :832]
        gain_one[:, z * SHARD : (z + 1) * SHARD] = values[5:6, :SHARD]
        gain_two[:, z * BLOCK : (z + 1) * BLOCK] = held[z, :, half_cols].astype(F32)[6:7]
    for d in range(GROUPS):
        cols = pl.ds(pl.multiple_of((2 * d + section) * BLOCK, LANES), BLOCK)
        cpar[:, d * BLOCK : (d + 1) * BLOCK] = full[:, cols]
    cpar[:, LOCAL:] = full[:, INNER:]
    values = held[0, :, :LANES].astype(F32)
    heads = [values[n : n + 1] + values[n + 1 : n + 2] + values[n + 2 : n + 3] for n in (7, 10, 13)]
    heads = jnp.concatenate(heads + [jnp.zeros((5, LANES), F32)], axis=0)
    head, lane = row_of((LANES, LANES)), lane_of((LANES, LANES))
    here = (head // OWN == 2 * (lane // 8) + section) & (head % OWN == lane % 8)
    hpar[...] = exact_dot(heads, here.astype(F32))


def unpack(info, arrays):
    shapes = ((8, MIXED), (1, WIDTH), (1, LOCAL), (8, LANES))
    return pl.pallas_call(
        functools.partial(unpack_body, len(arrays)),
        out_shape=[shape(dims) for dims in shapes],
        in_specs=[SMEM] + [ANYWHERE] * len(arrays),
        out_specs=[whole(dims) for dims in shapes],
        scratch_shapes=[
            pltpu.VMEM((4, 16, PACKED), BF16),
            pltpu.VMEM((8, CONV_CH), F32),
            pltpu.SemaphoreType.DMA((4,)),
        ],
        compiler_params=params(),
        cost_estimate=pl.CostEstimate(flops=0, bytes_accessed=400_000, transcendentals=0),
        name="unpack",
    )(info, *arrays)


def pick_zo_body(info, z_ref, o_ref, token, *outs):
    for out, side in zip(outs, (info[0], 1 - info[0]), strict=True):
        for d in range(GROUPS):
            cols = pl.ds(pl.multiple_of((2 * d + side) * BLOCK, LANES), BLOCK)
            out[:, d * BLOCK : (d + 1) * BLOCK] = z_ref[:, cols]
        rows = pl.ds(pl.multiple_of(side * SHARD, SHARD), SHARD)
        out[:, LOCAL:] = o_ref[rows, :]


def pick_zo(section, z, o, token):
    return pl.pallas_call(
        pick_zo_body,
        out_shape=[shape((SHARD, LOCAL + WIDTH), BF16)] * 2,
        in_specs=[SMEM, whole((SHARD, INNER)), whole((2 * SHARD, WIDTH)), ANYWHERE],
        out_specs=[whole((SHARD, LOCAL + WIDTH))] * 2,
        compiler_params=params(),
        cost_estimate=pl.CostEstimate(flops=0, bytes_accessed=9_000_000, transcendentals=0),
        name="pick_zo",
    )(section, z, o, token)


def head_lanes(values):
    rows = values.shape[0]
    grid = jnp.pad(values.reshape(rows, GROUPS, OWN), ((0, 0), (0, 0), (0, 8 - OWN)))
    return jnp.pad(grid.reshape(rows, 8 * GROUPS), ((0, 0), (0, LANES - 8 * GROUPS)))


def lanes_heads(values):
    rows = values.shape[0]
    return values[:, : 8 * GROUPS].reshape(rows, GROUPS, 8)[:, :, :OWN].reshape(rows, -1)


def on_device(
    boundary,
    lengths,
    norm_gain,
    w_z,
    w_xbc,
    w_dt,
    conv_weight,
    conv_bias,
    dt_bias,
    a_log,
    d_skip,
    gate_gain,
    w_out,
):
    section = lax.axis_index("section")
    group = lax.axis_index("dp")
    ctx = lax.axis_index("ctx")
    place = {"z": group, "y": ctx // 4, "x": ctx % 4}
    micro = ctx % 2
    chunk = ctx // 2

    def ordered(mine, came):
        return jnp.where(section == 0, mine, came), jnp.where(section == 0, came, mine)

    own_rows = lax.dynamic_index_in_dim(boundary[0], micro, 0, False)
    other_rows = lax.dynamic_index_in_dim(boundary[0], 1 - micro, 0, False)
    came = lax.ppermute(other_rows, "ctx", NEIGHBOURS)
    block = jnp.where(
        micro == 0, jnp.concatenate([own_rows, came]), jnp.concatenate([came, own_rows])
    )
    hidden, cotangent = ordered(block, swapped(block))

    pair = lengths[group, micro]
    padded = (pair[0] + SPAN - 1) // SPAN * SPAN
    offset = chunk * ROWS
    begin = jnp.where(offset >= padded, padded, 0)
    length = jnp.where(offset >= padded, pair[1], pair[0])
    live = jnp.clip(length - (offset - begin), 0, ROWS)
    offsets = jnp.arange(CHUNKS, dtype=jnp.int32) * ROWS
    keeps = ((offsets != 0) & (offsets != padded)).astype(jnp.int32)
    keep = (offset != 0) & (offset != padded)
    at = [place["z"], place["y"], place["x"], section]
    info = jnp.concatenate(
        [jnp.stack([live, keep]).astype(jnp.int32), keeps, jnp.stack(at).astype(jnp.int32)]
    )

    def forward(h, layer):
        cpar, hpar = cpars[layer], hpars[layer]
        normed, mixed, rate = in_proj(
            info, h, gains_one[layer], weights_x[layer], []
        )
        halo = halo_shift(mixed[ROWS - 16 :], 1)
        gate = gate_proj(info, normed, weights_z[layer], [] if layer else ready)
        xa, bca, cum, dt, s0, msg = state_call(info, mixed, halo, cpar, rate, hpar)
        came = exchange(msg)
        y_in = inside_call(xa, bca, cum, dt, hpar)
        hin = exchange(scan_call(info, came, False, y_in, *([] if layer else cpars[1:]))).reshape(GROUPS, STATE, BLOCK)
        y, part = out_proj(
            info, y_in, bca, cum, hin, s0, gate, gains_two[layer], weights_o[layer]
        )
        result, branch, scale = join(info, h, part, swapped(part), F32 if layer else BF16)
        saved = (h, normed, mixed, halo, rate, gate, xa, bca, cum, dt, s0, msg, hin, y, branch, scale)
        return result, saved

    def backward(cot, saved, layer, higher, tokens):
        h, normed, mixed, halo, rate, gate, xa, bca, cum, dt, s0, msg, hin, y, branch, scale = saved
        cpar, hpar = cpars[layer], hpars[layer]

        def first_stage(value):
            return lax.psum_scatter(value, "dp", tiled=True)

        bg, dy, dz, grad_o, d_gain_two = gate_back(
            info, cot, y, gate, gains_two[layer], branch, scale, weights_o[layer], layer == 1
        )
        own1, msg_back, grad_z = own_grad(dy, bca, cum, msg, dz, normed)
        sums = [first_stage(grad_z)] + ([first_stage(grad_o)] if layer else [])
        came = exchange(msg_back)
        dxi, d_skips, gsum, u, dbc = inside_back(dy, xa, bca, cum, dt, hpar)
        part = gate_in_back(info, dz, weights_z[layer], msg_back)
        lam = exchange(scan_call(info, came, True, part)).reshape(GROUPS, STATE, BLOCK)
        dmx, dmbc, tailx, tailbc, edgex, edgebc, d_parx, d_parbc, d_heads = finish_call(
            info, xa, dxi, dy, mixed, halo, cpar, bca, cum, dt, rate, hpar, lam, hin, s0, own1, u, gsum, dbc
        )
        edge = halo_shift(jnp.concatenate([edgex, edgebc], axis=1), -1)
        dxc = patch(dmx, dmbc, tailx, tailbc, edge, *tokens)
        middle = 7 * LANES
        if layer == 0:
            higher_rows, higher = higher
            normed_t = normed.T
            cuts = [(normed_t, dxc, slice(0, middle)), (grad_o, bg, slice(0, WIDTH // 2))]
            left = terms(info, "y", cuts, (), True)
            part, d_gain_one = mixed_back(
                info, dxc, part, h, normed, weights_x[layer], False, [left, *higher]
            )
        else:
            part, d_gain_one, grad_x = mixed_back(
                info, dxc, part, h, normed, weights_x[layer], True, []
            )
        dh, dh_low = norm_back(part, swapped(part), h, cot, gains_one[layer])
        d_skip_row = jnp.sum(d_skips[0:1].reshape(1, 4 * OWN, HEADDIM), axis=2)
        rows = jnp.where(jnp.arange(8)[:, None] == 5, d_gain_two, d_parx)
        rows = jnp.concatenate([rows, d_parbc], axis=1)
        more = jnp.concatenate(
            [
                d_gain_one[:1],
                jnp.pad(d_heads[:2], ((0, 0), (0, WIDTH - LANES))),
                jnp.pad(head_lanes(d_skip_row), ((0, 4), (0, WIDTH - LANES))),
            ]
        )
        rows = jnp.concatenate([rows, jnp.pad(more, ((0, 0), (0, 2 * STATE)))])
        if layer == 1:
            return dh, dh_low, sums + [first_stage(grad_x)], rows

        rows = jnp.concatenate([rows, higher_rows]).astype(BF16)
        cuts = [(normed_t, dxc, slice(middle, PACKED)), (grad_o, bg, slice(WIDTH // 2, WIDTH))]
        right = arrived(terms(info, "x", cuts, (rows,)), "x")
        near = (right[1], right[3])
        tall = fold(info, "y", [[v] for v in higher + sums], 1, 96, near, True)
        left = fold(info, "x", [[traded(left, "y")]], 4, 24, tall)
        right = fold(info, "y", [right], 4, 24, dh_low)
        tall = fold(info, "x", [[traded(tall, "y")]], 1, 24, right[0])
        left, right = arrived(left, "x"), arrived(right, "y")
        final = summed(arrived(last_fold(info, left, right, tall[0]), "z"))
        left, right = left[0].shape[1], right[0].shape[1]
        rows = final[24:, left:]
        final = final[:24]
        sum_x = jnp.concatenate(
            [final[:, :middle], final[:, left : left + PACKED - middle]], axis=1
        )
        sum_o = jnp.concatenate([final[:, middle:left], final[:, left + PACKED - middle :]], axis=1)
        return dh, [arrived(tall, "x"), sum_o], sum_x, rows

    at = section.reshape(1).astype(jnp.int32)
    smalls = (conv_weight[0], conv_bias, norm_gain, gate_gain, dt_bias, a_log, d_skip)
    mine_x, other_x = pick_x(at, w_xbc[0], w_dt[0], smalls)
    came_x = swapped(other_x)
    mine_zo, other_zo = pick_zo(at, w_z[0], w_out[0], mine_x)
    came_zo = swapped(other_zo)
    first = fetched(mine_x, came_x, 0, section, after([hidden], place))
    got = [first] + [send(first, "z", -r) for r in range(1, 4)]
    small_low = got
    low_x = pieces(mine_x, came_x, got, 0)
    got = lax.all_gather(fetched(mine_zo, came_zo, 0, section, after(got[1:], place)), "dp")
    low_params = unpack(info, small_low)
    late = after([*low_x[3:6], *low_x[7:10], low_params[0]], place)["z"]
    got = [None] + [lax.dynamic_index_in_dim(got, (late + r) % 4, 0, False) for r in range(1, 4)]
    low_zo = pieces(mine_zo, came_zo, got, 0)
    here = after([low_x[2], low_x[6]], {"section": section})["section"]
    high_x = [lax.all_gather(jnp.where(here == 1, mine_x, came_x), "dp", tiled=True)]
    high_zo = [lax.all_gather(jnp.where(here == 1, mine_zo, came_zo), "dp", tiled=True)]
    ready = low_zo[3:6] + low_zo[7:10]
    weights_x = [Weight(v, n, PACKED) for n, v in enumerate((low_x, high_x))]
    weights_z = [Weight(v, n, LOCAL) for n, v in enumerate((low_zo, high_zo))]
    weights_o = [Weight(v, n, WIDTH, LOCAL) for n, v in enumerate((low_zo, high_zo))]

    unpacked = [low_params, unpack(info, high_x)]
    cpars, gains_one, gains_two, hpars = zip(*unpacked, strict=True)

    def returned(rows, layer):
        pairs = [(layer * 16 + a, layer * 16 + b) for a, b in NEIGHBOURS]
        other, mine = (
            lax.dynamic_slice_in_dim(rows, n * HALF, HALF, 0) for n in (1 - micro, micro)
        )
        other = lax.ppermute(other, ("section", "ctx"), pairs)
        return jnp.where(micro == 0, jnp.stack([mine, other]), jnp.stack([other, mine]))

    middle, saved_low = forward(hidden, 0)
    out_high, saved_high = forward(middle, 1)
    top_high = returned(out_high, 1)
    _, back, higher, rows = backward(cotangent, saved_high, 1, None, [top_high])
    dh_low, (tall, low_o), low_x, rows = backward(back, saved_low, 0, (rows, higher), [rows])
    at = (LOCAL, LOCAL + WIDTH, LOCAL + WIDTH + PACKED)
    high_z, high_o, high_x, low_z = jnp.split(summed(tall), at, axis=1)

    own, given = ordered(rows[:16], rows[16:])
    rows_0, rows_1 = ordered(own, swapped(given))
    wide = jnp.concatenate(
        [turns(rows_0[:8, :LOCAL], rows_1[:8, :LOCAL]), rows_0[:8, LOCAL:] + rows_1[:8, LOCAL:]],
        axis=1,
    )
    head_rows = turns(lanes_heads(rows_0[9:12, :LANES]), lanes_heads(rows_1[9:12, :LANES]))
    index = group * 16 + ctx
    d_conv = lax.dynamic_slice(wide, (0, index * 52), (5, 52))
    d_gain_two = lax.dynamic_slice(wide, (5, index * 48), (1, 48))
    d_gain_one = lax.dynamic_slice(rows_0[8:9] + rows_1[8:9], (0, index * 24), (1, 24))

    own, given = ordered(
        jnp.concatenate([low_z, low_x], axis=1), jnp.concatenate([high_z, high_x], axis=1)
    )
    first, second = ordered(own, swapped(given))
    sum_z = turns(first[:, :LOCAL], second[:, :LOCAL])
    at_x, at_bc, at_dt = LOCAL, LOCAL + LOCAL, LOCAL + MIXED
    sum_x = turns(first[:, at_x:at_bc], second[:, at_x:at_bc])
    sum_bc = first[:, at_bc:at_dt] + second[:, at_bc:at_dt]
    sum_dt = turns(lanes_heads(first[:, at_dt:]), lanes_heads(second[:, at_dt:]))

    trips = []
    for flip in range(2):
        pairs = [
            (c * 16 + j, (flip ^ (j % 2)) * 16 + 8 * c + j // 2) for c in range(2) for j in range(16)
        ]
        value = jnp.where(micro == flip, low_o, high_o)
        trips.append(lax.ppermute(value, ("section", "ctx"), pairs))
    sum_o = jnp.concatenate(ordered(*trips))

    top = jnp.where(section == 0, returned(dh_low, 0), top_high)
    return (
        top[None],
        d_gain_one,
        sum_z[None],
        jnp.concatenate([sum_x, sum_bc], axis=1)[None],
        sum_dt[None],
        d_conv[None, :4],
        d_conv[4:5],
        head_rows[0:1],
        head_rows[1:2],
        head_rows[2:3],
        d_gain_two,
        sum_o[None],
    )


def solution(mesh):
    in_specs = (
        P("section", None, ("dp", "ctx"), None),
        P(),
        P("section", "dp"),
        P("section", "dp", None),
        P("section", "dp", None),
        P("section", "dp", None),
        P("section", None, "dp"),
        P("section", "dp"),
        P("section", None),
        P("section", None),
        P("section", None),
        P("section", "dp"),
        P("section", "dp", None),
    )
    out_specs = (
        P("section", None, ("dp", "ctx"), None),
        P("section", ("dp", "ctx")),
        P("section", ("dp", "ctx"), None),
        P("section", ("dp", "ctx"), None),
        P("section", ("dp", "ctx"), None),
        P("section", None, ("dp", "ctx")),
        P("section", ("dp", "ctx")),
        P("section", None),
        P("section", None),
        P("section", None),
        P("section", ("dp", "ctx")),
        P("section", ("dp", "ctx"), None),
    )
    return jax.shard_map(
        on_device, mesh=mesh, in_specs=in_specs, out_specs=out_specs, check_vma=False
    )
```
